32 devices in a mesh: dp: 8 (over z, x), ctx: 4 (over y, core).
Axes of the slice: x: 2, y: 2, z: 4, core: 2. Of those that a mesh axis runs over, the one named last changes fastest.
Arguments:
- tokens: bfloat16 [2, 16384, 576], P(None, ('dp', 'ctx')), may hold values from -6 to 6
- lengths: int32 [2, 8, 4], P(None, 'dp'), may hold values from 1 to 2045, as said below
- weights: float32 [3538944], P(('dp', 'ctx'))
- momentum: float32 [3538944], P(('dp', 'ctx'))
- norm_gains: float32 [2, 576], replicated, may hold values from 0.5 to 1.5
- gain_first: float32 [2, 576], replicated, may hold values from -57.926186 to 57.926186
- gain_second: float32 [2, 576], replicated, may hold values from 425.984 to 6553.6
- cotangent: bfloat16 [2, 16384, 576], P(None, ('dp', 'ctx')), may hold values from -12 to 12
Outputs:
- outputs: float32 [2, 16384, 576], P(None, ('dp', 'ctx'))
- d_tokens: float32 [2, 16384, 576], P(None, ('dp', 'ctx'))
- weight_grads: float32 [3538944], P(('dp', 'ctx'))
- new_momentum: float32 [3538944], P(('dp', 'ctx'))
- new_weights: float32 [3538944], P(('dp', 'ctx'))
- gain_first_new: float32 [2, 576], replicated
- gain_second_new: float32 [2, 576], replicated
- new_gains: float32 [2, 576], replicated
The draws below stay inside these ranges and needn't reach their ends.
Inputs may be any that keep to these rules, and one draw needn't show every extreme that they name: Each row of lengths sums to 2048; its entry 1 equals 2048 minus the other three, and each other entry lies between 1 and 255. In every draw one buffer has all three other entries equal to 1.
All inputs are finite; a program needn't handle non-finite values.
Results may differ from the reference program's by a relative error of at most 0.015.
Values may be sent and summed in bfloat16 or wider, within the bound.
No kernel may reach another device: no remote copies, remote signals or barrier semaphores. Data moves between devices by JAX's collectives and lax.ppermute only.
A program may use at most 384 MiB of HBM per device.

```python
import math
import jax
import jax.numpy as jnp
from jax import lax

HEADS = 9
KV_HEADS = 3
HEAD_DIM = 64
FF = 1536
TOK_MB = 512
MB = 2
DOCS = 4
NS_STEPS = 5
ADAM_STEP = 10
D = 576
KV_WIDTH = 192
SEQ = 2048
ROWS = 16384
WEIGHT_ENTRIES = 3538944
TOKENS_ALL = 32768
N_DP = 8


def matrix_shapes_drawn():
    return [(D, D), (D, KV_WIDTH), (D, KV_WIDTH), (D, D), (D, FF), (D, FF), (FF, D)]


def draw_lengths(key, part):
    key = jax.random.fold_in(key, 11)
    short_key, pick_key = jax.random.split(key)
    shorter = jax.random.randint(short_key, (MB, N_DP, DOCS - 1), 1, TOK_MB // 2, dtype=jnp.int32)
    chosen = jax.random.randint(pick_key, (), 0, MB * N_DP, dtype=jnp.int32)
    buffer_ids = jnp.arange(MB * N_DP, dtype=jnp.int32).reshape(MB, N_DP, 1)
    shorter = jnp.where(buffer_ids == chosen, jnp.int32(1), shorter).astype(jnp.int32)
    longest = (SEQ - jnp.sum(shorter, axis=-1, keepdims=True)).astype(jnp.int32)
    return jnp.concatenate([shorter[..., :1], longest, shorter[..., 1:]], axis=-1).astype(jnp.int32)


def draw_weights(key, part):
    key = jax.random.fold_in(key, 23)
    spreads = [D ** (-0.5), D ** (-0.5), D ** (-0.5), (SEQ / 8.0) ** 0.5 * D ** (-0.5), D ** (-0.5), D ** (-0.5), FF ** (-0.5)]
    scaling = jnp.concatenate([jnp.full((height * breadth,), spread, jnp.float32) for (height, breadth), spread in zip(matrix_shapes_drawn(), spreads)])
    entries = jax.random.truncated_normal(key, -4.0, 4.0, (WEIGHT_ENTRIES,), jnp.float32)
    return entries * scaling


def draw_momentum(key, part):
    key = jax.random.fold_in(key, 37)
    pieces = []
    base_scale = 0.2 * TOKENS_ALL ** 0.5
    for matrix_index, (height, breadth) in enumerate(matrix_shapes_drawn()):
        row_key, column_key, entry_key = jax.random.split(jax.random.fold_in(key, matrix_index), 3)
        reach = 0.5 * math.log(10.0)
        entries = jax.random.truncated_normal(entry_key, -4.0, 4.0, (height, breadth), jnp.float32)
        row_scale = jnp.exp(jax.random.uniform(row_key, (height, 1), jnp.float32, 0.0, reach))
        column_scale = jnp.exp(jax.random.uniform(column_key, (1, breadth), jnp.float32, 0.0, reach))
        pieces.append((entries * row_scale * column_scale * base_scale).reshape(-1))
    return jnp.concatenate(pieces)


def draw_cotangent(key, part):
    key = jax.random.fold_in(key, 53)
    entries = jax.random.truncated_normal(key, -4.0, 4.0, (MB, ROWS, D), jnp.float32)
    climb = 2.0
    rising = 1.0 + climb * jnp.arange(ROWS, dtype=jnp.float32) / ROWS
    return (entries * rising[None, :, None]).astype(jnp.bfloat16)


def shard_levels(rng, dims, cuts, least, high):
    loudness, own = 1.0, jax.random.fold_in(rng, 6)
    for axis_at, blocks in cuts:
        steps = jnp.exp(jax.random.uniform(jax.random.fold_in(own, axis_at), (blocks,), jnp.float32, least / len(cuts), high / len(cuts)))
        loudness = loudness * jnp.repeat(steps, dims[axis_at] // blocks).reshape([-1 if axis == axis_at else 1 for axis in range(len(dims))])
    return loudness


def scatter_about(rng, shape, deviation, most, cuts=(), kind=jnp.bfloat16):
    values = deviation * jax.random.normal(rng, shape, jnp.float32)
    if cuts:
        values = values * shard_levels(rng, shape, cuts, -0.22, 0.18)
    return jnp.clip(values, -most, most).astype(kind)


def setup_inputs(seed: int = 0) -> dict:
    arg_keys = jax.random.split(jax.random.key(seed), 9)
    tokens = scatter_about(arg_keys[0], (MB, ROWS, D), 1.0, 6.0, ((1, 32),))
    lengths = draw_lengths(jax.random.fold_in(arg_keys[8], 71), 0)
    weights = draw_weights(jax.random.fold_in(arg_keys[8], 71), 0)
    momentum = draw_momentum(jax.random.fold_in(arg_keys[8], 71), 0)
    norm_gains = jnp.clip(1.0 + 0.1 * jax.random.normal(arg_keys[4], (2, D), jnp.float32), 0.5, 1.5)
    gain_first = scatter_about(arg_keys[5], (2, D), (0.08 * TOKENS_ALL ** 0.5), 57.926186, (), jnp.float32)
    gain_second = jnp.clip(jnp.exp(jax.random.uniform(arg_keys[6], (2, D), jnp.float32, math.log(425.984), math.log(6553.6))), 425.984, 6553.6)
    cotangent = draw_cotangent(jax.random.fold_in(arg_keys[8], 71), 0)
    return dict(tokens=tokens, lengths=lengths, weights=weights, momentum=momentum, norm_gains=norm_gains, gain_first=gain_first, gain_second=gain_second, cotangent=cotangent)


@jax.custom_vjp
def low(v):
    return lax.optimization_barrier(v.astype(jnp.bfloat16)).astype(jnp.float32)

@jax.custom_vjp
def low_back(v):
    return v

def low_keep(v):
    return (low(v), None)

def low_pass(kept, grad):
    return (grad,)

def back_keep(v):
    return (v, None)

def back_low(kept, grad):
    return (low(grad),)
low.defvjp(low_keep, low_pass)
low_back.defvjp(back_keep, back_low)
norm_epsilon = 1e-05
rope_base = 100000.0
masked_score = -1e+30
newton_first = 3.4445
newton_second = -4.775
newton_third = 2.0315
momentum_decay = 0.95
matrix_rate = 0.2
weight_decay = 0.1
gain_rate = 0.2
first_decay = 0.9
second_decay = 0.95
adam_epsilon = 1e-08
frobenius_epsilon = 1e-07

def matrix_shapes():
    return [(D, D), (D, KV_WIDTH), (D, KV_WIDTH), (D, D), (D, FF), (D, FF), (FF, D)]

def unpack(flat_vector):
    matrices = []
    offset = 0
    for height, breadth in matrix_shapes():
        matrices.append(flat_vector[offset:offset + height * breadth].reshape(height, breadth))
        offset = offset + height * breadth
    return matrices

def multiply_high(left, right):
    return jnp.dot(left, right, precision=lax.Precision.HIGHEST, preferred_element_type=jnp.float32)

def layout(lengths_row, places):
    finish = jnp.cumsum(lengths_row).astype(jnp.int32)
    firsts = (finish - lengths_row).astype(jnp.int32)
    document = lax.optimization_barrier(jnp.sum((places[:, None] >= finish[None, :-1]).astype(jnp.int32), axis=1)).astype(jnp.int32)
    begins = lax.optimization_barrier(jnp.max(jnp.where(places[:, None] >= firsts[None, :], firsts[None, :], 0), axis=1)).astype(jnp.int32)
    return ((places - begins).astype(jnp.int32), document)

def rotate(values, offsets, direction):
    rotary_half_width = values.shape[-1] // 2
    inverse = jnp.exp(jnp.arange(rotary_half_width, dtype=jnp.float32) * (-2.0 * math.log(rope_base) / values.shape[-1]))
    angles = offsets.astype(jnp.float32)[:, None] * inverse[None, :]
    rotary_cosine = jnp.cos(angles)[:, None, :]
    sine_part = direction * jnp.sin(angles)[:, None, :]
    former = values[..., :rotary_half_width]
    latter = values[..., rotary_half_width:]
    return jnp.concatenate([former * rotary_cosine - latter * sine_part, latter * rotary_cosine + former * sine_part], axis=-1)

def normalize(values, gain):
    scaling = lax.rsqrt(lax.optimization_barrier(jnp.mean(values * values, axis=-1, keepdims=True)) + norm_epsilon)
    return values * scaling * gain

def orthogonalize(matrix):
    flipped = matrix.shape[0] > matrix.shape[1]
    current = matrix.T if flipped else matrix
    current = current / (jnp.sqrt(jnp.sum(current * current)) + frobenius_epsilon)
    for iteration in range(NS_STEPS):
        square = multiply_high(current, current.T)
        mixer = newton_second * square + newton_third * multiply_high(square, square)
        current = newton_first * current + multiply_high(mixer, current)
    result = current.T if flipped else current
    return result * (0.2 * math.sqrt(max(matrix.shape)))

def attention(query, keys, values, documents):
    length_rows = query.shape[0]
    block_rows = min(512, length_rows)
    block_count = length_rows // block_rows
    places = jnp.arange(length_rows, dtype=jnp.int32)
    grouped = query.reshape(block_count, block_rows, KV_HEADS, HEADS // KV_HEADS, HEAD_DIM)

    def one_block(block_item):
        rows_query, query_places, query_docs = block_item
        raw_scores = jnp.einsum('tgrd,kgd->grtk', rows_query, keys, precision=lax.Precision.HIGHEST)
        allowed = (query_docs[:, None] == documents[None, :]) & (places[None, :] <= query_places[:, None])
        scores = jnp.where(allowed, low_back(raw_scores) * 0.125, masked_score)
        highest = lax.optimization_barrier(jnp.max(scores, axis=-1, keepdims=True))
        summed = lax.optimization_barrier(jnp.sum(jnp.exp(scores - highest), axis=-1, keepdims=True))
        probs = low(jnp.exp(scores - (highest + jnp.log(summed))))
        return jnp.einsum('grtk,kgd->tgrd', probs, values, precision=lax.Precision.HIGHEST)
    mixed = lax.map(jax.checkpoint(one_block), (grouped, places.reshape(block_count, block_rows), documents.reshape(block_count, block_rows)))
    return mixed.reshape(length_rows, HEADS * HEAD_DIM)

def layer(inputs, flat_weights, norm_gain_couple, offsets, documents):
    w_query, w_key, w_value, w_out, w_gate, w_up, w_down = unpack(low(flat_weights))
    length_rows = inputs.shape[0]
    normed = low(normalize(inputs, norm_gain_couple[0]))
    query = low(rotate(low_back(multiply_high(normed, w_query)).reshape(length_rows, HEADS, HEAD_DIM), offsets, 1.0))
    keys = low(rotate(low_back(multiply_high(normed, w_key)).reshape(length_rows, KV_HEADS, HEAD_DIM), offsets, 1.0))
    values = low(low_back(multiply_high(normed, w_value))).reshape(length_rows, KV_HEADS, HEAD_DIM)
    mixed = low(low_back(attention(query, keys, values, documents)))
    hidden_state = inputs + low_back(multiply_high(mixed, w_out))
    normed_two = low(normalize(hidden_state, norm_gain_couple[1]))
    gate = low_back(multiply_high(normed_two, w_gate))
    upward = low_back(multiply_high(normed_two, w_up))
    hidden = low(jax.nn.silu(gate) * upward)
    return hidden_state + low_back(multiply_high(hidden, w_down))

def reference(tokens, lengths, weights, momentum, norm_gains, gain_first, gain_second, cotangent):
    buffer_count = MB * N_DP
    buffers = tokens.reshape(buffer_count, SEQ, D)
    length_rows = lengths.reshape(buffer_count, DOCS)
    backs = cotangent.reshape(buffer_count, SEQ, D)

    def step(carry, entry_item):
        grad_flat, grad_gains = carry
        buffer_rows, lengths_row, back_rows = entry_item
        places = jnp.arange(SEQ, dtype=jnp.int32)
        offsets, documents = layout(lengths_row, places)

        def forward(inputs, flat_weights, norm_gain_couple):
            return layer(inputs, flat_weights, norm_gain_couple, offsets, documents)
        result, pullback = jax.vjp(forward, buffer_rows.astype(jnp.float32), weights, norm_gains)
        grad_inputs, grad_weights, grad_gain = pullback(back_rows.astype(jnp.float32))
        return ((grad_flat + grad_weights, grad_gains + grad_gain), (result, grad_inputs))
    initial = (jnp.zeros((WEIGHT_ENTRIES,), jnp.float32), jnp.zeros((2, D), jnp.float32))
    (grad_flat, gain_grad), (results, input_grads) = lax.scan(step, initial, (buffers, length_rows, backs))
    new_momentum = momentum_decay * momentum + grad_flat
    updates = [orthogonalize(matrix) for matrix in unpack(new_momentum)]
    update_flat = jnp.concatenate([piece.reshape(-1) for piece in updates])
    new_weights = weights * (1.0 - matrix_rate * weight_decay) - matrix_rate * update_flat
    first_new = first_decay * gain_first + (1.0 - first_decay) * gain_grad
    second_new = second_decay * gain_second + (1.0 - second_decay) * gain_grad * gain_grad
    debiased_first_moment = first_new / (1.0 - first_decay ** ADAM_STEP)
    corrected_second = second_new / (1.0 - second_decay ** ADAM_STEP)
    new_gains = norm_gains * (1.0 - gain_rate * weight_decay) - gain_rate * debiased_first_moment / (jnp.sqrt(corrected_second) + adam_epsilon)
    outputs = results.reshape(MB, ROWS, D)
    d_tokens = input_grads.reshape(MB, ROWS, D)
    return (outputs, d_tokens, grad_flat, new_momentum, new_weights, first_new, second_new, new_gains)
```

```python
from functools import partial
import math

import jax
import jax.numpy as jnp
from jax import lax
from jax.experimental import pallas as pl
from jax.experimental.pallas import tpu as pltpu
from jax.sharding import Mesh, PartitionSpec as P

HEADS = 9
KV_HEADS = 3
HEAD_DIM = 64
FF = 1536
NS_STEPS = 5
ADAM_STEP = 10
D = 576
KV_WIDTH = 192
GROUPS = HEADS // KV_HEADS
TOK = 512
TILE = 256
COLS = GROUPS * TILE
ROW_CUT = 4
COL_CUT = 2
PLANE = ("half", "ctx")
EVERY = ("quarter", "rep", "half", "ctx")


norm_epsilon = 1e-05
rope_base = 100000.0
masked_score = -1e30
newton_first = 3.4445
newton_second = -4.775
newton_third = 2.0315
momentum_decay = 0.95
matrix_rate = 0.2
weight_decay = 0.1
gain_rate = 0.2
first_decay = 0.9
second_decay = 0.95
adam_epsilon = 1e-08
frobenius_epsilon = 1e-07


def layout(lengths_row, places):
    finish = jnp.cumsum(lengths_row)
    firsts = finish - lengths_row
    begins = jnp.max(jnp.where(places[:, None] >= firsts[None, :], firsts[None, :], 0), axis=1)
    return (places - begins, begins)


def rope_tables(offsets):
    half_width = HEAD_DIM // 2
    inverse = jnp.exp(
        jnp.arange(half_width, dtype=jnp.float32) * (-2.0 * math.log(rope_base) / HEAD_DIM)
    )
    angles = inverse[:, None] * offsets.astype(jnp.float32)[None, :]
    return (jnp.cos(angles), jnp.sin(angles))


def rotate_columns(values, cosine, sine):
    shaped = values.reshape(-1, 2, HEAD_DIM // 2, values.shape[-1])
    former, latter = shaped[:, 0], shaped[:, 1]
    return jnp.stack(
        [former * cosine - latter * sine, latter * cosine + former * sine], axis=1
    ).reshape(values.shape)


def normalize(values, gain):
    scaling = lax.rsqrt(jnp.mean(values * values, axis=-1, keepdims=True) + norm_epsilon)
    return values * scaling * gain


def normalize_back(values, gain, upstream):
    scaling = lax.rsqrt(jnp.mean(values * values, axis=-1, keepdims=True) + norm_epsilon)
    weighted = upstream * gain
    gain_grad = jnp.sum(upstream * values * scaling, axis=0)
    inner_term = jnp.mean(weighted * values, axis=-1, keepdims=True)
    return (scaling * weighted - values * (scaling * scaling * scaling) * inner_term, gain_grad)


def dot32(left, right):
    return jnp.dot(left, right, preferred_element_type=jnp.float32)


def masked(scores, key_block, begins, places):
    keys = key_block * TILE + lax.broadcasted_iota(jnp.int32, scores.shape, 0)
    return jnp.where((keys >= begins) & (keys <= places), scores, masked_score)


def tile_row(row, tile):
    part = row[:, tile * TILE : (tile + 1) * TILE]
    return jnp.concatenate([part] * GROUPS, axis=1)


def tile_heads(ref, group, tile):
    return jnp.concatenate(
        [ref[group, head, :, tile * TILE : (tile + 1) * TILE] for head in range(GROUPS)], axis=1
    )


def key_ranges(info, tile):
    first, full, last = info[1 + 3 * tile], info[2 + 3 * tile], info[3 + 3 * tile]
    return ((first, full, True), (full, last, False), (last, last + 1, True))


def forward_kernel(info, q_ref, kv_ref, begin_ref, o_ref, lse_ref, k_nat, v_ext):
    own = info[0]
    for block in range(4):

        @pl.when(block <= own)
        def _():
            for group in range(KV_HEADS):
                low = HEAD_DIM * group
                k_nat[group, TOK * block : TOK * (block + 1), :] = kv_ref[
                    block, low : low + HEAD_DIM, :
                ].T
                low = low + KV_WIDTH
                for part in range(TOK // TILE):
                    spot = block * (TOK // TILE) + part
                    v_ext[group, spot, :HEAD_DIM, :] = kv_ref[
                        block, low : low + HEAD_DIM, part * TILE : (part + 1) * TILE
                    ]
                    v_ext[group, spot, HEAD_DIM:, :] = jnp.ones((16, TILE), jnp.bfloat16)

    def one_group(group, unused):
        for tile in range(TOK // TILE):
            queries = tile_heads(q_ref, group, tile)
            begins = tile_row(begin_ref[...], tile)
            column = lax.broadcasted_iota(jnp.int32, (1, COLS), 1)
            places = own * TOK + tile * TILE + lax.rem(column, TILE)

            def step(is_masked, key_block, carry):
                top, total = carry
                start = pl.multiple_of(key_block * TILE, TILE)
                scores = dot32(k_nat[group, pl.ds(start, TILE), :], queries)
                if is_masked:
                    scores = masked(scores, key_block, begins, places)
                new_top = jnp.maximum(top, jnp.max(scores, axis=0, keepdims=True))
                probs = jnp.exp(scores - new_top).astype(jnp.bfloat16)
                total = total * jnp.exp(top - new_top) + dot32(v_ext[group, key_block], probs)
                return (new_top, total)

            carry = (
                jnp.full((1, COLS), masked_score, jnp.float32),
                jnp.zeros((HEAD_DIM + 16, COLS), jnp.float32),
            )
            for low, high, is_masked in key_ranges(info, tile):
                carry = lax.fori_loop(low, high, partial(step, is_masked), carry)
            top, total = carry
            weight = total[HEAD_DIM : HEAD_DIM + 1, :]
            mixed = (total[:HEAD_DIM, :] / weight).astype(jnp.bfloat16)
            log_total = top + jnp.log(weight)
            for head in range(GROUPS):
                o_ref[group, head, :, tile * TILE : (tile + 1) * TILE] = mixed[
                    :, head * TILE : (head + 1) * TILE
                ]
                lse_ref[group, head, :, tile * TILE : (tile + 1) * TILE] = log_total[
                    :, head * TILE : (head + 1) * TILE
                ]
        return unused

    lax.fori_loop(0, KV_HEADS, one_group, 0)


def backward_kernel(
    info, q_ref, kv_ref, begin_ref, o_ref, lse_ref, do_ref, cos_ref, sin_ref,
    dq_ref, dkv_ref, k_nat, v_nat, k_tall, dk_ref, dv_ref,
):
    own = info[0]
    for block in range(4):

        @pl.when(block <= own)
        def _():
            rows = slice(TOK * block, TOK * (block + 1))
            for group in range(KV_HEADS):
                low = HEAD_DIM * group
                k_nat[group, rows, :] = kv_ref[block, low : low + HEAD_DIM, :].T
                for part in range(TOK // TILE):
                    k_tall[group, block * (TOK // TILE) + part] = kv_ref[
                        block, low : low + HEAD_DIM, part * TILE : (part + 1) * TILE
                    ]
                low = low + KV_WIDTH
                v_nat[group, rows, :] = kv_ref[block, low : low + HEAD_DIM, :].T
                dk_ref[group, rows, :] = jnp.zeros((TOK, HEAD_DIM), jnp.float32)
                dv_ref[group, rows, :] = jnp.zeros((TOK, HEAD_DIM), jnp.float32)

    def one_group(group, unused):
        for tile in range(TOK // TILE):
            queries = tile_heads(q_ref, group, tile)
            upstream = tile_heads(do_ref, group, tile)
            mixed = tile_heads(o_ref, group, tile)
            log_total = tile_heads(lse_ref, group, tile)
            delta = jnp.sum(
                upstream.astype(jnp.float32) * mixed.astype(jnp.float32), axis=0, keepdims=True
            )
            queries_nat = queries.T
            upstream_nat = upstream.T
            begins = tile_row(begin_ref[...], tile)
            column = lax.broadcasted_iota(jnp.int32, (1, COLS), 1)
            places = own * TOK + tile * TILE + lax.rem(column, TILE)

            def step(is_masked, key_block, dq):
                start = pl.multiple_of(key_block * TILE, TILE)
                rows = pl.ds(start, TILE)
                scores = dot32(k_nat[group, rows, :], queries)
                if is_masked:
                    scores = masked(scores, key_block, begins, places)
                probs = jnp.exp(scores - log_total)
                grad_probs = dot32(v_nat[group, rows, :], upstream)
                grad_scores = (probs * (grad_probs - delta)).astype(jnp.bfloat16)
                dv_ref[group, rows, :] += dot32(probs.astype(jnp.bfloat16), upstream_nat)
                dk_ref[group, rows, :] += dot32(grad_scores, queries_nat)
                return dq + dot32(k_tall[group, key_block], grad_scores)

            dq = jnp.zeros((HEAD_DIM, COLS), jnp.float32)
            for low, high, is_masked in key_ranges(info, tile):
                dq = lax.fori_loop(low, high, partial(step, is_masked), dq)
            dq = dq * 0.125
            half_width = HEAD_DIM // 2
            cosine = tile_row(cos_ref[...], tile)
            sine = tile_row(sin_ref[...], tile)
            former, latter = dq[:half_width], dq[half_width:]
            turned = jnp.concatenate(
                [former * cosine + latter * sine, latter * cosine - former * sine], axis=0
            ).astype(jnp.bfloat16)
            for head in range(GROUPS):
                dq_ref[group, head, :, tile * TILE : (tile + 1) * TILE] = turned[
                    :, head * TILE : (head + 1) * TILE
                ]
        return unused

    lax.fori_loop(0, KV_HEADS, one_group, 0)
    for block in range(4):
        rows = slice(TOK * block, TOK * (block + 1))

        @pl.when(block <= own)
        def _():
            for group in range(KV_HEADS):
                low = HEAD_DIM * group
                dkv_ref[block, low : low + HEAD_DIM, :] = dk_ref[group, rows, :].T.astype(
                    jnp.bfloat16
                )
                low = low + KV_WIDTH
                dkv_ref[block, low : low + HEAD_DIM, :] = dv_ref[group, rows, :].T.astype(
                    jnp.bfloat16
                )

        @pl.when(block > own)
        def _():
            dkv_ref[block] = jnp.zeros((2 * KV_WIDTH, TOK), jnp.bfloat16)


def vmem():
    return pl.BlockSpec(memory_space=pltpu.VMEM)


def smem():
    return pl.BlockSpec(memory_space=pltpu.SMEM)


kernel_params = pltpu.CompilerParams(vmem_limit_bytes=48 * 1024 * 1024)
heads_shape = (KV_HEADS, GROUPS, HEAD_DIM, TOK)


def attend_forward(info, queries, keyvals, begins):
    return pl.pallas_call(
        forward_kernel,
        out_shape=(
            jax.ShapeDtypeStruct(heads_shape, jnp.bfloat16),
            jax.ShapeDtypeStruct((KV_HEADS, GROUPS, 1, TOK), jnp.float32),
        ),
        in_specs=[smem(), vmem(), vmem(), vmem()],
        out_specs=(vmem(), vmem()),
        scratch_shapes=[
            pltpu.VMEM((KV_HEADS, 4 * TOK, HEAD_DIM), jnp.bfloat16),
            pltpu.VMEM((KV_HEADS, 4 * TOK // TILE, HEAD_DIM + 16, TILE), jnp.bfloat16),
        ],
        compiler_params=kernel_params,
        cost_estimate=pl.CostEstimate(
            flops=4 * 9 * 64 * TOK * 2048, bytes_accessed=4000000, transcendentals=9 * TOK * 2048
        ),
        name="attend_forward",
    )(info, queries, keyvals, begins)


def attend_back(info, queries, keyvals, begins, mixed, log_total, grad_mixed, cosine, sine):
    return pl.pallas_call(
        backward_kernel,
        out_shape=(
            jax.ShapeDtypeStruct(heads_shape, jnp.bfloat16),
            jax.ShapeDtypeStruct((4, 2 * KV_WIDTH, TOK), jnp.bfloat16),
        ),
        in_specs=[smem()] + [vmem()] * 8,
        out_specs=(vmem(), vmem()),
        scratch_shapes=[
            pltpu.VMEM((KV_HEADS, 4 * TOK, HEAD_DIM), jnp.bfloat16),
            pltpu.VMEM((KV_HEADS, 4 * TOK, HEAD_DIM), jnp.bfloat16),
            pltpu.VMEM((KV_HEADS, 4 * TOK // TILE, HEAD_DIM, TILE), jnp.bfloat16),
            pltpu.VMEM((KV_HEADS, 4 * TOK, HEAD_DIM), jnp.float32),
            pltpu.VMEM((KV_HEADS, 4 * TOK, HEAD_DIM), jnp.float32),
        ],
        compiler_params=kernel_params,
        cost_estimate=pl.CostEstimate(
            flops=10 * 9 * 64 * TOK * 2048, bytes_accessed=8000000, transcendentals=9 * TOK * 2048
        ),
        name="attend_back",
    )(info, queries, keyvals, begins, mixed, log_total, grad_mixed, cosine, sine)


def quarter_matrix(quarter, flat):
    def mixed_case(flat):
        square = D * D
        narrow = D * KV_WIDTH
        return jnp.concatenate(
            [
                flat[:square].reshape(D, D),
                flat[square : square + narrow].reshape(D, KV_WIDTH),
                flat[square + narrow : square + 2 * narrow].reshape(D, KV_WIDTH),
                flat[square + 2 * narrow :].reshape(D, D),
            ],
            axis=1,
        )

    def wide_case(flat):
        return flat.reshape(D, FF)

    def tall_case(flat):
        return flat.reshape(FF, D).T

    return lax.switch(quarter, [mixed_case, wide_case, wide_case, tall_case], flat)


def newton(matrix, scale):
    current = matrix / (jnp.sqrt(jnp.sum(matrix * matrix)) + frobenius_epsilon)
    for iteration in range(NS_STEPS):
        low = current.astype(jnp.bfloat16)
        square = lax.dot_general(
            low, low, (((1,), (1,)), ((), ())), preferred_element_type=jnp.float32
        )
        square_low = square.astype(jnp.bfloat16)
        mixer = newton_second * square + newton_third * dot32(square_low, square_low)
        current = newton_first * current + dot32(mixer.astype(jnp.bfloat16), low)
    return current * (0.2 * math.sqrt(scale))


def own_update(quarter, within, shard_length, gradient, total):
    square = D * D
    narrow = D * KV_WIDTH

    def square_case(gradient, total):
        second = within >= square + 2 * narrow
        column = jnp.where(second, FF - D, 0)
        row = (within - jnp.where(second, square + 2 * narrow, 0)) // D
        rows = shard_length // D
        part = lax.dynamic_slice(total, (0, column), (D, D))
        result = newton(part, D)
        return (
            lax.dynamic_slice(gradient, (row, column), (rows, D)).reshape(-1),
            lax.dynamic_slice(result, (row, 0), (rows, D)).reshape(-1),
        )

    def narrow_case(gradient, total):
        second = within >= square + narrow
        column = D + jnp.where(second, KV_WIDTH, 0)
        row = (within - square - jnp.where(second, narrow, 0)) // KV_WIDTH
        rows = shard_length // KV_WIDTH
        part = lax.dynamic_slice(total, (0, column), (D, KV_WIDTH))
        result = newton(part.T, D).T
        return (
            lax.dynamic_slice(gradient, (row, column), (rows, KV_WIDTH)).reshape(-1),
            lax.dynamic_slice(result, (row, 0), (rows, KV_WIDTH)).reshape(-1),
        )

    def wide_case(gradient, total):
        row = within // FF
        rows = shard_length // FF
        result = newton(total, FF)
        return (
            lax.dynamic_slice(gradient, (row, 0), (rows, FF)).reshape(-1),
            lax.dynamic_slice(result, (row, 0), (rows, FF)).reshape(-1),
        )

    def tall_case(gradient, total):
        column = within // D
        columns = shard_length // D
        result = newton(total, FF)
        return (
            lax.dynamic_slice(gradient, (0, column), (D, columns)).T.reshape(-1),
            lax.dynamic_slice(result, (0, column), (D, columns)).T.reshape(-1),
        )

    is_narrow = (within >= square) & (within < square + 2 * narrow)
    kind = jnp.where(quarter == 0, jnp.where(is_narrow, 1, 0), jnp.where(quarter == 3, 3, 2))
    return lax.switch(
        kind, [square_case, narrow_case, wide_case, tall_case], gradient, total
    )


def cut(matrix):
    shaped = matrix.reshape(ROW_CUT, D // ROW_CUT, COL_CUT, FF // COL_CUT)
    return shaped.transpose(0, 2, 1, 3).reshape(ROW_CUT * COL_CUT, D // ROW_CUT, FF // COL_CUT)


def uncut(pieces):
    shaped = pieces.reshape(ROW_CUT, COL_CUT, D // ROW_CUT, FF // COL_CUT)
    return shaped.transpose(0, 2, 1, 3).reshape(D, FF)


def attention_info(ctx, begins):
    fields = [ctx]
    for tile in range(TOK // TILE):
        last = ctx * (TOK // TILE) + tile
        first = begins[tile * TILE] // TILE
        full = jnp.minimum(last, (begins[(tile + 1) * TILE - 1] + TILE - 1) // TILE)
        fields = fields + [first, full, last]
    return jnp.stack(fields).astype(jnp.int32)


def per_device(tokens, lengths, weights, momentum, norm_gains, gain_first, gain_second, cotangent):
    micro_count = tokens.shape[0]
    ctx = lax.axis_index("ctx")
    quarter = lax.axis_index("quarter")
    reps = lax.axis_size("rep")
    shard_length = weights.shape[0]
    within = lax.axis_index(("rep", "half", "ctx")) * shard_length

    full_weights = lax.all_gather(weights.astype(jnp.bfloat16), EVERY, axis=0, tiled=True)
    square, narrow, broad = D * D, D * KV_WIDTH, D * FF
    places_in = [0, square, square + narrow, square + 2 * narrow]
    w_qkv = jnp.concatenate(
        [
            full_weights[:square].reshape(D, D),
            full_weights[places_in[1] : places_in[2]].reshape(D, KV_WIDTH),
            full_weights[places_in[2] : places_in[3]].reshape(D, KV_WIDTH),
        ],
        axis=1,
    )
    w_out = full_weights[places_in[3] : places_in[3] + square].reshape(D, D)
    w_gate = full_weights[broad : 2 * broad].reshape(D, FF)
    w_up = full_weights[2 * broad : 3 * broad].reshape(D, FF)
    w_down = full_weights[3 * broad :].reshape(FF, D)

    own_places = ctx * TOK + jnp.arange(TOK, dtype=jnp.int32)
    inputs = tokens.astype(jnp.float32).reshape(-1, D)
    back = cotangent.reshape(-1, D)
    normed = normalize(inputs, norm_gains[0]).astype(jnp.bfloat16)
    infos, begin_rows, tables = [], [], []
    for micro in range(micro_count):
        offsets, begins = layout(lengths[micro, 0], own_places)
        infos.append(attention_info(ctx, begins))
        begin_rows.append(begins.reshape(1, TOK))
        tables.append(rope_tables(offsets))

    queries, keyvals, mixed, log_totals = [], [], [], []
    for micro in range(micro_count):
        rows = normed[micro * TOK : (micro + 1) * TOK]
        linear = jnp.einsum("de,td->et", w_qkv, rows, preferred_element_type=jnp.float32)
        turned = rotate_columns(linear[: D + KV_WIDTH], *tables[micro])
        scaled = turned[:D].astype(jnp.bfloat16) * jnp.bfloat16(0.125)
        queries.append(scaled.reshape(heads_shape))
        own_keyvals = jnp.concatenate([turned[D:], linear[D + KV_WIDTH :]], axis=0)
        keyvals.append(
            lax.all_gather(own_keyvals.astype(jnp.bfloat16), "ctx", axis=0, tiled=False)
        )
    for micro in range(micro_count):
        mixed_one, log_total = attend_forward(
            infos[micro], queries[micro], keyvals[micro], begin_rows[micro]
        )
        mixed.append(mixed_one)
        log_totals.append(log_total)
    mixed_all = jnp.concatenate([part.reshape(D, TOK) for part in mixed], axis=1)
    hidden_state = inputs + jnp.einsum(
        "et,ed->td", mixed_all, w_out, preferred_element_type=jnp.float32
    )
    normed_two = normalize(hidden_state, norm_gains[1]).astype(jnp.bfloat16)
    gate = dot32(normed_two, w_gate)
    upward = dot32(normed_two, w_up)
    sigmoid_gate = jax.nn.sigmoid(gate)
    activated = gate * sigmoid_gate
    hidden = (activated * upward).astype(jnp.bfloat16)
    result = hidden_state + dot32(hidden, w_down)
    grad_hidden = jnp.einsum("td,fd->tf", back, w_down, preferred_element_type=jnp.float32)
    grad_gate = (grad_hidden * upward * sigmoid_gate * (1.0 + gate * (1.0 - sigmoid_gate))).astype(
        jnp.bfloat16
    )
    grad_upward = (grad_hidden * activated).astype(jnp.bfloat16)

    def weight_term(left, right):
        return jnp.einsum(
            "td,tf->df", left, right, preferred_element_type=jnp.float32
        ).astype(jnp.bfloat16)

    grad_w_down = weight_term(back, hidden)
    grad_w_gate = weight_term(normed_two, grad_gate)
    grad_w_up = weight_term(normed_two, grad_upward)
    grad_normed_two = jnp.einsum(
        "tf,df->td", grad_gate, w_gate, preferred_element_type=jnp.float32
    ) + jnp.einsum("tf,df->td", grad_upward, w_up, preferred_element_type=jnp.float32)
    grad_state_norm, gain_two_grad = normalize_back(hidden_state, norm_gains[1], grad_normed_two)
    grad_state = back.astype(jnp.float32) + grad_state_norm
    grad_state_low = grad_state.astype(jnp.bfloat16)
    early = jnp.stack([cut(grad_w_gate), cut(grad_w_up), cut(grad_w_down)], axis=1)
    early = lax.psum_scatter(early, PLANE, scatter_dimension=0, tiled=False)
    grad_mixed = jnp.einsum(
        "ed,td->et", w_out, grad_state_low, preferred_element_type=jnp.float32
    ).astype(jnp.bfloat16)
    grad_w_out = jnp.einsum(
        "et,td->ed", mixed_all, grad_state_low, preferred_element_type=jnp.float32
    ).astype(jnp.bfloat16)

    grad_columns = []
    for micro in range(micro_count):
        dq, dkv = attend_back(
            infos[micro],
            queries[micro],
            keyvals[micro],
            begin_rows[micro],
            mixed[micro],
            log_totals[micro],
            grad_mixed[:, micro * TOK : (micro + 1) * TOK].reshape(heads_shape),
            *tables[micro],
        )
        dkv = lax.psum_scatter(dkv, "ctx", scatter_dimension=0, tiled=False)
        cosine, sine = tables[micro]
        dk = rotate_columns(dkv[:KV_WIDTH].astype(jnp.float32), cosine, -sine)
        grad_columns.append(
            jnp.concatenate(
                [dq.reshape(D, TOK), dk.astype(jnp.bfloat16), dkv[KV_WIDTH:]], axis=0
            )
        )
    grad_qkv = jnp.concatenate(grad_columns, axis=1)
    grad_w_qkv = jnp.einsum(
        "td,et->de", normed, grad_qkv, preferred_element_type=jnp.float32
    ).astype(jnp.bfloat16)
    late = cut(jnp.concatenate([grad_w_qkv, grad_w_out], axis=1))
    late = lax.psum_scatter(late, PLANE, scatter_dimension=0, tiled=False)
    grad_normed = jnp.einsum("et,de->td", grad_qkv, w_qkv, preferred_element_type=jnp.float32)
    grad_input_norm, gain_one_grad = normalize_back(inputs, norm_gains[0], grad_normed)
    grad_inputs = grad_state + grad_input_norm

    piece = lax.psum_scatter(
        jnp.concatenate([late[None], early], axis=0), "quarter", scatter_dimension=0, tiled=False
    )
    if reps > 1:
        piece = lax.psum(piece, "rep")
    gradient = uncut(lax.all_gather(piece, PLANE, axis=0, tiled=False))
    old = lax.all_gather(
        momentum.astype(jnp.bfloat16), ("rep", "half", "ctx"), axis=0, tiled=True
    )
    total = momentum_decay * quarter_matrix(quarter, old).astype(jnp.float32) + gradient.astype(
        jnp.float32
    )
    grad_shard, update_shard = own_update(quarter, within, shard_length, gradient, total)
    grad_shard = grad_shard.astype(jnp.float32)
    new_momentum = momentum_decay * momentum + grad_shard
    new_weights = weights * (1.0 - matrix_rate * weight_decay) - matrix_rate * update_shard

    gain_grad = lax.psum(jnp.stack([gain_one_grad, gain_two_grad]), EVERY)
    first_new = first_decay * gain_first + (1.0 - first_decay) * gain_grad
    second_new = second_decay * gain_second + (1.0 - second_decay) * gain_grad * gain_grad
    debiased_first_moment = first_new / (1.0 - first_decay**ADAM_STEP)
    corrected_second = second_new / (1.0 - second_decay**ADAM_STEP)
    new_gains = norm_gains * (
        1.0 - gain_rate * weight_decay
    ) - gain_rate * debiased_first_moment / (jnp.sqrt(corrected_second) + adam_epsilon)
    return (
        result.reshape(tokens.shape),
        grad_inputs.reshape(tokens.shape),
        grad_shard,
        new_momentum,
        new_weights,
        first_new,
        second_new,
        new_gains,
    )


def solution(mesh):
    devices = mesh.devices
    count = devices.size
    context = mesh.shape["ctx"]
    split = Mesh(
        devices.reshape(4, count // (8 * context), 2, context), ("quarter", "rep", "half", "ctx")
    )
    rows = P(None, EVERY, None)
    flat = P(EVERY)
    placed = (rows, P(None, ("quarter", "rep", "half"), None), flat, flat, P(), P(), P(), rows)
    return jax.shard_map(
        per_device,
        mesh=split,
        in_specs=placed,
        out_specs=(rows, rows, flat, flat, flat, P(), P(), P()),
        check_vma=False,
    )
```

```python
from functools import partial
import math

import jax
import jax.numpy as jnp
from jax import lax
from jax.experimental import pallas as pl
from jax.experimental.pallas import tpu as pltpu
from jax.sharding import Mesh, PartitionSpec as P

HEADS = 9
KV_HEADS = 3
HEAD_DIM = 64
FF = 1536
NS_STEPS = 5
ADAM_STEP = 10
D = 576
KV_WIDTH = 192
GROUPS = HEADS // KV_HEADS
TOK = 512
TILE = 256
COLS = GROUPS * TILE
ROW_CUT = 4
COL_CUT = 2
CHUNKS = ROW_CUT * COL_CUT
CHUNK_ROWS = D // ROW_CUT
CHUNK_COLS = FF // COL_CUT
PLANE = ("half", "ctx")
EVERY = ("quarter", "rep", "half", "ctx")


norm_epsilon = 1e-05
rope_base = 100000.0
masked_score = -1e30
newton_first = 3.4445
newton_second = -4.775
newton_third = 2.0315
momentum_decay = 0.95
matrix_rate = 0.2
weight_decay = 0.1
gain_rate = 0.2
first_decay = 0.9
second_decay = 0.95
adam_epsilon = 1e-08
frobenius_epsilon = 1e-07


def layout(lengths_row, places):
    finish = jnp.cumsum(lengths_row)
    firsts = finish - lengths_row
    begins = jnp.max(jnp.where(places[:, None] >= firsts[None, :], firsts[None, :], 0), axis=1)
    return (places - begins, begins)


def rope_tables(offsets):
    half_width = HEAD_DIM // 2
    inverse = jnp.exp(
        jnp.arange(half_width, dtype=jnp.float32) * (-2.0 * math.log(rope_base) / HEAD_DIM)
    )
    angles = inverse[:, None] * offsets.astype(jnp.float32)[None, :]
    return (jnp.cos(angles), jnp.sin(angles))


def rotate_columns(values, cosine, sine):
    shaped = values.reshape(-1, 2, HEAD_DIM // 2, values.shape[-1])
    former, latter = shaped[:, 0], shaped[:, 1]
    return jnp.stack(
        [former * cosine - latter * sine, latter * cosine + former * sine], axis=1
    ).reshape(values.shape)


def normalize(values, gain):
    scaling = lax.rsqrt(jnp.mean(values * values, axis=-1, keepdims=True) + norm_epsilon)
    return values * scaling * gain


def normalize_back(values, gain, upstream):
    scaling = lax.rsqrt(jnp.mean(values * values, axis=-1, keepdims=True) + norm_epsilon)
    weighted = upstream * gain
    gain_grad = jnp.sum(upstream * values * scaling, axis=0)
    inner_term = jnp.mean(weighted * values, axis=-1, keepdims=True)
    return (scaling * weighted - values * (scaling * scaling * scaling) * inner_term, gain_grad)


def dot32(left, right):
    return jnp.dot(left, right, preferred_element_type=jnp.float32)


def masked(scores, key_block, begins, places):
    keys = key_block * TILE + lax.broadcasted_iota(jnp.int32, scores.shape, 0)
    return jnp.where((keys >= begins) & (keys <= places), scores, masked_score)


def tile_row(row, tile):
    part = row[:, tile * TILE : (tile + 1) * TILE]
    return jnp.concatenate([part] * GROUPS, axis=1)


def tile_heads(ref, group, tile):
    return jnp.concatenate(
        [ref[group, head, :, tile * TILE : (tile + 1) * TILE] for head in range(GROUPS)], axis=1
    )


def key_loop(info, tile, step, carry):
    first, full, last = info[1 + 3 * tile], info[2 + 3 * tile], info[3 + 3 * tile]
    pairs = (last - full) // 2
    carry = lax.fori_loop(first, full, partial(step, True, 1), carry)
    carry = lax.fori_loop(
        0, pairs, lambda pair, held: step(False, 2, full + 2 * pair, held), carry
    )
    carry = lax.fori_loop(full + 2 * pairs, last, partial(step, False, 1), carry)
    return step(True, 1, last, carry)


def forward_kernel(backward_order, info, q_ref, kv_ref, begin_ref, o_ref, lse_ref, k_nat, v_ext):
    own = info[0]
    for block in range(4):

        @pl.when(block <= own)
        def _():
            for group in range(KV_HEADS):
                low = HEAD_DIM * group
                source = 3 - block if backward_order else block
                k_nat[group, TOK * block : TOK * (block + 1), :] = kv_ref[
                    source, low : low + HEAD_DIM, :
                ].T
                low = low + KV_WIDTH
                columns = slice(TOK * block, TOK * (block + 1))
                v_ext[group, :HEAD_DIM, columns] = kv_ref[source, low : low + HEAD_DIM, :]
                v_ext[group, HEAD_DIM:, columns] = jnp.ones((16, TOK), jnp.bfloat16)

    def one_group(group, unused):
        for tile in range(TOK // TILE):
            queries = tile_heads(q_ref, group, tile)
            begins = tile_row(begin_ref[...], tile)
            column = lax.broadcasted_iota(jnp.int32, (1, COLS), 1)
            places = own * TOK + tile * TILE + lax.rem(column, TILE)

            def step(is_masked, width, key_block, carry):
                top, total = carry
                keys = pl.ds(pl.multiple_of(key_block * TILE, TILE), width * TILE)
                scores = dot32(k_nat[group, keys, :], queries)
                if is_masked:
                    scores = masked(scores, key_block, begins, places)
                new_top = jnp.maximum(top, jnp.max(scores, axis=0, keepdims=True))
                probs = jnp.exp(scores - new_top).astype(jnp.bfloat16)
                total = total * jnp.exp(top - new_top) + dot32(v_ext[group, :, keys], probs)
                return (new_top, total)

            carry = (
                jnp.full((1, COLS), masked_score, jnp.float32),
                jnp.zeros((HEAD_DIM + 16, COLS), jnp.float32),
            )
            top, total = key_loop(info, tile, step, carry)
            weight = total[HEAD_DIM : HEAD_DIM + 1, :]
            mixed = (total[:HEAD_DIM, :] / weight).astype(jnp.bfloat16)
            log_total = top + jnp.log(weight)
            for head in range(GROUPS):
                o_ref[group, head, :, tile * TILE : (tile + 1) * TILE] = mixed[
                    :, head * TILE : (head + 1) * TILE
                ]
                lse_ref[group, head, :, tile * TILE : (tile + 1) * TILE] = log_total[
                    :, head * TILE : (head + 1) * TILE
                ]
        return unused

    lax.fori_loop(0, KV_HEADS, one_group, 0)


def backward_kernel(
    backward_order, info, q_ref, kv_ref, begin_ref, o_ref, lse_ref, do_ref, cos_ref, sin_ref,
    dq_ref, dkv_ref, k_nat, v_nat, k_tall, dk_ref, dv_ref,
):
    own = info[0]
    for block in range(4):

        @pl.when(block <= own)
        def _():
            rows = slice(TOK * block, TOK * (block + 1))
            for group in range(KV_HEADS):
                low = HEAD_DIM * group
                source = 3 - block if backward_order else block
                k_nat[group, rows, :] = kv_ref[source, low : low + HEAD_DIM, :].T
                k_tall[group, :, rows] = kv_ref[source, low : low + HEAD_DIM, :]
                low = low + KV_WIDTH
                v_nat[group, rows, :] = kv_ref[source, low : low + HEAD_DIM, :].T
                dk_ref[group, rows, :] = jnp.zeros((TOK, HEAD_DIM), jnp.float32)
                dv_ref[group, rows, :] = jnp.zeros((TOK, HEAD_DIM), jnp.float32)

    def one_group(group, unused):
        for tile in range(TOK // TILE):
            queries = tile_heads(q_ref, group, tile)
            upstream = tile_heads(do_ref, group, tile)
            mixed = tile_heads(o_ref, group, tile)
            log_total = tile_heads(lse_ref, group, tile)
            delta = jnp.sum(
                upstream.astype(jnp.float32) * mixed.astype(jnp.float32), axis=0, keepdims=True
            )
            queries_nat = queries.T
            upstream_nat = upstream.T
            begins = tile_row(begin_ref[...], tile)
            column = lax.broadcasted_iota(jnp.int32, (1, COLS), 1)
            places = own * TOK + tile * TILE + lax.rem(column, TILE)

            def step(is_masked, width, key_block, dq):
                rows = pl.ds(pl.multiple_of(key_block * TILE, TILE), width * TILE)
                scores = dot32(k_nat[group, rows, :], queries)
                if is_masked:
                    scores = masked(scores, key_block, begins, places)
                probs = jnp.exp(scores - log_total)
                grad_probs = dot32(v_nat[group, rows, :], upstream)
                grad_scores = (probs * (grad_probs - delta)).astype(jnp.bfloat16)
                dv_ref[group, rows, :] += dot32(probs.astype(jnp.bfloat16), upstream_nat)
                dk_ref[group, rows, :] += dot32(grad_scores, queries_nat)
                return dq + dot32(k_tall[group, :, rows], grad_scores)

            dq = jnp.zeros((HEAD_DIM, COLS), jnp.float32)
            dq = key_loop(info, tile, step, dq) * 0.125
            half_width = HEAD_DIM // 2
            cosine = tile_row(cos_ref[...], tile)
            sine = tile_row(sin_ref[...], tile)
            former, latter = dq[:half_width], dq[half_width:]
            turned = jnp.concatenate(
                [former * cosine + latter * sine, latter * cosine - former * sine], axis=0
            ).astype(jnp.bfloat16)
            for head in range(GROUPS):
                dq_ref[group, head, :, tile * TILE : (tile + 1) * TILE] = turned[
                    :, head * TILE : (head + 1) * TILE
                ]
        return unused

    lax.fori_loop(0, KV_HEADS, one_group, 0)
    for block in range(4):
        rows = slice(TOK * block, TOK * (block + 1))
        target = 3 - block if backward_order else block

        @pl.when(block <= own)
        def _():
            for group in range(KV_HEADS):
                low = HEAD_DIM * group
                dkv_ref[target, low : low + HEAD_DIM, :] = dk_ref[group, rows, :].T.astype(
                    jnp.bfloat16
                )
                low = low + KV_WIDTH
                dkv_ref[target, low : low + HEAD_DIM, :] = dv_ref[group, rows, :].T.astype(
                    jnp.bfloat16
                )

        @pl.when(block > own)
        def _():
            dkv_ref[target] = jnp.zeros((2 * KV_WIDTH, TOK), jnp.bfloat16)


def vmem():
    return pl.BlockSpec(memory_space=pltpu.VMEM)


def smem():
    return pl.BlockSpec(memory_space=pltpu.SMEM)


kernel_params = pltpu.CompilerParams(vmem_limit_bytes=56 * 1024 * 1024)
heads_shape = (KV_HEADS, GROUPS, HEAD_DIM, TOK)


def attend_forward(backward_order, info, queries, keyvals, begins):
    return pl.pallas_call(
        partial(forward_kernel, backward_order),
        out_shape=(
            jax.ShapeDtypeStruct(heads_shape, jnp.bfloat16),
            jax.ShapeDtypeStruct((KV_HEADS, GROUPS, 1, TOK), jnp.float32),
        ),
        in_specs=[smem(), vmem(), vmem(), vmem()],
        out_specs=(vmem(), vmem()),
        scratch_shapes=[
            pltpu.VMEM((KV_HEADS, 4 * TOK, HEAD_DIM), jnp.bfloat16),
            pltpu.VMEM((KV_HEADS, HEAD_DIM + 16, 4 * TOK), jnp.bfloat16),
        ],
        compiler_params=kernel_params,
        cost_estimate=pl.CostEstimate(
            flops=4 * 9 * 64 * TOK * 2048, bytes_accessed=4000000, transcendentals=9 * TOK * 2048
        ),
        name="attend_forward",
    )(info, queries, keyvals, begins)


def attend_back(
    backward_order, info, queries, keyvals, begins, mixed, log_total, grad_mixed, cosine, sine
):
    return pl.pallas_call(
        partial(backward_kernel, backward_order),
        out_shape=(
            jax.ShapeDtypeStruct(heads_shape, jnp.bfloat16),
            jax.ShapeDtypeStruct((4, 2 * KV_WIDTH, TOK), jnp.bfloat16),
        ),
        in_specs=[smem()] + [vmem()] * 8,
        out_specs=(vmem(), vmem()),
        scratch_shapes=[
            pltpu.VMEM((KV_HEADS, 4 * TOK, HEAD_DIM), jnp.bfloat16),
            pltpu.VMEM((KV_HEADS, 4 * TOK, HEAD_DIM), jnp.bfloat16),
            pltpu.VMEM((KV_HEADS, HEAD_DIM, 4 * TOK), jnp.bfloat16),
            pltpu.VMEM((KV_HEADS, 4 * TOK, HEAD_DIM), jnp.float32),
            pltpu.VMEM((KV_HEADS, 4 * TOK, HEAD_DIM), jnp.float32),
        ],
        compiler_params=kernel_params,
        cost_estimate=pl.CostEstimate(
            flops=10 * 9 * 64 * TOK * 2048, bytes_accessed=8000000, transcendentals=9 * TOK * 2048
        ),
        name="attend_back",
    )(info, queries, keyvals, begins, mixed, log_total, grad_mixed, cosine, sine)


def dot_with(left, right, left_side, right_side):
    return lax.dot_general(
        left, right, (((left_side,), (right_side,)), ((), ())), preferred_element_type=jnp.float32
    )


def norm_back(values, scaling, gain, upstream):
    weighted = upstream * gain
    inner = jnp.mean(weighted * values, axis=-1, keepdims=True)
    gain_grad = jnp.sum(upstream * values * scaling, axis=0, keepdims=True)
    return (scaling * weighted - values * (scaling * scaling * scaling) * inner, gain_grad)


def store_chunks(matrix, column, put):
    half, low = column // (FF // COL_CUT), column % (FF // COL_CUT)
    for row in range(ROW_CUT):
        part = matrix[row * CHUNK_ROWS : (row + 1) * CHUNK_ROWS].astype(jnp.bfloat16)
        put(row * COL_CUT + half, slice(low, low + matrix.shape[1]), part)


def mlp_kernel(
    x_ref, c_ref, o0_ref, o1_ref, wo_ref, wg_ref, wu_ref, wd_ref, gain_ref,
    out_ref, dh_ref, do0_ref, do1_ref, early_ref, gwo_ref, gg_ref,
    hid, dgate, dup, n2_tall, c_tall, dh_low,
):
    gain = gain_ref[...]
    gg_ref[...] = jnp.zeros((1, D), jnp.float32)
    block = 256
    for micro, (o_ref, do_ref) in enumerate(((o0_ref, do0_ref), (o1_ref, do1_ref))):
        rows = slice(micro * TOK, (micro + 1) * TOK)
        hidden_state = x_ref[micro].astype(jnp.float32) + dot32(o_ref[...].T, wo_ref[...])
        scaling = lax.rsqrt(
            jnp.mean(hidden_state * hidden_state, axis=-1, keepdims=True) + norm_epsilon
        )
        normed = (hidden_state * scaling * gain).astype(jnp.bfloat16)
        n2_tall[:, rows] = normed.T
        back = c_ref[micro]
        c_tall[:, rows] = back.T
        for column in range(0, FF, block):
            columns = slice(column, column + block)
            gate = dot32(normed, wg_ref[:, columns])
            upward = dot32(normed, wu_ref[:, columns])
            grad_hidden = dot_with(back, wd_ref[columns, :], 1, 1)
            sigmoid_gate = jax.nn.sigmoid(gate)
            activated = gate * sigmoid_gate
            hid[rows, columns] = (activated * upward).astype(jnp.bfloat16)
            dgate[rows, columns] = (
                grad_hidden * upward * sigmoid_gate * (1.0 + gate * (1.0 - sigmoid_gate))
            ).astype(jnp.bfloat16)
            dup[rows, columns] = (grad_hidden * activated).astype(jnp.bfloat16)
        out_ref[micro] = hidden_state + dot32(hid[rows, :], wd_ref[...])
        upstream = dot_with(dgate[rows, :], wg_ref[...], 1, 1) + dot_with(
            dup[rows, :], wu_ref[...], 1, 1
        )
        part, gain_grad = norm_back(hidden_state, scaling, gain, upstream)
        gg_ref[...] += gain_grad
        grad_state = back.astype(jnp.float32) + part
        dh_ref[micro] = grad_state
        low = grad_state.astype(jnp.bfloat16)
        dh_low[rows, :] = low
        do_ref[...] = dot_with(wo_ref[...], low, 1, 1).astype(jnp.bfloat16)
    for column in range(0, FF, block):
        columns = slice(column, column + block)
        for place, (left, right) in enumerate(((n2_tall, dgate), (n2_tall, dup), (c_tall, hid))):

            def put(spot, where, part):
                early_ref[spot, place, :, where] = part

            store_chunks(dot32(left[...], right[:, columns]), column, put)
    gwo_ref[...] = (
        dot32(o0_ref[...], dh_low[:TOK, :]) + dot32(o1_ref[...], dh_low[TOK:, :])
    ).astype(jnp.bfloat16)


def mlp(tokens, cotangent, mixed, w_out, w_gate, w_up, w_down, gain):
    rows = tokens.shape[0] * TOK
    low = jnp.bfloat16
    return pl.pallas_call(
        mlp_kernel,
        out_shape=(
            jax.ShapeDtypeStruct(tokens.shape, jnp.float32),
            jax.ShapeDtypeStruct(tokens.shape, jnp.float32),
            jax.ShapeDtypeStruct((D, TOK), low),
            jax.ShapeDtypeStruct((D, TOK), low),
            jax.ShapeDtypeStruct((CHUNKS, 3, CHUNK_ROWS, CHUNK_COLS), low),
            jax.ShapeDtypeStruct((D, D), low),
            jax.ShapeDtypeStruct((1, D), jnp.float32),
        ),
        in_specs=[vmem()] * 9,
        out_specs=(vmem(),) * 7,
        scratch_shapes=[
            pltpu.VMEM((rows, FF), low),
            pltpu.VMEM((rows, FF), low),
            pltpu.VMEM((rows, FF), low),
            pltpu.VMEM((D, rows), low),
            pltpu.VMEM((D, rows), low),
            pltpu.VMEM((rows, D), low),
        ],
        compiler_params=kernel_params,
        cost_estimate=pl.CostEstimate(
            flops=6 * rows * 3 * D * FF, bytes_accessed=25000000, transcendentals=rows * FF
        ),
        name="mlp",
    )(tokens, cotangent, mixed[0], mixed[1], w_out, w_gate, w_up, w_down, gain)


def projection_kernel(
    n_ref, dq0_ref, dq1_ref, dkv0_ref, dkv1_ref, cos0_ref, sin0_ref, cos1_ref, sin1_ref, gwo_ref,
    late_ref, all_ref, held,
):
    half_width = HEAD_DIM // 2
    parts = ((dq0_ref, dkv0_ref, cos0_ref, sin0_ref), (dq1_ref, dkv1_ref, cos1_ref, sin1_ref))
    for micro, (dq_ref, dkv_ref, cos_ref, sin_ref) in enumerate(parts):
        columns = slice(micro * TOK, (micro + 1) * TOK)
        all_ref[:D, columns] = dq_ref[...]
        cosine, sine = cos_ref[...], sin_ref[...]
        for head in range(KV_HEADS):
            low = head * HEAD_DIM
            former = dkv_ref[low : low + half_width, :].astype(jnp.float32)
            latter = dkv_ref[low + half_width : low + HEAD_DIM, :].astype(jnp.float32)
            all_ref[D + low : D + low + half_width, columns] = (
                former * cosine + latter * sine
            ).astype(jnp.bfloat16)
            all_ref[D + low + half_width : D + low + HEAD_DIM, columns] = (
                latter * cosine - former * sine
            ).astype(jnp.bfloat16)
        all_ref[D + KV_WIDTH :, columns] = dkv_ref[KV_WIDTH:, :]
    held[:, : D + 2 * KV_WIDTH] = dot_with(n_ref[...].T, all_ref[...], 1, 1)
    held[:, D + 2 * KV_WIDTH :] = gwo_ref[...].astype(jnp.float32)

    def put(spot, where, part):
        late_ref[spot, :, where] = part

    for column in range(0, FF, CHUNK_COLS):
        store_chunks(held[:, column : column + CHUNK_COLS], column, put)


def projection_grads(normed, dqs, dkvs, tables, gwo):
    rows = normed.shape[0]
    return pl.pallas_call(
        projection_kernel,
        out_shape=(
            jax.ShapeDtypeStruct((CHUNKS, CHUNK_ROWS, CHUNK_COLS), jnp.bfloat16),
            jax.ShapeDtypeStruct((D + 2 * KV_WIDTH, rows), jnp.bfloat16),
        ),
        in_specs=[vmem()] * 10,
        out_specs=(vmem(),) * 2,
        scratch_shapes=[pltpu.VMEM((D, FF), jnp.float32)],
        compiler_params=kernel_params,
        cost_estimate=pl.CostEstimate(
            flops=2 * rows * D * 960, bytes_accessed=8000000, transcendentals=0
        ),
        name="projection_grads",
    )(normed, *dqs, *dkvs, *tables[0], *tables[1], gwo)


def inputs_kernel(all_ref, w_ref, x_ref, dh_ref, gain_ref, out0_ref, out1_ref, gg_ref):
    gain = gain_ref[...]
    gg_ref[...] = jnp.zeros((1, D), jnp.float32)
    for micro, out_ref in enumerate((out0_ref, out1_ref)):
        columns = slice(micro * TOK, (micro + 1) * TOK)
        upstream = dot_with(all_ref[:, columns].T, w_ref[...], 1, 1)
        values = x_ref[micro].astype(jnp.float32)
        scaling = lax.rsqrt(jnp.mean(values * values, axis=-1, keepdims=True) + norm_epsilon)
        part, gain_grad = norm_back(values, scaling, gain, upstream)
        gg_ref[...] += gain_grad
        out_ref[...] = (dh_ref[micro] + part).astype(out_ref.dtype)


def input_grads(grad_qkv, w_qkv, tokens, grad_state, gain):
    rows = grad_qkv.shape[1]
    return pl.pallas_call(
        inputs_kernel,
        out_shape=(
            jax.ShapeDtypeStruct((TOK, D), jnp.float32),
            jax.ShapeDtypeStruct((TOK, D), jnp.bfloat16),
            jax.ShapeDtypeStruct((1, D), jnp.float32),
        ),
        in_specs=[vmem()] * 5,
        out_specs=(vmem(),) * 3,
        compiler_params=kernel_params,
        cost_estimate=pl.CostEstimate(
            flops=2 * rows * D * 960, bytes_accessed=8000000, transcendentals=0
        ),
        name="input_grads",
    )(grad_qkv, w_qkv, tokens, grad_state, gain)


def newton_loop(matrix, scale):
    current = matrix / (jnp.sqrt(jnp.sum(matrix * matrix)) + frobenius_epsilon)

    def iterate(unused, held):
        low = held.astype(jnp.bfloat16)
        square = dot_with(low, low, 1, 1)
        square_low = square.astype(jnp.bfloat16)
        mixer = newton_second * square + newton_third * dot32(square_low, square_low)
        return newton_first * held + dot32(mixer.astype(jnp.bfloat16), low)

    return lax.fori_loop(0, NS_STEPS, iterate, current) * (0.2 * math.sqrt(scale))


def newton_kernel(info, pieces_ref, old_ref, grad_ref, out_ref, total):
    spot, kind = info[0], info[1]
    for chunk in range(CHUNKS):
        row, column = chunk // COL_CUT * CHUNK_ROWS, chunk % COL_CUT * CHUNK_COLS
        rows, columns = slice(row, row + CHUNK_ROWS), slice(column, column + CHUNK_COLS)
        part = pieces_ref[chunk ^ spot]
        grad_ref[rows, columns] = part
        total[rows, columns] = momentum_decay * old_ref[rows, columns].astype(
            jnp.float32
        ) + part.astype(jnp.float32)

    @pl.when(kind == 0)
    def _():
        out_ref[...] = newton_loop(total[...], FF)

    for place, low in ((1, 0), (2, FF - D)):

        @pl.when(kind == place)
        def _():
            out_ref[:, low : low + D] = newton_loop(total[:, low : low + D], D)

    for place, low in ((3, D), (4, D + KV_WIDTH)):

        @pl.when(kind == place)
        def _():
            out_ref[:, low : low + KV_WIDTH] = newton_loop(total[:, low : low + KV_WIDTH].T, D).T


def newton(info, pieces, old):
    return pl.pallas_call(
        newton_kernel,
        out_shape=(
            jax.ShapeDtypeStruct((D, FF), jnp.bfloat16),
            jax.ShapeDtypeStruct((D, FF), jnp.float32),
        ),
        in_specs=[smem(), vmem(), vmem()],
        out_specs=(vmem(),) * 2,
        scratch_shapes=[pltpu.VMEM((D, FF), jnp.float32)],
        compiler_params=kernel_params,
        cost_estimate=pl.CostEstimate(
            flops=12000000000, bytes_accessed=9000000, transcendentals=0
        ),
        name="newton",
    )(info, pieces, old)


def quarter_matrix(quarter, flat):
    def mixed_case(flat):
        square = D * D
        narrow = D * KV_WIDTH
        return jnp.concatenate(
            [
                flat[:square].reshape(D, D),
                flat[square : square + narrow].reshape(D, KV_WIDTH),
                flat[square + narrow : square + 2 * narrow].reshape(D, KV_WIDTH),
                flat[square + 2 * narrow :].reshape(D, D),
            ],
            axis=1,
        )

    def wide_case(flat):
        return flat.reshape(D, FF)

    def tall_case(flat):
        return flat.reshape(FF, D).T

    return lax.switch(quarter, [mixed_case, wide_case, wide_case, tall_case], flat)


def own_kind(quarter, within):
    square = D * D
    narrow = D * KV_WIDTH
    edges = (square, square + narrow, square + 2 * narrow)
    passed = sum((within >= edge).astype(jnp.int32) for edge in edges)
    mixed = jnp.array([1, 3, 4, 2], jnp.int32)[passed]
    starts = jnp.array([0, square, square + narrow, square + 2 * narrow], jnp.int32)
    inside = within - jnp.where(quarter == 0, starts[passed], 0)
    return (jnp.where(quarter == 0, mixed, 0), inside)


def own_rows(quarter, kind, inside, shard_length, gradient, update):
    def block_case(low, width):
        def run(gradient, update):
            start = (inside // width, low)
            size = (shard_length // width, width)
            return tuple(
                lax.dynamic_slice(whole, start, size).reshape(-1) for whole in (gradient, update)
            )

        return run

    def tall_case(gradient, update):
        start = (0, inside // D)
        size = (D, shard_length // D)
        return tuple(
            lax.dynamic_slice(whole, start, size).T.reshape(-1) for whole in (gradient, update)
        )

    cases = [
        block_case(0, FF),
        block_case(0, D),
        block_case(FF - D, D),
        block_case(D, KV_WIDTH),
        block_case(D + KV_WIDTH, KV_WIDTH),
        tall_case,
    ]
    return lax.switch(jnp.where(quarter == 3, 5, kind), cases, gradient, update)


CORE_SWAP = [(0, 1), (1, 0), (2, 3), (3, 2)]
CHIP_SWAP = [(0, 2), (2, 0), (1, 3), (3, 1)]
SIDE_SWAP = [(0, 1), (1, 0)]
END_SWAP = [(0, 3), (3, 0), (1, 2), (2, 1)]


def plane_steps():
    ctx = lax.axis_index("ctx")
    return (
        ("ctx", CORE_SWAP, lax.rem(ctx, 2)),
        ("ctx", CHIP_SWAP, ctx // 2),
        ("half", SIDE_SWAP, lax.axis_index("half")),
    )


def plane_sum(chunks):
    for axis, swap, bit in plane_steps():
        halves = chunks.reshape(2, chunks.shape[0] // 2, *chunks.shape[1:])
        sent = lax.dynamic_index_in_dim(halves, 1 - bit, 0, keepdims=False)
        kept = lax.dynamic_index_in_dim(halves, bit, 0, keepdims=False)
        got = lax.ppermute(sent, axis, swap)
        chunks = (kept.astype(jnp.float32) + got.astype(jnp.float32)).astype(jnp.bfloat16)
    return chunks[0]


def plane_gather(piece):
    pieces = piece[None]
    for axis, swap, bit in reversed(plane_steps()):
        pieces = jnp.concatenate([pieces, lax.ppermute(pieces, axis, swap)], axis=0)
    return pieces


def depth_sum(late, early):
    quarter = lax.axis_index("quarter")
    pieces = jnp.concatenate([late[None], early], axis=0)
    total = lax.dynamic_index_in_dim(pieces, quarter, 0, keepdims=False).astype(jnp.float32)
    for shift in range(1, 4):
        target = lax.rem(quarter + shift, 4)
        sent = lax.dynamic_index_in_dim(pieces, target, 0, keepdims=False)
        got = lax.ppermute(sent, "quarter", [(place, (place + shift) % 4) for place in range(4)])
        total = total + got.astype(jnp.float32)
    return total.astype(jnp.bfloat16)


def attention_info(ctx, begins):
    fields = [ctx]
    for tile in range(TOK // TILE):
        last = ctx * (TOK // TILE) + tile
        first = begins[tile * TILE] // TILE
        full = jnp.minimum(last, (begins[(tile + 1) * TILE - 1] + TILE - 1) // TILE)
        fields = fields + [first, full, last]
    return jnp.stack(fields).astype(jnp.int32)


def per_device(tokens, lengths, weights, momentum, norm_gains, gain_first, gain_second, cotangent):
    micro_count = tokens.shape[0]
    ctx = lax.axis_index("ctx")
    quarter = lax.axis_index("quarter")
    reps = lax.axis_size("rep")
    shard_length = weights.shape[0]
    within = lax.axis_index(("rep", "half", "ctx")) * shard_length
    spot = lax.rem(ctx, 2) * 4 + ctx // 2 * 2 + lax.axis_index("half")

    full_weights = lax.all_gather(weights.astype(jnp.bfloat16), EVERY, axis=0, tiled=True)
    square, narrow, broad = D * D, D * KV_WIDTH, D * FF
    places_in = [0, square, square + narrow, square + 2 * narrow]
    w_qkv = jnp.concatenate(
        [
            full_weights[:square].reshape(D, D),
            full_weights[places_in[1] : places_in[2]].reshape(D, KV_WIDTH),
            full_weights[places_in[2] : places_in[3]].reshape(D, KV_WIDTH),
        ],
        axis=1,
    )
    w_out = full_weights[places_in[3] : places_in[3] + square].reshape(D, D)
    w_gate = full_weights[broad : 2 * broad].reshape(D, FF)
    w_up = full_weights[2 * broad : 3 * broad].reshape(D, FF)
    w_down = full_weights[3 * broad :].reshape(FF, D)

    swapped = lax.ppermute(jnp.stack([tokens[1], cotangent[1]]), "ctx", END_SWAP)
    tokens_here = jnp.stack([tokens[0], swapped[0]])
    back = jnp.stack([cotangent[0], swapped[1]])
    inputs = tokens_here.astype(jnp.float32).reshape(-1, D)
    normed = normalize(inputs, norm_gains[0]).astype(jnp.bfloat16)
    infos, begin_rows, tables = [], [], []
    for micro in range(micro_count):
        block = ctx if micro == 0 else 3 - ctx
        own_places = block * TOK + jnp.arange(TOK, dtype=jnp.int32)
        offsets, begins = layout(lengths[micro, 0], own_places)
        infos.append(attention_info(block, begins))
        begin_rows.append(begins.reshape(1, TOK))
        tables.append(rope_tables(offsets))

    queries, keyvals, mixed, log_totals = [], [], [], []
    for micro in range(micro_count):
        rows = normed[micro * TOK : (micro + 1) * TOK]
        linear = jnp.einsum("de,td->et", w_qkv, rows, preferred_element_type=jnp.float32)
        turned = rotate_columns(linear[: D + KV_WIDTH], *tables[micro])
        scaled = turned[:D].astype(jnp.bfloat16) * jnp.bfloat16(0.125)
        queries.append(scaled.reshape(heads_shape))
        own_keyvals = jnp.concatenate([turned[D:], linear[D + KV_WIDTH :]], axis=0)
        keyvals.append(own_keyvals.astype(jnp.bfloat16))
    gathered = lax.all_gather(jnp.stack(keyvals), "ctx", axis=1, tiled=False)
    keyvals = [gathered[micro] for micro in range(micro_count)]
    for micro in range(micro_count):
        mixed_one, log_total = attend_forward(
            micro == 1, infos[micro], queries[micro], keyvals[micro], begin_rows[micro]
        )
        mixed.append(mixed_one)
        log_totals.append(log_total)
    result, grad_state, grad_mixed_0, grad_mixed_1, early, grad_w_out, gain_two_grad = mlp(
        tokens_here,
        back,
        [part.reshape(D, TOK) for part in mixed],
        w_out,
        w_gate,
        w_up,
        w_down,
        norm_gains[1:2],
    )
    returned = lax.ppermute(result[1].astype(jnp.bfloat16), "ctx", END_SWAP)
    result = jnp.stack([result[0], returned.astype(jnp.float32)])
    early = plane_sum(early)
    old = lax.all_gather(
        momentum.astype(jnp.bfloat16), ("rep", "half", "ctx"), axis=0, tiled=True
    )

    grad_queries, grad_keyvals = [], []
    for micro, grad_mixed in enumerate((grad_mixed_0, grad_mixed_1)):
        dq, dkv = attend_back(
            micro == 1,
            infos[micro],
            queries[micro],
            keyvals[micro],
            begin_rows[micro],
            mixed[micro],
            log_totals[micro],
            grad_mixed.reshape(heads_shape),
            *tables[micro],
        )
        for step, (swap, bit) in enumerate(((CORE_SWAP, lax.rem(ctx, 2)), (CHIP_SWAP, ctx // 2))):
            shaped = dkv.reshape(2, 2, 2 * KV_WIDTH, TOK) if step == 0 else dkv
            axis = 1 if step == 0 else 0
            sent = lax.dynamic_index_in_dim(shaped, 1 - bit, axis, keepdims=False)
            kept = lax.dynamic_index_in_dim(shaped, bit, axis, keepdims=False)
            got = lax.ppermute(sent, "ctx", swap)
            dkv = (kept.astype(jnp.float32) + got.astype(jnp.float32)).astype(jnp.bfloat16)
        grad_queries.append(dq.reshape(D, TOK))
        grad_keyvals.append(dkv)
    late, grad_qkv = projection_grads(normed, grad_queries, grad_keyvals, tables, grad_w_out)
    late = plane_sum(late)
    grad_inputs_0, grad_inputs_1, gain_one_grad = input_grads(
        grad_qkv, w_qkv, tokens_here, grad_state, norm_gains[0:1]
    )
    returned = lax.ppermute(grad_inputs_1, "ctx", END_SWAP)
    grad_inputs = jnp.stack([grad_inputs_0, returned.astype(jnp.float32)])
    gain_parts = lax.all_gather(
        jnp.concatenate([gain_one_grad, gain_two_grad], axis=0), EVERY, axis=0, tiled=False
    )
    gain_grad = jnp.sum(gain_parts, axis=0)

    piece = depth_sum(late, early)
    if reps > 1:
        piece = lax.psum(piece, "rep")
    pieces = plane_gather(piece)
    kind, inside = own_kind(quarter, within)
    gradient, update = newton(
        jnp.stack([spot, kind]).astype(jnp.int32), pieces, quarter_matrix(quarter, old)
    )
    grad_shard, update_shard = own_rows(quarter, kind, inside, shard_length, gradient, update)
    grad_shard = grad_shard.astype(jnp.float32)
    new_momentum = momentum_decay * momentum + grad_shard
    new_weights = weights * (1.0 - matrix_rate * weight_decay) - matrix_rate * update_shard

    first_new = first_decay * gain_first + (1.0 - first_decay) * gain_grad
    second_new = second_decay * gain_second + (1.0 - second_decay) * gain_grad * gain_grad
    debiased_first_moment = first_new / (1.0 - first_decay**ADAM_STEP)
    corrected_second = second_new / (1.0 - second_decay**ADAM_STEP)
    new_gains = norm_gains * (
        1.0 - gain_rate * weight_decay
    ) - gain_rate * debiased_first_moment / (jnp.sqrt(corrected_second) + adam_epsilon)
    return (
        result,
        grad_inputs,
        grad_shard,
        new_momentum,
        new_weights,
        first_new,
        second_new,
        new_gains,
    )


def solution(mesh):
    devices = mesh.devices
    count = devices.size
    context = mesh.shape["ctx"]
    split = Mesh(
        devices.reshape(4, count // (8 * context), 2, context), ("quarter", "rep", "half", "ctx")
    )
    rows = P(None, EVERY, None)
    flat = P(EVERY)
    placed = (rows, P(None, ("quarter", "rep", "half"), None), flat, flat, P(), P(), P(), rows)
    return jax.shard_map(
        per_device,
        mesh=split,
        in_specs=placed,
        out_specs=(rows, rows, flat, flat, flat, P(), P(), P()),
        check_vma=False,
    )
```

```python
from functools import partial
import math

import jax
import jax.numpy as jnp
from jax import lax
from jax.experimental import pallas as pl
from jax.experimental.pallas import tpu as pltpu
from jax.sharding import Mesh, PartitionSpec as P

HEADS = 9
KV_HEADS = 3
HEAD_DIM = 64
FF = 1536
NS_STEPS = 5
ADAM_STEP = 10
D = 576
KV_WIDTH = 192
GROUPS = HEADS // KV_HEADS
TOK = 512
TILE = 256
COLS = GROUPS * TILE
ROW_CUT = 4
COL_CUT = 2
CHUNKS = ROW_CUT * COL_CUT
CHUNK_ROWS = D // ROW_CUT
CHUNK_COLS = FF // COL_CUT
PLANE = ("half", "ctx")
EVERY = ("quarter", "rep", "half", "ctx")


norm_epsilon = 1e-05
rope_base = 100000.0
masked_score = -1e30
newton_first = 3.4445
newton_second = -4.775
newton_third = 2.0315
momentum_decay = 0.95
matrix_rate = 0.2
weight_decay = 0.1
gain_rate = 0.2
first_decay = 0.9
second_decay = 0.95
adam_epsilon = 1e-08
frobenius_epsilon = 1e-07


def layout(lengths_row, places):
    finish = jnp.cumsum(lengths_row)
    firsts = finish - lengths_row
    begins = jnp.max(jnp.where(places[:, None] >= firsts[None, :], firsts[None, :], 0), axis=1)
    return (places - begins, begins)


def rope_tables(offsets):
    half_width = HEAD_DIM // 2
    inverse = jnp.exp(
        jnp.arange(half_width, dtype=jnp.float32) * (-2.0 * math.log(rope_base) / HEAD_DIM)
    )
    angles = inverse[:, None] * offsets.astype(jnp.float32)[None, :]
    return (jnp.cos(angles), jnp.sin(angles))


def dot32(left, right):
    return jnp.dot(left, right, preferred_element_type=jnp.float32)


def masked(scores, key_block, begins, places):
    keys = key_block * TILE + lax.broadcasted_iota(jnp.int32, scores.shape, 0)
    return jnp.where((keys >= begins) & (keys <= places), scores, masked_score)


def tile_row(row, tile):
    part = row[:, tile * TILE : (tile + 1) * TILE]
    return jnp.concatenate([part] * GROUPS, axis=1)


def tile_heads(ref, group, tile):
    return jnp.concatenate(
        [ref[group, head, :, tile * TILE : (tile + 1) * TILE] for head in range(GROUPS)], axis=1
    )


def key_loop(info, tile, step, carry):
    first, full, last = info[1 + 3 * tile], info[2 + 3 * tile], info[3 + 3 * tile]
    pairs = (last - full) // 2
    carry = lax.fori_loop(first, full, partial(step, True, 1), carry)
    carry = lax.fori_loop(
        0, pairs, lambda pair, held: step(False, 2, full + 2 * pair, held), carry
    )
    carry = lax.fori_loop(full + 2 * pairs, last, partial(step, False, 1), carry)
    return step(True, 1, last, carry)


def key_slots(own, micro, kv_ref, other_ref, far_ref, far_other_ref):
    refs = (kv_ref.at[micro], other_ref.at[micro], far_ref, far_other_ref)
    return [(own ^ place, ref) for place, ref in enumerate(refs)]


def block_rows(block):
    return pl.ds(pl.multiple_of(block * TOK, TOK), TOK)


def forward_kernel(
    micro, info, q_ref, kv_ref, other_ref, far_ref, far_other_ref, begin_ref, tie_ref,
    o_ref, lse_ref, k_nat, v_ext,
):
    own = info[0]
    for block, source in key_slots(own, micro, kv_ref, other_ref, far_ref, far_other_ref):

        @pl.when(block <= own)
        def _():
            rows = block_rows(block)
            for group in range(KV_HEADS):
                low = HEAD_DIM * group
                k_nat[group, rows, :] = source[low : low + HEAD_DIM, :].T
                low = low + KV_WIDTH
                v_ext[group, :HEAD_DIM, rows] = source[low : low + HEAD_DIM, :]
                v_ext[group, HEAD_DIM:, rows] = jnp.ones((16, TOK), jnp.bfloat16)

    def one_group(group, unused):
        for tile in range(TOK // TILE):
            queries = tile_heads(q_ref, group, tile)
            begins = tile_row(begin_ref[...], tile)
            column = lax.broadcasted_iota(jnp.int32, (1, COLS), 1)
            places = own * TOK + tile * TILE + lax.rem(column, TILE)

            def step(is_masked, width, key_block, carry):
                top, total = carry
                keys = pl.ds(pl.multiple_of(key_block * TILE, TILE), width * TILE)
                scores = dot32(k_nat[group, keys, :], queries)
                if is_masked:
                    scores = masked(scores, key_block, begins, places)
                new_top = jnp.maximum(top, jnp.max(scores, axis=0, keepdims=True))
                probs = jnp.exp(scores - new_top).astype(jnp.bfloat16)
                total = total * jnp.exp(top - new_top) + dot32(v_ext[group, :, keys], probs)
                return (new_top, total)

            carry = (
                jnp.full((1, COLS), masked_score, jnp.float32),
                jnp.zeros((HEAD_DIM + 16, COLS), jnp.float32),
            )
            top, total = key_loop(info, tile, step, carry)
            weight = total[HEAD_DIM : HEAD_DIM + 1, :]
            mixed = (total[:HEAD_DIM, :] / weight).astype(jnp.bfloat16)
            log_total = top + jnp.log(weight)
            for head in range(GROUPS):
                o_ref[group, head, :, tile * TILE : (tile + 1) * TILE] = mixed[
                    :, head * TILE : (head + 1) * TILE
                ]
                lse_ref[group, head, :, tile * TILE : (tile + 1) * TILE] = log_total[
                    :, head * TILE : (head + 1) * TILE
                ]
        return unused

    lax.fori_loop(0, KV_HEADS, one_group, 0)


def backward_kernel(
    micro, info, q_ref, kv_ref, other_ref, far_ref, far_other_ref, begin_ref, o_ref, lse_ref,
    do_ref, cos_ref, sin_ref, tie_ref,
    dq_ref, keep_ref, send_ref, k_nat, v_nat, k_tall, dk_ref, dv_ref,
):
    own = info[0]
    slots = key_slots(own, micro, kv_ref, other_ref, far_ref, far_other_ref)
    for block, source in slots:

        @pl.when(block <= own)
        def _():
            rows = block_rows(block)
            for group in range(KV_HEADS):
                low = HEAD_DIM * group
                k_nat[group, rows, :] = source[low : low + HEAD_DIM, :].T
                k_tall[group, :, rows] = source[low : low + HEAD_DIM, :]
                low = low + KV_WIDTH
                v_nat[group, rows, :] = source[low : low + HEAD_DIM, :].T
                dk_ref[group, rows, :] = jnp.zeros((TOK, HEAD_DIM), jnp.float32)
                dv_ref[group, rows, :] = jnp.zeros((TOK, HEAD_DIM), jnp.float32)

    def one_group(group, unused):
        for tile in range(TOK // TILE):
            queries = tile_heads(q_ref, group, tile)
            upstream = tile_heads(do_ref, group, tile)
            mixed = tile_heads(o_ref, group, tile)
            log_total = tile_heads(lse_ref, group, tile)
            delta = jnp.sum(
                upstream.astype(jnp.float32) * mixed.astype(jnp.float32), axis=0, keepdims=True
            )
            queries_nat = queries.T
            upstream_nat = upstream.T
            begins = tile_row(begin_ref[...], tile)
            column = lax.broadcasted_iota(jnp.int32, (1, COLS), 1)
            places = own * TOK + tile * TILE + lax.rem(column, TILE)

            def step(is_masked, width, key_block, dq):
                rows = pl.ds(pl.multiple_of(key_block * TILE, TILE), width * TILE)
                scores = dot32(k_nat[group, rows, :], queries)
                if is_masked:
                    scores = masked(scores, key_block, begins, places)
                probs = jnp.exp(scores - log_total)
                grad_probs = dot32(v_nat[group, rows, :], upstream)
                grad_scores = (probs * (grad_probs - delta)).astype(jnp.bfloat16)
                dv_ref[group, rows, :] += dot32(probs.astype(jnp.bfloat16), upstream_nat)
                dk_ref[group, rows, :] += dot32(grad_scores, queries_nat)
                return dq + dot32(k_tall[group, :, rows], grad_scores)

            dq = jnp.zeros((HEAD_DIM, COLS), jnp.float32)
            dq = key_loop(info, tile, step, dq) * 0.125
            half_width = HEAD_DIM // 2
            cosine = tile_row(cos_ref[...], tile)
            sine = tile_row(sin_ref[...], tile)
            former, latter = dq[:half_width], dq[half_width:]
            turned = jnp.concatenate(
                [former * cosine + latter * sine, latter * cosine - former * sine], axis=0
            ).astype(jnp.bfloat16)
            for head in range(GROUPS):
                dq_ref[group, head, :, tile * TILE : (tile + 1) * TILE] = turned[
                    :, head * TILE : (head + 1) * TILE
                ]
        return unused

    lax.fori_loop(0, KV_HEADS, one_group, 0)
    for place, (block, _) in enumerate(slots):
        out_ref = (keep_ref, send_ref)[place % 2]

        @pl.when(block <= own)
        def _():
            rows = block_rows(block)
            for group in range(KV_HEADS):
                low = HEAD_DIM * group
                out_ref[place // 2, low : low + HEAD_DIM, :] = dk_ref[group, rows, :].T.astype(
                    jnp.bfloat16
                )
                low = low + KV_WIDTH
                out_ref[place // 2, low : low + HEAD_DIM, :] = dv_ref[group, rows, :].T.astype(
                    jnp.bfloat16
                )

        @pl.when(block > own)
        def _():
            out_ref[place // 2] = jnp.zeros((2 * KV_WIDTH, TOK), jnp.bfloat16)


def vmem():
    return pl.BlockSpec(memory_space=pltpu.VMEM)


def smem():
    return pl.BlockSpec(memory_space=pltpu.SMEM)


def anywhere():
    return pl.BlockSpec(memory_space=pl.ANY)


kernel_params = pltpu.CompilerParams(vmem_limit_bytes=56 * 1024 * 1024)
heads_shape = (KV_HEADS, GROUPS, HEAD_DIM, TOK)


def attend_forward(micro, info, queries, keyvals, begins, tie):
    return pl.pallas_call(
        partial(forward_kernel, micro),
        out_shape=(
            jax.ShapeDtypeStruct(heads_shape, jnp.bfloat16),
            jax.ShapeDtypeStruct((KV_HEADS, GROUPS, 1, TOK), jnp.float32),
        ),
        in_specs=[smem()] + [vmem()] * 6 + [anywhere()],
        out_specs=(vmem(), vmem()),
        scratch_shapes=[
            pltpu.VMEM((KV_HEADS, 4 * TOK, HEAD_DIM), jnp.bfloat16),
            pltpu.VMEM((KV_HEADS, HEAD_DIM + 16, 4 * TOK), jnp.bfloat16),
        ],
        compiler_params=kernel_params,
        cost_estimate=pl.CostEstimate(
            flops=4 * 9 * 64 * TOK * 2048, bytes_accessed=4000000, transcendentals=9 * TOK * 2048
        ),
        name="attend_forward",
    )(info, queries, *keyvals, begins, tie)


def attend_back(
    micro, info, queries, keyvals, begins, mixed, log_total, grad_mixed, cosine, sine, tie
):
    half_shape = (2, 2 * KV_WIDTH, TOK)
    return pl.pallas_call(
        partial(backward_kernel, micro),
        out_shape=(
            jax.ShapeDtypeStruct(heads_shape, jnp.bfloat16),
            jax.ShapeDtypeStruct(half_shape, jnp.bfloat16),
            jax.ShapeDtypeStruct(half_shape, jnp.bfloat16),
        ),
        in_specs=[smem()] + [vmem()] * 11 + [anywhere()],
        out_specs=(vmem(),) * 3,
        scratch_shapes=[
            pltpu.VMEM((KV_HEADS, 4 * TOK, HEAD_DIM), jnp.bfloat16),
            pltpu.VMEM((KV_HEADS, 4 * TOK, HEAD_DIM), jnp.bfloat16),
            pltpu.VMEM((KV_HEADS, HEAD_DIM, 4 * TOK), jnp.bfloat16),
            pltpu.VMEM((KV_HEADS, 4 * TOK, HEAD_DIM), jnp.float32),
            pltpu.VMEM((KV_HEADS, 4 * TOK, HEAD_DIM), jnp.float32),
        ],
        compiler_params=kernel_params,
        cost_estimate=pl.CostEstimate(
            flops=10 * 9 * 64 * TOK * 2048, bytes_accessed=8000000, transcendentals=9 * TOK * 2048
        ),
        name="attend_back",
    )(info, queries, *keyvals, begins, mixed, log_total, grad_mixed, cosine, sine, tie)


def dot_with(left, right, left_side, right_side):
    return lax.dot_general(
        left, right, (((left_side,), (right_side,)), ((), ())), preferred_element_type=jnp.float32
    )


def norm_back(values, scaling, gain, upstream):
    weighted = upstream * gain
    inner = jnp.mean(weighted * values, axis=-1, keepdims=True)
    gain_grad = jnp.sum(upstream * values * scaling, axis=0, keepdims=True)
    return (scaling * weighted - values * (scaling * scaling * scaling) * inner, gain_grad)


def row_parts(held, spot, side):
    for turn in range(ROW_CUT):
        start = (turn ^ (spot // COL_CUT)) * CHUNK_ROWS
        part = held[pl.ds(pl.multiple_of(start, CHUNK_ROWS), CHUNK_ROWS), :]
        yield (turn * COL_CUT + side, part.astype(jnp.bfloat16))


def mlp_kernel(
    info, x_ref, c_ref, o0_ref, o1_ref, wo_ref, wg_ref, wu_ref, wd_ref, gain_ref,
    out_ref, dh_ref, do0_ref, do1_ref, keep_ref, send_ref, gwo_ref, gg_ref,
    hid, dgate, dup, n2_tall, c_tall, dh_low, held,
):
    gain = gain_ref[...]
    gg_ref[...] = jnp.zeros((1, D), jnp.float32)
    block = 256
    for micro, (o_ref, do_ref) in enumerate(((o0_ref, do0_ref), (o1_ref, do1_ref))):
        rows = slice(micro * TOK, (micro + 1) * TOK)
        hidden_state = x_ref[micro].astype(jnp.float32) + dot32(o_ref[...].T, wo_ref[...])
        scaling = lax.rsqrt(
            jnp.mean(hidden_state * hidden_state, axis=-1, keepdims=True) + norm_epsilon
        )
        normed = (hidden_state * scaling * gain).astype(jnp.bfloat16)
        n2_tall[:, rows] = normed.T
        back = c_ref[micro]
        c_tall[:, rows] = back.T
        for column in range(0, FF, block):
            columns = slice(column, column + block)
            gate = dot32(normed, wg_ref[:, columns])
            upward = dot32(normed, wu_ref[:, columns])
            grad_hidden = dot_with(back, wd_ref[columns, :], 1, 1)
            sigmoid_gate = jax.nn.sigmoid(gate)
            activated = gate * sigmoid_gate
            hid[rows, columns] = (activated * upward).astype(jnp.bfloat16)
            dgate[rows, columns] = (
                grad_hidden * upward * sigmoid_gate * (1.0 + gate * (1.0 - sigmoid_gate))
            ).astype(jnp.bfloat16)
            dup[rows, columns] = (grad_hidden * activated).astype(jnp.bfloat16)
        out_ref[micro] = hidden_state + dot32(hid[rows, :], wd_ref[...])
        upstream = dot_with(dgate[rows, :], wg_ref[...], 1, 1) + dot_with(
            dup[rows, :], wu_ref[...], 1, 1
        )
        part, gain_grad = norm_back(hidden_state, scaling, gain, upstream)
        gg_ref[...] += gain_grad
        grad_state = back.astype(jnp.float32) + part
        dh_ref[micro] = grad_state
        low = grad_state.astype(jnp.bfloat16)
        dh_low[rows, :] = low
        do_ref[...] = dot_with(wo_ref[...], low, 1, 1).astype(jnp.bfloat16)
    for place, (left, right) in enumerate(((n2_tall, dgate), (n2_tall, dup), (c_tall, hid))):
        for side in range(COL_CUT):
            start = (side ^ (info[0] % COL_CUT)) * CHUNK_COLS
            for column in range(0, CHUNK_COLS, block):
                columns = pl.ds(pl.multiple_of(start + column, block), block)
                held[...] = dot32(left[...], right[:, columns])
                for index, part in row_parts(held, info[0], side):
                    out = (keep_ref, send_ref)[index // 4]
                    out[index % 4, place, :, column : column + block] = part
    gwo_ref[...] = (
        dot32(o0_ref[...], dh_low[:TOK, :]) + dot32(o1_ref[...], dh_low[TOK:, :])
    ).astype(jnp.bfloat16)


def mlp(info, tokens, cotangent, mixed, w_out, w_gate, w_up, w_down, gain):
    rows = tokens.shape[0] * TOK
    low = jnp.bfloat16
    return pl.pallas_call(
        mlp_kernel,
        out_shape=(
            jax.ShapeDtypeStruct(tokens.shape, jnp.float32),
            jax.ShapeDtypeStruct(tokens.shape, jnp.float32),
            jax.ShapeDtypeStruct((D, TOK), low),
            jax.ShapeDtypeStruct((D, TOK), low),
            jax.ShapeDtypeStruct((CHUNKS // 2, 3, CHUNK_ROWS, CHUNK_COLS), low),
            jax.ShapeDtypeStruct((CHUNKS // 2, 3, CHUNK_ROWS, CHUNK_COLS), low),
            jax.ShapeDtypeStruct((D, D), low),
            jax.ShapeDtypeStruct((1, D), jnp.float32),
        ),
        in_specs=[smem()] + [vmem()] * 9,
        out_specs=(vmem(),) * 8,
        scratch_shapes=[
            pltpu.VMEM((rows, FF), low),
            pltpu.VMEM((rows, FF), low),
            pltpu.VMEM((rows, FF), low),
            pltpu.VMEM((D, rows), low),
            pltpu.VMEM((D, rows), low),
            pltpu.VMEM((rows, D), low),
            pltpu.VMEM((D, 256), jnp.float32),
        ],
        compiler_params=kernel_params,
        cost_estimate=pl.CostEstimate(
            flops=6 * rows * 3 * D * FF, bytes_accessed=25000000, transcendentals=rows * FF
        ),
        name="mlp",
    )(info, tokens, cotangent, mixed[0], mixed[1], w_out, w_gate, w_up, w_down, gain)


def natural_tiles(flat, base, rows, width):
    pairs, step, whole = rows // 2, width * 2 // 128, width // 128
    parts = [flat[pl.ds(base + place, pairs, stride=step), :] for place in range(step)]
    even = parts[:whole] + [parts[whole][:, :HEAD_DIM]]
    odd = jnp.concatenate([parts[whole][:, HEAD_DIM:]] + parts[whole + 1 :], axis=1)
    return even, [odd[:, low : low + 128] for low in range(0, width, 128)]


def unflatten(flat, base, rows, width, tiles):
    even, odd = natural_tiles(flat, base, rows, width)
    for place, (first, second) in enumerate(zip(even, odd)):
        breadth = first.shape[1]
        if breadth < 128:
            blank = jnp.zeros((rows // 2, 128 - breadth), jnp.float32)
            first = jnp.concatenate([first, blank], axis=1)
            second = jnp.concatenate([second, blank], axis=1)
        tiles[place, pl.ds(0, rows // 2, stride=2), :] = first
        tiles[place, pl.ds(1, rows // 2, stride=2), :] = second


def tile_widths(width):
    return [(place, low, min(128, width - low)) for place, low in enumerate(range(0, width, 128))]


MIXED = ((0, 0, D), (2592, D, KV_WIDTH), (3456, D + KV_WIDTH, KV_WIDTH), (4320, FF - D, D))


def project_kernel(
    info, pieces_ref, x_ref, gain_ref, cos0_ref, sin0_ref, cos1_ref, sin1_ref,
    q0_ref, q1_ref, kv_ref, w_ref, wo_ref, n_ref, flat, tiles,
):
    spot = info[0]
    length = flat.shape[0] // CHUNKS
    for place in range(CHUNKS):
        half, chip, core = place // 4, place // 2 % 2, place % 2
        chunk = core * 4 + half * 2 + chip
        flat[place * length : (place + 1) * length, :] = pieces_ref[chunk ^ spot].astype(
            jnp.float32
        )
    for base, start, width in MIXED:
        unflatten(flat, base, D, width, tiles)
        for place, low, breadth in tile_widths(width):
            part = tiles[place][:D, :breadth].astype(jnp.bfloat16)
            if start < FF - D:
                w_ref[:, start + low : start + low + breadth] = part
            else:
                wo_ref[:, low : low + breadth] = part
    tall = w_ref[...].T
    half_width = HEAD_DIM // 2
    tables = ((q0_ref, cos0_ref, sin0_ref), (q1_ref, cos1_ref, sin1_ref))
    for micro, (q_ref, cos_ref, sin_ref) in enumerate(tables):
        values = x_ref[micro].astype(jnp.float32)
        scaling = lax.rsqrt(jnp.mean(values * values, axis=-1, keepdims=True) + norm_epsilon)
        normed = (values * scaling * gain_ref[...]).astype(jnp.bfloat16)
        n_ref[micro * TOK : (micro + 1) * TOK, :] = normed
        linear = dot_with(tall, normed, 1, 1)
        cosine, sine = cos_ref[...], sin_ref[...]
        for head in range(HEADS + KV_HEADS):
            low = head * HEAD_DIM
            former = linear[low : low + half_width]
            latter = linear[low + half_width : low + HEAD_DIM]
            turned = jnp.concatenate(
                [former * cosine - latter * sine, latter * cosine + former * sine], axis=0
            ).astype(jnp.bfloat16)
            if head < HEADS:
                scaled = turned.astype(jnp.float32) * 0.125
                q_ref[head // GROUPS, head % GROUPS] = scaled.astype(jnp.bfloat16)
            else:
                low = low - D
                kv_ref[micro, low : low + HEAD_DIM, :] = turned
        kv_ref[micro, KV_WIDTH:, :] = linear[D + KV_WIDTH :].astype(jnp.bfloat16)


def project(info, pieces, tokens, gain, tables):
    low = jnp.bfloat16
    return pl.pallas_call(
        project_kernel,
        out_shape=(
            jax.ShapeDtypeStruct(heads_shape, low),
            jax.ShapeDtypeStruct(heads_shape, low),
            jax.ShapeDtypeStruct((2, 2 * KV_WIDTH, TOK), low),
            jax.ShapeDtypeStruct((D, D + 2 * KV_WIDTH), low),
            jax.ShapeDtypeStruct((D, D), low),
            jax.ShapeDtypeStruct((2 * TOK, D), low),
        ),
        in_specs=[smem()] + [vmem()] * 7,
        out_specs=(vmem(),) * 6,
        scratch_shapes=[
            pltpu.VMEM((D * FF // 128, 128), jnp.float32),
            pltpu.VMEM((5, D, 128), jnp.float32),
        ],
        compiler_params=kernel_params,
        cost_estimate=pl.CostEstimate(
            flops=4 * TOK * D * 960, bytes_accessed=8000000, transcendentals=0
        ),
        name="project",
    )(info, pieces, tokens, gain, *tables[0], *tables[1])


def projection_kernel(
    info, n_ref, dq0_ref, dq1_ref, kept0_ref, kept1_ref, got_ref, far_ref,
    cos0_ref, sin0_ref, cos1_ref, sin1_ref, gwo_ref, tie_ref,
    keep_ref, send_ref, all_ref, held, cut,
):
    spot, chip = info[0], info[1]
    half_width = HEAD_DIM // 2
    parts = ((dq0_ref, kept0_ref, cos0_ref, sin0_ref), (dq1_ref, kept1_ref, cos1_ref, sin1_ref))
    for micro, (dq_ref, kept_ref, cos_ref, sin_ref) in enumerate(parts):
        columns = slice(micro * TOK, (micro + 1) * TOK)
        all_ref[:D, columns] = dq_ref[...]
        cosine, sine = cos_ref[...], sin_ref[...]
        summed = kept_ref[0].astype(jnp.float32) + got_ref[2 * micro].astype(jnp.float32)
        summed = summed + jnp.where(chip == micro, far_ref[...].astype(jnp.float32), 0.0)
        for head in range(KV_HEADS):
            low = head * HEAD_DIM
            former = summed[low : low + half_width, :]
            latter = summed[low + half_width : low + HEAD_DIM, :]
            all_ref[D + low : D + low + half_width, columns] = (
                former * cosine + latter * sine
            ).astype(jnp.bfloat16)
            all_ref[D + low + half_width : D + low + HEAD_DIM, columns] = (
                latter * cosine - former * sine
            ).astype(jnp.bfloat16)
        all_ref[D + KV_WIDTH :, columns] = summed[KV_WIDTH:, :].astype(jnp.bfloat16)
    held[:, : D + 2 * KV_WIDTH] = dot_with(n_ref[...].T, all_ref[...], 1, 1)
    held[:, D + 2 * KV_WIDTH :] = gwo_ref[...].astype(jnp.float32)
    for side in range(COL_CUT):
        start = (side ^ (spot % COL_CUT)) * CHUNK_COLS
        cut[...] = held[:, pl.ds(pl.multiple_of(start, CHUNK_COLS), CHUNK_COLS)]
        for index, part in row_parts(cut, spot, side):
            (keep_ref, send_ref)[index // 4][index % 4] = part


def projection_grads(info, normed, dqs, kept, got, far, tables, gwo, tie):
    rows = normed.shape[0]
    chunk_shape = (CHUNKS // 2, CHUNK_ROWS, CHUNK_COLS)
    return pl.pallas_call(
        projection_kernel,
        out_shape=(
            jax.ShapeDtypeStruct(chunk_shape, jnp.bfloat16),
            jax.ShapeDtypeStruct(chunk_shape, jnp.bfloat16),
            jax.ShapeDtypeStruct((D + 2 * KV_WIDTH, rows), jnp.bfloat16),
        ),
        in_specs=[smem()] + [vmem()] * 12 + [anywhere()],
        out_specs=(vmem(),) * 3,
        scratch_shapes=[
            pltpu.VMEM((D, FF), jnp.float32),
            pltpu.VMEM((D, CHUNK_COLS), jnp.float32),
        ],
        compiler_params=kernel_params,
        cost_estimate=pl.CostEstimate(
            flops=2 * rows * D * 960, bytes_accessed=8000000, transcendentals=0
        ),
        name="projection_grads",
    )(info, normed, *dqs, *kept, got, far, *tables[0], *tables[1], gwo, tie)


def add_kernel(left_ref, right_ref, tie_ref, out_ref):
    total = left_ref[...].astype(jnp.float32) + right_ref[...].astype(jnp.float32)
    out_ref[...] = total.astype(out_ref.dtype)


def tied_add(left, right, tie):
    return pl.pallas_call(
        add_kernel,
        out_shape=jax.ShapeDtypeStruct(left.shape, left.dtype),
        in_specs=[vmem(), vmem(), anywhere()],
        out_specs=vmem(),
        compiler_params=kernel_params,
        name="tied_add",
    )(left, right, tie)


def cast_kernel(value_ref, tie_ref, out_ref):
    out_ref[...] = value_ref[...].astype(out_ref.dtype)


def tied_cast(value, tie):
    return pl.pallas_call(
        cast_kernel,
        out_shape=jax.ShapeDtypeStruct(value.shape, jnp.bfloat16),
        in_specs=[vmem(), anywhere()],
        out_specs=vmem(),
        compiler_params=kernel_params,
        name="tied_cast",
    )(value, tie)


def inputs_kernel(all_ref, w_ref, x_ref, dh_ref, gain_ref, out0_ref, out1_ref, gg_ref):
    gain = gain_ref[...]
    gg_ref[...] = jnp.zeros((1, D), jnp.float32)
    for micro, out_ref in enumerate((out0_ref, out1_ref)):
        columns = slice(micro * TOK, (micro + 1) * TOK)
        upstream = dot_with(all_ref[:, columns].T, w_ref[...], 1, 1)
        values = x_ref[micro].astype(jnp.float32)
        scaling = lax.rsqrt(jnp.mean(values * values, axis=-1, keepdims=True) + norm_epsilon)
        part, gain_grad = norm_back(values, scaling, gain, upstream)
        gg_ref[...] += gain_grad
        out_ref[...] = (dh_ref[micro] + part).astype(out_ref.dtype)


def input_grads(grad_qkv, w_qkv, tokens, grad_state, gain):
    rows = grad_qkv.shape[1]
    return pl.pallas_call(
        inputs_kernel,
        out_shape=(
            jax.ShapeDtypeStruct((TOK, D), jnp.float32),
            jax.ShapeDtypeStruct((TOK, D), jnp.bfloat16),
            jax.ShapeDtypeStruct((1, D), jnp.float32),
        ),
        in_specs=[vmem()] * 5,
        out_specs=(vmem(),) * 3,
        compiler_params=kernel_params,
        cost_estimate=pl.CostEstimate(
            flops=2 * rows * D * 960, bytes_accessed=8000000, transcendentals=0
        ),
        name="input_grads",
    )(grad_qkv, w_qkv, tokens, grad_state, gain)


def newton_loop(matrix, scale):
    current = matrix / (jnp.sqrt(jnp.sum(matrix * matrix)) + frobenius_epsilon)

    def iterate(unused, held):
        low = held.astype(jnp.bfloat16)
        square = dot_with(low, low, 1, 1)
        square_low = square.astype(jnp.bfloat16)
        mixer = newton_second * square + newton_third * dot32(square_low, square_low)
        return newton_first * held + dot32(mixer.astype(jnp.bfloat16), low)

    return lax.fori_loop(0, NS_STEPS, iterate, current) * (0.2 * math.sqrt(scale))


def flatten_rows(tiles, start, rows, width, out):
    pairs, step, whole = rows // 2, width * 2 // 128, width // 128
    spans = range(whole + 1)
    even = [tiles[place, pl.ds(start, pairs, stride=2), :] for place in spans]
    odd = [tiles[place, pl.ds(start + 1, pairs, stride=2), :] for place in spans]
    for place in range(whole):
        out[pl.ds(place, pairs, stride=step), :] = even[place]
    rest = width - whole * 128
    joined = jnp.concatenate([even[whole][:, :rest]] + odd[:whole] + [odd[whole][:, :rest]], axis=1)
    for place in range(whole, step):
        low = (place - whole) * 128
        out[pl.ds(place, pairs, stride=step), :] = joined[:, low : low + 128]


def shard_rows(kind, start, matrix, tiles, out):
    length = out.shape[0] * 128

    @pl.when(kind == 0)
    def _():
        rows = length // FF
        for place in range(FF // 128):
            out[pl.ds(place, rows, stride=FF // 128), :] = matrix[
                pl.ds(pl.multiple_of(start, 8), rows), place * 128 : (place + 1) * 128
            ]

    @pl.when(kind == 5)
    def _():
        for place, low, breadth in tile_widths(D):
            tiles[place, :, :breadth] = matrix[low : low + breadth, :].T
        flatten_rows(tiles, start, length // D, D, out)

    for place, (base, low, width) in zip((1, 3, 4, 2), MIXED):

        @pl.when(kind == place)
        def _():
            for tile, column, breadth in tile_widths(width):
                tiles[tile, :D, :breadth] = matrix[:, low + column : low + column + breadth]
            flatten_rows(tiles, start, length // width, width, out)


def newton_kernel(local, info, pieces_ref, old_ref, *refs):
    spot, kind, start = info[0], info[1], info[2]
    grad, total, tiles = refs[-3:]
    for chunk in range(CHUNKS):
        row, column = chunk // COL_CUT * CHUNK_ROWS, chunk % COL_CUT * CHUNK_COLS
        rows, columns = slice(row, row + CHUNK_ROWS), slice(column, column + CHUNK_COLS)
        grad[rows, columns] = pieces_ref[chunk ^ spot].astype(jnp.float32)

    def newton_body(flat):
        flat[...] = old_ref[...].astype(jnp.float32) * momentum_decay

        @pl.when(kind == 0)
        def _():
            for place in range(FF // 128):
                columns = slice(place * 128, (place + 1) * 128)
                total[:, columns] = flat[pl.ds(place, D, stride=FF // 128), :] + grad[:, columns]

        @pl.when(kind == 5)
        def _():
            unflatten(flat, 0, FF, D, tiles)
            for place, low, breadth in tile_widths(D):
                rows = slice(low, low + breadth)
                total[rows, :] = tiles[place].T[:breadth] + grad[rows, :]

        @pl.when((kind == 0) | (kind == 5))
        def _():
            total[...] = newton_loop(total[...], FF)

        for place, (base, low, width) in zip((1, 3, 4, 2), MIXED):

            @pl.when(kind == place)
            def _():
                unflatten(flat, base, D, width, tiles)
                part = jnp.concatenate(
                    [tiles[tile][:D, :breadth] for tile, _, breadth in tile_widths(width)], axis=1
                )
                columns = slice(low, low + width)
                part = part + grad[:, columns]
                if width == D:
                    total[:, columns] = newton_loop(part, D)
                else:
                    total[:, columns] = newton_loop(part.T, D).T

    pl.run_scoped(newton_body, pltpu.VMEM((D * FF // 128, 128), jnp.float32))
    if local:
        weights_ref, momentum_ref, grad_ref, new_momentum_ref, new_weights_ref = refs[:5]
        shard_rows(kind, start, grad, tiles, grad_ref)
        shard_rows(kind, start, total, tiles, new_weights_ref)
        new_momentum_ref[...] = momentum_decay * momentum_ref[...] + grad_ref[...]
        new_weights_ref[...] = (
            weights_ref[...] * (1.0 - matrix_rate * weight_decay)
            - matrix_rate * new_weights_ref[...]
        )
    else:
        refs[0][...] = grad[...]
        refs[1][...] = total[...]


def newton(info, pieces, old, *shards):
    local = len(shards) > 0
    if local:
        outs = (jax.ShapeDtypeStruct(shards[0].shape, jnp.float32),) * 3
    else:
        outs = (jax.ShapeDtypeStruct((D, FF), jnp.float32),) * 2
    return pl.pallas_call(
        partial(newton_kernel, local),
        out_shape=outs,
        in_specs=[smem()] + [vmem()] * (2 + len(shards)),
        out_specs=(vmem(),) * len(outs),
        scratch_shapes=[
            pltpu.VMEM((D, FF), jnp.float32),
            pltpu.VMEM((D, FF), jnp.float32),
            pltpu.VMEM((5, FF, 128), jnp.float32),
        ],
        compiler_params=kernel_params,
        cost_estimate=pl.CostEstimate(
            flops=12000000000, bytes_accessed=9000000, transcendentals=0
        ),
        name="newton",
    )(info, pieces, old, *shards)


def own_kind(quarter, within):
    square = D * D
    narrow = D * KV_WIDTH
    edges = (square, square + narrow, square + 2 * narrow)
    passed = sum((within >= edge).astype(jnp.int32) for edge in edges)
    mixed = jnp.array([1, 3, 4, 2], jnp.int32)[passed]
    starts = jnp.array([0, square, square + narrow, square + 2 * narrow], jnp.int32)
    inside = within - jnp.where(quarter == 0, starts[passed], 0)
    return (jnp.where(quarter == 0, mixed, jnp.where(quarter == 3, 5, 0)), inside)


def own_rows(kind, inside, shard_length, gradient, update):
    def block_case(low, width):
        def run(gradient, update):
            start = (inside // width, low)
            size = (shard_length // width, width)
            return tuple(
                lax.dynamic_slice(whole, start, size).reshape(-1) for whole in (gradient, update)
            )

        return run

    def tall_case(gradient, update):
        start = (0, inside // D)
        size = (D, shard_length // D)
        return tuple(
            lax.dynamic_slice(whole, start, size).T.reshape(-1) for whole in (gradient, update)
        )

    cases = [
        block_case(0, FF),
        block_case(0, D),
        block_case(FF - D, D),
        block_case(D, KV_WIDTH),
        block_case(D + KV_WIDTH, KV_WIDTH),
        tall_case,
    ]
    return lax.switch(kind, cases, gradient, update)


CORE_SWAP = [(0, 1), (1, 0), (2, 3), (3, 2)]
CHIP_SWAP = [(0, 2), (2, 0), (1, 3), (3, 1)]
SIDE_SWAP = [(0, 1), (1, 0)]
END_SWAP = [(0, 3), (3, 0), (1, 2), (2, 1)]


def plane_swap(value, bit):
    axis, swap = (("ctx", CHIP_SWAP), ("half", SIDE_SWAP), ("ctx", CORE_SWAP))[bit]
    return lax.ppermute(value, axis, swap)


def low_sum(left, right):
    return (left.astype(jnp.float32) + right.astype(jnp.float32)).astype(jnp.bfloat16)


def plane_gather(piece):
    pieces = piece[None]
    for bit in range(3):
        pieces = jnp.concatenate([pieces, plane_swap(pieces, bit)], axis=0)
    return pieces


def depth_sum(late, early):
    quarter = lax.axis_index("quarter")
    pieces = jnp.concatenate([late[None], early], axis=0)
    total = lax.dynamic_index_in_dim(pieces, quarter, 0, keepdims=False).astype(jnp.float32)
    for shift in range(1, 4):
        target = lax.rem(quarter + shift, 4)
        sent = lax.dynamic_index_in_dim(pieces, target, 0, keepdims=False)
        got = lax.ppermute(sent, "quarter", [(place, (place + shift) % 4) for place in range(4)])
        total = total + got.astype(jnp.float32)
    return total.astype(jnp.bfloat16)


def attention_info(ctx, begins):
    fields = [ctx]
    for tile in range(TOK // TILE):
        last = ctx * (TOK // TILE) + tile
        first = begins[tile * TILE] // TILE
        full = jnp.minimum(last, (begins[(tile + 1) * TILE - 1] + TILE - 1) // TILE)
        fields = fields + [first, full, last]
    return jnp.stack(fields).astype(jnp.int32)


def gather_weights(low, spot):
    rows = low.shape[0]
    if lax.axis_size("rep") > 1:
        full = lax.all_gather(low, EVERY, axis=0, tiled=True).reshape(4, D * FF)
        order = [4 * (place // 2 % 2) + 2 * (place % 2) + place // 4 for place in range(CHUNKS)]
        mixed = full[0].reshape(CHUNKS, -1, 128)
        mixed = jnp.stack([mixed[place] for place in order])
        return (mixed, jnp.zeros_like(spot)), [
            full[1].reshape(D, FF),
            full[2].reshape(D, FF),
            full[3].reshape(FF, D),
        ]
    depth = lax.all_gather(low, "quarter", axis=0, tiled=False)
    mixed = plane_gather(depth[0])
    shapes = ((D // CHUNKS, FF), (D // CHUNKS, FF), (FF // CHUNKS, D))
    rest = [
        lax.all_gather(depth[place + 1].reshape(shape), PLANE, axis=0, tiled=True)
        for place, shape in enumerate(shapes)
    ]
    return (mixed, spot), rest


def per_device(tokens, lengths, weights, momentum, norm_gains, gain_first, gain_second, cotangent):
    ctx = lax.axis_index("ctx")
    core, chip = lax.rem(ctx, 2), ctx // 2
    quarter = lax.axis_index("quarter")
    reps = lax.axis_size("rep")
    shard_length = weights.shape[0]
    flat_shape = (shard_length // 128, 128)
    within = lax.axis_index(("rep", "half", "ctx")) * shard_length
    spot = core * 4 + lax.axis_index("half") * 2 + chip
    place_info = jnp.stack([spot, chip]).astype(jnp.int32)

    (mixed_weights, mixed_spot), (w_gate, w_up, w_down) = gather_weights(
        weights.reshape(flat_shape).astype(jnp.bfloat16), spot
    )
    swapped = lax.ppermute(jnp.stack([tokens[1], cotangent[1]]), "ctx", END_SWAP)
    tokens_here = jnp.stack([tokens[0], swapped[0]])
    back = jnp.stack([cotangent[0], swapped[1]])
    infos, begin_rows, tables = [], [], []
    for micro in range(2):
        block = ctx if micro == 0 else 3 - ctx
        own_places = block * TOK + jnp.arange(TOK, dtype=jnp.int32)
        offsets, begins = layout(lengths[micro, 0], own_places)
        infos.append(attention_info(block, begins))
        begin_rows.append(begins.reshape(1, TOK))
        tables.append(rope_tables(offsets))

    q0, q1, keyvals, w_qkv, w_out, normed = project(
        mixed_spot.reshape(1).astype(jnp.int32), mixed_weights, tokens_here, norm_gains[0:1], tables
    )
    queries = (q0, q1)
    far = lax.ppermute(
        lax.dynamic_index_in_dim(keyvals, chip, 0, keepdims=False), "ctx", CHIP_SWAP
    )
    keyvals = (
        keyvals,
        lax.ppermute(keyvals, "ctx", CORE_SWAP),
        far,
        lax.ppermute(far, "ctx", CORE_SWAP),
    )
    mixed, log_totals = [], []
    tie = norm_gains
    for micro in range(2):
        mixed_one, log_total = attend_forward(
            micro, infos[micro], queries[micro], keyvals, begin_rows[micro], tie
        )
        mixed.append(mixed_one)
        log_totals.append(log_total)
    old = lax.all_gather(
        tied_cast(momentum.reshape(flat_shape), mixed[0]),
        ("rep", "half", "ctx"),
        axis=0,
        tiled=True,
    )
    result, grad_state, grad_mixed_0, grad_mixed_1, keep, send, grad_w_out, gain_two_grad = mlp(
        place_info,
        tokens_here,
        back,
        [part.reshape(D, TOK) for part in mixed],
        w_out,
        w_gate,
        w_up,
        w_down,
        norm_gains[1:2],
    )
    returned = lax.ppermute(result[1].astype(jnp.bfloat16), "ctx", END_SWAP)
    result = jnp.stack([result[0], returned.astype(jnp.float32)])

    def back_pass(micro, grad_mixed, tie):
        return attend_back(
            micro,
            infos[micro],
            queries[micro],
            keyvals,
            begin_rows[micro],
            mixed[micro],
            log_totals[micro],
            grad_mixed.reshape(heads_shape),
            *tables[micro],
            tie,
        )

    got = plane_swap(send, 2)
    dq0, kept0, sent0 = back_pass(0, grad_mixed_0, old)
    early = low_sum(keep, got)
    got = plane_swap(early[2:], 1)
    dq1, kept1, sent1 = back_pass(1, grad_mixed_1, early)
    traded = lax.ppermute(jnp.concatenate([sent0, sent1], axis=0), "ctx", CORE_SWAP)
    heavy = chip == 0
    crossing = low_sum(
        jnp.where(heavy, kept1[1], kept0[1]), jnp.where(heavy, traded[3], traded[1])
    )
    crossed = lax.ppermute(crossing, "ctx", CHIP_SWAP)
    early = low_sum(early[:2], got)
    late_keep, late_send, grad_qkv = projection_grads(
        place_info,
        normed,
        (dq0.reshape(D, TOK), dq1.reshape(D, TOK)),
        (kept0, kept1),
        traded,
        crossed,
        tables,
        grad_w_out,
        early,
    )
    early = low_sum(early[0], plane_swap(early[1], 0))
    late = low_sum(late_keep, plane_swap(late_send, 2))
    late = low_sum(late[:2], plane_swap(late[2:], 1))
    grad_inputs_0, grad_inputs_1, gain_one_grad = input_grads(
        grad_qkv, w_qkv, tokens_here, grad_state, norm_gains[0:1]
    )
    late = tied_add(late[0], plane_swap(late[1], 0), gain_one_grad)
    returned = lax.ppermute(grad_inputs_1, "ctx", END_SWAP)
    grad_inputs = jnp.stack([grad_inputs_0, returned.astype(jnp.float32)])
    gain_grad = jnp.concatenate([gain_one_grad, gain_two_grad], axis=0)
    for bit in range(3):
        gain_grad = gain_grad + plane_swap(gain_grad, bit)
    gain_grad = gain_grad + sum(
        lax.ppermute(gain_grad, "quarter", [(place, (place + shift) % 4) for place in range(4)])
        for shift in range(1, 4)
    )

    piece = depth_sum(late, early)
    if reps > 1:
        piece = lax.psum(piece, "rep")
        gain_grad = lax.psum(gain_grad, "rep")
    pieces = plane_gather(piece)
    kind, inside = own_kind(quarter, within)
    if flat_shape[0] % 8 == 0:
        width = jnp.array([FF, D, D, KV_WIDTH, KV_WIDTH, D], jnp.int32)[kind]
        grad_shard, new_momentum, new_weights = newton(
            jnp.stack([spot, kind, inside // width]).astype(jnp.int32),
            pieces,
            old,
            weights.reshape(flat_shape),
            momentum.reshape(flat_shape),
        )
    else:
        gradient, update = newton(
            jnp.stack([spot, kind, kind]).astype(jnp.int32), pieces, old
        )
        grad_shard, update_shard = own_rows(kind, inside, shard_length, gradient, update)
        new_momentum = momentum_decay * momentum + grad_shard
        new_weights = weights * (1.0 - matrix_rate * weight_decay) - matrix_rate * update_shard

    first_new = first_decay * gain_first + (1.0 - first_decay) * gain_grad
    second_new = second_decay * gain_second + (1.0 - second_decay) * gain_grad * gain_grad
    debiased_first_moment = first_new / (1.0 - first_decay**ADAM_STEP)
    corrected_second = second_new / (1.0 - second_decay**ADAM_STEP)
    new_gains = norm_gains * (
        1.0 - gain_rate * weight_decay
    ) - gain_rate * debiased_first_moment / (jnp.sqrt(corrected_second) + adam_epsilon)
    return (
        result,
        grad_inputs,
        grad_shard.reshape(weights.shape),
        new_momentum.reshape(weights.shape),
        new_weights.reshape(weights.shape),
        first_new,
        second_new,
        new_gains,
    )


def solution(mesh):
    devices = mesh.devices
    count = devices.size
    context = mesh.shape["ctx"]
    split = Mesh(
        devices.reshape(4, count // (8 * context), 2, context), ("quarter", "rep", "half", "ctx")
    )
    rows = P(None, EVERY, None)
    flat = P(EVERY)
    placed = (rows, P(None, ("quarter", "rep", "half"), None), flat, flat, P(), P(), P(), rows)
    return jax.shard_map(
        per_device,
        mesh=split,
        in_specs=placed,
        out_specs=(rows, rows, flat, flat, flat, P(), P(), P()),
        check_vma=False,
    )
```

```python
from functools import partial
import math

import jax
import jax.numpy as jnp
from jax import lax
from jax.experimental import pallas as pl
from jax.experimental.pallas import tpu as pltpu
from jax.sharding import Mesh, PartitionSpec as P

HEADS = 9
KV_HEADS = 3
HEAD_DIM = 64
FF = 1536
NS_STEPS = 5
ADAM_STEP = 10
D = 576
KV_WIDTH = 192
GROUPS = HEADS // KV_HEADS
TOK = 512
TILE = 256
COLS = GROUPS * TILE
ROW_CUT = 4
COL_CUT = 2
CHUNKS = ROW_CUT * COL_CUT
CHUNK_ROWS = D // ROW_CUT
CHUNK_COLS = FF // COL_CUT
PLANE = ("half", "ctx")
EVERY = ("quarter", "rep", "half", "ctx")


norm_epsilon = 1e-05
rope_base = 100000.0
masked_score = -1e30
newton_first = 3.4445
newton_second = -4.775
newton_third = 2.0315
momentum_decay = 0.95
matrix_rate = 0.2
weight_decay = 0.1
gain_rate = 0.2
first_decay = 0.9
second_decay = 0.95
adam_epsilon = 1e-08
frobenius_epsilon = 1e-07


def layout(lengths_row, places):
    finish = jnp.cumsum(lengths_row)
    firsts = finish - lengths_row
    begins = jnp.max(jnp.where(places[:, None] >= firsts[None, :], firsts[None, :], 0), axis=1)
    return (places - begins, begins)


def rope_tables(offsets):
    half_width = HEAD_DIM // 2
    inverse = jnp.exp(
        jnp.arange(half_width, dtype=jnp.float32) * (-2.0 * math.log(rope_base) / HEAD_DIM)
    )
    angles = inverse[:, None] * offsets.astype(jnp.float32)[None, :]
    return (jnp.cos(angles), jnp.sin(angles))


def dot32(left, right):
    return jnp.dot(left, right, preferred_element_type=jnp.float32)


def masked(scores, key_block, begins, places):
    keys = key_block * TILE + lax.broadcasted_iota(jnp.int32, scores.shape, 0)
    return jnp.where((keys >= begins) & (keys <= places), scores, masked_score)


def tile_row(row, tile):
    part = row[:, tile * TILE : (tile + 1) * TILE]
    return jnp.concatenate([part] * GROUPS, axis=1)


def tile_heads(ref, group, tile):
    return jnp.concatenate(
        [ref[group, head, :, tile * TILE : (tile + 1) * TILE] for head in range(GROUPS)], axis=1
    )


def positions():
    ctx = lax.axis_index("ctx")
    return (lax.axis_index("quarter"), lax.axis_index("half"), lax.div(ctx, 2), lax.rem(ctx, 2))


def chunk_spot():
    _, half, chip, core = positions()
    return core * 4 + half * 2 + chip


def first_key(lengths_ref, micro, row):
    begin = jnp.int32(0)
    first = jnp.int32(0)
    for place in range(3):
        first = first + lengths_ref[micro, place]
        begin = jnp.where(row >= first, first, begin)
    return begin


def key_loop(lengths_ref, micro, own, tile, step, carry):
    last = own * (TOK // TILE) + tile
    first = lax.div(first_key(lengths_ref, micro, last * TILE), TILE)
    full = lax.div(first_key(lengths_ref, micro, last * TILE + TILE - 1) + TILE - 1, TILE)
    full = jnp.minimum(full, last)
    pairs = lax.div(last - full, 2)
    carry = lax.fori_loop(first, full, partial(step, True, 1), carry)
    carry = lax.fori_loop(
        0, pairs, lambda pair, held: step(False, 2, full + 2 * pair, held), carry
    )
    carry = lax.fori_loop(full + 2 * pairs, last, partial(step, False, 1), carry)
    return step(True, 1, last, carry)


def own_block(micro):
    ctx = lax.axis_index("ctx")
    return ctx if micro == 0 else 3 - ctx


def key_slots(own, micro, kv_ref, other_ref, far_ref, far_other_ref):
    refs = (kv_ref.at[micro], other_ref.at[micro], far_ref, far_other_ref)
    return [(own ^ place, ref) for place, ref in enumerate(refs)]


def block_rows(block):
    return pl.ds(pl.multiple_of(block * TOK, TOK), TOK)


def forward_kernel(
    micro, lengths_ref, q_ref, kv_ref, other_ref, far_ref, far_other_ref, begin_ref, tie_ref,
    o_ref, lse_ref, k_nat, v_ext,
):
    own = own_block(micro)
    for block, source in key_slots(own, micro, kv_ref, other_ref, far_ref, far_other_ref):

        @pl.when(block <= own)
        def _():
            rows = block_rows(block)
            for group in range(KV_HEADS):
                low = HEAD_DIM * group
                k_nat[group, rows, :] = source[low : low + HEAD_DIM, :].T
                low = low + KV_WIDTH
                v_ext[group, :HEAD_DIM, rows] = source[low : low + HEAD_DIM, :]
                v_ext[group, HEAD_DIM:, rows] = jnp.ones((16, TOK), jnp.bfloat16)

    def one_group(group, unused):
        for tile in range(TOK // TILE):
            queries = tile_heads(q_ref, group, tile)
            begins = tile_row(begin_ref[...], tile)
            column = lax.broadcasted_iota(jnp.int32, (1, COLS), 1)
            places = own * TOK + tile * TILE + lax.rem(column, TILE)

            def step(is_masked, width, key_block, carry):
                top, total = carry
                keys = pl.ds(pl.multiple_of(key_block * TILE, TILE), width * TILE)
                scores = dot32(k_nat[group, keys, :], queries)
                if is_masked:
                    scores = masked(scores, key_block, begins, places)
                new_top = jnp.maximum(top, jnp.max(scores, axis=0, keepdims=True))
                probs = jnp.exp(scores - new_top).astype(jnp.bfloat16)
                total = total * jnp.exp(top - new_top) + dot32(v_ext[group, :, keys], probs)
                return (new_top, total)

            carry = (
                jnp.full((1, COLS), masked_score, jnp.float32),
                jnp.zeros((HEAD_DIM + 16, COLS), jnp.float32),
            )
            top, total = key_loop(lengths_ref, micro, own, tile, step, carry)
            weight = total[HEAD_DIM : HEAD_DIM + 1, :]
            mixed = (total[:HEAD_DIM, :] / weight).astype(jnp.bfloat16)
            log_total = top + jnp.log(weight)
            for head in range(GROUPS):
                o_ref[group, head, :, tile * TILE : (tile + 1) * TILE] = mixed[
                    :, head * TILE : (head + 1) * TILE
                ]
                lse_ref[group, head, :, tile * TILE : (tile + 1) * TILE] = log_total[
                    :, head * TILE : (head + 1) * TILE
                ]
        return unused

    lax.fori_loop(0, KV_HEADS, one_group, 0)


def backward_kernel(
    micro, lengths_ref, q_ref, kv_ref, other_ref, far_ref, far_other_ref, begin_ref, o_ref, lse_ref,
    do_ref, cos_ref, sin_ref, tie_ref,
    dq_ref, keep_ref, send_ref, k_nat, v_nat, k_tall, dk_ref, dv_ref,
):
    own = own_block(micro)
    slots = key_slots(own, micro, kv_ref, other_ref, far_ref, far_other_ref)
    for block, source in slots:

        @pl.when(block <= own)
        def _():
            rows = block_rows(block)
            for group in range(KV_HEADS):
                low = HEAD_DIM * group
                k_nat[group, rows, :] = source[low : low + HEAD_DIM, :].T
                k_tall[group, :, rows] = source[low : low + HEAD_DIM, :]
                low = low + KV_WIDTH
                v_nat[group, rows, :] = source[low : low + HEAD_DIM, :].T
                dk_ref[group, rows, :] = jnp.zeros((TOK, HEAD_DIM), jnp.float32)
                dv_ref[group, rows, :] = jnp.zeros((TOK, HEAD_DIM), jnp.float32)

    def one_group(group, unused):
        for tile in range(TOK // TILE):
            queries = tile_heads(q_ref, group, tile)
            upstream = tile_heads(do_ref, group, tile)
            mixed = tile_heads(o_ref, group, tile)
            log_total = tile_heads(lse_ref, group, tile)
            delta = jnp.sum(
                upstream.astype(jnp.float32) * mixed.astype(jnp.float32), axis=0, keepdims=True
            )
            queries_nat = queries.T
            upstream_nat = upstream.T
            begins = tile_row(begin_ref[...], tile)
            column = lax.broadcasted_iota(jnp.int32, (1, COLS), 1)
            places = own * TOK + tile * TILE + lax.rem(column, TILE)

            def step(is_masked, width, key_block, dq):
                rows = pl.ds(pl.multiple_of(key_block * TILE, TILE), width * TILE)
                scores = dot32(k_nat[group, rows, :], queries)
                if is_masked:
                    scores = masked(scores, key_block, begins, places)
                probs = jnp.exp(scores - log_total)
                grad_probs = dot32(v_nat[group, rows, :], upstream)
                grad_scores = (probs * (grad_probs - delta)).astype(jnp.bfloat16)
                dv_ref[group, rows, :] += dot32(probs.astype(jnp.bfloat16), upstream_nat)
                dk_ref[group, rows, :] += dot32(grad_scores, queries_nat)
                return dq + dot32(k_tall[group, :, rows], grad_scores)

            dq = jnp.zeros((HEAD_DIM, COLS), jnp.float32)
            dq = key_loop(lengths_ref, micro, own, tile, step, dq) * 0.125
            half_width = HEAD_DIM // 2
            cosine = tile_row(cos_ref[...], tile)
            sine = tile_row(sin_ref[...], tile)
            former, latter = dq[:half_width], dq[half_width:]
            turned = jnp.concatenate(
                [former * cosine + latter * sine, latter * cosine - former * sine], axis=0
            ).astype(jnp.bfloat16)
            for head in range(GROUPS):
                dq_ref[group, head, :, tile * TILE : (tile + 1) * TILE] = turned[
                    :, head * TILE : (head + 1) * TILE
                ]
        return unused

    lax.fori_loop(0, KV_HEADS, one_group, 0)
    for place, (block, _) in enumerate(slots):
        out_ref = (keep_ref, send_ref)[place % 2]

        @pl.when(block <= own)
        def _():
            rows = block_rows(block)
            for group in range(KV_HEADS):
                low = HEAD_DIM * group
                out_ref[place // 2, low : low + HEAD_DIM, :] = dk_ref[group, rows, :].T.astype(
                    jnp.bfloat16
                )
                low = low + KV_WIDTH
                out_ref[place // 2, low : low + HEAD_DIM, :] = dv_ref[group, rows, :].T.astype(
                    jnp.bfloat16
                )

        @pl.when(block > own)
        def _():
            out_ref[place // 2] = jnp.zeros((2 * KV_WIDTH, TOK), jnp.bfloat16)


def vmem():
    return pl.BlockSpec(memory_space=pltpu.VMEM)


def smem():
    return pl.BlockSpec(memory_space=pltpu.SMEM)


def anywhere():
    return pl.BlockSpec(memory_space=pl.ANY)


kernel_params = pltpu.CompilerParams(vmem_limit_bytes=56 * 1024 * 1024)
heads_shape = (KV_HEADS, GROUPS, HEAD_DIM, TOK)


def attend_forward(micro, lengths, queries, keyvals, begins, tie):
    return pl.pallas_call(
        partial(forward_kernel, micro),
        out_shape=(
            jax.ShapeDtypeStruct(heads_shape, jnp.bfloat16),
            jax.ShapeDtypeStruct((KV_HEADS, GROUPS, 1, TOK), jnp.float32),
        ),
        in_specs=[smem()] + [vmem()] * 6 + [anywhere()],
        out_specs=(vmem(), vmem()),
        scratch_shapes=[
            pltpu.VMEM((KV_HEADS, 4 * TOK, HEAD_DIM), jnp.bfloat16),
            pltpu.VMEM((KV_HEADS, HEAD_DIM + 16, 4 * TOK), jnp.bfloat16),
        ],
        compiler_params=kernel_params,
        cost_estimate=pl.CostEstimate(
            flops=4 * 9 * 64 * TOK * 2048, bytes_accessed=4000000, transcendentals=9 * TOK * 2048
        ),
        name="attend_forward",
    )(lengths, queries, *keyvals, begins, tie)


def attend_back(
    micro, lengths, queries, keyvals, begins, mixed, log_total, grad_mixed, cosine, sine, tie
):
    half_shape = (2, 2 * KV_WIDTH, TOK)
    return pl.pallas_call(
        partial(backward_kernel, micro),
        out_shape=(
            jax.ShapeDtypeStruct(heads_shape, jnp.bfloat16),
            jax.ShapeDtypeStruct(half_shape, jnp.bfloat16),
            jax.ShapeDtypeStruct(half_shape, jnp.bfloat16),
        ),
        in_specs=[smem()] + [vmem()] * 11 + [anywhere()],
        out_specs=(vmem(),) * 3,
        scratch_shapes=[
            pltpu.VMEM((KV_HEADS, 4 * TOK, HEAD_DIM), jnp.bfloat16),
            pltpu.VMEM((KV_HEADS, 4 * TOK, HEAD_DIM), jnp.bfloat16),
            pltpu.VMEM((KV_HEADS, HEAD_DIM, 4 * TOK), jnp.bfloat16),
            pltpu.VMEM((KV_HEADS, 4 * TOK, HEAD_DIM), jnp.float32),
            pltpu.VMEM((KV_HEADS, 4 * TOK, HEAD_DIM), jnp.float32),
        ],
        compiler_params=kernel_params,
        cost_estimate=pl.CostEstimate(
            flops=10 * 9 * 64 * TOK * 2048, bytes_accessed=8000000, transcendentals=9 * TOK * 2048
        ),
        name="attend_back",
    )(lengths, queries, *keyvals, begins, mixed, log_total, grad_mixed, cosine, sine, tie)


def dot_with(left, right, left_side, right_side):
    return lax.dot_general(
        left, right, (((left_side,), (right_side,)), ((), ())), preferred_element_type=jnp.float32
    )


def norm_back(values, scaling, gain, upstream, axis):
    weighted = upstream * gain
    inner = jnp.mean(weighted * values, axis=axis, keepdims=True)
    gain_grad = jnp.sum(upstream * values * scaling, axis=1 - axis, keepdims=True)
    return (scaling * weighted - values * (scaling * scaling * scaling) * inner, gain_grad)


def norm_scaling(values, axis):
    return lax.rsqrt(jnp.mean(values * values, axis=axis, keepdims=True) + norm_epsilon)


def row_parts(held, spot, side):
    for turn in range(ROW_CUT):
        start = (turn ^ lax.div(spot, COL_CUT)) * CHUNK_ROWS
        part = held[pl.ds(pl.multiple_of(start, CHUNK_ROWS), CHUNK_ROWS), :]
        yield (turn * COL_CUT + side, part.astype(jnp.bfloat16))


def mlp_kernel(
    x_ref, x1_ref, c_ref, c1_ref, o0_ref, o1_ref, wo_ref, wg_ref, wu_ref, wd_ref, gain_ref,
    out_ref, out1_ref, dh_ref, do0_ref, do1_ref, keep_ref, send_ref, gwo_ref, gg_ref,
    hid, dgate, dup, n2_tall, dh_low, held,
):
    gain = gain_ref[...]
    gg_ref[...] = jnp.zeros((1, D), jnp.float32)
    block = 256
    spot = chunk_spot()
    for micro, (o_ref, do_ref) in enumerate(((o0_ref, do0_ref), (o1_ref, do1_ref))):
        rows = slice(micro * TOK, (micro + 1) * TOK)
        x_tall = x1_ref[...] if micro else x_ref[0]
        c_tall = c1_ref[...] if micro else c_ref[0]
        hidden_state = (x_tall.astype(jnp.float32) + dot_with(wo_ref[...], o_ref[...], 0, 0)).T
        scaling = norm_scaling(hidden_state, 1)
        normed = (hidden_state * scaling * gain).astype(jnp.bfloat16)
        n2_tall[:, rows] = normed.T
        back = c_tall.T
        for column in range(0, FF, block):
            columns = slice(column, column + block)
            gate = dot32(normed, wg_ref[:, columns])
            upward = dot32(normed, wu_ref[:, columns])
            grad_hidden = dot_with(back, wd_ref[columns, :], 1, 1)
            sigmoid_gate = jax.nn.sigmoid(gate)
            activated = gate * sigmoid_gate
            hid[rows, columns] = (activated * upward).astype(jnp.bfloat16)
            dgate[rows, columns] = (
                grad_hidden * upward * sigmoid_gate * (1.0 + gate * (1.0 - sigmoid_gate))
            ).astype(jnp.bfloat16)
            dup[rows, columns] = (grad_hidden * activated).astype(jnp.bfloat16)
        result = (hidden_state + dot32(hid[rows, :], wd_ref[...])).T
        if micro:
            out1_ref[...] = result.astype(jnp.bfloat16)
        else:
            out_ref[0] = result
        upstream = dot_with(dgate[rows, :], wg_ref[...], 1, 1) + dot_with(
            dup[rows, :], wu_ref[...], 1, 1
        )
        part, gain_grad = norm_back(hidden_state, scaling, gain, upstream, 1)
        gg_ref[...] += gain_grad
        grad_state = back.astype(jnp.float32) + part
        dh_low[rows, :] = grad_state.astype(jnp.bfloat16)
        grad_tall = grad_state.T
        dh_ref[micro] = grad_tall
        do_ref[...] = dot32(wo_ref[...], grad_tall.astype(jnp.bfloat16)).astype(jnp.bfloat16)
    c_parts = (c_ref.at[0], c1_ref)
    for place, right in enumerate((dgate, dup, hid)):
        for side in range(COL_CUT):
            start = (side ^ lax.rem(spot, COL_CUT)) * CHUNK_COLS
            for column in range(0, CHUNK_COLS, block):
                columns = pl.ds(pl.multiple_of(start + column, block), block)
                if place < 2:
                    held[...] = dot32(n2_tall[...], right[:, columns])
                else:
                    held[...] = dot32(c_parts[0][...], right[:TOK, columns]) + dot32(
                        c_parts[1][...], right[TOK:, columns]
                    )
                for index, part in row_parts(held, spot, side):
                    out = (keep_ref, send_ref)[index // 4]
                    out[index % 4, place, :, column : column + block] = part
    gwo_ref[...] = (
        dot32(o0_ref[...], dh_low[:TOK, :]) + dot32(o1_ref[...], dh_low[TOK:, :])
    ).astype(jnp.bfloat16)


def mlp(tokens, tokens_1, cotangent, cotangent_1, mixed, w_out, w_gate, w_up, w_down, gain):
    rows = 2 * TOK
    low = jnp.bfloat16
    chunk_shape = (CHUNKS // 2, 3, CHUNK_ROWS, CHUNK_COLS)
    return pl.pallas_call(
        mlp_kernel,
        out_shape=(
            jax.ShapeDtypeStruct((2, D, TOK), jnp.float32),
            jax.ShapeDtypeStruct((D, TOK), low),
            jax.ShapeDtypeStruct((2, D, TOK), jnp.float32),
            jax.ShapeDtypeStruct((D, TOK), low),
            jax.ShapeDtypeStruct((D, TOK), low),
            jax.ShapeDtypeStruct(chunk_shape, low),
            jax.ShapeDtypeStruct(chunk_shape, low),
            jax.ShapeDtypeStruct((D, D), low),
            jax.ShapeDtypeStruct((1, D), jnp.float32),
        ),
        in_specs=[vmem()] * 11,
        out_specs=(vmem(),) * 9,
        scratch_shapes=[
            pltpu.VMEM((rows, FF), low),
            pltpu.VMEM((rows, FF), low),
            pltpu.VMEM((rows, FF), low),
            pltpu.VMEM((D, rows), low),
            pltpu.VMEM((rows, D), low),
            pltpu.VMEM((D, 256), jnp.float32),
        ],
        compiler_params=kernel_params,
        cost_estimate=pl.CostEstimate(
            flops=6 * rows * 3 * D * FF, bytes_accessed=25000000, transcendentals=rows * FF
        ),
        name="mlp",
    )(tokens, tokens_1, cotangent, cotangent_1, *mixed, w_out, w_gate, w_up, w_down, gain)


def natural_tiles(flat, base, rows, width):
    pairs, step, whole = rows // 2, width * 2 // 128, width // 128
    parts = [flat[pl.ds(base + place, pairs, stride=step), :] for place in range(step)]
    even = parts[:whole] + [parts[whole][:, :HEAD_DIM]]
    odd = jnp.concatenate([parts[whole][:, HEAD_DIM:]] + parts[whole + 1 :], axis=1)
    return even, [odd[:, low : low + 128] for low in range(0, width, 128)]


def unflatten(flat, base, rows, width, tiles):
    even, odd = natural_tiles(flat, base, rows, width)
    for place, (first, second) in enumerate(zip(even, odd)):
        breadth = first.shape[1]
        if breadth < 128:
            blank = jnp.zeros((rows // 2, 128 - breadth), jnp.float32)
            first = jnp.concatenate([first, blank], axis=1)
            second = jnp.concatenate([second, blank], axis=1)
        tiles[place, pl.ds(0, rows // 2, stride=2), :] = first
        tiles[place, pl.ds(1, rows // 2, stride=2), :] = second


def tile_widths(width):
    return [(place, low, min(128, width - low)) for place, low in enumerate(range(0, width, 128))]


MIXED = ((0, 0, D), (2592, D, KV_WIDTH), (3456, D + KV_WIDTH, KV_WIDTH), (4320, FF - D, D))


def project_kernel(
    near_ref, next_ref, x_ref, x1_ref, gain_ref, cos0_ref, sin0_ref, cos1_ref, sin1_ref,
    q0_ref, q1_ref, kv_ref, w_ref, wo_ref, n_ref, flat, tiles,
):
    spot = chunk_spot()
    length = flat.shape[0] // CHUNKS
    for index in range(CHUNKS):
        chunk = spot ^ index
        core, half, chip = lax.div(chunk, 4), lax.rem(lax.div(chunk, 2), 2), lax.rem(chunk, 2)
        start = pl.multiple_of((half * 4 + chip * 2 + core) * length, 8)
        part = (near_ref, next_ref)[index // 4][index % 4]
        flat[pl.ds(start, length), :] = part.astype(jnp.float32)
    for base, start, width in MIXED:
        unflatten(flat, base, D, width, tiles)
        for place, low, breadth in tile_widths(width):
            part = tiles[place][:D, :breadth].astype(jnp.bfloat16)
            if start < FF - D:
                w_ref[:, start + low : start + low + breadth] = part
            else:
                wo_ref[:, low : low + breadth] = part
    tall = w_ref[...].T
    half_width = HEAD_DIM // 2
    tables = ((q0_ref, cos0_ref, sin0_ref), (q1_ref, cos1_ref, sin1_ref))
    for micro, (q_ref, cos_ref, sin_ref) in enumerate(tables):
        values = (x1_ref[...] if micro else x_ref[0]).astype(jnp.float32)
        normed = (values * norm_scaling(values, 0) * gain_ref[:, 0:1]).astype(jnp.bfloat16)
        n_ref[:, micro * TOK : (micro + 1) * TOK] = normed
        linear = dot32(tall, normed)
        cosine, sine = cos_ref[...], sin_ref[...]
        for head in range(HEADS + KV_HEADS):
            low = head * HEAD_DIM
            former = linear[low : low + half_width]
            latter = linear[low + half_width : low + HEAD_DIM]
            turned = jnp.concatenate(
                [former * cosine - latter * sine, latter * cosine + former * sine], axis=0
            ).astype(jnp.bfloat16)
            if head < HEADS:
                scaled = turned.astype(jnp.float32) * 0.125
                q_ref[head // GROUPS, head % GROUPS] = scaled.astype(jnp.bfloat16)
            else:
                low = low - D
                kv_ref[micro, low : low + HEAD_DIM, :] = turned
        kv_ref[micro, KV_WIDTH:, :] = linear[D + KV_WIDTH :].astype(jnp.bfloat16)


def project(near, following, tokens, tokens_1, gain_columns, tables):
    low = jnp.bfloat16
    return pl.pallas_call(
        project_kernel,
        out_shape=(
            jax.ShapeDtypeStruct(heads_shape, low),
            jax.ShapeDtypeStruct(heads_shape, low),
            jax.ShapeDtypeStruct((2, 2 * KV_WIDTH, TOK), low),
            jax.ShapeDtypeStruct((D, D + 2 * KV_WIDTH), low),
            jax.ShapeDtypeStruct((D, D), low),
            jax.ShapeDtypeStruct((D, 2 * TOK), low),
        ),
        in_specs=[vmem()] * 9,
        out_specs=(vmem(),) * 6,
        scratch_shapes=[
            pltpu.VMEM((D * FF // 128, 128), jnp.float32),
            pltpu.VMEM((5, D, 128), jnp.float32),
        ],
        compiler_params=kernel_params,
        cost_estimate=pl.CostEstimate(
            flops=4 * TOK * D * 960, bytes_accessed=8000000, transcendentals=0
        ),
        name="project",
    )(near, following, tokens, tokens_1, gain_columns, *tables[0], *tables[1])


def projection_kernel(
    n_ref, dq0_ref, dq1_ref, kept0_ref, kept1_ref, got_ref, far_ref,
    cos0_ref, sin0_ref, cos1_ref, sin1_ref, gwo_ref, tie_ref,
    keep_ref, send_ref, all_ref, held, cut,
):
    spot, chip = chunk_spot(), positions()[2]
    half_width = HEAD_DIM // 2
    parts = ((dq0_ref, kept0_ref, cos0_ref, sin0_ref), (dq1_ref, kept1_ref, cos1_ref, sin1_ref))
    for micro, (dq_ref, kept_ref, cos_ref, sin_ref) in enumerate(parts):
        columns = slice(micro * TOK, (micro + 1) * TOK)
        all_ref[:D, columns] = dq_ref[...]
        cosine, sine = cos_ref[...], sin_ref[...]
        summed = kept_ref[0].astype(jnp.float32) + got_ref[2 * micro].astype(jnp.float32)
        summed = summed + jnp.where(chip == micro, far_ref[...].astype(jnp.float32), 0.0)
        for head in range(KV_HEADS):
            low = head * HEAD_DIM
            former = summed[low : low + half_width, :]
            latter = summed[low + half_width : low + HEAD_DIM, :]
            all_ref[D + low : D + low + half_width, columns] = (
                former * cosine + latter * sine
            ).astype(jnp.bfloat16)
            all_ref[D + low + half_width : D + low + HEAD_DIM, columns] = (
                latter * cosine - former * sine
            ).astype(jnp.bfloat16)
        all_ref[D + KV_WIDTH :, columns] = summed[KV_WIDTH:, :].astype(jnp.bfloat16)
    held[:, : D + 2 * KV_WIDTH] = dot_with(n_ref[...], all_ref[...], 1, 1)
    held[:, D + 2 * KV_WIDTH :] = gwo_ref[...].astype(jnp.float32)
    for side in range(COL_CUT):
        start = (side ^ lax.rem(spot, COL_CUT)) * CHUNK_COLS
        cut[...] = held[:, pl.ds(pl.multiple_of(start, CHUNK_COLS), CHUNK_COLS)]
        for index, part in row_parts(cut, spot, side):
            (keep_ref, send_ref)[index // 4][index % 4] = part


def projection_grads(normed, dqs, kept, got, far, tables, gwo, tie):
    rows = normed.shape[1]
    chunk_shape = (CHUNKS // 2, CHUNK_ROWS, CHUNK_COLS)
    return pl.pallas_call(
        projection_kernel,
        out_shape=(
            jax.ShapeDtypeStruct(chunk_shape, jnp.bfloat16),
            jax.ShapeDtypeStruct(chunk_shape, jnp.bfloat16),
            jax.ShapeDtypeStruct((D + 2 * KV_WIDTH, rows), jnp.bfloat16),
        ),
        in_specs=[vmem()] * 12 + [anywhere()],
        out_specs=(vmem(),) * 3,
        scratch_shapes=[
            pltpu.VMEM((D, FF), jnp.float32),
            pltpu.VMEM((D, CHUNK_COLS), jnp.float32),
        ],
        compiler_params=kernel_params,
        cost_estimate=pl.CostEstimate(
            flops=2 * rows * D * 960, bytes_accessed=8000000, transcendentals=0
        ),
        name="projection_grads",
    )(normed, *dqs, *kept, got, far, *tables[0], *tables[1], gwo, tie)


def both(left_ref, right_ref, where=...):
    total = left_ref[where].astype(jnp.float32) + right_ref[where].astype(jnp.float32)
    return total.astype(jnp.bfloat16)


def plain_call(kernel, outs, operands, ties, name):
    outs = [jax.ShapeDtypeStruct(shape, jnp.bfloat16) for shape in outs]
    ties = ties if isinstance(ties, tuple) else (ties,)
    count = len(operands)

    def run(*refs):
        kernel(*refs[: count + 1], *refs[count + len(ties) :])

    return pl.pallas_call(
        run,
        out_shape=outs,
        in_specs=[vmem()] * count + [anywhere()] * len(ties),
        out_specs=[vmem()] * len(outs),
        compiler_params=kernel_params,
        name=name,
    )(*operands, *ties)


def early_first_kernel(keep_ref, got_ref, tie_ref, side_keep, side_send, chip_keep, chip_send):
    middle = CHUNK_COLS // 2
    for index in range(4):
        total = both(keep_ref, got_ref, index)
        (side_keep, side_send)[index // 2][index % 2] = total[:, :, :middle]
        (chip_keep, chip_send)[index % 2][index // 2] = total[:, :, middle:]


def early_first(keep, got, tie):
    shape = (2, 3, CHUNK_ROWS, CHUNK_COLS // 2)
    return plain_call(early_first_kernel, [shape] * 4, (keep, got), tie, "early_first")


def early_second_kernel(keep0, got0, keep1, got1, tie_ref, kept0, sent0, kept1, sent1):
    for keep, got, kept, sent in ((keep0, got0, kept0, sent0), (keep1, got1, kept1, sent1)):
        kept[...] = both(keep, got, 0)
        sent[...] = both(keep, got, 1)


def early_second(operands, tie):
    shape = (3, CHUNK_ROWS, CHUNK_COLS // 2)
    return plain_call(early_second_kernel, [shape] * 4, operands, tie, "early_second")


def early_third_kernel(keep0, got0, keep1, got1, tie_ref, *outs):
    quarter = positions()[0]
    middle = CHUNK_COLS // 2
    for shift, out in enumerate(outs):
        place = jnp.maximum(lax.rem(quarter + shift, 4) - 1, 0)
        out[:, :middle] = both(keep0, got0, place)
        out[:, middle:] = both(keep1, got1, place)


def early_third(operands, tie):
    shape = (CHUNK_ROWS, CHUNK_COLS)
    return plain_call(early_third_kernel, [shape] * 4, operands, tie, "early_third")


def sum_kernel(*refs):
    total = refs[0][...].astype(jnp.float32)
    for ref in refs[1:-2]:
        total = total + ref[...].astype(jnp.float32)
    refs[-1][...] = total.astype(jnp.bfloat16)


def tied_sum(operands, tie):
    return plain_call(sum_kernel, [operands[0].shape], operands, tie, "tied_sum")[0]


def late_kernel(keep_ref, got_ref, tie_ref, keep_out, send_out):
    size = keep_out.shape[0]
    keep_out[...] = both(keep_ref, got_ref, slice(0, size))
    send_out[...] = both(keep_ref, got_ref, slice(size, 2 * size))


def late_halves(keep, got, tie):
    shape = (keep.shape[0] // 2, *keep.shape[1:])
    return plain_call(late_kernel, [shape] * 2, (keep, got), tie, "late_halves")


def pair_kernel(first_ref, second_ref, tie_ref, out_ref):
    out_ref[:2] = first_ref[...]
    out_ref[2:] = second_ref[...]


def tied_pair(first, second, tie):
    shape = (4, *first.shape[1:])
    return plain_call(pair_kernel, [shape], (first, second), tie, "tied_pair")[0]


def pick_kernel(own_ref, got1_ref, got2_ref, got3_ref, tie_ref, *outs):
    quarter = positions()[0]
    for place, out in enumerate(outs):
        for shift, ref in enumerate((own_ref, got1_ref, got2_ref, got3_ref)):

            @pl.when(lax.rem(quarter - place + 4, 4) == shift)
            def _():
                out[...] = ref[...]


def pick(pieces, tie):
    return plain_call(pick_kernel, [pieces[0].shape] * 4, pieces, tie, "pick")


def cast_kernel(value_ref, tie_ref, out_ref):
    out_ref[...] = value_ref[...].astype(out_ref.dtype)


def tied_cast(value, tie):
    return pl.pallas_call(
        cast_kernel,
        out_shape=jax.ShapeDtypeStruct(value.shape, jnp.bfloat16),
        in_specs=[vmem(), anywhere()],
        out_specs=vmem(),
        compiler_params=kernel_params,
        name="tied_cast",
    )(value, tie)


def inputs_kernel(all_ref, w_ref, x_ref, x1_ref, dh_ref, gain_ref, out_ref, out1_ref, gg_ref):
    gain = gain_ref[:, 0:1]
    total = jnp.zeros((D, 1), jnp.float32)
    for micro in range(2):
        columns = slice(micro * TOK, (micro + 1) * TOK)
        upstream = dot32(w_ref[...], all_ref[:, columns])
        values = (x1_ref[...] if micro else x_ref[0]).astype(jnp.float32)
        part, gain_grad = norm_back(values, norm_scaling(values, 0), gain, upstream, 0)
        total = total + gain_grad
        grad = dh_ref[micro] + part
        if micro:
            out1_ref[...] = grad.astype(out1_ref.dtype)
        else:
            out_ref[0] = grad
    gg_ref[...] = jnp.broadcast_to(total, gg_ref.shape)


def input_grads(grad_qkv, w_qkv, tokens, tokens_1, grad_state, gain_columns):
    return pl.pallas_call(
        inputs_kernel,
        out_shape=(
            jax.ShapeDtypeStruct((2, D, TOK), jnp.float32),
            jax.ShapeDtypeStruct((D, TOK), jnp.bfloat16),
            jax.ShapeDtypeStruct((D, 128), jnp.float32),
        ),
        in_specs=[vmem()] * 6,
        out_specs=(vmem(),) * 3,
        compiler_params=kernel_params,
        cost_estimate=pl.CostEstimate(
            flops=4 * TOK * D * 960, bytes_accessed=8000000, transcendentals=0
        ),
        name="input_grads",
    )(grad_qkv, w_qkv, tokens, tokens_1, grad_state, gain_columns)


def newton_loop(matrix, scale):
    current = matrix / (jnp.sqrt(jnp.sum(matrix * matrix)) + frobenius_epsilon)

    def iterate(unused, held):
        low = held.astype(jnp.bfloat16)
        square = dot_with(low, low, 1, 1)
        square_low = square.astype(jnp.bfloat16)
        mixer = newton_second * square + newton_third * dot32(square_low, square_low)
        return newton_first * held + dot32(mixer.astype(jnp.bfloat16), low)

    return lax.fori_loop(0, NS_STEPS, iterate, current) * (0.2 * math.sqrt(scale))


def flatten_rows(tiles, start, rows, width, out):
    pairs, step, whole = rows // 2, width * 2 // 128, width // 128
    spans = range(whole + 1)
    even = [tiles[place, pl.ds(start, pairs, stride=2), :] for place in spans]
    odd = [tiles[place, pl.ds(start + 1, pairs, stride=2), :] for place in spans]
    for place in range(whole):
        out[pl.ds(place, pairs, stride=step), :] = even[place]
    rest = width - whole * 128
    joined = jnp.concatenate([even[whole][:, :rest]] + odd[:whole] + [odd[whole][:, :rest]], axis=1)
    for place in range(whole, step):
        low = (place - whole) * 128
        out[pl.ds(place, pairs, stride=step), :] = joined[:, low : low + 128]


def shard_rows(kind, kinds, start, matrix, tiles, out):
    length = out.shape[0] * 128

    if 0 in kinds:

        @pl.when(kind == 0)
        def _():
            rows = length // FF
            for place in range(FF // 128):
                out[pl.ds(place, rows, stride=FF // 128), :] = matrix[
                    pl.ds(pl.multiple_of(start, 8), rows), place * 128 : (place + 1) * 128
                ]

        @pl.when(kind == 5)
        def _():
            for place, low, breadth in tile_widths(D):
                tiles[place, :, :breadth] = matrix[low : low + breadth, :].T
            flatten_rows(tiles, start, length // D, D, out)

    for place, (base, low, width) in zip((1, 3, 4, 2), MIXED):
        if place not in kinds:
            continue

        @pl.when(kind == place)
        def _():
            for tile, column, breadth in tile_widths(width):
                tiles[tile, :D, :breadth] = matrix[:, low + column : low + column + breadth]
            flatten_rows(tiles, start, length // width, width, out)


def own_kind(length):
    square, narrow = D * D, D * KV_WIDTH
    quarter = lax.axis_index("quarter")
    index = lax.axis_index("rep") * 2 + lax.axis_index("half")
    within = (index * lax.axis_size("ctx") + lax.axis_index("ctx")) * length
    kind = jnp.where(quarter == 3, 5, 0)
    start = jnp.where(quarter == 3, lax.div(within, D), lax.div(within, FF))
    edges = ((0, 1, D), (square, 3, KV_WIDTH), (square + narrow, 4, KV_WIDTH))
    for edge, place, width in (*edges, (square + 2 * narrow, 2, D)):
        inside = (quarter == 0) & (within >= edge)
        kind = jnp.where(inside, place, kind)
        start = jnp.where(inside, lax.div(within - edge, width), start)
    return (kind, start)


def load_matrix(kind, kinds, old_ref, flat, grad, total, tiles):
    flat[...] = old_ref[...].astype(jnp.float32) * momentum_decay
    if 0 in kinds:

        @pl.when(kind == 0)
        def _():
            for place in range(FF // 128):
                columns = slice(place * 128, (place + 1) * 128)
                total[:, columns] = flat[pl.ds(place, D, stride=FF // 128), :] + grad[:, columns]

        @pl.when(kind == 5)
        def _():
            unflatten(flat, 0, FF, D, tiles)
            for place, low, breadth in tile_widths(D):
                rows = slice(low, low + breadth)
                total[rows, :] = tiles[place].T[:breadth] + grad[rows, :]

    for place, (base, low, width) in zip((1, 3, 4, 2), MIXED):
        if place not in kinds:
            continue

        @pl.when(kind == place)
        def _():
            unflatten(flat, base, D, width, tiles)
            part = jnp.concatenate(
                [tiles[tile][:D, :breadth] for tile, _, breadth in tile_widths(width)], axis=1
            )
            columns = slice(low, low + width)
            total[:, columns] = part + grad[:, columns]


def update_matrix(kind, kinds, total):
    if 0 in kinds:

        @pl.when((kind == 0) | (kind == 5))
        def _():
            total[...] = newton_loop(total[...], FF)

    for place, (base, low, width) in zip((1, 3, 4, 2), MIXED):
        if place not in kinds:
            continue

        @pl.when(kind == place)
        def _():
            columns = slice(low, low + width)
            if width == D:
                total[:, columns] = newton_loop(total[:, columns], D)
            else:
                total[:, columns] = newton_loop(total[:, columns].T, D).T


def newton_kernel(early, local, length, *refs):
    count = 3 if local else 2
    grad, total, tiles = refs[-3:]
    outs = refs[-3 - count : -3]
    pieces, (old_ref, *rest) = (refs[:1], refs[1:-3]) if early else (refs[:2], refs[2:-3])
    kind, start = own_kind(length)
    mine = (lax.axis_index("quarter") != 0) == early
    spot = chunk_spot()

    @pl.when(mine)
    def _():
        for index in range(CHUNKS):
            if early:
                half, chip, core = index // 4, index // 2 % 2, index % 2
                chunk = core * 4 + half * 2 + chip
                row, column = chunk // COL_CUT * CHUNK_ROWS, chunk % COL_CUT * CHUNK_COLS
                rows, columns = slice(row, row + CHUNK_ROWS), slice(column, column + CHUNK_COLS)
                part = pieces[0][index]
            else:
                chunk = spot ^ index
                row = pl.multiple_of(lax.div(chunk, COL_CUT) * CHUNK_ROWS, CHUNK_ROWS)
                column = pl.multiple_of(lax.rem(chunk, COL_CUT) * CHUNK_COLS, CHUNK_COLS)
                rows, columns = pl.ds(row, CHUNK_ROWS), pl.ds(column, CHUNK_COLS)
                part = pieces[index // 4][index % 4]
            grad[rows, columns] = part.astype(jnp.float32)
        kinds = (0, 5) if early else (1, 2, 3, 4)
        pl.run_scoped(
            lambda flat: load_matrix(kind, kinds, old_ref, flat, grad, total, tiles),
            pltpu.VMEM((D * FF // 128, 128), jnp.float32),
        )
        update_matrix(kind, kinds, total)
        if local:
            weights_ref, momentum_ref = rest[:2]
            grad_ref, new_momentum_ref, new_weights_ref = outs
            shard_rows(kind, kinds, start, grad, tiles, grad_ref)
            shard_rows(kind, kinds, start, total, tiles, new_weights_ref)
            new_momentum_ref[...] = momentum_decay * momentum_ref[...] + grad_ref[...]
            new_weights_ref[...] = (
                weights_ref[...] * (1.0 - matrix_rate * weight_decay)
                - matrix_rate * new_weights_ref[...]
            )
        else:
            outs[0][...] = grad[...]
            outs[1][...] = total[...]

    if not early:

        @pl.when(jnp.logical_not(mine))
        def _():
            for out, before in zip(outs, rest[2:] if local else rest):
                out[...] = before[...]


def newton(early, length, pieces, old, shards, before, tie):
    local = len(shards) > 0
    if local:
        outs = (jax.ShapeDtypeStruct(shards[0].shape, jnp.float32),) * 3
    else:
        outs = (jax.ShapeDtypeStruct((D, FF), jnp.float32),) * 2
    operands = (*pieces, old, *shards, *before)

    def kernel(*refs):
        newton_kernel(early, local, length, *refs[: len(operands)], *refs[len(operands) + 1 :])

    return pl.pallas_call(
        kernel,
        out_shape=outs,
        in_specs=[vmem()] * len(operands) + [anywhere()],
        out_specs=(vmem(),) * len(outs),
        scratch_shapes=[
            pltpu.VMEM((D, FF), jnp.float32),
            pltpu.VMEM((D, FF), jnp.float32),
            pltpu.VMEM((5, FF, 128), jnp.float32),
        ],
        compiler_params=kernel_params,
        cost_estimate=pl.CostEstimate(
            flops=12000000000, bytes_accessed=9000000, transcendentals=0
        ),
        name="newton_early" if early else "newton_late",
    )(*operands, tie)


def own_rows(kind, row, shard_length, gradient, update):
    def block_case(low, width):
        def run(gradient, update):
            start = (row, low)
            size = (shard_length // width, width)
            return tuple(
                lax.dynamic_slice(whole, start, size).reshape(-1) for whole in (gradient, update)
            )

        return run

    def tall_case(gradient, update):
        start = (0, row)
        size = (D, shard_length // D)
        return tuple(
            lax.dynamic_slice(whole, start, size).T.reshape(-1) for whole in (gradient, update)
        )

    cases = [
        block_case(0, FF),
        block_case(0, D),
        block_case(FF - D, D),
        block_case(D, KV_WIDTH),
        block_case(D + KV_WIDTH, KV_WIDTH),
        tall_case,
    ]
    return lax.switch(kind, cases, gradient, update)


CORE_SWAP = [(0, 1), (1, 0), (2, 3), (3, 2)]
CHIP_SWAP = [(0, 2), (2, 0), (1, 3), (3, 1)]
SIDE_SWAP = [(0, 1), (1, 0)]
END_SWAP = [(0, 3), (3, 0), (1, 2), (2, 1)]


def plane_pairs(bit):
    return [(place, place ^ (2, 4, 1)[bit]) for place in range(8)]


def plane_swap(value, bit):
    axis, swap = (("ctx", CHIP_SWAP), ("half", SIDE_SWAP), ("ctx", CORE_SWAP))[bit]
    return lax.ppermute(value, axis, swap)


def first_plane_swap(value, bit):
    return lax.ppermute(value, ("quarter", "half", "ctx"), plane_pairs(bit))


def plane_gather(piece, swap):
    pieces = piece[None]
    for bit in range(2):
        pieces = jnp.concatenate([pieces, swap(pieces, bit)], axis=0)
    return (pieces, swap(pieces, 2))


def depth_shift(value, shift, targets):
    pairs = [(place, (place + shift) % 4) for place in range(4)]
    return lax.ppermute(value, "quarter", [pair for pair in pairs if pair[1] in targets])


def sum_everywhere(value):
    parts = [
        lax.ppermute(value, ("half", "ctx"), [(place, place ^ turn) for place in range(8)])
        for turn in range(1, 8)
    ]
    value = value + sum(parts)
    parts = [depth_shift(value, shift, range(4)) for shift in range(1, 4)]
    return value + sum(parts)


def gather_weights(low, tie):
    if lax.axis_size("rep") > 1:
        full = lax.all_gather(low, EVERY, axis=0, tiled=True).reshape(4, D * FF)
        ctx = lax.axis_index("ctx")
        spot = lax.rem(ctx, 2) * 4 + lax.axis_index("half") * 2 + ctx // 2
        chunk = jnp.arange(CHUNKS, dtype=jnp.int32) ^ spot
        order = 4 * (chunk // 2 % 2) + 2 * (chunk % 2) + chunk // 4
        mixed = full[0].reshape(CHUNKS, -1, 128)[order]
        return (mixed[:4], mixed[4:]), [
            full[1].reshape(D, FF),
            full[2].reshape(D, FF),
            full[3].reshape(FF, D),
        ]
    pieces = [low] + [depth_shift(low, shift, range(4)) for shift in range(1, 4)]
    mixed, *depth = pick(pieces, tie)
    shapes = ((D // CHUNKS, FF), (D // CHUNKS, FF), (FF // CHUNKS, D))
    rest = [
        lax.all_gather(piece.reshape(shape), PLANE, axis=0, tiled=True)
        for piece, shape in zip(depth, shapes)
    ]
    return plane_gather(mixed, plane_swap), rest


def per_device(tokens, lengths, weights, momentum, norm_gains, gain_first, gain_second, cotangent):
    ctx = lax.axis_index("ctx")
    chip = ctx // 2
    reps = lax.axis_size("rep")
    shard_length = weights.shape[0]
    flat_shape = (shard_length // 128, 128)
    lengths = lengths[:, 0]
    tokens = jnp.swapaxes(tokens, 1, 2)
    cotangent = jnp.swapaxes(cotangent, 1, 2)
    gain_columns = norm_gains.T

    tokens_1 = lax.ppermute(tokens[1], "ctx", END_SWAP)
    mixed_weights, (w_gate, w_up, w_down) = gather_weights(
        weights.reshape(flat_shape).astype(jnp.bfloat16), tokens_1
    )
    begin_rows, tables = [], []
    for micro in range(2):
        block = ctx if micro == 0 else 3 - ctx
        own_places = block * TOK + jnp.arange(TOK, dtype=jnp.int32)
        offsets, begins = layout(lengths[micro], own_places)
        begin_rows.append(begins.reshape(1, TOK))
        tables.append(rope_tables(offsets))

    q0, q1, keyvals, w_qkv, w_out, normed = project(
        *mixed_weights, tokens, tokens_1, gain_columns, tables
    )
    queries = (q0, q1)
    far = lax.ppermute(
        lax.dynamic_index_in_dim(keyvals, chip, 0, keepdims=False), "ctx", CHIP_SWAP
    )
    keyvals = (
        keyvals,
        lax.ppermute(keyvals, "ctx", CORE_SWAP),
        far,
        lax.ppermute(far, "ctx", CORE_SWAP),
    )
    mixed, log_totals = [], []
    for micro in range(2):
        mixed_one, log_total = attend_forward(
            micro, lengths, queries[micro], keyvals, begin_rows[micro], norm_gains
        )
        mixed.append(mixed_one)
        log_totals.append(log_total)
    cotangent_1 = lax.ppermute(cotangent[1], "ctx", END_SWAP)
    old = lax.all_gather(
        tied_cast(momentum.reshape(flat_shape), mixed[0]),
        ("rep", "half", "ctx"),
        axis=0,
        tiled=True,
    )
    outs = mlp(
        tokens,
        tokens_1,
        cotangent,
        cotangent_1,
        [part.reshape(D, TOK) for part in mixed],
        w_out,
        w_gate,
        w_up,
        w_down,
        norm_gains[1:2],
    )
    result, result_1, grad_state, grad_mixed_0, grad_mixed_1 = outs[:5]
    keep, send, grad_w_out, gain_two_grad = outs[5:]
    returned = lax.ppermute(result_1, "ctx", END_SWAP)

    def back_pass(micro, grad_mixed, tie):
        return attend_back(
            micro,
            lengths,
            queries[micro],
            keyvals,
            begin_rows[micro],
            mixed[micro],
            log_totals[micro],
            grad_mixed.reshape(heads_shape),
            *tables[micro],
            tie,
        )

    got = plane_swap(send, 2)
    dq0, kept0, sent0 = back_pass(0, grad_mixed_0, old)
    side_keep, side_send, chip_keep, chip_send = early_first(keep, got, (dq0, returned))
    side_got, chip_got = plane_swap(side_send, 1), plane_swap(chip_send, 0)
    dq1, kept1, sent1 = back_pass(1, grad_mixed_1, side_keep)
    kept_a, sent_a, kept_b, sent_b = early_second((side_keep, side_got, chip_keep, chip_got), dq1)
    got_a, got_b = plane_swap(sent_a, 0), plane_swap(sent_b, 1)
    traded = lax.ppermute(tied_pair(sent0, sent1, kept_a), "ctx", CORE_SWAP)
    heavy = chip == 0
    crossing = jnp.where(heavy, kept1[1], kept0[1]).astype(jnp.float32) + jnp.where(
        heavy, traded[3], traded[1]
    ).astype(jnp.float32)
    crossed = lax.ppermute(crossing.astype(jnp.bfloat16), "ctx", CHIP_SWAP)
    early, *turns = early_third((kept_a, got_a, kept_b, got_b), traded)
    early_parts = [
        depth_shift(turn, shift, range(1, 4)) for shift, turn in enumerate(turns, start=1)
    ]
    late_keep, late_send, grad_qkv = projection_grads(
        normed,
        (dq0.reshape(D, TOK), dq1.reshape(D, TOK)),
        (kept0, kept1),
        traded,
        crossed,
        tables,
        grad_w_out,
        early,
    )
    late_got = plane_swap(late_send, 2)
    early = tied_sum((early, *early_parts), late_keep)
    if reps > 1:
        early = lax.psum(early, "rep")
    early_pieces = lax.all_gather(early, PLANE, axis=0, tiled=False)
    late_keep, late_send = late_halves(late_keep, late_got, early)
    late_got = plane_swap(late_send, 1)
    grad_inputs, grad_inputs_1, gain_one_grad = input_grads(
        grad_qkv, w_qkv, tokens, tokens_1, grad_state, gain_columns
    )
    late_keep, late_send = late_halves(late_keep, late_got, gain_one_grad)
    late = tied_sum((late_keep[0], plane_swap(late_send, 0)[0]), gain_one_grad)
    gain_grad = sum_everywhere(
        jnp.concatenate([gain_one_grad[:, 0].reshape(1, D), gain_two_grad], axis=0)
    )
    late_parts = [depth_shift(late, shift, (0,)) for shift in range(1, 4)]

    shards, before = (), ()
    if flat_shape[0] % 8 == 0:
        shards = (weights.reshape(flat_shape), momentum.reshape(flat_shape))
    before = newton(True, shard_length, (early_pieces,), old, shards, (), late)
    late = tied_sum((late, *late_parts), before[0])
    if reps > 1:
        late = lax.psum(late, "rep")
        gain_grad = lax.psum(gain_grad, "rep")
    late_pieces = plane_gather(late, first_plane_swap)
    outs = newton(False, shard_length, late_pieces, old, shards, before, gain_columns)
    if len(shards) > 0:
        grad_shard, new_momentum, new_weights = [out.reshape(weights.shape) for out in outs]
    else:
        kind, start = own_kind(shard_length)
        grad_shard, update_shard = own_rows(kind, start, shard_length, *outs)
        new_momentum = momentum_decay * momentum + grad_shard
        new_weights = weights * (1.0 - matrix_rate * weight_decay) - matrix_rate * update_shard

    def placed(whole, part):
        whole = lax.dynamic_update_index_in_dim(whole, part.astype(jnp.float32), 1, 0)
        return jnp.swapaxes(whole, 1, 2)

    grad_inputs_1 = lax.ppermute(tied_cast(grad_inputs_1, late_pieces[1]), "ctx", END_SWAP)
    first_new = first_decay * gain_first + (1.0 - first_decay) * gain_grad
    second_new = second_decay * gain_second + (1.0 - second_decay) * gain_grad * gain_grad
    debiased_first_moment = first_new / (1.0 - first_decay**ADAM_STEP)
    corrected_second = second_new / (1.0 - second_decay**ADAM_STEP)
    new_gains = norm_gains * (
        1.0 - gain_rate * weight_decay
    ) - gain_rate * debiased_first_moment / (jnp.sqrt(corrected_second) + adam_epsilon)
    return (
        placed(result, returned),
        placed(grad_inputs, grad_inputs_1),
        grad_shard,
        new_momentum,
        new_weights,
        first_new,
        second_new,
        new_gains,
    )


def solution(mesh):
    devices = mesh.devices
    count = devices.size
    context = mesh.shape["ctx"]
    split = Mesh(
        devices.reshape(4, count // (8 * context), 2, context), ("quarter", "rep", "half", "ctx")
    )
    rows = P(None, EVERY, None)
    flat = P(EVERY)
    placed = (rows, P(None, ("quarter", "rep", "half"), None), flat, flat, P(), P(), P(), rows)
    return jax.shard_map(
        per_device,
        mesh=split,
        in_specs=placed,
        out_specs=(rows, rows, flat, flat, flat, P(), P(), P()),
        check_vma=False,
    )
```

```python
from functools import partial
import math

import jax
import jax.numpy as jnp
from jax import lax
from jax.experimental import pallas as pl
from jax.experimental.pallas import tpu as pltpu
from jax.sharding import Mesh, PartitionSpec as P

HEADS = 9
KV_HEADS = 3
HEAD_DIM = 64
FF = 1536
NS_STEPS = 5
ADAM_STEP = 10
D = 576
KV_WIDTH = 192
GROUPS = HEADS // KV_HEADS
TOK = 512
TILE = 256
COLS = GROUPS * TILE
ROW_CUT = 4
COL_CUT = 2
CHUNKS = ROW_CUT * COL_CUT
CHUNK_ROWS = D // ROW_CUT
CHUNK_COLS = FF // COL_CUT
PLANE = ("half", "ctx")
EVERY = ("quarter", "rep", "half", "ctx")


norm_epsilon = 1e-05
rope_base = 100000.0
masked_score = -1e30
newton_first = 3.4445
newton_second = -4.775
newton_third = 2.0315
momentum_decay = 0.95
matrix_rate = 0.2
weight_decay = 0.1
gain_rate = 0.2
first_decay = 0.9
second_decay = 0.95
adam_epsilon = 1e-08
frobenius_epsilon = 1e-07


def layout(lengths_row, places):
    finish = jnp.cumsum(lengths_row)
    firsts = finish - lengths_row
    begins = jnp.max(jnp.where(places[:, None] >= firsts[None, :], firsts[None, :], 0), axis=1)
    return (places - begins, begins)


def rope_tables(offsets):
    half_width = HEAD_DIM // 2
    inverse = jnp.exp(
        jnp.arange(half_width, dtype=jnp.float32) * (-2.0 * math.log(rope_base) / HEAD_DIM)
    )
    angles = inverse[:, None] * offsets.astype(jnp.float32)[None, :]
    return (jnp.cos(angles), jnp.sin(angles))


def dot32(left, right):
    return jnp.dot(left, right, preferred_element_type=jnp.float32)


def masked(scores, key_block, begins, places):
    keys = key_block * TILE + lax.broadcasted_iota(jnp.int32, scores.shape, 0)
    return jnp.where((keys >= begins) & (keys <= places), scores, masked_score)


def tile_row(row, tile):
    part = row[:, tile * TILE : (tile + 1) * TILE]
    return jnp.concatenate([part] * GROUPS, axis=1)


def tile_heads(ref, group, tile):
    return jnp.concatenate(
        [ref[group, head, :, tile * TILE : (tile + 1) * TILE] for head in range(GROUPS)], axis=1
    )


def positions():
    ctx = lax.axis_index("ctx")
    return (lax.axis_index("quarter"), lax.axis_index("half"), lax.div(ctx, 2), lax.rem(ctx, 2))


def chunk_spot():
    _, half, chip, core = positions()
    return core * 4 + half * 2 + chip


def first_key(lengths_ref, micro, row):
    begin = jnp.int32(0)
    first = jnp.int32(0)
    for place in range(3):
        first = first + lengths_ref[micro, place]
        begin = jnp.where(row >= first, first, begin)
    return begin


def key_loop(lengths_ref, micro, own, tile, step, carry):
    last = own * (TOK // TILE) + tile
    first = lax.div(first_key(lengths_ref, micro, last * TILE), TILE)
    full = lax.div(first_key(lengths_ref, micro, last * TILE + TILE - 1) + TILE - 1, TILE)
    full = jnp.minimum(full, last)
    pairs = lax.div(last - full, 2)
    carry = lax.fori_loop(first, full, partial(step, True, 1), carry)
    carry = lax.fori_loop(
        0, pairs, lambda pair, held: step(False, 2, full + 2 * pair, held), carry
    )
    carry = lax.fori_loop(full + 2 * pairs, last, partial(step, False, 1), carry)
    return step(True, 1, last, carry)


def own_block(micro):
    ctx = lax.axis_index("ctx")
    return ctx if micro == 0 else 3 - ctx


def key_slots(own, micro, kv_ref, other_ref, far_ref, far_other_ref):
    refs = (kv_ref.at[micro], other_ref.at[micro], far_ref, far_other_ref)
    return [(own ^ place, ref) for place, ref in enumerate(refs)]


def block_rows(block):
    return pl.ds(pl.multiple_of(block * TOK, TOK), TOK)


def forward_kernel(
    micro, lengths_ref, q_ref, kv_ref, other_ref, far_ref, far_other_ref, begin_ref, tie_ref,
    o_ref, lse_ref, k_nat, v_ext, s_ref, p_ref,
):
    own = own_block(micro)
    for block, source in key_slots(own, micro, kv_ref, other_ref, far_ref, far_other_ref):

        @pl.when(block <= own)
        def _():
            rows = block_rows(block)
            for group in range(KV_HEADS):
                low = HEAD_DIM * group
                k_nat[group, rows, :] = source[low : low + HEAD_DIM, :].T
                low = low + KV_WIDTH
                v_ext[group, :HEAD_DIM, rows] = source[low : low + HEAD_DIM, :]
                v_ext[group, HEAD_DIM:, rows] = jnp.ones((16, TOK), jnp.bfloat16)

    def one_group(group, unused):
        for tile in range(TOK // TILE):
            queries = tile_heads(q_ref, group, tile)
            begins = tile_row(begin_ref[...], tile)
            column = lax.broadcasted_iota(jnp.int32, (1, COLS), 1)
            places = own * TOK + tile * TILE + lax.rem(column, TILE)

            def step(is_masked, width, key_block, carry):
                top, total = carry
                keys = pl.ds(pl.multiple_of(key_block * TILE, TILE), width * TILE)
                count = width * TILE
                scores = dot32(k_nat[group, keys, :], queries)
                s_ref[:count] = masked(scores, key_block, begins, places) if is_masked else scores
                highest = s_ref[:16]
                for low in range(16, count, 16):
                    highest = jnp.maximum(highest, s_ref[low : low + 16])
                new_top = jnp.maximum(top, jnp.max(highest, axis=0, keepdims=True))
                for low in range(0, count, 16):
                    rows = slice(low, low + 16)
                    p_ref[rows] = jnp.exp(s_ref[rows] - new_top).astype(jnp.bfloat16)
                total = total * jnp.exp(top - new_top) + dot32(
                    v_ext[group, :, keys], p_ref[:count]
                )
                return (new_top, total)

            carry = (
                jnp.full((1, COLS), masked_score, jnp.float32),
                jnp.zeros((HEAD_DIM + 16, COLS), jnp.float32),
            )
            top, total = key_loop(lengths_ref, micro, own, tile, step, carry)
            weight = total[HEAD_DIM : HEAD_DIM + 1, :]
            mixed = (total[:HEAD_DIM, :] / weight).astype(jnp.bfloat16)
            log_total = top + jnp.log(weight)
            for head in range(GROUPS):
                o_ref[group, head, :, tile * TILE : (tile + 1) * TILE] = mixed[
                    :, head * TILE : (head + 1) * TILE
                ]
                lse_ref[group, head, :, tile * TILE : (tile + 1) * TILE] = log_total[
                    :, head * TILE : (head + 1) * TILE
                ]
        return unused

    lax.fori_loop(0, KV_HEADS, one_group, 0)


def backward_kernel(
    micro, lengths_ref, q_ref, kv_ref, other_ref, far_ref, far_other_ref, begin_ref, o_ref, lse_ref,
    do_ref, cos_ref, sin_ref, tie_ref,
    dq_ref, keep_ref, send_ref, k_nat, v_nat, k_tall, dk_ref, dv_ref, s_ref, g_ref, p_ref, ds_ref,
):
    own = own_block(micro)
    slots = key_slots(own, micro, kv_ref, other_ref, far_ref, far_other_ref)
    for block, source in slots:

        @pl.when(block <= own)
        def _():
            rows = block_rows(block)
            for group in range(KV_HEADS):
                low = HEAD_DIM * group
                k_nat[group, rows, :] = source[low : low + HEAD_DIM, :].T
                k_tall[group, :, rows] = source[low : low + HEAD_DIM, :]
                low = low + KV_WIDTH
                v_nat[group, rows, :] = source[low : low + HEAD_DIM, :].T
                dk_ref[group, rows, :] = jnp.zeros((TOK, HEAD_DIM), jnp.float32)
                dv_ref[group, rows, :] = jnp.zeros((TOK, HEAD_DIM), jnp.float32)

    def one_group(group, unused):
        for tile in range(TOK // TILE):
            queries = tile_heads(q_ref, group, tile)
            upstream = tile_heads(do_ref, group, tile)
            mixed = tile_heads(o_ref, group, tile)
            log_total = tile_heads(lse_ref, group, tile)
            delta = jnp.sum(
                upstream.astype(jnp.float32) * mixed.astype(jnp.float32), axis=0, keepdims=True
            )
            queries_nat = queries.T
            upstream_nat = upstream.T
            begins = tile_row(begin_ref[...], tile)
            column = lax.broadcasted_iota(jnp.int32, (1, COLS), 1)
            places = own * TOK + tile * TILE + lax.rem(column, TILE)

            def step(is_masked, width, key_block, dq):
                rows = pl.ds(pl.multiple_of(key_block * TILE, TILE), width * TILE)
                count = width * TILE
                scores = dot32(k_nat[group, rows, :], queries)
                s_ref[:count] = masked(scores, key_block, begins, places) if is_masked else scores
                g_ref[:count] = dot32(v_nat[group, rows, :], upstream)
                for low in range(0, count, 16):
                    part = slice(low, low + 16)
                    probs = jnp.exp(s_ref[part] - log_total)
                    p_ref[part] = probs.astype(jnp.bfloat16)
                    ds_ref[part] = (probs * (g_ref[part] - delta)).astype(jnp.bfloat16)
                dv_ref[group, rows, :] += dot32(p_ref[:count], upstream_nat)
                dk_ref[group, rows, :] += dot32(ds_ref[:count], queries_nat)
                return dq + dot32(k_tall[group, :, rows], ds_ref[:count])

            dq = jnp.zeros((HEAD_DIM, COLS), jnp.float32)
            dq = key_loop(lengths_ref, micro, own, tile, step, dq) * 0.125
            half_width = HEAD_DIM // 2
            cosine = tile_row(cos_ref[...], tile)
            sine = tile_row(sin_ref[...], tile)
            former, latter = dq[:half_width], dq[half_width:]
            turned = jnp.concatenate(
                [former * cosine + latter * sine, latter * cosine - former * sine], axis=0
            ).astype(jnp.bfloat16)
            for head in range(GROUPS):
                dq_ref[group, head, :, tile * TILE : (tile + 1) * TILE] = turned[
                    :, head * TILE : (head + 1) * TILE
                ]
        return unused

    lax.fori_loop(0, KV_HEADS, one_group, 0)
    for place, (block, _) in enumerate(slots):
        out_ref = (keep_ref, send_ref)[place % 2]

        @pl.when(block <= own)
        def _():
            rows = block_rows(block)
            for group in range(KV_HEADS):
                low = HEAD_DIM * group
                out_ref[place // 2, low : low + HEAD_DIM, :] = dk_ref[group, rows, :].T.astype(
                    jnp.bfloat16
                )
                low = low + KV_WIDTH
                out_ref[place // 2, low : low + HEAD_DIM, :] = dv_ref[group, rows, :].T.astype(
                    jnp.bfloat16
                )

        @pl.when(block > own)
        def _():
            out_ref[place // 2] = jnp.zeros((2 * KV_WIDTH, TOK), jnp.bfloat16)


def vmem():
    return pl.BlockSpec(memory_space=pltpu.VMEM)


def smem():
    return pl.BlockSpec(memory_space=pltpu.SMEM)


def anywhere():
    return pl.BlockSpec(memory_space=pl.ANY)


kernel_params = pltpu.CompilerParams(vmem_limit_bytes=56 * 1024 * 1024)
heads_shape = (KV_HEADS, GROUPS, HEAD_DIM, TOK)


def attend_forward(micro, lengths, queries, keyvals, begins, tie):
    return pl.pallas_call(
        partial(forward_kernel, micro),
        out_shape=(
            jax.ShapeDtypeStruct(heads_shape, jnp.bfloat16),
            jax.ShapeDtypeStruct((KV_HEADS, GROUPS, 1, TOK), jnp.float32),
        ),
        in_specs=[smem()] + [vmem()] * 6 + [anywhere()],
        out_specs=(vmem(), vmem()),
        scratch_shapes=[
            pltpu.VMEM((KV_HEADS, 4 * TOK, HEAD_DIM), jnp.bfloat16),
            pltpu.VMEM((KV_HEADS, HEAD_DIM + 16, 4 * TOK), jnp.bfloat16),
            pltpu.VMEM((2 * TILE, COLS), jnp.float32),
            pltpu.VMEM((2 * TILE, COLS), jnp.bfloat16),
        ],
        compiler_params=kernel_params,
        cost_estimate=pl.CostEstimate(
            flops=4 * 9 * 64 * TOK * 2048, bytes_accessed=4000000, transcendentals=9 * TOK * 2048
        ),
        name="attend_forward",
    )(lengths, queries, *keyvals, begins, tie)


def attend_back(
    micro, lengths, queries, keyvals, begins, mixed, log_total, grad_mixed, cosine, sine, tie
):
    half_shape = (2, 2 * KV_WIDTH, TOK)
    return pl.pallas_call(
        partial(backward_kernel, micro),
        out_shape=(
            jax.ShapeDtypeStruct(heads_shape, jnp.bfloat16),
            jax.ShapeDtypeStruct(half_shape, jnp.bfloat16),
            jax.ShapeDtypeStruct(half_shape, jnp.bfloat16),
        ),
        in_specs=[smem()] + [vmem()] * 11 + [anywhere()],
        out_specs=(vmem(),) * 3,
        scratch_shapes=[
            pltpu.VMEM((KV_HEADS, 4 * TOK, HEAD_DIM), jnp.bfloat16),
            pltpu.VMEM((KV_HEADS, 4 * TOK, HEAD_DIM), jnp.bfloat16),
            pltpu.VMEM((KV_HEADS, HEAD_DIM, 4 * TOK), jnp.bfloat16),
            pltpu.VMEM((KV_HEADS, 4 * TOK, HEAD_DIM), jnp.float32),
            pltpu.VMEM((KV_HEADS, 4 * TOK, HEAD_DIM), jnp.float32),
            pltpu.VMEM((2 * TILE, COLS), jnp.float32),
            pltpu.VMEM((2 * TILE, COLS), jnp.float32),
            pltpu.VMEM((2 * TILE, COLS), jnp.bfloat16),
            pltpu.VMEM((2 * TILE, COLS), jnp.bfloat16),
        ],
        compiler_params=kernel_params,
        cost_estimate=pl.CostEstimate(
            flops=10 * 9 * 64 * TOK * 2048, bytes_accessed=8000000, transcendentals=9 * TOK * 2048
        ),
        name="attend_back",
    )(lengths, queries, *keyvals, begins, mixed, log_total, grad_mixed, cosine, sine, tie)


def dot_with(left, right, left_side, right_side):
    return lax.dot_general(
        left, right, (((left_side,), (right_side,)), ((), ())), preferred_element_type=jnp.float32
    )


def norm_back(values, scaling, gain, upstream, axis):
    weighted = upstream * gain
    inner = jnp.mean(weighted * values, axis=axis, keepdims=True)
    gain_grad = jnp.sum(upstream * values * scaling, axis=1 - axis, keepdims=True)
    return (scaling * weighted - values * (scaling * scaling * scaling) * inner, gain_grad)


def norm_scaling(values, axis):
    return lax.rsqrt(jnp.mean(values * values, axis=axis, keepdims=True) + norm_epsilon)


def row_parts(held, spot, side):
    for turn in range(ROW_CUT):
        start = (turn ^ lax.div(spot, COL_CUT)) * CHUNK_ROWS
        part = held[pl.ds(pl.multiple_of(start, CHUNK_ROWS), CHUNK_ROWS), :]
        yield (turn * COL_CUT + side, part.astype(jnp.bfloat16))


def mlp_kernel(
    x_ref, x1_ref, c_ref, c1_ref, o0_ref, o1_ref, wo_ref, wg_ref, wu_ref, wd_ref, gain_ref,
    out_ref, out1_ref, dh_ref, do0_ref, do1_ref, keep_ref, send_ref, gwo_ref, gg_ref,
    hid, dgate, dup, n2_tall, dh_low, held, gate_ref, up_ref, da_ref,
):
    gain = gain_ref[...]
    gg_ref[...] = jnp.zeros((1, D), jnp.float32)
    block = 256
    spot = chunk_spot()
    for micro, (o_ref, do_ref) in enumerate(((o0_ref, do0_ref), (o1_ref, do1_ref))):
        rows = slice(micro * TOK, (micro + 1) * TOK)
        x_tall = x1_ref[...] if micro else x_ref[0]
        c_tall = c1_ref[...] if micro else c_ref[0]
        hidden_state = (x_tall.astype(jnp.float32) + dot_with(wo_ref[...], o_ref[...], 0, 0)).T
        scaling = norm_scaling(hidden_state, 1)
        normed = (hidden_state * scaling * gain).astype(jnp.bfloat16)
        n2_tall[:, rows] = normed.T
        back = c_tall.T
        for column in range(0, FF, block):
            columns = slice(column, column + block)
            gate_ref[...] = dot32(normed, wg_ref[:, columns])
            up_ref[...] = dot32(normed, wu_ref[:, columns])
            da_ref[...] = dot_with(back, wd_ref[columns, :], 1, 1)
            for low in range(0, TOK, 32):
                part, spot_rows = slice(low, low + 32), slice(micro * TOK + low, micro * TOK + low + 32)
                gate, upward, grad_hidden = gate_ref[part], up_ref[part], da_ref[part]
                sigmoid_gate = jax.nn.sigmoid(gate)
                activated = gate * sigmoid_gate
                hid[spot_rows, columns] = (activated * upward).astype(jnp.bfloat16)
                dup[spot_rows, columns] = (grad_hidden * activated).astype(jnp.bfloat16)
                slope = sigmoid_gate * (1.0 + gate * (1.0 - sigmoid_gate))
                dgate[spot_rows, columns] = (grad_hidden * upward * slope).astype(jnp.bfloat16)
        result = (hidden_state + dot32(hid[rows, :], wd_ref[...])).T
        if micro:
            out1_ref[...] = result.astype(jnp.bfloat16)
        else:
            out_ref[0] = result
        upstream = dot_with(dgate[rows, :], wg_ref[...], 1, 1) + dot_with(
            dup[rows, :], wu_ref[...], 1, 1
        )
        part, gain_grad = norm_back(hidden_state, scaling, gain, upstream, 1)
        gg_ref[...] += gain_grad
        grad_state = back.astype(jnp.float32) + part
        dh_low[rows, :] = grad_state.astype(jnp.bfloat16)
        grad_tall = grad_state.T
        dh_ref[micro] = grad_tall
        do_ref[...] = dot32(wo_ref[...], grad_tall.astype(jnp.bfloat16)).astype(jnp.bfloat16)
    c_parts = (c_ref.at[0], c1_ref)
    for place, right in enumerate((dgate, dup, hid)):
        for side in range(COL_CUT):
            start = (side ^ lax.rem(spot, COL_CUT)) * CHUNK_COLS
            for column in range(0, CHUNK_COLS, block):
                columns = pl.ds(pl.multiple_of(start + column, block), block)
                if place < 2:
                    held[...] = dot32(n2_tall[...], right[:, columns])
                else:
                    held[...] = dot32(c_parts[0][...], right[:TOK, columns]) + dot32(
                        c_parts[1][...], right[TOK:, columns]
                    )
                for index, part in row_parts(held, spot, side):
                    out = (keep_ref, send_ref)[index // 4]
                    out[index % 4, place, :, column : column + block] = part
    gwo_ref[...] = (
        dot32(o0_ref[...], dh_low[:TOK, :]) + dot32(o1_ref[...], dh_low[TOK:, :])
    ).astype(jnp.bfloat16)


def mlp(tokens, tokens_1, cotangent, cotangent_1, mixed, w_out, w_gate, w_up, w_down, gain):
    rows = 2 * TOK
    low = jnp.bfloat16
    chunk_shape = (CHUNKS // 2, 3, CHUNK_ROWS, CHUNK_COLS)
    return pl.pallas_call(
        mlp_kernel,
        out_shape=(
            jax.ShapeDtypeStruct((2, D, TOK), jnp.float32),
            jax.ShapeDtypeStruct((D, TOK), low),
            jax.ShapeDtypeStruct((2, D, TOK), jnp.float32),
            jax.ShapeDtypeStruct((D, TOK), low),
            jax.ShapeDtypeStruct((D, TOK), low),
            jax.ShapeDtypeStruct(chunk_shape, low),
            jax.ShapeDtypeStruct(chunk_shape, low),
            jax.ShapeDtypeStruct((D, D), low),
            jax.ShapeDtypeStruct((1, D), jnp.float32),
        ),
        in_specs=[vmem()] * 11,
        out_specs=(vmem(),) * 9,
        scratch_shapes=[
            pltpu.VMEM((rows, FF), low),
            pltpu.VMEM((rows, FF), low),
            pltpu.VMEM((rows, FF), low),
            pltpu.VMEM((D, rows), low),
            pltpu.VMEM((rows, D), low),
            pltpu.VMEM((D, 256), jnp.float32),
            pltpu.VMEM((TOK, 256), jnp.float32),
            pltpu.VMEM((TOK, 256), jnp.float32),
            pltpu.VMEM((TOK, 256), jnp.float32),
        ],
        compiler_params=kernel_params,
        cost_estimate=pl.CostEstimate(
            flops=6 * rows * 3 * D * FF, bytes_accessed=25000000, transcendentals=rows * FF
        ),
        name="mlp",
    )(tokens, tokens_1, cotangent, cotangent_1, *mixed, w_out, w_gate, w_up, w_down, gain)


def natural_tiles(flat, base, rows, width):
    pairs, step, whole = rows // 2, width * 2 // 128, width // 128
    parts = [flat[pl.ds(base + place, pairs, stride=step), :] for place in range(step)]
    even = parts[:whole] + [parts[whole][:, :HEAD_DIM]]
    odd = jnp.concatenate([parts[whole][:, HEAD_DIM:]] + parts[whole + 1 :], axis=1)
    return even, [odd[:, low : low + 128] for low in range(0, width, 128)]


def unflatten(flat, base, rows, width, tiles):
    even, odd = natural_tiles(flat, base, rows, width)
    for place, (first, second) in enumerate(zip(even, odd)):
        breadth = first.shape[1]
        if breadth < 128:
            blank = jnp.zeros((rows // 2, 128 - breadth), jnp.float32)
            first = jnp.concatenate([first, blank], axis=1)
            second = jnp.concatenate([second, blank], axis=1)
        tiles[place, pl.ds(0, rows // 2, stride=2), :] = first
        tiles[place, pl.ds(1, rows // 2, stride=2), :] = second


def tile_widths(width):
    return [(place, low, min(128, width - low)) for place, low in enumerate(range(0, width, 128))]


MIXED = ((0, 0, D), (2592, D, KV_WIDTH), (3456, D + KV_WIDTH, KV_WIDTH), (4320, FF - D, D))


def project_kernel(
    near_ref, next_ref, x_ref, x1_ref, gain_ref, cos0_ref, sin0_ref, cos1_ref, sin1_ref,
    q0_ref, q1_ref, kv_ref, w_ref, wo_ref, n_ref, flat, tiles,
):
    spot = chunk_spot()
    length = flat.shape[0] // CHUNKS
    for index in range(CHUNKS):
        chunk = spot ^ index
        core, half, chip = lax.div(chunk, 4), lax.rem(lax.div(chunk, 2), 2), lax.rem(chunk, 2)
        start = pl.multiple_of((half * 4 + chip * 2 + core) * length, 8)
        part = (near_ref, next_ref)[index // 4][index % 4]
        flat[pl.ds(start, length), :] = part.astype(jnp.float32)
    for base, start, width in MIXED:
        unflatten(flat, base, D, width, tiles)
        for place, low, breadth in tile_widths(width):
            part = tiles[place][:D, :breadth].astype(jnp.bfloat16)
            if start < FF - D:
                w_ref[:, start + low : start + low + breadth] = part
            else:
                wo_ref[:, low : low + breadth] = part
    tall = w_ref[...].T
    half_width = HEAD_DIM // 2
    tables = ((q0_ref, cos0_ref, sin0_ref), (q1_ref, cos1_ref, sin1_ref))
    for micro, (q_ref, cos_ref, sin_ref) in enumerate(tables):
        values = (x1_ref[...] if micro else x_ref[0]).astype(jnp.float32)
        normed = (values * norm_scaling(values, 0) * gain_ref[:, 0:1]).astype(jnp.bfloat16)
        n_ref[:, micro * TOK : (micro + 1) * TOK] = normed
        linear = dot32(tall, normed)
        cosine, sine = cos_ref[...], sin_ref[...]
        for head in range(HEADS + KV_HEADS):
            low = head * HEAD_DIM
            former = linear[low : low + half_width]
            latter = linear[low + half_width : low + HEAD_DIM]
            turned = jnp.concatenate(
                [former * cosine - latter * sine, latter * cosine + former * sine], axis=0
            ).astype(jnp.bfloat16)
            if head < HEADS:
                scaled = turned.astype(jnp.float32) * 0.125
                q_ref[head // GROUPS, head % GROUPS] = scaled.astype(jnp.bfloat16)
            else:
                low = low - D
                kv_ref[micro, low : low + HEAD_DIM, :] = turned
        kv_ref[micro, KV_WIDTH:, :] = linear[D + KV_WIDTH :].astype(jnp.bfloat16)


def project(near, following, tokens, tokens_1, gain_columns, tables):
    low = jnp.bfloat16
    return pl.pallas_call(
        project_kernel,
        out_shape=(
            jax.ShapeDtypeStruct(heads_shape, low),
            jax.ShapeDtypeStruct(heads_shape, low),
            jax.ShapeDtypeStruct((2, 2 * KV_WIDTH, TOK), low),
            jax.ShapeDtypeStruct((D, D + 2 * KV_WIDTH), low),
            jax.ShapeDtypeStruct((D, D), low),
            jax.ShapeDtypeStruct((D, 2 * TOK), low),
        ),
        in_specs=[vmem()] * 9,
        out_specs=(vmem(),) * 6,
        scratch_shapes=[
            pltpu.VMEM((D * FF // 128, 128), jnp.float32),
            pltpu.VMEM((5, D, 128), jnp.float32),
        ],
        compiler_params=kernel_params,
        cost_estimate=pl.CostEstimate(
            flops=4 * TOK * D * 960, bytes_accessed=8000000, transcendentals=0
        ),
        name="project",
    )(near, following, tokens, tokens_1, gain_columns, *tables[0], *tables[1])


def projection_kernel(
    n_ref, dq0_ref, dq1_ref, kept0_ref, kept1_ref, got_ref, far_ref,
    cos0_ref, sin0_ref, cos1_ref, sin1_ref, gwo_ref, tie_ref,
    keep_ref, send_ref, all_ref, held, cut,
):
    spot, chip = chunk_spot(), positions()[2]
    half_width = HEAD_DIM // 2
    parts = ((dq0_ref, kept0_ref, cos0_ref, sin0_ref), (dq1_ref, kept1_ref, cos1_ref, sin1_ref))
    for micro, (dq_ref, kept_ref, cos_ref, sin_ref) in enumerate(parts):
        columns = slice(micro * TOK, (micro + 1) * TOK)
        all_ref[:D, columns] = dq_ref[...]
        cosine, sine = cos_ref[...], sin_ref[...]
        summed = kept_ref[0].astype(jnp.float32) + got_ref[2 * micro].astype(jnp.float32)
        summed = summed + jnp.where(chip == micro, far_ref[...].astype(jnp.float32), 0.0)
        for head in range(KV_HEADS):
            low = head * HEAD_DIM
            former = summed[low : low + half_width, :]
            latter = summed[low + half_width : low + HEAD_DIM, :]
            all_ref[D + low : D + low + half_width, columns] = (
                former * cosine + latter * sine
            ).astype(jnp.bfloat16)
            all_ref[D + low + half_width : D + low + HEAD_DIM, columns] = (
                latter * cosine - former * sine
            ).astype(jnp.bfloat16)
        all_ref[D + KV_WIDTH :, columns] = summed[KV_WIDTH:, :].astype(jnp.bfloat16)
    held[:, : D + 2 * KV_WIDTH] = dot_with(n_ref[...], all_ref[...], 1, 1)
    held[:, D + 2 * KV_WIDTH :] = gwo_ref[...].astype(jnp.float32)
    for side in range(COL_CUT):
        start = (side ^ lax.rem(spot, COL_CUT)) * CHUNK_COLS
        cut[...] = held[:, pl.ds(pl.multiple_of(start, CHUNK_COLS), CHUNK_COLS)]
        for index, part in row_parts(cut, spot, side):
            (keep_ref, send_ref)[index // 4][index % 4] = part


def projection_grads(normed, dqs, kept, got, far, tables, gwo, tie):
    rows = normed.shape[1]
    chunk_shape = (CHUNKS // 2, CHUNK_ROWS, CHUNK_COLS)
    return pl.pallas_call(
        projection_kernel,
        out_shape=(
            jax.ShapeDtypeStruct(chunk_shape, jnp.bfloat16),
            jax.ShapeDtypeStruct(chunk_shape, jnp.bfloat16),
            jax.ShapeDtypeStruct((D + 2 * KV_WIDTH, rows), jnp.bfloat16),
        ),
        in_specs=[vmem()] * 12 + [anywhere()],
        out_specs=(vmem(),) * 3,
        scratch_shapes=[
            pltpu.VMEM((D, FF), jnp.float32),
            pltpu.VMEM((D, CHUNK_COLS), jnp.float32),
        ],
        compiler_params=kernel_params,
        cost_estimate=pl.CostEstimate(
            flops=2 * rows * D * 960, bytes_accessed=8000000, transcendentals=0
        ),
        name="projection_grads",
    )(normed, *dqs, *kept, got, far, *tables[0], *tables[1], gwo, tie)


def both(left_ref, right_ref, where=...):
    total = left_ref[where].astype(jnp.float32) + right_ref[where].astype(jnp.float32)
    return total.astype(jnp.bfloat16)


def plain_call(kernel, outs, operands, ties, name):
    outs = [jax.ShapeDtypeStruct(shape, jnp.bfloat16) for shape in outs]
    ties = ties if isinstance(ties, tuple) else (ties,)
    count = len(operands)

    def run(*refs):
        kernel(*refs[: count + 1], *refs[count + len(ties) :])

    return pl.pallas_call(
        run,
        out_shape=outs,
        in_specs=[vmem()] * count + [anywhere()] * len(ties),
        out_specs=[vmem()] * len(outs),
        compiler_params=kernel_params,
        name=name,
    )(*operands, *ties)


def early_third_kernel(keep_ref, got_ref, tie_ref, *outs):
    quarter = positions()[0]
    for shift, out in enumerate(outs):
        out[...] = both(keep_ref, got_ref, (0, jnp.maximum(lax.rem(quarter + shift, 4) - 1, 0)))


def early_third(keep, got, tie):
    shape = (CHUNK_ROWS, CHUNK_COLS)
    return plain_call(early_third_kernel, [shape] * 4, (keep, got), tie, "early_third")


def sum_kernel(*refs):
    total = refs[0][...].astype(jnp.float32)
    for ref in refs[1:-2]:
        total = total + ref[...].astype(jnp.float32)
    refs[-1][...] = total.astype(jnp.bfloat16)


def tied_sum(operands, tie):
    return plain_call(sum_kernel, [operands[0].shape], operands, tie, "tied_sum")[0]


def late_kernel(keep_ref, got_ref, tie_ref, keep_out, send_out):
    size = keep_out.shape[0]
    keep_out[...] = both(keep_ref, got_ref, slice(0, size))
    send_out[...] = both(keep_ref, got_ref, slice(size, 2 * size))


def late_halves(keep, got, tie):
    shape = (keep.shape[0] // 2, *keep.shape[1:])
    return plain_call(late_kernel, [shape] * 2, (keep, got), tie, "late_halves")


def pair_kernel(first_ref, second_ref, tie_ref, out_ref):
    out_ref[:2] = first_ref[...]
    out_ref[2:] = second_ref[...]


def tied_pair(first, second, tie):
    shape = (4, *first.shape[1:])
    return plain_call(pair_kernel, [shape], (first, second), tie, "tied_pair")[0]


def pick_first_kernel(own_ref, got1_ref, got2_ref, got3_ref, tie_ref, out_ref):
    quarter = positions()[0]
    for place, ref in enumerate((own_ref, got1_ref, got2_ref, got3_ref)):

        @pl.when(quarter == place)
        def _():
            out_ref[...] = ref[...]


def pick_first(pieces, tie):
    return plain_call(pick_first_kernel, [pieces[0].shape], pieces, tie, "pick_first")[0]


def pick_rest_kernel(own_ref, got1_ref, got2_ref, got3_ref, tie_ref, g_ref, u_ref, d_ref):
    quarter = positions()[0]

    def run(flat, tiles):
        for place, out in enumerate((g_ref, u_ref, d_ref), start=1):
            for shift, ref in enumerate((own_ref, got1_ref, got2_ref, got3_ref)):

                @pl.when(lax.rem(quarter - place + 4, 4) == shift)
                def _():
                    flat[...] = ref[...].astype(jnp.float32)

            rows, width = out.shape
            if width == FF:
                for tile in range(FF // 128):
                    out[:, tile * 128 : (tile + 1) * 128] = flat[
                        pl.ds(tile, rows, stride=FF // 128), :
                    ].astype(jnp.bfloat16)
            else:
                unflatten(flat, 0, rows, width, tiles)
                for tile, low, breadth in tile_widths(width):
                    out[:, low : low + breadth] = tiles[tile][:, :breadth].astype(jnp.bfloat16)

    pl.run_scoped(
        run,
        pltpu.VMEM(own_ref.shape, jnp.float32),
        pltpu.VMEM((5, FF // CHUNKS, 128), jnp.float32),
    )


def pick_rest(pieces, tie):
    shapes = [(D // CHUNKS, FF), (D // CHUNKS, FF), (FF // CHUNKS, D)]
    return plain_call(pick_rest_kernel, shapes, pieces, tie, "pick_rest")


def cast_kernel(value_ref, tie_ref, out_ref):
    out_ref[...] = value_ref[...].astype(out_ref.dtype)


def tied_cast(value, tie):
    return pl.pallas_call(
        cast_kernel,
        out_shape=jax.ShapeDtypeStruct(value.shape, jnp.bfloat16),
        in_specs=[vmem(), anywhere()],
        out_specs=vmem(),
        compiler_params=kernel_params,
        name="tied_cast",
    )(value, tie)


def inputs_kernel(all_ref, w_ref, x_ref, x1_ref, dh_ref, gain_ref, out_ref, out1_ref, gg_ref):
    gain = gain_ref[:, 0:1]
    total = jnp.zeros((D, 1), jnp.float32)
    for micro in range(2):
        columns = slice(micro * TOK, (micro + 1) * TOK)
        upstream = dot32(w_ref[...], all_ref[:, columns])
        values = (x1_ref[...] if micro else x_ref[0]).astype(jnp.float32)
        part, gain_grad = norm_back(values, norm_scaling(values, 0), gain, upstream, 0)
        total = total + gain_grad
        grad = dh_ref[micro] + part
        if micro:
            out1_ref[...] = grad.astype(out1_ref.dtype)
        else:
            out_ref[0] = grad
    gg_ref[...] = jnp.broadcast_to(total, gg_ref.shape)


def input_grads(grad_qkv, w_qkv, tokens, tokens_1, grad_state, gain_columns):
    return pl.pallas_call(
        inputs_kernel,
        out_shape=(
            jax.ShapeDtypeStruct((2, D, TOK), jnp.float32),
            jax.ShapeDtypeStruct((D, TOK), jnp.bfloat16),
            jax.ShapeDtypeStruct((D, 128), jnp.float32),
        ),
        in_specs=[vmem()] * 6,
        out_specs=(vmem(),) * 3,
        compiler_params=kernel_params,
        cost_estimate=pl.CostEstimate(
            flops=4 * TOK * D * 960, bytes_accessed=8000000, transcendentals=0
        ),
        name="input_grads",
    )(grad_qkv, w_qkv, tokens, tokens_1, grad_state, gain_columns)


def newton_loop(matrix, scale):
    current = matrix / (jnp.sqrt(jnp.sum(matrix * matrix)) + frobenius_epsilon)

    def iterate(unused, held):
        low = held.astype(jnp.bfloat16)
        square = dot_with(low, low, 1, 1)
        square_low = square.astype(jnp.bfloat16)
        mixer = newton_second * square + newton_third * dot32(square_low, square_low)
        return newton_first * held + dot32(mixer.astype(jnp.bfloat16), low)

    return lax.fori_loop(0, NS_STEPS, iterate, current) * (0.2 * math.sqrt(scale))


def newton_wide(total):
    def run(low, square, square_low, mixer, step):
        height, breadth = total.shape
        block = 256

        def scale_by(factor, keep_low):
            for row in range(0, height, 16):
                part = total[row : row + 16, :] * factor
                total[row : row + 16, :] = part
                if keep_low:
                    low[row : row + 16, :] = part.astype(jnp.bfloat16)

        norm = jnp.zeros((8, breadth), jnp.float32)
        for row in range(0, height, 8):
            part = total[row : row + 8, :]
            norm = norm + part * part
        scale_by(1.0 / (jnp.sqrt(jnp.sum(norm)) + frobenius_epsilon), True)

        def iterate(unused, held):
            square[...] = dot_with(low[...], low[...], 1, 1)
            for row in range(0, height, 16):
                rows = slice(row, row + 16)
                square_low[rows, :] = square[rows, :].astype(jnp.bfloat16)
            step[:, :height] = dot32(square_low[...], square_low[...])
            for row in range(0, height, 16):
                rows = slice(row, row + 16)
                mixed = newton_second * square[rows, :] + newton_third * step[rows, :height]
                mixer[rows, :] = mixed.astype(jnp.bfloat16)
            for column in range(0, breadth, block):
                columns = slice(column, column + block)
                step[:, :block] = dot32(mixer[...], low[:, columns])
                for row in range(0, height, 32):
                    rows = slice(row, row + 32)
                    part = newton_first * total[rows, columns] + step[rows, :block]
                    total[rows, columns] = part
                    low[rows, columns] = part.astype(jnp.bfloat16)
            return held

        lax.fori_loop(0, NS_STEPS, iterate, 0)
        scale_by(0.2 * math.sqrt(breadth), False)

    height, breadth = total.shape
    pl.run_scoped(
        run,
        pltpu.VMEM((height, breadth), jnp.bfloat16),
        pltpu.VMEM((height, height), jnp.float32),
        pltpu.VMEM((height, height), jnp.bfloat16),
        pltpu.VMEM((height, height), jnp.bfloat16),
        pltpu.VMEM((height, height), jnp.float32),
    )


def flatten_rows(tiles, start, rows, width, out):
    pairs, step, whole = rows // 2, width * 2 // 128, width // 128
    spans = range(whole + 1)
    even = [tiles[place, pl.ds(start, pairs, stride=2), :] for place in spans]
    odd = [tiles[place, pl.ds(start + 1, pairs, stride=2), :] for place in spans]
    for place in range(whole):
        out[pl.ds(place, pairs, stride=step), :] = even[place]
    rest = width - whole * 128
    joined = jnp.concatenate([even[whole][:, :rest]] + odd[:whole] + [odd[whole][:, :rest]], axis=1)
    for place in range(whole, step):
        low = (place - whole) * 128
        out[pl.ds(place, pairs, stride=step), :] = joined[:, low : low + 128]


def shard_rows(kind, kinds, start, matrix, tiles, out):
    length = out.shape[0] * 128

    if 0 in kinds:

        @pl.when(kind == 0)
        def _():
            rows = length // FF
            for place in range(FF // 128):
                out[pl.ds(place, rows, stride=FF // 128), :] = matrix[
                    pl.ds(pl.multiple_of(start, 8), rows), place * 128 : (place + 1) * 128
                ]

        @pl.when(kind == 5)
        def _():
            for place, low, breadth in tile_widths(D):
                tiles[place, :, :breadth] = matrix[low : low + breadth, :].T
            flatten_rows(tiles, start, length // D, D, out)

    for place, (base, low, width) in zip((1, 3, 4, 2), MIXED):
        if place not in kinds:
            continue

        @pl.when(kind == place)
        def _():
            for tile, column, breadth in tile_widths(width):
                tiles[tile, :D, :breadth] = matrix[:, low + column : low + column + breadth]
            flatten_rows(tiles, start, length // width, width, out)


def own_kind(length):
    square, narrow = D * D, D * KV_WIDTH
    quarter = lax.axis_index("quarter")
    index = lax.axis_index("rep") * 2 + lax.axis_index("half")
    within = (index * lax.axis_size("ctx") + lax.axis_index("ctx")) * length
    kind = jnp.where(quarter == 3, 5, 0)
    start = jnp.where(quarter == 3, lax.div(within, D), lax.div(within, FF))
    edges = ((0, 1, D), (square, 3, KV_WIDTH), (square + narrow, 4, KV_WIDTH))
    for edge, place, width in (*edges, (square + 2 * narrow, 2, D)):
        inside = (quarter == 0) & (within >= edge)
        kind = jnp.where(inside, place, kind)
        start = jnp.where(inside, lax.div(within - edge, width), start)
    return (kind, start)


def load_matrix(kind, kinds, old_ref, flat, grad, total, tiles):
    flat[...] = old_ref[...].astype(jnp.float32) * momentum_decay
    if 0 in kinds:

        @pl.when(kind == 0)
        def _():
            for place in range(FF // 128):
                columns = slice(place * 128, (place + 1) * 128)
                total[:, columns] = flat[pl.ds(place, D, stride=FF // 128), :] + grad[:, columns]

        @pl.when(kind == 5)
        def _():
            unflatten(flat, 0, FF, D, tiles)
            for place, low, breadth in tile_widths(D):
                rows = slice(low, low + breadth)
                total[rows, :] = tiles[place].T[:breadth] + grad[rows, :]

    for place, (base, low, width) in zip((1, 3, 4, 2), MIXED):
        if place not in kinds:
            continue

        @pl.when(kind == place)
        def _():
            unflatten(flat, base, D, width, tiles)
            part = jnp.concatenate(
                [tiles[tile][:D, :breadth] for tile, _, breadth in tile_widths(width)], axis=1
            )
            columns = slice(low, low + width)
            total[:, columns] = part + grad[:, columns]


def update_matrix(kind, kinds, total):
    if 0 in kinds:

        @pl.when((kind == 0) | (kind == 5))
        def _():
            newton_wide(total)

    for place, (base, low, width) in zip((1, 3, 4, 2), MIXED):
        if place not in kinds:
            continue

        @pl.when(kind == place)
        def _():
            columns = slice(low, low + width)
            if width == D:
                total[:, columns] = newton_loop(total[:, columns], D)
            else:
                total[:, columns] = newton_loop(total[:, columns].T, D).T


def newton_kernel(early, local, length, *refs):
    count = 3 if local else 2
    grad, total, tiles = refs[-3:]
    outs = refs[-3 - count : -3]
    pieces, (old_ref, *rest) = refs[:2], refs[2:-3]
    kind, start = own_kind(length)
    mine = (lax.axis_index("quarter") != 0) == early
    spot = chunk_spot()

    @pl.when(mine)
    def _():
        for index in range(CHUNKS):
            chunk = spot ^ index
            row = pl.multiple_of(lax.div(chunk, COL_CUT) * CHUNK_ROWS, CHUNK_ROWS)
            column = pl.multiple_of(lax.rem(chunk, COL_CUT) * CHUNK_COLS, CHUNK_COLS)
            rows, columns = pl.ds(row, CHUNK_ROWS), pl.ds(column, CHUNK_COLS)
            part = pieces[index // 4][index % 4]
            grad[rows, columns] = part.astype(jnp.float32)
        kinds = (0, 5) if early else (1, 2, 3, 4)
        pl.run_scoped(
            lambda flat: load_matrix(kind, kinds, old_ref, flat, grad, total, tiles),
            pltpu.VMEM((D * FF // 128, 128), jnp.float32),
        )
        update_matrix(kind, kinds, total)
        if local:
            weights_ref, momentum_ref = rest[:2]
            grad_ref, new_momentum_ref, new_weights_ref = outs
            shard_rows(kind, kinds, start, grad, tiles, grad_ref)
            shard_rows(kind, kinds, start, total, tiles, new_weights_ref)
            new_momentum_ref[...] = momentum_decay * momentum_ref[...] + grad_ref[...]
            new_weights_ref[...] = (
                weights_ref[...] * (1.0 - matrix_rate * weight_decay)
                - matrix_rate * new_weights_ref[...]
            )
        else:
            outs[0][...] = grad[...]
            outs[1][...] = total[...]

    if not early:

        @pl.when(jnp.logical_not(mine))
        def _():
            for out, before in zip(outs, rest[2:] if local else rest):
                out[...] = before[...]


def newton(early, length, pieces, old, shards, before, ties):
    local = len(shards) > 0
    if local:
        outs = (jax.ShapeDtypeStruct(shards[0].shape, jnp.float32),) * 3
    else:
        outs = (jax.ShapeDtypeStruct((D, FF), jnp.float32),) * 2
    operands = (*pieces, old, *shards, *before)

    def kernel(*refs):
        newton_kernel(early, local, length, *refs[: len(operands)], *refs[len(operands) + len(ties) :])

    return pl.pallas_call(
        kernel,
        out_shape=outs,
        in_specs=[vmem()] * len(operands) + [anywhere()] * len(ties),
        out_specs=(vmem(),) * len(outs),
        scratch_shapes=[
            pltpu.VMEM((D, FF), jnp.float32),
            pltpu.VMEM((D, FF), jnp.float32),
            pltpu.VMEM((5, FF, 128), jnp.float32),
        ],
        compiler_params=kernel_params,
        cost_estimate=pl.CostEstimate(
            flops=12000000000, bytes_accessed=9000000, transcendentals=0
        ),
        name="newton_early" if early else "newton_late",
    )(*operands, *ties)


def own_rows(kind, row, shard_length, gradient, update):
    def block_case(low, width):
        def run(gradient, update):
            start = (row, low)
            size = (shard_length // width, width)
            return tuple(
                lax.dynamic_slice(whole, start, size).reshape(-1) for whole in (gradient, update)
            )

        return run

    def tall_case(gradient, update):
        start = (0, row)
        size = (D, shard_length // D)
        return tuple(
            lax.dynamic_slice(whole, start, size).T.reshape(-1) for whole in (gradient, update)
        )

    cases = [
        block_case(0, FF),
        block_case(0, D),
        block_case(FF - D, D),
        block_case(D, KV_WIDTH),
        block_case(D + KV_WIDTH, KV_WIDTH),
        tall_case,
    ]
    return lax.switch(kind, cases, gradient, update)


CORE_SWAP = [(0, 1), (1, 0), (2, 3), (3, 2)]
CHIP_SWAP = [(0, 2), (2, 0), (1, 3), (3, 1)]
SIDE_SWAP = [(0, 1), (1, 0)]
END_SWAP = [(0, 3), (3, 0), (1, 2), (2, 1)]


def plane_pairs(bit):
    return [(place, place ^ (2, 4, 1)[bit]) for place in range(8)]


def plane_swap(value, bit):
    axis, swap = (("ctx", CHIP_SWAP), ("half", SIDE_SWAP), ("ctx", CORE_SWAP))[bit]
    return lax.ppermute(value, axis, swap)


def first_plane_swap(value, bit):
    return lax.ppermute(value, ("quarter", "half", "ctx"), plane_pairs(bit))


def plane_gather(piece, swap):
    pieces = piece[None]
    for bit in range(2):
        pieces = jnp.concatenate([pieces, swap(pieces, bit)], axis=0)
    return (pieces, swap(pieces, 2))


def depth_shift(value, shift, targets):
    pairs = [(place, (place + shift) % 4) for place in range(4)]
    return lax.ppermute(value, "quarter", [pair for pair in pairs if pair[1] in targets])


def plane_total(value):
    parts = [
        lax.ppermute(value, ("half", "ctx"), [(place, place ^ turn) for place in range(8)])
        for turn in range(1, 8)
    ]
    return value + sum(parts)


def depth_total(value):
    return value + sum(depth_shift(value, shift, range(4)) for shift in range(1, 4))


def gather_weights(low, tie):
    if lax.axis_size("rep") > 1:
        full = lax.all_gather(low, EVERY, axis=0, tiled=True).reshape(4, D * FF)
        ctx = lax.axis_index("ctx")
        spot = lax.rem(ctx, 2) * 4 + lax.axis_index("half") * 2 + ctx // 2
        chunk = jnp.arange(CHUNKS, dtype=jnp.int32) ^ spot
        order = 4 * (chunk // 2 % 2) + 2 * (chunk % 2) + chunk // 4
        mixed = full[0].reshape(CHUNKS, -1, 128)[order]
        return (mixed[:4], mixed[4:]), [
            full[1].reshape(D, FF),
            full[2].reshape(D, FF),
            full[3].reshape(FF, D),
        ]
    first = [lax.ppermute(low, "quarter", [(0, shift)]) for shift in range(1, 4)]
    mixed = pick_first((low, *first), tie)
    others = [
        lax.ppermute(low, "quarter", [(place, (place + shift) % 4) for place in range(1, 4)])
        for shift in range(1, 4)
    ]
    rest = [
        lax.all_gather(piece, PLANE, axis=0, tiled=True)
        for piece in pick_rest((low, *others), mixed)
    ]
    return plane_gather(mixed, plane_swap), rest


def per_device(tokens, lengths, weights, momentum, norm_gains, gain_first, gain_second, cotangent):
    ctx = lax.axis_index("ctx")
    chip = ctx // 2
    reps = lax.axis_size("rep")
    shard_length = weights.shape[0]
    flat_shape = (shard_length // 128, 128)
    lengths = lengths[:, 0]
    tokens = jnp.swapaxes(tokens, 1, 2)
    cotangent = jnp.swapaxes(cotangent, 1, 2)
    gain_columns = norm_gains.T

    tokens_1 = lax.ppermute(tokens[1], "ctx", END_SWAP)
    mixed_weights, (w_gate, w_up, w_down) = gather_weights(
        weights.reshape(flat_shape).astype(jnp.bfloat16), tokens_1
    )
    begin_rows, tables = [], []
    for micro in range(2):
        block = ctx if micro == 0 else 3 - ctx
        own_places = block * TOK + jnp.arange(TOK, dtype=jnp.int32)
        offsets, begins = layout(lengths[micro], own_places)
        begin_rows.append(begins.reshape(1, TOK))
        tables.append(rope_tables(offsets))

    q0, q1, keyvals, w_qkv, w_out, normed = project(
        *mixed_weights, tokens, tokens_1, gain_columns, tables
    )
    queries = (q0, q1)
    far = lax.ppermute(
        lax.dynamic_index_in_dim(keyvals, chip, 0, keepdims=False), "ctx", CHIP_SWAP
    )
    keyvals = (
        keyvals,
        lax.ppermute(keyvals, "ctx", CORE_SWAP),
        far,
        lax.ppermute(far, "ctx", CORE_SWAP),
    )
    mixed, log_totals = [], []
    for micro in range(2):
        mixed_one, log_total = attend_forward(
            micro, lengths, queries[micro], keyvals, begin_rows[micro], norm_gains
        )
        mixed.append(mixed_one)
        log_totals.append(log_total)
    cotangent_1 = lax.ppermute(cotangent[1], "ctx", END_SWAP)
    old = lax.all_gather(
        tied_cast(momentum.reshape(flat_shape), mixed[0]),
        ("rep", "half", "ctx"),
        axis=0,
        tiled=True,
    )
    outs = mlp(
        tokens,
        tokens_1,
        cotangent,
        cotangent_1,
        [part.reshape(D, TOK) for part in mixed],
        w_out,
        w_gate,
        w_up,
        w_down,
        norm_gains[1:2],
    )
    result, result_1, grad_state, grad_mixed_0, grad_mixed_1 = outs[:5]
    keep, send, grad_w_out, gain_two_grad = outs[5:]
    returned = lax.ppermute(result_1, "ctx", END_SWAP)

    def back_pass(micro, grad_mixed, tie):
        return attend_back(
            micro,
            lengths,
            queries[micro],
            keyvals,
            begin_rows[micro],
            mixed[micro],
            log_totals[micro],
            grad_mixed.reshape(heads_shape),
            *tables[micro],
            tie,
        )

    got = plane_swap(send, 2)
    dq0, kept0, sent0 = back_pass(0, grad_mixed_0, old)
    keep, send = late_halves(keep, got, (dq0, returned))
    got = plane_swap(send, 1)
    dq1, kept1, sent1 = back_pass(1, grad_mixed_1, keep)
    traded = lax.ppermute(tied_pair(sent0, sent1, dq1), "ctx", CORE_SWAP)
    heavy = chip == 0
    crossing = jnp.where(heavy, kept1[1], kept0[1]).astype(jnp.float32) + jnp.where(
        heavy, traded[3], traded[1]
    ).astype(jnp.float32)
    crossing = crossing.astype(jnp.bfloat16)
    crossed = lax.ppermute(crossing, "ctx", CHIP_SWAP)
    keep, send = late_halves(keep, got, crossing)
    got = plane_swap(send, 0)
    late_keep, late_send, grad_qkv = projection_grads(
        normed,
        (dq0.reshape(D, TOK), dq1.reshape(D, TOK)),
        (kept0, kept1),
        traded,
        crossed,
        tables,
        grad_w_out,
        keep,
    )
    late_got = plane_swap(late_send, 2)
    late_keep, late_send = late_halves(late_keep, late_got, keep)
    early, *turns = early_third(keep, got, late_keep)
    early_parts = [
        depth_shift(turn, shift, range(1, 4)) for shift, turn in enumerate(turns, start=1)
    ]
    late_got = plane_swap(late_send, 1)
    grad_inputs, grad_inputs_1, gain_one_grad = input_grads(
        grad_qkv, w_qkv, tokens, tokens_1, grad_state, gain_columns
    )
    late_keep, late_send = late_halves(late_keep, late_got, gain_one_grad)
    early = tied_sum((early, *early_parts), late_keep)
    if reps > 1:
        early = lax.psum(early, "rep")
    late = tied_sum((late_keep[0], plane_swap(late_send, 0)[0]), gain_one_grad)
    late_parts = [depth_shift(late, shift, (0,)) for shift in range(1, 4)]
    early_pieces = plane_gather(early, plane_swap)
    gain_grad = plane_total(
        jnp.concatenate([gain_one_grad[:, 0].reshape(1, D), gain_two_grad], axis=0)
    )
    grad_inputs_1 = lax.ppermute(tied_cast(grad_inputs_1, late), "ctx", END_SWAP)

    shards = ()
    if flat_shape[0] % 8 == 0:
        shards = (weights.reshape(flat_shape), momentum.reshape(flat_shape))
    before = newton(True, shard_length, early_pieces, old, shards, (), (late, gain_grad))
    late = tied_sum((late, *late_parts), before[0])
    gain_grad = depth_total(gain_grad)
    if reps > 1:
        late = lax.psum(late, "rep")
        gain_grad = lax.psum(gain_grad, "rep")
    late_pieces = plane_gather(late, first_plane_swap)
    outs = newton(
        False, shard_length, late_pieces, old, shards, before, (gain_grad, grad_inputs_1)
    )
    if len(shards) > 0:
        grad_shard, new_momentum, new_weights = [out.reshape(weights.shape) for out in outs]
    else:
        kind, start = own_kind(shard_length)
        grad_shard, update_shard = own_rows(kind, start, shard_length, *outs)
        new_momentum = momentum_decay * momentum + grad_shard
        new_weights = weights * (1.0 - matrix_rate * weight_decay) - matrix_rate * update_shard

    def placed(whole, part):
        whole = lax.dynamic_update_index_in_dim(whole, part.astype(jnp.float32), 1, 0)
        return jnp.swapaxes(whole, 1, 2)

    first_new = first_decay * gain_first + (1.0 - first_decay) * gain_grad
    second_new = second_decay * gain_second + (1.0 - second_decay) * gain_grad * gain_grad
    debiased_first_moment = first_new / (1.0 - first_decay**ADAM_STEP)
    corrected_second = second_new / (1.0 - second_decay**ADAM_STEP)
    new_gains = norm_gains * (
        1.0 - gain_rate * weight_decay
    ) - gain_rate * debiased_first_moment / (jnp.sqrt(corrected_second) + adam_epsilon)
    return (
        placed(result, returned),
        placed(grad_inputs, grad_inputs_1),
        grad_shard,
        new_momentum,
        new_weights,
        first_new,
        second_new,
        new_gains,
    )


def solution(mesh):
    devices = mesh.devices
    count = devices.size
    context = mesh.shape["ctx"]
    split = Mesh(
        devices.reshape(4, count // (8 * context), 2, context), ("quarter", "rep", "half", "ctx")
    )
    rows = P(None, EVERY, None)
    flat = P(EVERY)
    placed = (rows, P(None, ("quarter", "rep", "half"), None), flat, flat, P(), P(), P(), rows)
    return jax.shard_map(
        per_device,
        mesh=split,
        in_specs=placed,
        out_specs=(rows, rows, flat, flat, flat, P(), P(), P()),
        check_vma=False,
    )
```

```python
from functools import partial
import math

import jax
import jax.numpy as jnp
from jax import lax
from jax.experimental import pallas as pl
from jax.experimental.pallas import tpu as pltpu
from jax.sharding import Mesh, PartitionSpec as P

HEADS = 9
KV_HEADS = 3
HEAD_DIM = 64
FF = 1536
NS_STEPS = 5
ADAM_STEP = 10
D = 576
KV_WIDTH = 192
GROUPS = HEADS // KV_HEADS
TOK = 512
TILE = 256
COLS = GROUPS * TILE
ROW_CUT = 4
COL_CUT = 2
CHUNKS = ROW_CUT * COL_CUT
CHUNK_ROWS = D // ROW_CUT
CHUNK_COLS = FF // COL_CUT
PLANE = ("half", "ctx")
EVERY = ("quarter", "rep", "half", "ctx")


norm_epsilon = 1e-05
rope_base = 100000.0
masked_score = -1e30
newton_first = 3.4445
newton_second = -4.775
newton_third = 2.0315
momentum_decay = 0.95
matrix_rate = 0.2
weight_decay = 0.1
gain_rate = 0.2
first_decay = 0.9
second_decay = 0.95
adam_epsilon = 1e-08
frobenius_epsilon = 1e-07


def layout(lengths_row, places):
    finish = jnp.cumsum(lengths_row)
    firsts = finish - lengths_row
    begins = jnp.max(jnp.where(places[:, None] >= firsts[None, :], firsts[None, :], 0), axis=1)
    return (places - begins, begins)


def rope_tables(offsets):
    half_width = HEAD_DIM // 2
    inverse = jnp.exp(
        jnp.arange(half_width, dtype=jnp.float32) * (-2.0 * math.log(rope_base) / HEAD_DIM)
    )
    angles = inverse[:, None] * offsets.astype(jnp.float32)[None, :]
    return (jnp.cos(angles), jnp.sin(angles))


def dot32(left, right):
    return jnp.dot(left, right, preferred_element_type=jnp.float32)


def masked(scores, key_block, begins, places):
    keys = key_block * TILE + lax.broadcasted_iota(jnp.int32, scores.shape, 0)
    return jnp.where((keys >= begins) & (keys <= places), scores, masked_score)


def tile_row(row, tile):
    part = row[:, tile * TILE : (tile + 1) * TILE]
    return jnp.concatenate([part] * GROUPS, axis=1)


def tile_heads(ref, group, tile):
    return jnp.concatenate(
        [ref[group, head, :, tile * TILE : (tile + 1) * TILE] for head in range(GROUPS)], axis=1
    )


def positions():
    ctx = lax.axis_index("ctx")
    return (lax.axis_index("quarter"), lax.axis_index("half"), lax.div(ctx, 2), lax.rem(ctx, 2))


def chunk_spot():
    _, half, chip, core = positions()
    return core * 4 + half * 2 + chip


def first_key(lengths_ref, slot, row):
    micro = slot ^ positions()[2]
    begin = jnp.int32(0)
    first = jnp.int32(0)
    for place in range(3):
        first = first + lengths_ref[micro, place]
        begin = jnp.where(row >= first, first, begin)
    return begin


def key_loop(lengths_ref, micro, own, tile, step, carry):
    last = own * (TOK // TILE) + tile
    first = lax.div(first_key(lengths_ref, micro, last * TILE), TILE)
    full = lax.div(first_key(lengths_ref, micro, last * TILE + TILE - 1) + TILE - 1, TILE)
    full = jnp.minimum(full, last)
    pairs = lax.div(last - full, 2)
    carry = lax.fori_loop(first, full, partial(step, True, 1), carry)
    carry = lax.fori_loop(
        0, pairs, lambda pair, held: step(False, 2, full + 2 * pair, held), carry
    )
    carry = lax.fori_loop(full + 2 * pairs, last, partial(step, False, 1), carry)
    return step(True, 1, last, carry)


def own_block(slot):
    ctx = lax.axis_index("ctx")
    return jnp.maximum(ctx, 3 - ctx) if slot else jnp.minimum(ctx, 3 - ctx)


def key_slots(own, micro, kv_ref, other_ref, far_ref, far_other_ref):
    refs = (kv_ref.at[micro], other_ref.at[micro], far_ref, far_other_ref)[: 2 + 2 * micro]
    return [(own ^ place, ref) for place, ref in enumerate(refs)]


def block_rows(block):
    return pl.ds(pl.multiple_of(block * TOK, TOK), TOK)


def forward_kernel(
    micro, lengths_ref, q_ref, kv_ref, other_ref, far_ref, far_other_ref, begin_ref, tie_ref,
    o_ref, lse_ref, k_nat, v_ext, s_ref, p_ref,
):
    own = own_block(micro)
    for block, source in key_slots(own, micro, kv_ref, other_ref, far_ref, far_other_ref):

        @pl.when(block <= own)
        def _():
            rows = block_rows(block)
            for group in range(KV_HEADS):
                low = HEAD_DIM * group
                k_nat[group, rows, :] = source[low : low + HEAD_DIM, :].T
                low = low + KV_WIDTH
                v_ext[group, :HEAD_DIM, rows] = source[low : low + HEAD_DIM, :]
                v_ext[group, HEAD_DIM:, rows] = jnp.ones((16, TOK), jnp.bfloat16)

    def one_group(group, unused):
        for tile in range(TOK // TILE):
            queries = tile_heads(q_ref, group, tile)
            begins = tile_row(begin_ref[...], tile)
            column = lax.broadcasted_iota(jnp.int32, (1, COLS), 1)
            places = own * TOK + tile * TILE + lax.rem(column, TILE)

            def step(is_masked, width, key_block, carry):
                top, total = carry
                keys = pl.ds(pl.multiple_of(key_block * TILE, TILE), width * TILE)
                count = width * TILE
                scores = dot32(k_nat[group, keys, :], queries)
                s_ref[:count] = masked(scores, key_block, begins, places) if is_masked else scores
                highest = s_ref[:16]
                for low in range(16, count, 16):
                    highest = jnp.maximum(highest, s_ref[low : low + 16])
                new_top = jnp.maximum(top, jnp.max(highest, axis=0, keepdims=True))
                for low in range(0, count, 16):
                    rows = slice(low, low + 16)
                    p_ref[rows] = jnp.exp(s_ref[rows] - new_top).astype(jnp.bfloat16)
                total = total * jnp.exp(top - new_top) + dot32(
                    v_ext[group, :, keys], p_ref[:count]
                )
                return (new_top, total)

            carry = (
                jnp.full((1, COLS), masked_score, jnp.float32),
                jnp.zeros((HEAD_DIM + 16, COLS), jnp.float32),
            )
            top, total = key_loop(lengths_ref, micro, own, tile, step, carry)
            weight = total[HEAD_DIM : HEAD_DIM + 1, :]
            mixed = (total[:HEAD_DIM, :] / weight).astype(jnp.bfloat16)
            log_total = top + jnp.log(weight)
            for head in range(GROUPS):
                o_ref[group, head, :, tile * TILE : (tile + 1) * TILE] = mixed[
                    :, head * TILE : (head + 1) * TILE
                ]
                lse_ref[group, head, :, tile * TILE : (tile + 1) * TILE] = log_total[
                    :, head * TILE : (head + 1) * TILE
                ]
        return unused

    lax.fori_loop(0, KV_HEADS, one_group, 0)


def backward_kernel(
    micro, lengths_ref, q_ref, kv_ref, other_ref, far_ref, far_other_ref, begin_ref, o_ref, lse_ref,
    do_ref, cos_ref, sin_ref, tie_ref,
    dq_ref, keep_ref, send_ref, k_nat, v_nat, k_tall, dk_ref, dv_ref, s_ref, g_ref, p_ref, ds_ref,
):
    own = own_block(micro)
    slots = key_slots(own, micro, kv_ref, other_ref, far_ref, far_other_ref)
    for block, source in slots:

        @pl.when(block <= own)
        def _():
            rows = block_rows(block)
            for group in range(KV_HEADS):
                low = HEAD_DIM * group
                k_nat[group, rows, :] = source[low : low + HEAD_DIM, :].T
                k_tall[group, :, rows] = source[low : low + HEAD_DIM, :]
                low = low + KV_WIDTH
                v_nat[group, rows, :] = source[low : low + HEAD_DIM, :].T
                dk_ref[group, rows, :] = jnp.zeros((TOK, HEAD_DIM), jnp.float32)
                dv_ref[group, rows, :] = jnp.zeros((TOK, HEAD_DIM), jnp.float32)

    def one_group(group, unused):
        for tile in range(TOK // TILE):
            queries = tile_heads(q_ref, group, tile)
            upstream = tile_heads(do_ref, group, tile)
            mixed = tile_heads(o_ref, group, tile)
            log_total = tile_heads(lse_ref, group, tile)
            delta = jnp.sum(
                upstream.astype(jnp.float32) * mixed.astype(jnp.float32), axis=0, keepdims=True
            )
            queries_nat = queries.T
            upstream_nat = upstream.T
            begins = tile_row(begin_ref[...], tile)
            column = lax.broadcasted_iota(jnp.int32, (1, COLS), 1)
            places = own * TOK + tile * TILE + lax.rem(column, TILE)

            def step(is_masked, width, key_block, dq):
                rows = pl.ds(pl.multiple_of(key_block * TILE, TILE), width * TILE)
                count = width * TILE
                scores = dot32(k_nat[group, rows, :], queries)
                s_ref[:count] = masked(scores, key_block, begins, places) if is_masked else scores
                g_ref[:count] = dot32(v_nat[group, rows, :], upstream)
                for low in range(0, count, 16):
                    part = slice(low, low + 16)
                    probs = jnp.exp(s_ref[part] - log_total)
                    p_ref[part] = probs.astype(jnp.bfloat16)
                    ds_ref[part] = (probs * (g_ref[part] - delta)).astype(jnp.bfloat16)
                dv_ref[group, rows, :] += dot32(p_ref[:count], upstream_nat)
                dk_ref[group, rows, :] += dot32(ds_ref[:count], queries_nat)
                return dq + dot32(k_tall[group, :, rows], ds_ref[:count])

            dq = jnp.zeros((HEAD_DIM, COLS), jnp.float32)
            dq = key_loop(lengths_ref, micro, own, tile, step, dq) * 0.125
            half_width = HEAD_DIM // 2
            cosine = tile_row(cos_ref[...], tile)
            sine = tile_row(sin_ref[...], tile)
            former, latter = dq[:half_width], dq[half_width:]
            turned = jnp.concatenate(
                [former * cosine + latter * sine, latter * cosine - former * sine], axis=0
            ).astype(jnp.bfloat16)
            for head in range(GROUPS):
                dq_ref[group, head, :, tile * TILE : (tile + 1) * TILE] = turned[
                    :, head * TILE : (head + 1) * TILE
                ]
        return unused

    lax.fori_loop(0, KV_HEADS, one_group, 0)
    for place, (block, _) in enumerate(slots):
        out_ref = (keep_ref, send_ref)[place % 2]

        @pl.when(block <= own)
        def _():
            rows = block_rows(block)
            for group in range(KV_HEADS):
                low = HEAD_DIM * group
                out_ref[place // 2, low : low + HEAD_DIM, :] = dk_ref[group, rows, :].T.astype(
                    jnp.bfloat16
                )
                low = low + KV_WIDTH
                out_ref[place // 2, low : low + HEAD_DIM, :] = dv_ref[group, rows, :].T.astype(
                    jnp.bfloat16
                )

        @pl.when(block > own)
        def _():
            out_ref[place // 2] = jnp.zeros((2 * KV_WIDTH, TOK), jnp.bfloat16)


def vmem():
    return pl.BlockSpec(memory_space=pltpu.VMEM)


def smem():
    return pl.BlockSpec(memory_space=pltpu.SMEM)


def anywhere():
    return pl.BlockSpec(memory_space=pl.ANY)


kernel_params = pltpu.CompilerParams(vmem_limit_bytes=56 * 1024 * 1024)
heads_shape = (KV_HEADS, GROUPS, HEAD_DIM, TOK)


def attend_forward(micro, lengths, queries, keyvals, begins, tie):
    return pl.pallas_call(
        partial(forward_kernel, micro),
        out_shape=(
            jax.ShapeDtypeStruct(heads_shape, jnp.bfloat16),
            jax.ShapeDtypeStruct((KV_HEADS, GROUPS, 1, TOK), jnp.float32),
        ),
        in_specs=[smem()] + [vmem()] * 6 + [anywhere()],
        out_specs=(vmem(), vmem()),
        scratch_shapes=[
            pltpu.VMEM((KV_HEADS, 4 * TOK, HEAD_DIM), jnp.bfloat16),
            pltpu.VMEM((KV_HEADS, HEAD_DIM + 16, 4 * TOK), jnp.bfloat16),
            pltpu.VMEM((2 * TILE, COLS), jnp.float32),
            pltpu.VMEM((2 * TILE, COLS), jnp.bfloat16),
        ],
        compiler_params=kernel_params,
        cost_estimate=pl.CostEstimate(
            flops=4 * 9 * 64 * TOK * 2048, bytes_accessed=4000000, transcendentals=9 * TOK * 2048
        ),
        name="attend_forward",
    )(lengths, queries, *keyvals, begins, tie)


def attend_back(
    micro, lengths, queries, keyvals, begins, mixed, log_total, grad_mixed, cosine, sine, tie
):
    half_shape = (1 + micro, 2 * KV_WIDTH, TOK)
    return pl.pallas_call(
        partial(backward_kernel, micro),
        out_shape=(
            jax.ShapeDtypeStruct(heads_shape, jnp.bfloat16),
            jax.ShapeDtypeStruct(half_shape, jnp.bfloat16),
            jax.ShapeDtypeStruct(half_shape, jnp.bfloat16),
        ),
        in_specs=[smem()] + [vmem()] * 11 + [anywhere()],
        out_specs=(vmem(),) * 3,
        scratch_shapes=[
            pltpu.VMEM((KV_HEADS, 4 * TOK, HEAD_DIM), jnp.bfloat16),
            pltpu.VMEM((KV_HEADS, 4 * TOK, HEAD_DIM), jnp.bfloat16),
            pltpu.VMEM((KV_HEADS, HEAD_DIM, 4 * TOK), jnp.bfloat16),
            pltpu.VMEM((KV_HEADS, 4 * TOK, HEAD_DIM), jnp.float32),
            pltpu.VMEM((KV_HEADS, 4 * TOK, HEAD_DIM), jnp.float32),
            pltpu.VMEM((2 * TILE, COLS), jnp.float32),
            pltpu.VMEM((2 * TILE, COLS), jnp.float32),
            pltpu.VMEM((2 * TILE, COLS), jnp.bfloat16),
            pltpu.VMEM((2 * TILE, COLS), jnp.bfloat16),
        ],
        compiler_params=kernel_params,
        cost_estimate=pl.CostEstimate(
            flops=10 * 9 * 64 * TOK * 2048, bytes_accessed=8000000, transcendentals=9 * TOK * 2048
        ),
        name="attend_back",
    )(lengths, queries, *keyvals, begins, mixed, log_total, grad_mixed, cosine, sine, tie)


def dot_with(left, right, left_side, right_side):
    return lax.dot_general(
        left, right, (((left_side,), (right_side,)), ((), ())), preferred_element_type=jnp.float32
    )


def norm_back(values, scaling, gain, upstream, axis):
    weighted = upstream * gain
    inner = jnp.mean(weighted * values, axis=axis, keepdims=True)
    gain_grad = jnp.sum(upstream * values * scaling, axis=1 - axis, keepdims=True)
    return (scaling * weighted - values * (scaling * scaling * scaling) * inner, gain_grad)


def norm_scaling(values, axis):
    return lax.rsqrt(jnp.mean(values * values, axis=axis, keepdims=True) + norm_epsilon)


def row_parts(held, spot, side):
    for turn in range(ROW_CUT):
        start = (turn ^ lax.div(spot, COL_CUT)) * CHUNK_ROWS
        part = held[pl.ds(pl.multiple_of(start, CHUNK_ROWS), CHUNK_ROWS), :]
        yield (turn * COL_CUT + side, part.astype(jnp.bfloat16))


def store_result(slot, result, out_ref, moved_ref):
    chip = positions()[2]

    @pl.when(chip == slot)
    def _():
        out_ref[0] = result

    @pl.when(chip != slot)
    def _():
        moved_ref[...] = result.astype(jnp.bfloat16)


def mlp_kernel(
    x_ref, x1_ref, c_ref, c1_ref, o0_ref, o1_ref, wo_ref, w_ref, wd_ref, gain_ref,
    out_ref, out1_ref, dh_ref, do0_ref, do1_ref, keep_ref, send_ref, gwo_ref, gg_ref,
    hid, dgate, dup, n2_tall, dh_low, held, gate_ref, up_ref, da_ref,
):
    gain = gain_ref[...]
    gg_ref[...] = jnp.zeros((1, D), jnp.float32)
    block = 256
    spot = chunk_spot()
    for micro, (o_ref, do_ref) in enumerate(((o0_ref, do0_ref), (o1_ref, do1_ref))):
        rows = slice(micro * TOK, (micro + 1) * TOK)
        x_tall = (x1_ref if micro else x_ref)[...]
        c_tall = (c1_ref if micro else c_ref)[...]
        hidden_state = (x_tall.astype(jnp.float32) + dot_with(wo_ref[...], o_ref[...], 0, 0)).T
        scaling = norm_scaling(hidden_state, 1)
        normed = (hidden_state * scaling * gain).astype(jnp.bfloat16)
        n2_tall[:, rows] = normed.T
        back = c_tall.T
        for column in range(0, FF, block):
            columns = slice(column, column + block)
            gate_ref[...] = dot32(normed, w_ref[:, columns])
            up_ref[...] = dot32(normed, w_ref[:, FF + column : FF + column + block])
            da_ref[...] = dot_with(back, wd_ref[columns, :], 1, 1)
            for low in range(0, TOK, 32):
                part, spot_rows = slice(low, low + 32), slice(micro * TOK + low, micro * TOK + low + 32)
                gate, upward, grad_hidden = gate_ref[part], up_ref[part], da_ref[part]
                sigmoid_gate = jax.nn.sigmoid(gate)
                activated = gate * sigmoid_gate
                hid[spot_rows, columns] = (activated * upward).astype(jnp.bfloat16)
                dup[spot_rows, columns] = (grad_hidden * activated).astype(jnp.bfloat16)
                slope = sigmoid_gate * (1.0 + gate * (1.0 - sigmoid_gate))
                dgate[spot_rows, columns] = (grad_hidden * upward * slope).astype(jnp.bfloat16)
        result = (hidden_state + dot32(hid[rows, :], wd_ref[...])).T
        store_result(micro, result, out_ref, out1_ref)
        upstream = dot_with(dgate[rows, :], w_ref[:, :FF], 1, 1) + dot_with(
            dup[rows, :], w_ref[:, FF:], 1, 1
        )
        part, gain_grad = norm_back(hidden_state, scaling, gain, upstream, 1)
        gg_ref[...] += gain_grad
        grad_state = back.astype(jnp.float32) + part
        dh_low[rows, :] = grad_state.astype(jnp.bfloat16)
        grad_tall = grad_state.T
        dh_ref[micro] = grad_tall
        do_ref[...] = dot32(wo_ref[...], grad_tall.astype(jnp.bfloat16)).astype(jnp.bfloat16)
    c_parts = (c_ref, c1_ref)
    for place, right in enumerate((dgate, dup, hid)):
        for side in range(COL_CUT):
            start = (side ^ lax.rem(spot, COL_CUT)) * CHUNK_COLS
            for column in range(0, CHUNK_COLS, block):
                columns = pl.ds(pl.multiple_of(start + column, block), block)
                if place < 2:
                    held[...] = dot32(n2_tall[...], right[:, columns])
                else:
                    held[...] = dot32(c_parts[0][...], right[:TOK, columns]) + dot32(
                        c_parts[1][...], right[TOK:, columns]
                    )
                for index, part in row_parts(held, spot, side):
                    out = (keep_ref, send_ref)[index // 4]
                    out[index % 4, place, :, column : column + block] = part
    gwo_ref[...] = (
        dot32(o0_ref[...], dh_low[:TOK, :]) + dot32(o1_ref[...], dh_low[TOK:, :])
    ).astype(jnp.bfloat16)


def mlp(tokens, tokens_1, cotangent, cotangent_1, mixed, w_out, w_gate_up, w_down, gain):
    rows = 2 * TOK
    low = jnp.bfloat16
    chunk_shape = (CHUNKS // 2, 3, CHUNK_ROWS, CHUNK_COLS)
    return pl.pallas_call(
        mlp_kernel,
        out_shape=(
            jax.ShapeDtypeStruct((2, D, TOK), jnp.float32),
            jax.ShapeDtypeStruct((D, TOK), low),
            jax.ShapeDtypeStruct((2, D, TOK), jnp.float32),
            jax.ShapeDtypeStruct((D, TOK), low),
            jax.ShapeDtypeStruct((D, TOK), low),
            jax.ShapeDtypeStruct(chunk_shape, low),
            jax.ShapeDtypeStruct(chunk_shape, low),
            jax.ShapeDtypeStruct((D, D), low),
            jax.ShapeDtypeStruct((1, D), jnp.float32),
        ),
        in_specs=[vmem()] * 10,
        out_specs=(vmem(),) * 9,
        scratch_shapes=[
            pltpu.VMEM((rows, FF), low),
            pltpu.VMEM((rows, FF), low),
            pltpu.VMEM((rows, FF), low),
            pltpu.VMEM((D, rows), low),
            pltpu.VMEM((rows, D), low),
            pltpu.VMEM((D, 256), jnp.float32),
            pltpu.VMEM((TOK, 256), jnp.float32),
            pltpu.VMEM((TOK, 256), jnp.float32),
            pltpu.VMEM((TOK, 256), jnp.float32),
        ],
        compiler_params=kernel_params,
        cost_estimate=pl.CostEstimate(
            flops=6 * rows * 3 * D * FF, bytes_accessed=25000000, transcendentals=rows * FF
        ),
        name="mlp",
    )(tokens, tokens_1, cotangent, cotangent_1, *mixed, w_out, w_gate_up, w_down, gain)


def natural_tiles(flat, base, rows, width):
    pairs, step, whole = rows // 2, width * 2 // 128, width // 128
    parts = [flat[pl.ds(base + place, pairs, stride=step), :] for place in range(step)]
    even = parts[:whole] + [parts[whole][:, :HEAD_DIM]]
    odd = jnp.concatenate([parts[whole][:, HEAD_DIM:]] + parts[whole + 1 :], axis=1)
    return even, [odd[:, low : low + 128] for low in range(0, width, 128)]


def unflatten(flat, base, rows, width, tiles):
    even, odd = natural_tiles(flat, base, rows, width)
    for place, (first, second) in enumerate(zip(even, odd)):
        breadth = first.shape[1]
        if breadth < 128:
            blank = jnp.zeros((rows // 2, 128 - breadth), jnp.float32)
            first = jnp.concatenate([first, blank], axis=1)
            second = jnp.concatenate([second, blank], axis=1)
        tiles[place, pl.ds(0, rows // 2, stride=2), :] = first
        tiles[place, pl.ds(1, rows // 2, stride=2), :] = second


def tile_widths(width):
    return [(place, low, min(128, width - low)) for place, low in enumerate(range(0, width, 128))]


MIXED = ((0, 0, D), (2592, D, KV_WIDTH), (3456, D + KV_WIDTH, KV_WIDTH), (4320, FF - D, D))


def project_kernel(
    near_ref, next_ref, x_ref, x1_ref, gain_ref, cos0_ref, sin0_ref, cos1_ref, sin1_ref,
    q0_ref, q1_ref, kv_ref, w_ref, wo_ref, n_ref, flat, tiles,
):
    spot = chunk_spot()
    length = flat.shape[0] // CHUNKS
    for index in range(CHUNKS):
        chunk = spot ^ index
        core, half, chip = lax.div(chunk, 4), lax.rem(lax.div(chunk, 2), 2), lax.rem(chunk, 2)
        start = pl.multiple_of((half * 4 + chip * 2 + core) * length, 8)
        part = (near_ref, next_ref)[index // 4][index % 4]
        flat[pl.ds(start, length), :] = part.astype(jnp.float32)
    for base, start, width in MIXED:
        unflatten(flat, base, D, width, tiles)
        for place, low, breadth in tile_widths(width):
            part = tiles[place][:D, :breadth].astype(jnp.bfloat16)
            if start < FF - D:
                w_ref[:, start + low : start + low + breadth] = part
            else:
                wo_ref[:, low : low + breadth] = part
    tall = w_ref[...].T
    half_width = HEAD_DIM // 2
    tables = ((q0_ref, cos0_ref, sin0_ref), (q1_ref, cos1_ref, sin1_ref))
    for micro, (q_ref, cos_ref, sin_ref) in enumerate(tables):
        values = (x1_ref if micro else x_ref)[...].astype(jnp.float32)
        normed = (values * norm_scaling(values, 0) * gain_ref[:, 0:1]).astype(jnp.bfloat16)
        n_ref[:, micro * TOK : (micro + 1) * TOK] = normed
        linear = dot32(tall, normed)
        cosine, sine = cos_ref[...], sin_ref[...]
        for head in range(HEADS + KV_HEADS):
            low = head * HEAD_DIM
            former = linear[low : low + half_width]
            latter = linear[low + half_width : low + HEAD_DIM]
            turned = jnp.concatenate(
                [former * cosine - latter * sine, latter * cosine + former * sine], axis=0
            ).astype(jnp.bfloat16)
            if head < HEADS:
                scaled = turned.astype(jnp.float32) * 0.125
                q_ref[head // GROUPS, head % GROUPS] = scaled.astype(jnp.bfloat16)
            else:
                low = low - D
                kv_ref[micro, low : low + HEAD_DIM, :] = turned
        kv_ref[micro, KV_WIDTH:, :] = linear[D + KV_WIDTH :].astype(jnp.bfloat16)


def project(near, following, tokens, tokens_1, gain_columns, tables):
    low = jnp.bfloat16
    return pl.pallas_call(
        project_kernel,
        out_shape=(
            jax.ShapeDtypeStruct(heads_shape, low),
            jax.ShapeDtypeStruct(heads_shape, low),
            jax.ShapeDtypeStruct((2, 2 * KV_WIDTH, TOK), low),
            jax.ShapeDtypeStruct((D, D + 2 * KV_WIDTH), low),
            jax.ShapeDtypeStruct((D, D), low),
            jax.ShapeDtypeStruct((D, 2 * TOK), low),
        ),
        in_specs=[vmem()] * 9,
        out_specs=(vmem(),) * 6,
        scratch_shapes=[
            pltpu.VMEM((D * FF // 128, 128), jnp.float32),
            pltpu.VMEM((5, D, 128), jnp.float32),
        ],
        compiler_params=kernel_params,
        cost_estimate=pl.CostEstimate(
            flops=4 * TOK * D * 960, bytes_accessed=8000000, transcendentals=0
        ),
        name="project",
    )(near, following, tokens, tokens_1, gain_columns, *tables[0], *tables[1])


def projection_kernel(
    n_ref, dq0_ref, dq1_ref, kept0_ref, kept1_ref, got_ref, far_ref,
    cos0_ref, sin0_ref, cos1_ref, sin1_ref, gwo_ref, tie_ref,
    keep_ref, send_ref, all_ref, held, cut,
):
    spot = chunk_spot()
    half_width = HEAD_DIM // 2
    parts = ((dq0_ref, kept0_ref, cos0_ref, sin0_ref), (dq1_ref, kept1_ref, cos1_ref, sin1_ref))
    for micro, (dq_ref, kept_ref, cos_ref, sin_ref) in enumerate(parts):
        columns = slice(micro * TOK, (micro + 1) * TOK)
        all_ref[:D, columns] = dq_ref[...]
        cosine, sine = cos_ref[...], sin_ref[...]
        summed = kept_ref[0].astype(jnp.float32) + got_ref[micro].astype(jnp.float32)
        if micro == 0:
            summed = summed + far_ref[...].astype(jnp.float32)
        for head in range(KV_HEADS):
            low = head * HEAD_DIM
            former = summed[low : low + half_width, :]
            latter = summed[low + half_width : low + HEAD_DIM, :]
            all_ref[D + low : D + low + half_width, columns] = (
                former * cosine + latter * sine
            ).astype(jnp.bfloat16)
            all_ref[D + low + half_width : D + low + HEAD_DIM, columns] = (
                latter * cosine - former * sine
            ).astype(jnp.bfloat16)
        all_ref[D + KV_WIDTH :, columns] = summed[KV_WIDTH:, :].astype(jnp.bfloat16)
    held[:, : D + 2 * KV_WIDTH] = dot_with(n_ref[...], all_ref[...], 1, 1)
    held[:, D + 2 * KV_WIDTH :] = gwo_ref[...].astype(jnp.float32)
    for side in range(COL_CUT):
        start = (side ^ lax.rem(spot, COL_CUT)) * CHUNK_COLS
        cut[...] = held[:, pl.ds(pl.multiple_of(start, CHUNK_COLS), CHUNK_COLS)]
        for index, part in row_parts(cut, spot, side):
            (keep_ref, send_ref)[index // 4][index % 4] = part


def projection_grads(normed, dqs, kept, got, far, tables, gwo, tie):
    rows = normed.shape[1]
    chunk_shape = (CHUNKS // 2, CHUNK_ROWS, CHUNK_COLS)
    return pl.pallas_call(
        projection_kernel,
        out_shape=(
            jax.ShapeDtypeStruct(chunk_shape, jnp.bfloat16),
            jax.ShapeDtypeStruct(chunk_shape, jnp.bfloat16),
            jax.ShapeDtypeStruct((D + 2 * KV_WIDTH, rows), jnp.bfloat16),
        ),
        in_specs=[vmem()] * 12 + [anywhere()],
        out_specs=(vmem(),) * 3,
        scratch_shapes=[
            pltpu.VMEM((D, FF), jnp.float32),
            pltpu.VMEM((D, CHUNK_COLS), jnp.float32),
        ],
        compiler_params=kernel_params,
        cost_estimate=pl.CostEstimate(
            flops=2 * rows * D * 960, bytes_accessed=8000000, transcendentals=0
        ),
        name="projection_grads",
    )(normed, *dqs, *kept, got, far, *tables[0], *tables[1], gwo, tie)


def both(left_ref, right_ref, where=...):
    total = left_ref[where].astype(jnp.float32) + right_ref[where].astype(jnp.float32)
    return total.astype(jnp.bfloat16)


def plain_call(kernel, outs, operands, ties, name):
    outs = [jax.ShapeDtypeStruct(shape, jnp.bfloat16) for shape in outs]
    ties = ties if isinstance(ties, tuple) else (ties,)
    count = len(operands)

    def run(*refs):
        kernel(*refs[: count + 1], *refs[count + len(ties) :])

    return pl.pallas_call(
        run,
        out_shape=outs,
        in_specs=[vmem()] * count + [anywhere()] * len(ties),
        out_specs=[vmem()] * len(outs),
        compiler_params=kernel_params,
        name=name,
    )(*operands, *ties)


def early_third_kernel(keep_ref, got_ref, tie_ref, *outs):
    quarter = positions()[0]
    for shift, out in enumerate(outs):
        out[...] = both(keep_ref, got_ref, (0, jnp.maximum(lax.rem(quarter + shift, 4) - 1, 0)))


def early_third(keep, got, tie):
    shape = (CHUNK_ROWS, CHUNK_COLS)
    return plain_call(early_third_kernel, [shape] * 4, (keep, got), tie, "early_third")


def sum_kernel(*refs):
    total = refs[0][...].astype(jnp.float32)
    for ref in refs[1:-2]:
        total = total + ref[...].astype(jnp.float32)
    refs[-1][...] = total.astype(jnp.bfloat16)


def tied_sum(operands, tie):
    return plain_call(sum_kernel, [operands[0].shape], operands, tie, "tied_sum")[0]


def late_kernel(keep_ref, got_ref, tie_ref, keep_out, send_out):
    size = keep_out.shape[0]
    keep_out[...] = both(keep_ref, got_ref, slice(0, size))
    send_out[...] = both(keep_ref, got_ref, slice(size, 2 * size))


def late_halves(keep, got, tie):
    shape = (keep.shape[0] // 2, *keep.shape[1:])
    return plain_call(late_kernel, [shape] * 2, (keep, got), tie, "late_halves")


def pair_kernel(first_ref, second_ref, tie_ref, out_ref):
    out_ref[:1] = first_ref[...]
    out_ref[1:] = second_ref[...]


def tied_pair(first, second, tie):
    shape = (3, *first.shape[1:])
    return plain_call(pair_kernel, [shape], (first, second), tie, "tied_pair")[0]


def pick_first_kernel(own_ref, got1_ref, got2_ref, got3_ref, tie_ref, out_ref):
    quarter = positions()[0]
    for place, ref in enumerate((own_ref, got1_ref, got2_ref, got3_ref)):

        @pl.when(quarter == place)
        def _():
            out_ref[...] = ref[...]


def pick_first(pieces, tie):
    return plain_call(pick_first_kernel, [pieces[0].shape], pieces, tie, "pick_first")[0]


def pick_rest_kernel(own_ref, got1_ref, got2_ref, got3_ref, tie_ref, gu_ref, d_ref):
    quarter = positions()[0]

    def run(flat, tiles):
        for place, out in ((1, gu_ref), (2, gu_ref), (3, d_ref)):
            for shift, ref in enumerate((own_ref, got1_ref, got2_ref, got3_ref)):

                @pl.when(lax.rem(quarter - place + 4, 4) == shift)
                def _():
                    flat[...] = ref[...].astype(jnp.float32)

            rows, width = out.shape
            if width > D:
                for tile in range(FF // 128):
                    low = (place - 1) * FF + tile * 128
                    out[:, low : low + 128] = flat[
                        pl.ds(tile, rows, stride=FF // 128), :
                    ].astype(jnp.bfloat16)
            else:
                unflatten(flat, 0, rows, width, tiles)
                for tile, low, breadth in tile_widths(width):
                    out[:, low : low + breadth] = tiles[tile][:, :breadth].astype(jnp.bfloat16)

    pl.run_scoped(
        run,
        pltpu.VMEM(own_ref.shape, jnp.float32),
        pltpu.VMEM((5, FF // CHUNKS, 128), jnp.float32),
    )


def pick_rest(pieces, tie):
    shapes = [(D // CHUNKS, 2 * FF), (FF // CHUNKS, D)]
    return plain_call(pick_rest_kernel, shapes, pieces, tie, "pick_rest")


def cast_kernel(value_ref, tie_ref, out_ref):
    out_ref[...] = value_ref[...].astype(out_ref.dtype)


def tied_cast(value, tie):
    return pl.pallas_call(
        cast_kernel,
        out_shape=jax.ShapeDtypeStruct(value.shape, jnp.bfloat16),
        in_specs=[vmem(), anywhere()],
        out_specs=vmem(),
        compiler_params=kernel_params,
        name="tied_cast",
    )(value, tie)


def inputs_kernel(all_ref, w_ref, x_ref, x1_ref, dh_ref, gain_ref, out_ref, out1_ref, gg_ref):
    gain = gain_ref[:, 0:1]
    total = jnp.zeros((D, 1), jnp.float32)
    for micro in range(2):
        columns = slice(micro * TOK, (micro + 1) * TOK)
        upstream = dot32(w_ref[...], all_ref[:, columns])
        values = (x1_ref if micro else x_ref)[...].astype(jnp.float32)
        part, gain_grad = norm_back(values, norm_scaling(values, 0), gain, upstream, 0)
        total = total + gain_grad
        grad = dh_ref[micro] + part
        store_result(micro, grad, out_ref, out1_ref)
    gg_ref[...] = jnp.broadcast_to(total, gg_ref.shape)


def input_grads(grad_qkv, w_qkv, tokens, tokens_1, grad_state, gain_columns):
    return pl.pallas_call(
        inputs_kernel,
        out_shape=(
            jax.ShapeDtypeStruct((2, D, TOK), jnp.float32),
            jax.ShapeDtypeStruct((D, TOK), jnp.bfloat16),
            jax.ShapeDtypeStruct((D, 128), jnp.float32),
        ),
        in_specs=[vmem()] * 6,
        out_specs=(vmem(),) * 3,
        compiler_params=kernel_params,
        cost_estimate=pl.CostEstimate(
            flops=4 * TOK * D * 960, bytes_accessed=8000000, transcendentals=0
        ),
        name="input_grads",
    )(grad_qkv, w_qkv, tokens, tokens_1, grad_state, gain_columns)


def newton_loop(matrix, scale):
    current = matrix / (jnp.sqrt(jnp.sum(matrix * matrix)) + frobenius_epsilon)

    def iterate(unused, held):
        low = held.astype(jnp.bfloat16)
        square = dot_with(low, low, 1, 1)
        square_low = square.astype(jnp.bfloat16)
        mixer = newton_second * square + newton_third * dot32(square_low, square_low)
        return newton_first * held + dot32(mixer.astype(jnp.bfloat16), low)

    return lax.fori_loop(0, NS_STEPS, iterate, current) * (0.2 * math.sqrt(scale))


def newton_wide(total):
    def run(low, square, square_low, mixer, step):
        height, breadth = total.shape
        block = 256

        def scale_by(factor, keep_low):
            for row in range(0, height, 16):
                part = total[row : row + 16, :] * factor
                total[row : row + 16, :] = part
                if keep_low:
                    low[row : row + 16, :] = part.astype(jnp.bfloat16)

        norm = jnp.zeros((8, breadth), jnp.float32)
        for row in range(0, height, 8):
            part = total[row : row + 8, :]
            norm = norm + part * part
        scale_by(1.0 / (jnp.sqrt(jnp.sum(norm)) + frobenius_epsilon), True)

        def iterate(unused, held):
            square[...] = dot_with(low[...], low[...], 1, 1)
            for row in range(0, height, 16):
                rows = slice(row, row + 16)
                square_low[rows, :] = square[rows, :].astype(jnp.bfloat16)
            step[:, :height] = dot32(square_low[...], square_low[...])
            for row in range(0, height, 16):
                rows = slice(row, row + 16)
                mixed = newton_second * square[rows, :] + newton_third * step[rows, :height]
                mixer[rows, :] = mixed.astype(jnp.bfloat16)
            for column in range(0, breadth, block):
                columns = slice(column, column + block)
                step[:, :block] = dot32(mixer[...], low[:, columns])
                for row in range(0, height, 32):
                    rows = slice(row, row + 32)
                    part = newton_first * total[rows, columns] + step[rows, :block]
                    total[rows, columns] = part
                    low[rows, columns] = part.astype(jnp.bfloat16)
            return held

        lax.fori_loop(0, NS_STEPS, iterate, 0)
        scale_by(0.2 * math.sqrt(breadth), False)

    height, breadth = total.shape
    pl.run_scoped(
        run,
        pltpu.VMEM((height, breadth), jnp.bfloat16),
        pltpu.VMEM((height, height), jnp.float32),
        pltpu.VMEM((height, height), jnp.bfloat16),
        pltpu.VMEM((height, height), jnp.bfloat16),
        pltpu.VMEM((height, height), jnp.float32),
    )


def flatten_rows(tiles, start, rows, width, out):
    pairs, step, whole = rows // 2, width * 2 // 128, width // 128
    spans = range(whole + 1)
    even = [tiles[place, pl.ds(start, pairs, stride=2), :] for place in spans]
    odd = [tiles[place, pl.ds(start + 1, pairs, stride=2), :] for place in spans]
    for place in range(whole):
        out[pl.ds(place, pairs, stride=step), :] = even[place]
    rest = width - whole * 128
    joined = jnp.concatenate([even[whole][:, :rest]] + odd[:whole] + [odd[whole][:, :rest]], axis=1)
    for place in range(whole, step):
        low = (place - whole) * 128
        out[pl.ds(place, pairs, stride=step), :] = joined[:, low : low + 128]


def shard_rows(kind, kinds, start, matrix, tiles, out):
    length = out.shape[0] * 128

    if 0 in kinds:

        @pl.when(kind == 0)
        def _():
            rows = length // FF
            for place in range(FF // 128):
                out[pl.ds(place, rows, stride=FF // 128), :] = matrix[
                    pl.ds(pl.multiple_of(start, 8), rows), place * 128 : (place + 1) * 128
                ]

        @pl.when(kind == 5)
        def _():
            for place, low, breadth in tile_widths(D):
                tiles[place, :, :breadth] = matrix[low : low + breadth, :].T
            flatten_rows(tiles, start, length // D, D, out)

    for place, (base, low, width) in zip((1, 3, 4, 2), MIXED):
        if place not in kinds:
            continue

        @pl.when(kind == place)
        def _():
            for tile, column, breadth in tile_widths(width):
                tiles[tile, :D, :breadth] = matrix[:, low + column : low + column + breadth]
            flatten_rows(tiles, start, length // width, width, out)


def own_kind(length):
    square, narrow = D * D, D * KV_WIDTH
    quarter = lax.axis_index("quarter")
    index = lax.axis_index("rep") * 2 + lax.axis_index("half")
    within = (index * lax.axis_size("ctx") + lax.axis_index("ctx")) * length
    kind = jnp.where(quarter == 3, 5, 0)
    start = jnp.where(quarter == 3, lax.div(within, D), lax.div(within, FF))
    edges = ((0, 1, D), (square, 3, KV_WIDTH), (square + narrow, 4, KV_WIDTH))
    for edge, place, width in (*edges, (square + 2 * narrow, 2, D)):
        inside = (quarter == 0) & (within >= edge)
        kind = jnp.where(inside, place, kind)
        start = jnp.where(inside, lax.div(within - edge, width), start)
    return (kind, start)


def load_matrix(kind, kinds, old_ref, flat, grad, total, tiles):
    flat[...] = old_ref[...].astype(jnp.float32) * momentum_decay
    if 0 in kinds:

        @pl.when(kind == 0)
        def _():
            for place in range(FF // 128):
                columns = slice(place * 128, (place + 1) * 128)
                total[:, columns] = flat[pl.ds(place, D, stride=FF // 128), :] + grad[:, columns]

        @pl.when(kind == 5)
        def _():
            unflatten(flat, 0, FF, D, tiles)
            for place, low, breadth in tile_widths(D):
                rows = slice(low, low + breadth)
                total[rows, :] = tiles[place].T[:breadth] + grad[rows, :]

    for place, (base, low, width) in zip((1, 3, 4, 2), MIXED):
        if place not in kinds:
            continue

        @pl.when(kind == place)
        def _():
            unflatten(flat, base, D, width, tiles)
            part = jnp.concatenate(
                [tiles[tile][:D, :breadth] for tile, _, breadth in tile_widths(width)], axis=1
            )
            columns = slice(low, low + width)
            total[:, columns] = part + grad[:, columns]


def update_matrix(kind, kinds, total):
    if 0 in kinds:

        @pl.when((kind == 0) | (kind == 5))
        def _():
            newton_wide(total)

    for place, (base, low, width) in zip((1, 3, 4, 2), MIXED):
        if place not in kinds:
            continue

        @pl.when(kind == place)
        def _():
            columns = slice(low, low + width)
            if width == D:
                total[:, columns] = newton_loop(total[:, columns], D)
            else:
                total[:, columns] = newton_loop(total[:, columns].T, D).T


def newton_kernel(early, local, length, *refs):
    count = 3 if local else 2
    grad, total, tiles = refs[-3:]
    outs = refs[-3 - count : -3]
    pieces, (old_ref, *rest) = refs[:2], refs[2:-3]
    kind, start = own_kind(length)
    mine = (lax.axis_index("quarter") != 0) == early
    spot = chunk_spot()

    @pl.when(mine)
    def _():
        for index in range(CHUNKS):
            chunk = spot ^ index
            row = pl.multiple_of(lax.div(chunk, COL_CUT) * CHUNK_ROWS, CHUNK_ROWS)
            column = pl.multiple_of(lax.rem(chunk, COL_CUT) * CHUNK_COLS, CHUNK_COLS)
            rows, columns = pl.ds(row, CHUNK_ROWS), pl.ds(column, CHUNK_COLS)
            part = pieces[index // 4][index % 4]
            grad[rows, columns] = part.astype(jnp.float32)
        kinds = (0, 5) if early else (1, 2, 3, 4)
        pl.run_scoped(
            lambda flat: load_matrix(kind, kinds, old_ref, flat, grad, total, tiles),
            pltpu.VMEM((D * FF // 128, 128), jnp.float32),
        )
        update_matrix(kind, kinds, total)
        if local:
            weights_ref, momentum_ref = rest[:2]
            grad_ref, new_momentum_ref, new_weights_ref = outs
            shard_rows(kind, kinds, start, grad, tiles, grad_ref)
            shard_rows(kind, kinds, start, total, tiles, new_weights_ref)
            new_momentum_ref[...] = momentum_decay * momentum_ref[...] + grad_ref[...]
            new_weights_ref[...] = (
                weights_ref[...] * (1.0 - matrix_rate * weight_decay)
                - matrix_rate * new_weights_ref[...]
            )
        else:
            outs[0][...] = grad[...]
            outs[1][...] = total[...]

    if not early:

        @pl.when(jnp.logical_not(mine))
        def _():
            for out, before in zip(outs, rest[2:] if local else rest):
                out[...] = before[...]


def newton(early, length, pieces, old, shards, before, ties):
    local = len(shards) > 0
    if local:
        outs = (jax.ShapeDtypeStruct(shards[0].shape, jnp.float32),) * 3
    else:
        outs = (jax.ShapeDtypeStruct((D, FF), jnp.float32),) * 2
    operands = (*pieces, old, *shards, *before)

    def kernel(*refs):
        newton_kernel(early, local, length, *refs[: len(operands)], *refs[len(operands) + len(ties) :])

    return pl.pallas_call(
        kernel,
        out_shape=outs,
        in_specs=[vmem()] * len(operands) + [anywhere()] * len(ties),
        out_specs=(vmem(),) * len(outs),
        scratch_shapes=[
            pltpu.VMEM((D, FF), jnp.float32),
            pltpu.VMEM((D, FF), jnp.float32),
            pltpu.VMEM((5, FF, 128), jnp.float32),
        ],
        compiler_params=kernel_params,
        cost_estimate=pl.CostEstimate(
            flops=12000000000, bytes_accessed=9000000, transcendentals=0
        ),
        name="newton_early" if early else "newton_late",
    )(*operands, *ties)


def own_rows(kind, row, shard_length, gradient, update):
    def block_case(low, width):
        def run(gradient, update):
            start = (row, low)
            size = (shard_length // width, width)
            return tuple(
                lax.dynamic_slice(whole, start, size).reshape(-1) for whole in (gradient, update)
            )

        return run

    def tall_case(gradient, update):
        start = (0, row)
        size = (D, shard_length // D)
        return tuple(
            lax.dynamic_slice(whole, start, size).T.reshape(-1) for whole in (gradient, update)
        )

    cases = [
        block_case(0, FF),
        block_case(0, D),
        block_case(FF - D, D),
        block_case(D, KV_WIDTH),
        block_case(D + KV_WIDTH, KV_WIDTH),
        tall_case,
    ]
    return lax.switch(kind, cases, gradient, update)


CORE_SWAP = [(0, 1), (1, 0), (2, 3), (3, 2)]
CHIP_SWAP = [(0, 2), (2, 0), (1, 3), (3, 1)]
SIDE_SWAP = [(0, 1), (1, 0)]
END_SWAP = [(0, 3), (3, 0), (1, 2), (2, 1)]


def plane_pairs(bit):
    return [(place, place ^ (2, 4, 1)[bit]) for place in range(8)]


def plane_swap(value, bit):
    axis, swap = (("ctx", CHIP_SWAP), ("half", SIDE_SWAP), ("ctx", CORE_SWAP))[bit]
    return lax.ppermute(value, axis, swap)


def first_plane_swap(value, bit):
    return lax.ppermute(value, ("quarter", "half", "ctx"), plane_pairs(bit))


def low_sum(left, right):
    return (left.astype(jnp.float32) + right.astype(jnp.float32)).astype(jnp.bfloat16)


def low_total(first, others):
    total = first.astype(jnp.float32)
    for part in others:
        total = total + part.astype(jnp.float32)
    return total.astype(jnp.bfloat16)


def plane_gather(piece, swap):
    pieces = piece[None]
    for bit in range(2):
        pieces = jnp.concatenate([pieces, swap(pieces, bit)], axis=0)
    return (pieces, swap(pieces, 2))


def depth_shift(value, shift, targets):
    pairs = [(place, (place + shift) % 4) for place in range(4)]
    return lax.ppermute(value, "quarter", [pair for pair in pairs if pair[1] in targets])


def plane_total(value):
    parts = [
        lax.ppermute(value, ("half", "ctx"), [(place, place ^ turn) for place in range(8)])
        for turn in range(1, 8)
    ]
    return value + sum(parts)


def depth_total(value):
    return value + sum(depth_shift(value, shift, range(4)) for shift in range(1, 4))


def gather_weights(low, tie):
    if lax.axis_size("rep") > 1:
        full = lax.all_gather(low, EVERY, axis=0, tiled=True).reshape(4, D * FF)
        ctx = lax.axis_index("ctx")
        spot = lax.rem(ctx, 2) * 4 + lax.axis_index("half") * 2 + ctx // 2
        chunk = jnp.arange(CHUNKS, dtype=jnp.int32) ^ spot
        order = 4 * (chunk // 2 % 2) + 2 * (chunk % 2) + chunk // 4
        mixed = full[0].reshape(CHUNKS, -1, 128)[order]
        return (mixed[:4], mixed[4:]), [
            jnp.concatenate([full[1].reshape(D, FF), full[2].reshape(D, FF)], axis=1),
            full[3].reshape(FF, D),
        ]
    first = [lax.ppermute(low, "quarter", [(0, shift)]) for shift in range(1, 4)]
    mixed = pick_first((low, *first), tie)
    others = [
        lax.ppermute(low, "quarter", [(place, (place + shift) % 4) for place in range(1, 4)])
        for shift in range(1, 4)
    ]
    rest = [
        lax.all_gather(piece, PLANE, axis=0, tiled=True)
        for piece in pick_rest((low, *others), mixed)
    ]
    return plane_gather(mixed, plane_swap), rest


def per_device(tokens, lengths, weights, momentum, norm_gains, gain_first, gain_second, cotangent):
    ctx = lax.axis_index("ctx")
    chip = ctx // 2
    reps = lax.axis_size("rep")
    shard_length = weights.shape[0]
    flat_shape = (shard_length // 128, 128)
    lengths = lengths[:, 0]
    tokens = jnp.swapaxes(tokens, 1, 2)
    cotangent = jnp.swapaxes(cotangent, 1, 2)
    gain_columns = norm_gains.T

    tokens_1 = lax.ppermute(tokens[1], "ctx", END_SWAP)
    mixed_weights, (w_gate_up, w_down) = gather_weights(
        weights.reshape(flat_shape).astype(jnp.bfloat16), tokens_1
    )
    near = chip == 0

    def slots(first, second):
        return jnp.where(near, first, second), jnp.where(near, second, first)

    x0, x1 = slots(tokens[0], tokens_1)
    begin_rows, tables = [], []
    for micro, own_lengths in enumerate(slots(lengths[0], lengths[1])):
        own_places = own_block(micro) * TOK + jnp.arange(TOK, dtype=jnp.int32)
        offsets, begins = layout(own_lengths, own_places)
        begin_rows.append(begins.reshape(1, TOK))
        tables.append(rope_tables(offsets))

    q0, q1, keyvals, w_qkv, w_out, normed = project(
        *mixed_weights, x0, x1, gain_columns, tables
    )
    queries = (q0, q1)
    far = lax.ppermute(keyvals[0], "ctx", CHIP_SWAP)
    keyvals = (
        keyvals,
        lax.ppermute(keyvals, "ctx", CORE_SWAP),
        far,
        lax.ppermute(far, "ctx", CORE_SWAP),
    )
    mixed, log_totals = [], []
    for micro in range(2):
        mixed_one, log_total = attend_forward(
            micro, lengths, queries[micro], keyvals, begin_rows[micro], norm_gains
        )
        mixed.append(mixed_one)
        log_totals.append(log_total)
    cotangent_1 = lax.ppermute(cotangent[1], "ctx", END_SWAP)
    old = lax.all_gather(
        tied_cast(momentum.reshape(flat_shape), mixed[0]),
        ("rep", "half", "ctx"),
        axis=0,
        tiled=True,
    )
    outs = mlp(
        x0,
        x1,
        *slots(cotangent[0], cotangent_1),
        [part.reshape(D, TOK) for part in mixed],
        w_out,
        w_gate_up,
        w_down,
        norm_gains[1:2],
    )
    result, result_1, grad_state, grad_mixed_0, grad_mixed_1 = outs[:5]
    keep, send, grad_w_out, gain_two_grad = outs[5:]
    returned = lax.ppermute(result_1, "ctx", END_SWAP)

    def back_pass(micro, grad_mixed, tie):
        return attend_back(
            micro,
            lengths,
            queries[micro],
            keyvals,
            begin_rows[micro],
            mixed[micro],
            log_totals[micro],
            grad_mixed.reshape(heads_shape),
            *tables[micro],
            tie,
        )

    got = plane_swap(send, 2)
    dq0, kept0, sent0 = back_pass(0, grad_mixed_0, old)
    keep, send = late_halves(keep, got, (dq0, returned))
    got = plane_swap(send, 1)
    dq1, kept1, sent1 = back_pass(1, grad_mixed_1, keep)
    keep, send = late_halves(keep, got, dq1)
    got = plane_swap(send, 0)
    traded = lax.ppermute(tied_pair(sent0, sent1, keep), "ctx", CORE_SWAP)
    crossing = low_sum(kept1[1], traded[2])
    crossed = lax.ppermute(crossing, "ctx", CHIP_SWAP)
    early, *turns = early_third(keep, got, crossing)
    early_parts = [
        depth_shift(turn, shift, range(1, 4)) for shift, turn in enumerate(turns, start=1)
    ]
    late_keep, late_send, grad_qkv = projection_grads(
        normed,
        (dq0.reshape(D, TOK), dq1.reshape(D, TOK)),
        (kept0, kept1),
        traded,
        crossed,
        tables,
        grad_w_out,
        early,
    )
    late_got = plane_swap(late_send, 2)
    early = low_total(early, early_parts)
    if reps > 1:
        early = lax.psum(early, "rep")
    late_keep, late_send = late_halves(late_keep, late_got, early)
    late_got = plane_swap(late_send, 1)
    grad_inputs, grad_inputs_1, gain_one_grad = input_grads(
        grad_qkv, w_qkv, x0, x1, grad_state, gain_columns
    )
    early_near, early_next = plane_gather(early, plane_swap)
    gain_grad = plane_total(
        jnp.concatenate([gain_one_grad[:, 0].reshape(1, D), gain_two_grad], axis=0)
    )
    late_keep, late_send = late_halves(late_keep, late_got, (gain_grad, early_near))
    late = low_sum(late_keep[0], plane_swap(late_send, 0)[0])
    late_parts = [depth_shift(late, shift, (0,)) for shift in range(1, 4)]
    gain_grad = depth_total(gain_grad)
    grad_inputs_1 = lax.ppermute(grad_inputs_1, "ctx", END_SWAP)

    shards = ()
    if flat_shape[0] % 8 == 0:
        shards = (weights.reshape(flat_shape), momentum.reshape(flat_shape))
    before = newton(
        True, shard_length, (early_near, early_next), old, shards, (), (late, gain_grad)
    )
    late = tied_sum((late, *late_parts), before[0])
    if reps > 1:
        late = lax.psum(late, "rep")
        gain_grad = lax.psum(gain_grad, "rep")
    late_pieces = plane_gather(late, first_plane_swap)
    outs = newton(False, shard_length, late_pieces, old, shards, before, (grad_inputs_1,))
    if len(shards) > 0:
        grad_shard, new_momentum, new_weights = [out.reshape(weights.shape) for out in outs]
    else:
        kind, start = own_kind(shard_length)
        grad_shard, update_shard = own_rows(kind, start, shard_length, *outs)
        new_momentum = momentum_decay * momentum + grad_shard
        new_weights = weights * (1.0 - matrix_rate * weight_decay) - matrix_rate * update_shard

    def placed(whole, part):
        whole = lax.dynamic_update_index_in_dim(whole, part.astype(jnp.float32), 1, 0)
        return jnp.swapaxes(whole, 1, 2)

    first_new = first_decay * gain_first + (1.0 - first_decay) * gain_grad
    second_new = second_decay * gain_second + (1.0 - second_decay) * gain_grad * gain_grad
    debiased_first_moment = first_new / (1.0 - first_decay**ADAM_STEP)
    corrected_second = second_new / (1.0 - second_decay**ADAM_STEP)
    new_gains = norm_gains * (
        1.0 - gain_rate * weight_decay
    ) - gain_rate * debiased_first_moment / (jnp.sqrt(corrected_second) + adam_epsilon)
    return (
        placed(result, returned),
        placed(grad_inputs, grad_inputs_1),
        grad_shard,
        new_momentum,
        new_weights,
        first_new,
        second_new,
        new_gains,
    )


def solution(mesh):
    devices = mesh.devices
    count = devices.size
    context = mesh.shape["ctx"]
    split = Mesh(
        devices.reshape(4, count // (8 * context), 2, context), ("quarter", "rep", "half", "ctx")
    )
    rows = P(None, EVERY, None)
    flat = P(EVERY)
    placed = (rows, P(None, ("quarter", "rep", "half"), None), flat, flat, P(), P(), P(), rows)
    return jax.shard_map(
        per_device,
        mesh=split,
        in_specs=placed,
        out_specs=(rows, rows, flat, flat, flat, P(), P(), P()),
        check_vma=False,
    )
```

```python
from functools import partial
import math

import jax
import jax.numpy as jnp
from jax import lax
from jax.experimental import pallas as pl
from jax.experimental.pallas import tpu as pltpu
from jax.sharding import Mesh, PartitionSpec as P

HEADS = 9
KV_HEADS = 3
HEAD_DIM = 64
FF = 1536
NS_STEPS = 5
ADAM_STEP = 10
D = 576
KV_WIDTH = 192
GROUPS = HEADS // KV_HEADS
TOK = 512
TILE = 256
COLS = GROUPS * TILE
ROW_CUT = 4
COL_CUT = 2
CHUNKS = ROW_CUT * COL_CUT
CHUNK_ROWS = D // ROW_CUT
CHUNK_COLS = FF // COL_CUT
PLANE = ("half", "ctx")
EVERY = ("quarter", "rep", "half", "ctx")


norm_epsilon = 1e-05
rope_base = 100000.0
masked_score = -1e30
newton_first = 3.4445
newton_second = -4.775
newton_third = 2.0315
momentum_decay = 0.95
matrix_rate = 0.2
weight_decay = 0.1
gain_rate = 0.2
first_decay = 0.9
second_decay = 0.95
adam_epsilon = 1e-08
frobenius_epsilon = 1e-07


def layout(lengths_row, places):
    finish = jnp.cumsum(lengths_row)
    firsts = finish - lengths_row
    begins = jnp.max(jnp.where(places[:, None] >= firsts[None, :], firsts[None, :], 0), axis=1)
    return (places - begins, begins)


def rope_tables(offsets):
    half_width = HEAD_DIM // 2
    inverse = jnp.exp(
        jnp.arange(half_width, dtype=jnp.float32) * (-2.0 * math.log(rope_base) / HEAD_DIM)
    )
    angles = inverse[:, None] * offsets.astype(jnp.float32)[None, :]
    return (jnp.cos(angles), jnp.sin(angles))


def dot32(left, right):
    return jnp.dot(left, right, preferred_element_type=jnp.float32)


def masked(scores, key_block, begins, places):
    keys = key_block * TILE + lax.broadcasted_iota(jnp.int32, scores.shape, 0)
    return jnp.where((keys >= begins) & (keys <= places), scores, masked_score)


def tile_row(row, tile):
    part = row[:, tile * TILE : (tile + 1) * TILE]
    return jnp.concatenate([part] * GROUPS, axis=1)


def tile_heads(ref, group, tile):
    return jnp.concatenate(
        [ref[group, head, :, tile * TILE : (tile + 1) * TILE] for head in range(GROUPS)], axis=1
    )


def positions():
    ctx = lax.axis_index("ctx")
    return (lax.axis_index("quarter"), lax.axis_index("half"), lax.div(ctx, 2), lax.rem(ctx, 2))


def chunk_spot():
    _, half, chip, core = positions()
    return core * 4 + half * 2 + chip


def first_key(lengths_ref, slot, row):
    micro = slot ^ positions()[2]
    begin = jnp.int32(0)
    first = jnp.int32(0)
    for place in range(3):
        first = first + lengths_ref[micro, place]
        begin = jnp.where(row >= first, first, begin)
    return begin


def key_loop(lengths_ref, micro, own, tile, step, carry):
    last = own * (TOK // TILE) + tile
    first = lax.div(first_key(lengths_ref, micro, last * TILE), TILE)
    full = lax.div(first_key(lengths_ref, micro, last * TILE + TILE - 1) + TILE - 1, TILE)
    full = jnp.minimum(full, last)
    pairs = lax.div(last - full, 2)
    carry = lax.fori_loop(first, full, partial(step, True, 1), carry)
    carry = lax.fori_loop(
        0, pairs, lambda pair, held: step(False, 2, full + 2 * pair, held), carry
    )
    carry = lax.fori_loop(full + 2 * pairs, last, partial(step, False, 1), carry)
    return step(True, 1, last, carry)


def own_block(slot):
    ctx = lax.axis_index("ctx")
    return jnp.maximum(ctx, 3 - ctx) if slot else jnp.minimum(ctx, 3 - ctx)


def key_slots(own, micro, kv_ref, other_ref, far_ref, far_other_ref):
    refs = (kv_ref.at[micro], other_ref.at[micro], far_ref, far_other_ref)[: 2 + 2 * micro]
    return [(own ^ place, ref) for place, ref in enumerate(refs)]


def block_rows(block):
    return pl.ds(pl.multiple_of(block * TOK, TOK), TOK)


def forward_kernel(
    micro, lengths_ref, q_ref, kv_ref, other_ref, far_ref, far_other_ref, begin_ref, tie_ref,
    o_ref, lse_ref, k_nat, v_ext, s_ref, p_ref,
):
    own = own_block(micro)
    for block, source in key_slots(own, micro, kv_ref, other_ref, far_ref, far_other_ref):

        @pl.when(block <= own)
        def _():
            rows = block_rows(block)
            for group in range(KV_HEADS):
                low = HEAD_DIM * group
                k_nat[group, rows, :] = source[low : low + HEAD_DIM, :].T
                low = low + KV_WIDTH
                v_ext[group, :HEAD_DIM, rows] = source[low : low + HEAD_DIM, :]
                v_ext[group, HEAD_DIM:, rows] = jnp.ones((16, TOK), jnp.bfloat16)

    def one_group(group, unused):
        for tile in range(TOK // TILE):
            queries = tile_heads(q_ref, group, tile)
            begins = tile_row(begin_ref[...], tile)
            column = lax.broadcasted_iota(jnp.int32, (1, COLS), 1)
            places = own * TOK + tile * TILE + lax.rem(column, TILE)

            def step(is_masked, width, key_block, carry):
                top, total = carry
                keys = pl.ds(pl.multiple_of(key_block * TILE, TILE), width * TILE)
                count = width * TILE
                scores = dot32(k_nat[group, keys, :], queries)
                s_ref[:count] = masked(scores, key_block, begins, places) if is_masked else scores
                highest = s_ref[:16]
                for low in range(16, count, 16):
                    highest = jnp.maximum(highest, s_ref[low : low + 16])
                new_top = jnp.maximum(top, jnp.max(highest, axis=0, keepdims=True))
                for low in range(0, count, 16):
                    rows = slice(low, low + 16)
                    p_ref[rows] = jnp.exp(s_ref[rows] - new_top).astype(jnp.bfloat16)
                total = total * jnp.exp(top - new_top) + dot32(
                    v_ext[group, :, keys], p_ref[:count]
                )
                return (new_top, total)

            carry = (
                jnp.full((1, COLS), masked_score, jnp.float32),
                jnp.zeros((HEAD_DIM + 16, COLS), jnp.float32),
            )
            top, total = key_loop(lengths_ref, micro, own, tile, step, carry)
            weight = total[HEAD_DIM : HEAD_DIM + 1, :]
            mixed = (total[:HEAD_DIM, :] / weight).astype(jnp.bfloat16)
            log_total = top + jnp.log(weight)
            for head in range(GROUPS):
                o_ref[group, head, :, tile * TILE : (tile + 1) * TILE] = mixed[
                    :, head * TILE : (head + 1) * TILE
                ]
                lse_ref[group, head, :, tile * TILE : (tile + 1) * TILE] = log_total[
                    :, head * TILE : (head + 1) * TILE
                ]
        return unused

    lax.fori_loop(0, KV_HEADS, one_group, 0)


def backward_kernel(
    micro, lengths_ref, q_ref, kv_ref, other_ref, far_ref, far_other_ref, begin_ref, o_ref, lse_ref,
    do_ref, cos_ref, sin_ref, tie_ref,
    dq_ref, keep_ref, send_ref, k_nat, v_nat, k_tall, dk_ref, dv_ref, s_ref, g_ref, p_ref, ds_ref,
):
    own = own_block(micro)
    slots = key_slots(own, micro, kv_ref, other_ref, far_ref, far_other_ref)
    for block, source in slots:

        @pl.when(block <= own)
        def _():
            rows = block_rows(block)
            for group in range(KV_HEADS):
                low = HEAD_DIM * group
                k_nat[group, rows, :] = source[low : low + HEAD_DIM, :].T
                k_tall[group, :, rows] = source[low : low + HEAD_DIM, :]
                low = low + KV_WIDTH
                v_nat[group, rows, :] = source[low : low + HEAD_DIM, :].T
                dk_ref[group, rows, :] = jnp.zeros((TOK, HEAD_DIM), jnp.float32)
                dv_ref[group, rows, :] = jnp.zeros((TOK, HEAD_DIM), jnp.float32)

    def one_group(group, unused):
        for tile in range(TOK // TILE):
            queries = tile_heads(q_ref, group, tile)
            upstream = tile_heads(do_ref, group, tile)
            mixed = tile_heads(o_ref, group, tile)
            log_total = tile_heads(lse_ref, group, tile)
            delta = jnp.sum(
                upstream.astype(jnp.float32) * mixed.astype(jnp.float32), axis=0, keepdims=True
            )
            queries_nat = queries.T
            upstream_nat = upstream.T
            begins = tile_row(begin_ref[...], tile)
            column = lax.broadcasted_iota(jnp.int32, (1, COLS), 1)
            places = own * TOK + tile * TILE + lax.rem(column, TILE)

            def step(is_masked, width, key_block, dq):
                rows = pl.ds(pl.multiple_of(key_block * TILE, TILE), width * TILE)
                count = width * TILE
                scores = dot32(k_nat[group, rows, :], queries)
                s_ref[:count] = masked(scores, key_block, begins, places) if is_masked else scores
                g_ref[:count] = dot32(v_nat[group, rows, :], upstream)
                for low in range(0, count, 16):
                    part = slice(low, low + 16)
                    probs = jnp.exp(s_ref[part] - log_total)
                    p_ref[part] = probs.astype(jnp.bfloat16)
                    ds_ref[part] = (probs * (g_ref[part] - delta)).astype(jnp.bfloat16)
                dv_ref[group, rows, :] += dot32(p_ref[:count], upstream_nat)
                dk_ref[group, rows, :] += dot32(ds_ref[:count], queries_nat)
                return dq + dot32(k_tall[group, :, rows], ds_ref[:count])

            dq = jnp.zeros((HEAD_DIM, COLS), jnp.float32)
            dq = key_loop(lengths_ref, micro, own, tile, step, dq) * 0.125
            half_width = HEAD_DIM // 2
            cosine = tile_row(cos_ref[...], tile)
            sine = tile_row(sin_ref[...], tile)
            former, latter = dq[:half_width], dq[half_width:]
            turned = jnp.concatenate(
                [former * cosine + latter * sine, latter * cosine - former * sine], axis=0
            ).astype(jnp.bfloat16)
            for head in range(GROUPS):
                dq_ref[group, head, :, tile * TILE : (tile + 1) * TILE] = turned[
                    :, head * TILE : (head + 1) * TILE
                ]
        return unused

    lax.fori_loop(0, KV_HEADS, one_group, 0)
    for place, (block, _) in enumerate(slots):
        out_ref = (keep_ref, send_ref)[place % 2]

        @pl.when(block <= own)
        def _():
            rows = block_rows(block)
            for group in range(KV_HEADS):
                low = HEAD_DIM * group
                out_ref[place // 2, low : low + HEAD_DIM, :] = dk_ref[group, rows, :].T.astype(
                    jnp.bfloat16
                )
                low = low + KV_WIDTH
                out_ref[place // 2, low : low + HEAD_DIM, :] = dv_ref[group, rows, :].T.astype(
                    jnp.bfloat16
                )

        @pl.when(block > own)
        def _():
            out_ref[place // 2] = jnp.zeros((2 * KV_WIDTH, TOK), jnp.bfloat16)


def vmem():
    return pl.BlockSpec(memory_space=pltpu.VMEM)


def smem():
    return pl.BlockSpec(memory_space=pltpu.SMEM)


def anywhere():
    return pl.BlockSpec(memory_space=pl.ANY)


kernel_params = pltpu.CompilerParams(vmem_limit_bytes=56 * 1024 * 1024)
heads_shape = (KV_HEADS, GROUPS, HEAD_DIM, TOK)


def attend_forward(micro, lengths, queries, keyvals, begins, tie):
    return pl.pallas_call(
        partial(forward_kernel, micro),
        out_shape=(
            jax.ShapeDtypeStruct(heads_shape, jnp.bfloat16),
            jax.ShapeDtypeStruct((KV_HEADS, GROUPS, 1, TOK), jnp.float32),
        ),
        in_specs=[smem()] + [vmem()] * 6 + [anywhere()],
        out_specs=(vmem(), vmem()),
        scratch_shapes=[
            pltpu.VMEM((KV_HEADS, 4 * TOK, HEAD_DIM), jnp.bfloat16),
            pltpu.VMEM((KV_HEADS, HEAD_DIM + 16, 4 * TOK), jnp.bfloat16),
            pltpu.VMEM((2 * TILE, COLS), jnp.float32),
            pltpu.VMEM((2 * TILE, COLS), jnp.bfloat16),
        ],
        compiler_params=kernel_params,
        cost_estimate=pl.CostEstimate(
            flops=4 * 9 * 64 * TOK * 2048, bytes_accessed=4000000, transcendentals=9 * TOK * 2048
        ),
        name="attend_forward",
    )(lengths, queries, *keyvals, begins, tie)


def attend_back(
    micro, lengths, queries, keyvals, begins, mixed, log_total, grad_mixed, cosine, sine, tie
):
    half_shape = (1 + micro, 2 * KV_WIDTH, TOK)
    return pl.pallas_call(
        partial(backward_kernel, micro),
        out_shape=(
            jax.ShapeDtypeStruct(heads_shape, jnp.bfloat16),
            jax.ShapeDtypeStruct(half_shape, jnp.bfloat16),
            jax.ShapeDtypeStruct(half_shape, jnp.bfloat16),
        ),
        in_specs=[smem()] + [vmem()] * 11 + [anywhere()],
        out_specs=(vmem(),) * 3,
        scratch_shapes=[
            pltpu.VMEM((KV_HEADS, 4 * TOK, HEAD_DIM), jnp.bfloat16),
            pltpu.VMEM((KV_HEADS, 4 * TOK, HEAD_DIM), jnp.bfloat16),
            pltpu.VMEM((KV_HEADS, HEAD_DIM, 4 * TOK), jnp.bfloat16),
            pltpu.VMEM((KV_HEADS, 4 * TOK, HEAD_DIM), jnp.float32),
            pltpu.VMEM((KV_HEADS, 4 * TOK, HEAD_DIM), jnp.float32),
            pltpu.VMEM((2 * TILE, COLS), jnp.float32),
            pltpu.VMEM((2 * TILE, COLS), jnp.float32),
            pltpu.VMEM((2 * TILE, COLS), jnp.bfloat16),
            pltpu.VMEM((2 * TILE, COLS), jnp.bfloat16),
        ],
        compiler_params=kernel_params,
        cost_estimate=pl.CostEstimate(
            flops=10 * 9 * 64 * TOK * 2048, bytes_accessed=8000000, transcendentals=9 * TOK * 2048
        ),
        name="attend_back",
    )(lengths, queries, *keyvals, begins, mixed, log_total, grad_mixed, cosine, sine, tie)


def dot_with(left, right, left_side, right_side):
    return lax.dot_general(
        left, right, (((left_side,), (right_side,)), ((), ())), preferred_element_type=jnp.float32
    )


def norm_back(values, scaling, gain, upstream, axis):
    weighted = upstream * gain
    inner = jnp.mean(weighted * values, axis=axis, keepdims=True)
    gain_grad = jnp.sum(upstream * values * scaling, axis=1 - axis, keepdims=True)
    return (scaling * weighted - values * (scaling * scaling * scaling) * inner, gain_grad)


def norm_scaling(values, axis):
    return lax.rsqrt(jnp.mean(values * values, axis=axis, keepdims=True) + norm_epsilon)


def row_parts(held, spot, side):
    for turn in range(ROW_CUT):
        start = (turn ^ lax.div(spot, COL_CUT)) * CHUNK_ROWS
        part = held[pl.ds(pl.multiple_of(start, CHUNK_ROWS), CHUNK_ROWS), :]
        yield (turn * COL_CUT + side, part.astype(jnp.bfloat16))


def store_result(slot, result, out_ref, moved_ref):
    chip = positions()[2]

    @pl.when(chip == slot)
    def _():
        out_ref[0] = result

    @pl.when(chip != slot)
    def _():
        moved_ref[...] = result.astype(jnp.bfloat16)


def mlp_kernel(
    x_ref, x1_ref, c_ref, c1_ref, o0_ref, o1_ref, wo_ref, w_ref, wd_ref, gain_ref,
    out_ref, out1_ref, dh_ref, do0_ref, do1_ref, keep_ref, send_ref, gwo_ref, gg_ref,
    hid, dgate, dup, n2_tall, dh_low, held, gate_ref, up_ref, da_ref, c_slots,
):
    gain = gain_ref[...]
    gg_ref[...] = jnp.zeros((1, D), jnp.float32)
    block = 256
    spot = chunk_spot()
    for micro, (o_ref, do_ref) in enumerate(((o0_ref, do0_ref), (o1_ref, do1_ref))):
        rows = slice(micro * TOK, (micro + 1) * TOK)
        x_tall = (x1_ref if micro else x_ref)[...]
        c_tall_ref = c_slots.at[micro]
        chip = positions()[2]

        @pl.when(chip == micro)
        def _():
            c_tall_ref[...] = c_ref[0]

        @pl.when(chip != micro)
        def _():
            c_tall_ref[...] = c1_ref[...]

        c_tall = c_tall_ref[...]
        hidden_state = (x_tall.astype(jnp.float32) + dot_with(wo_ref[...], o_ref[...], 0, 0)).T
        scaling = norm_scaling(hidden_state, 1)
        normed = (hidden_state * scaling * gain).astype(jnp.bfloat16)
        n2_tall[:, rows] = normed.T
        back = c_tall.T
        for column in range(0, FF, block):
            columns = slice(column, column + block)
            gate_ref[...] = dot32(normed, w_ref[:, columns])
            up_ref[...] = dot32(normed, w_ref[:, FF + column : FF + column + block])
            da_ref[...] = dot_with(back, wd_ref[columns, :], 1, 1)
            for low in range(0, TOK, 32):
                part, spot_rows = slice(low, low + 32), slice(micro * TOK + low, micro * TOK + low + 32)
                gate, upward, grad_hidden = gate_ref[part], up_ref[part], da_ref[part]
                sigmoid_gate = jax.nn.sigmoid(gate)
                activated = gate * sigmoid_gate
                hid[spot_rows, columns] = (activated * upward).astype(jnp.bfloat16)
                dup[spot_rows, columns] = (grad_hidden * activated).astype(jnp.bfloat16)
                slope = sigmoid_gate * (1.0 + gate * (1.0 - sigmoid_gate))
                dgate[spot_rows, columns] = (grad_hidden * upward * slope).astype(jnp.bfloat16)
        result = (hidden_state + dot32(hid[rows, :], wd_ref[...])).T
        store_result(micro, result, out_ref, out1_ref)
        upstream = dot_with(dgate[rows, :], w_ref[:, :FF], 1, 1) + dot_with(
            dup[rows, :], w_ref[:, FF:], 1, 1
        )
        part, gain_grad = norm_back(hidden_state, scaling, gain, upstream, 1)
        gg_ref[...] += gain_grad
        grad_state = back.astype(jnp.float32) + part
        dh_low[rows, :] = grad_state.astype(jnp.bfloat16)
        grad_tall = grad_state.T
        dh_ref[micro] = grad_tall
        do_ref[...] = dot32(wo_ref[...], grad_tall.astype(jnp.bfloat16)).astype(jnp.bfloat16)
    c_parts = (c_slots.at[0], c_slots.at[1])
    for place, right in enumerate((dgate, dup, hid)):
        for side in range(COL_CUT):
            start = (side ^ lax.rem(spot, COL_CUT)) * CHUNK_COLS
            for column in range(0, CHUNK_COLS, block):
                columns = pl.ds(pl.multiple_of(start + column, block), block)
                if place < 2:
                    held[...] = dot32(n2_tall[...], right[:, columns])
                else:
                    held[...] = dot32(c_parts[0][...], right[:TOK, columns]) + dot32(
                        c_parts[1][...], right[TOK:, columns]
                    )
                for index, part in row_parts(held, spot, side):
                    out = (keep_ref, send_ref)[index // 4]
                    out[index % 4, place, :, column : column + block] = part
    gwo_ref[...] = (
        dot32(o0_ref[...], dh_low[:TOK, :]) + dot32(o1_ref[...], dh_low[TOK:, :])
    ).astype(jnp.bfloat16)


def mlp(tokens, tokens_1, cotangent, cotangent_1, mixed, w_out, w_gate_up, w_down, gain):
    rows = 2 * TOK
    low = jnp.bfloat16
    chunk_shape = (CHUNKS // 2, 3, CHUNK_ROWS, CHUNK_COLS)
    return pl.pallas_call(
        mlp_kernel,
        out_shape=(
            jax.ShapeDtypeStruct((2, D, TOK), jnp.float32),
            jax.ShapeDtypeStruct((D, TOK), low),
            jax.ShapeDtypeStruct((2, D, TOK), jnp.float32),
            jax.ShapeDtypeStruct((D, TOK), low),
            jax.ShapeDtypeStruct((D, TOK), low),
            jax.ShapeDtypeStruct(chunk_shape, low),
            jax.ShapeDtypeStruct(chunk_shape, low),
            jax.ShapeDtypeStruct((D, D), low),
            jax.ShapeDtypeStruct((1, D), jnp.float32),
        ),
        in_specs=[vmem()] * 10,
        out_specs=(vmem(),) * 9,
        scratch_shapes=[
            pltpu.VMEM((rows, FF), low),
            pltpu.VMEM((rows, FF), low),
            pltpu.VMEM((rows, FF), low),
            pltpu.VMEM((D, rows), low),
            pltpu.VMEM((rows, D), low),
            pltpu.VMEM((D, 256), jnp.float32),
            pltpu.VMEM((TOK, 256), jnp.float32),
            pltpu.VMEM((TOK, 256), jnp.float32),
            pltpu.VMEM((TOK, 256), jnp.float32),
            pltpu.VMEM((2, D, TOK), low),
        ],
        compiler_params=kernel_params,
        cost_estimate=pl.CostEstimate(
            flops=6 * rows * 3 * D * FF, bytes_accessed=25000000, transcendentals=rows * FF
        ),
        name="mlp",
    )(tokens, tokens_1, cotangent, cotangent_1, *mixed, w_out, w_gate_up, w_down, gain)


def natural_tiles(flat, base, rows, width):
    pairs, step, whole = rows // 2, width * 2 // 128, width // 128
    parts = [flat[pl.ds(base + place, pairs, stride=step), :] for place in range(step)]
    even = parts[:whole] + [parts[whole][:, :HEAD_DIM]]
    odd = jnp.concatenate([parts[whole][:, HEAD_DIM:]] + parts[whole + 1 :], axis=1)
    return even, [odd[:, low : low + 128] for low in range(0, width, 128)]


def unflatten(flat, base, rows, width, tiles):
    even, odd = natural_tiles(flat, base, rows, width)
    for place, (first, second) in enumerate(zip(even, odd)):
        breadth = first.shape[1]
        if breadth < 128:
            blank = jnp.zeros((rows // 2, 128 - breadth), jnp.float32)
            first = jnp.concatenate([first, blank], axis=1)
            second = jnp.concatenate([second, blank], axis=1)
        tiles[place, pl.ds(0, rows // 2, stride=2), :] = first
        tiles[place, pl.ds(1, rows // 2, stride=2), :] = second


def tile_widths(width):
    return [(place, low, min(128, width - low)) for place, low in enumerate(range(0, width, 128))]


MIXED = ((0, 0, D), (2592, D, KV_WIDTH), (3456, D + KV_WIDTH, KV_WIDTH), (4320, FF - D, D))


def project_kernel(
    near_ref, next_ref, x_ref, x1_ref, gain_ref, cos0_ref, sin0_ref, cos1_ref, sin1_ref,
    q0_ref, q1_ref, kv_ref, w_ref, wo_ref, n_ref, flat, tiles,
):
    spot = chunk_spot()
    length = flat.shape[0] // CHUNKS
    for index in range(CHUNKS):
        chunk = spot ^ index
        core, half, chip = lax.div(chunk, 4), lax.rem(lax.div(chunk, 2), 2), lax.rem(chunk, 2)
        start = pl.multiple_of((half * 4 + chip * 2 + core) * length, 8)
        part = (near_ref, next_ref)[index // 4][index % 4]
        flat[pl.ds(start, length), :] = part.astype(jnp.float32)
    for base, start, width in MIXED:
        unflatten(flat, base, D, width, tiles)
        for place, low, breadth in tile_widths(width):
            part = tiles[place][:D, :breadth].astype(jnp.bfloat16)
            if start < FF - D:
                w_ref[:, start + low : start + low + breadth] = part
            else:
                wo_ref[:, low : low + breadth] = part
    tall = w_ref[...].T
    half_width = HEAD_DIM // 2
    tables = ((q0_ref, cos0_ref, sin0_ref), (q1_ref, cos1_ref, sin1_ref))
    for micro, (q_ref, cos_ref, sin_ref) in enumerate(tables):
        values = (x1_ref if micro else x_ref)[...].astype(jnp.float32)
        normed = (values * norm_scaling(values, 0) * gain_ref[:, 0:1]).astype(jnp.bfloat16)
        n_ref[:, micro * TOK : (micro + 1) * TOK] = normed
        linear = dot32(tall, normed)
        cosine, sine = cos_ref[...], sin_ref[...]
        for head in range(HEADS + KV_HEADS):
            low = head * HEAD_DIM
            former = linear[low : low + half_width]
            latter = linear[low + half_width : low + HEAD_DIM]
            turned = jnp.concatenate(
                [former * cosine - latter * sine, latter * cosine + former * sine], axis=0
            ).astype(jnp.bfloat16)
            if head < HEADS:
                scaled = turned.astype(jnp.float32) * 0.125
                q_ref[head // GROUPS, head % GROUPS] = scaled.astype(jnp.bfloat16)
            else:
                low = low - D
                kv_ref[micro, low : low + HEAD_DIM, :] = turned
        kv_ref[micro, KV_WIDTH:, :] = linear[D + KV_WIDTH :].astype(jnp.bfloat16)


def project(near, following, tokens, tokens_1, gain_columns, tables):
    low = jnp.bfloat16
    return pl.pallas_call(
        project_kernel,
        out_shape=(
            jax.ShapeDtypeStruct(heads_shape, low),
            jax.ShapeDtypeStruct(heads_shape, low),
            jax.ShapeDtypeStruct((2, 2 * KV_WIDTH, TOK), low),
            jax.ShapeDtypeStruct((D, D + 2 * KV_WIDTH), low),
            jax.ShapeDtypeStruct((D, D), low),
            jax.ShapeDtypeStruct((D, 2 * TOK), low),
        ),
        in_specs=[vmem()] * 9,
        out_specs=(vmem(),) * 6,
        scratch_shapes=[
            pltpu.VMEM((D * FF // 128, 128), jnp.float32),
            pltpu.VMEM((5, D, 128), jnp.float32),
        ],
        compiler_params=kernel_params,
        cost_estimate=pl.CostEstimate(
            flops=4 * TOK * D * 960, bytes_accessed=8000000, transcendentals=0
        ),
        name="project",
    )(near, following, tokens, tokens_1, gain_columns, *tables[0], *tables[1])


def projection_kernel(
    n_ref, dq0_ref, dq1_ref, kept0_ref, kept1_ref, got_ref, far_ref,
    cos0_ref, sin0_ref, cos1_ref, sin1_ref, gwo_ref, tie_ref,
    keep_ref, send_ref, all_ref, held, cut,
):
    spot = chunk_spot()
    half_width = HEAD_DIM // 2
    parts = ((dq0_ref, kept0_ref, cos0_ref, sin0_ref), (dq1_ref, kept1_ref, cos1_ref, sin1_ref))
    for micro, (dq_ref, kept_ref, cos_ref, sin_ref) in enumerate(parts):
        columns = slice(micro * TOK, (micro + 1) * TOK)
        all_ref[:D, columns] = dq_ref[...]
        cosine, sine = cos_ref[...], sin_ref[...]
        summed = kept_ref[0].astype(jnp.float32) + got_ref[micro].astype(jnp.float32)
        if micro == 0:
            summed = summed + far_ref[...].astype(jnp.float32)
        for head in range(KV_HEADS):
            low = head * HEAD_DIM
            former = summed[low : low + half_width, :]
            latter = summed[low + half_width : low + HEAD_DIM, :]
            all_ref[D + low : D + low + half_width, columns] = (
                former * cosine + latter * sine
            ).astype(jnp.bfloat16)
            all_ref[D + low + half_width : D + low + HEAD_DIM, columns] = (
                latter * cosine - former * sine
            ).astype(jnp.bfloat16)
        all_ref[D + KV_WIDTH :, columns] = summed[KV_WIDTH:, :].astype(jnp.bfloat16)
    held[:, : D + 2 * KV_WIDTH] = dot_with(n_ref[...], all_ref[...], 1, 1)
    held[:, D + 2 * KV_WIDTH :] = gwo_ref[...].astype(jnp.float32)
    for side in range(COL_CUT):
        start = (side ^ lax.rem(spot, COL_CUT)) * CHUNK_COLS
        cut[...] = held[:, pl.ds(pl.multiple_of(start, CHUNK_COLS), CHUNK_COLS)]
        for index, part in row_parts(cut, spot, side):
            (keep_ref, send_ref)[index // 4][index % 4] = part


def projection_grads(normed, dqs, kept, got, far, tables, gwo, tie):
    rows = normed.shape[1]
    chunk_shape = (CHUNKS // 2, CHUNK_ROWS, CHUNK_COLS)
    return pl.pallas_call(
        projection_kernel,
        out_shape=(
            jax.ShapeDtypeStruct(chunk_shape, jnp.bfloat16),
            jax.ShapeDtypeStruct(chunk_shape, jnp.bfloat16),
            jax.ShapeDtypeStruct((D + 2 * KV_WIDTH, rows), jnp.bfloat16),
        ),
        in_specs=[vmem()] * 12 + [anywhere()],
        out_specs=(vmem(),) * 3,
        scratch_shapes=[
            pltpu.VMEM((D, FF), jnp.float32),
            pltpu.VMEM((D, CHUNK_COLS), jnp.float32),
        ],
        compiler_params=kernel_params,
        cost_estimate=pl.CostEstimate(
            flops=2 * rows * D * 960, bytes_accessed=8000000, transcendentals=0
        ),
        name="projection_grads",
    )(normed, *dqs, *kept, got, far, *tables[0], *tables[1], gwo, tie)


def both(left_ref, right_ref, where=...):
    total = left_ref[where].astype(jnp.float32) + right_ref[where].astype(jnp.float32)
    return total.astype(jnp.bfloat16)


def plain_call(kernel, outs, operands, ties, name):
    outs = [jax.ShapeDtypeStruct(shape, jnp.bfloat16) for shape in outs]
    ties = ties if isinstance(ties, tuple) else (ties,)
    count = len(operands)

    def run(*refs):
        kernel(*refs[: count + 1], *refs[count + len(ties) :])

    return pl.pallas_call(
        run,
        out_shape=outs,
        in_specs=[vmem()] * count + [anywhere()] * len(ties),
        out_specs=[vmem()] * len(outs),
        compiler_params=kernel_params,
        name=name,
    )(*operands, *ties)


def turns_kernel(late_ref, early_ref, *outs):
    quarter = positions()[0]
    for shift, out in enumerate(outs[1:]):
        target = lax.rem(quarter + shift, 4)

        @pl.when(target == 0)
        def _():
            out[...] = late_ref[...]

        @pl.when(target != 0)
        def _():
            out[...] = early_ref[jnp.maximum(target - 1, 0)]


def depth_turns(late, early, tie):
    return plain_call(turns_kernel, [late.shape] * 4, (late, early), tie, "depth_turns")


def sum_kernel(*refs):
    total = refs[0][...].astype(jnp.float32)
    for ref in refs[1:-2]:
        total = total + ref[...].astype(jnp.float32)
    refs[-1][...] = total.astype(jnp.bfloat16)


def tied_sum(operands, tie):
    return plain_call(sum_kernel, [operands[0].shape], operands, tie, "tied_sum")[0]


def late_kernel(keep_ref, got_ref, tie_ref, keep_out, send_out):
    size = keep_out.shape[0]
    keep_out[...] = both(keep_ref, got_ref, slice(0, size))
    send_out[...] = both(keep_ref, got_ref, slice(size, 2 * size))


def late_halves(keep, got, tie):
    shape = (keep.shape[0] // 2, *keep.shape[1:])
    return plain_call(late_kernel, [shape] * 2, (keep, got), tie, "late_halves")


def pair_kernel(first_ref, second_ref, tie_ref, out_ref):
    out_ref[:1] = first_ref[...]
    out_ref[1:] = second_ref[...]


def tied_pair(first, second, tie):
    shape = (3, *first.shape[1:])
    return plain_call(pair_kernel, [shape], (first, second), tie, "tied_pair")[0]


def pick_first_kernel(own_ref, got1_ref, got2_ref, got3_ref, tie_ref, out_ref):
    quarter = positions()[0]
    for place, ref in enumerate((own_ref, got1_ref, got2_ref, got3_ref)):

        @pl.when(quarter == place)
        def _():
            out_ref[...] = ref[...]


def pick_first(pieces, tie):
    return plain_call(pick_first_kernel, [pieces[0].shape], pieces, tie, "pick_first")[0]


def pick_rest_kernel(own_ref, got1_ref, got2_ref, got3_ref, tie_ref, gu_ref, d_ref):
    quarter = positions()[0]

    def run(flat, tiles):
        for place, out in ((1, gu_ref), (2, gu_ref), (3, d_ref)):
            for shift, ref in enumerate((own_ref, got1_ref, got2_ref, got3_ref)):

                @pl.when(lax.rem(quarter - place + 4, 4) == shift)
                def _():
                    flat[...] = ref[...].astype(jnp.float32)

            rows, width = out.shape
            if width > D:
                for tile in range(FF // 128):
                    low = (place - 1) * FF + tile * 128
                    out[:, low : low + 128] = flat[
                        pl.ds(tile, rows, stride=FF // 128), :
                    ].astype(jnp.bfloat16)
            else:
                unflatten(flat, 0, rows, width, tiles)
                for tile, low, breadth in tile_widths(width):
                    out[:, low : low + breadth] = tiles[tile][:, :breadth].astype(jnp.bfloat16)

    pl.run_scoped(
        run,
        pltpu.VMEM(own_ref.shape, jnp.float32),
        pltpu.VMEM((5, FF // CHUNKS, 128), jnp.float32),
    )


def pick_rest(pieces, tie):
    shapes = [(D // CHUNKS, 2 * FF), (FF // CHUNKS, D)]
    return plain_call(pick_rest_kernel, shapes, pieces, tie, "pick_rest")


def cast_kernel(value_ref, tie_ref, out_ref):
    out_ref[...] = value_ref[...].astype(out_ref.dtype)


def tied_cast(value, tie):
    return pl.pallas_call(
        cast_kernel,
        out_shape=jax.ShapeDtypeStruct(value.shape, jnp.bfloat16),
        in_specs=[vmem(), anywhere()],
        out_specs=vmem(),
        compiler_params=kernel_params,
        name="tied_cast",
    )(value, tie)


def inputs_kernel(
    all_ref, w_ref, x_ref, x1_ref, dh_ref, gain_ref, tie_ref, out_ref, out1_ref, gg_ref
):
    gain = gain_ref[:, 0:1]
    total = jnp.zeros((D, 1), jnp.float32)
    for micro in range(2):
        columns = slice(micro * TOK, (micro + 1) * TOK)
        upstream = dot32(w_ref[...], all_ref[:, columns])
        values = (x1_ref if micro else x_ref)[...].astype(jnp.float32)
        part, gain_grad = norm_back(values, norm_scaling(values, 0), gain, upstream, 0)
        total = total + gain_grad
        grad = dh_ref[micro] + part
        store_result(micro, grad, out_ref, out1_ref)
    gg_ref[...] = jnp.broadcast_to(total, gg_ref.shape)


def input_grads(grad_qkv, w_qkv, tokens, tokens_1, grad_state, gain_columns, tie):
    return pl.pallas_call(
        inputs_kernel,
        out_shape=(
            jax.ShapeDtypeStruct((2, D, TOK), jnp.float32),
            jax.ShapeDtypeStruct((D, TOK), jnp.bfloat16),
            jax.ShapeDtypeStruct((D, 128), jnp.float32),
        ),
        in_specs=[vmem()] * 6 + [anywhere()],
        out_specs=(vmem(),) * 3,
        compiler_params=kernel_params,
        cost_estimate=pl.CostEstimate(
            flops=4 * TOK * D * 960, bytes_accessed=8000000, transcendentals=0
        ),
        name="input_grads",
    )(grad_qkv, w_qkv, tokens, tokens_1, grad_state, gain_columns, tie)


def place_kernel(whole_ref, part_ref, tie_ref, out_ref):
    out_ref[0] = part_ref[...].astype(out_ref.dtype)


def place_last(whole, part, tie):
    return pl.pallas_call(
        place_kernel,
        out_shape=jax.ShapeDtypeStruct(whole.shape, whole.dtype),
        grid=(1,),
        in_specs=[anywhere(), pl.BlockSpec(part.shape, lambda step: (0, 0)), anywhere()],
        out_specs=pl.BlockSpec((1, *part.shape), lambda step: (1, 0, 0)),
        input_output_aliases={0: 0},
        compiler_params=kernel_params,
        name="place_last",
    )(whole, part, tie)


def newton_loop(matrix, scale):
    current = matrix / (jnp.sqrt(jnp.sum(matrix * matrix)) + frobenius_epsilon)

    def iterate(unused, held):
        low = held.astype(jnp.bfloat16)
        square = dot_with(low, low, 1, 1)
        square_low = square.astype(jnp.bfloat16)
        mixer = newton_second * square + newton_third * dot32(square_low, square_low)
        return newton_first * held + dot32(mixer.astype(jnp.bfloat16), low)

    return lax.fori_loop(0, NS_STEPS, iterate, current) * (0.2 * math.sqrt(scale))


def newton_wide(total):
    def run(low, square, square_low, mixer, step):
        height, breadth = total.shape
        block = 256

        def scale_by(factor, keep_low):
            for row in range(0, height, 16):
                part = total[row : row + 16, :] * factor
                total[row : row + 16, :] = part
                if keep_low:
                    low[row : row + 16, :] = part.astype(jnp.bfloat16)

        norm = jnp.zeros((8, breadth), jnp.float32)
        for row in range(0, height, 8):
            part = total[row : row + 8, :]
            norm = norm + part * part
        scale_by(1.0 / (jnp.sqrt(jnp.sum(norm)) + frobenius_epsilon), True)

        def iterate(unused, held):
            square[...] = dot_with(low[...], low[...], 1, 1)
            for row in range(0, height, 16):
                rows = slice(row, row + 16)
                square_low[rows, :] = square[rows, :].astype(jnp.bfloat16)
            step[:, :height] = dot32(square_low[...], square_low[...])
            for row in range(0, height, 16):
                rows = slice(row, row + 16)
                mixed = newton_second * square[rows, :] + newton_third * step[rows, :height]
                mixer[rows, :] = mixed.astype(jnp.bfloat16)
            for column in range(0, breadth, block):
                columns = slice(column, column + block)
                step[:, :block] = dot32(mixer[...], low[:, columns])
                for row in range(0, height, 32):
                    rows = slice(row, row + 32)
                    part = newton_first * total[rows, columns] + step[rows, :block]
                    total[rows, columns] = part
                    low[rows, columns] = part.astype(jnp.bfloat16)
            return held

        lax.fori_loop(0, NS_STEPS, iterate, 0)
        scale_by(0.2 * math.sqrt(breadth), False)

    height, breadth = total.shape
    pl.run_scoped(
        run,
        pltpu.VMEM((height, breadth), jnp.bfloat16),
        pltpu.VMEM((height, height), jnp.float32),
        pltpu.VMEM((height, height), jnp.bfloat16),
        pltpu.VMEM((height, height), jnp.bfloat16),
        pltpu.VMEM((height, height), jnp.float32),
    )


def flatten_rows(tiles, start, rows, width, out):
    pairs, step, whole = rows // 2, width * 2 // 128, width // 128
    spans = range(whole + 1)
    even = [tiles[place, pl.ds(start, pairs, stride=2), :] for place in spans]
    odd = [tiles[place, pl.ds(start + 1, pairs, stride=2), :] for place in spans]
    for place in range(whole):
        out[pl.ds(place, pairs, stride=step), :] = even[place]
    rest = width - whole * 128
    joined = jnp.concatenate([even[whole][:, :rest]] + odd[:whole] + [odd[whole][:, :rest]], axis=1)
    for place in range(whole, step):
        low = (place - whole) * 128
        out[pl.ds(place, pairs, stride=step), :] = joined[:, low : low + 128]


def shard_rows(kind, kinds, start, matrix, tiles, out):
    length = out.shape[0] * 128

    if 0 in kinds:

        @pl.when(kind == 0)
        def _():
            rows = length // FF
            for place in range(FF // 128):
                out[pl.ds(place, rows, stride=FF // 128), :] = matrix[
                    pl.ds(pl.multiple_of(start, 8), rows), place * 128 : (place + 1) * 128
                ]

        @pl.when(kind == 5)
        def _():
            for place, low, breadth in tile_widths(D):
                tiles[place, :, :breadth] = matrix[low : low + breadth, :].T
            flatten_rows(tiles, start, length // D, D, out)

    for place, (base, low, width) in zip((1, 3, 4, 2), MIXED):
        if place not in kinds:
            continue

        @pl.when(kind == place)
        def _():
            for tile, column, breadth in tile_widths(width):
                tiles[tile, :D, :breadth] = matrix[:, low + column : low + column + breadth]
            flatten_rows(tiles, start, length // width, width, out)


def own_kind(length):
    square, narrow = D * D, D * KV_WIDTH
    quarter = lax.axis_index("quarter")
    index = lax.axis_index("rep") * 2 + lax.axis_index("half")
    within = (index * lax.axis_size("ctx") + lax.axis_index("ctx")) * length
    kind = jnp.where(quarter == 3, 5, 0)
    start = jnp.where(quarter == 3, lax.div(within, D), lax.div(within, FF))
    edges = ((0, 1, D), (square, 3, KV_WIDTH), (square + narrow, 4, KV_WIDTH))
    for edge, place, width in (*edges, (square + 2 * narrow, 2, D)):
        inside = (quarter == 0) & (within >= edge)
        kind = jnp.where(inside, place, kind)
        start = jnp.where(inside, lax.div(within - edge, width), start)
    return (kind, start)


def load_matrix(kind, kinds, old_ref, flat, grad, total, tiles):
    flat[...] = old_ref[...].astype(jnp.float32) * momentum_decay
    if 0 in kinds:

        @pl.when(kind == 0)
        def _():
            for place in range(FF // 128):
                columns = slice(place * 128, (place + 1) * 128)
                total[:, columns] = flat[pl.ds(place, D, stride=FF // 128), :] + grad[:, columns]

        @pl.when(kind == 5)
        def _():
            unflatten(flat, 0, FF, D, tiles)
            for place, low, breadth in tile_widths(D):
                rows = slice(low, low + breadth)
                total[rows, :] = tiles[place].T[:breadth] + grad[rows, :]

    for place, (base, low, width) in zip((1, 3, 4, 2), MIXED):
        if place not in kinds:
            continue

        @pl.when(kind == place)
        def _():
            unflatten(flat, base, D, width, tiles)
            part = jnp.concatenate(
                [tiles[tile][:D, :breadth] for tile, _, breadth in tile_widths(width)], axis=1
            )
            columns = slice(low, low + width)
            total[:, columns] = part + grad[:, columns]


def update_matrix(kind, kinds, total):
    if 0 in kinds:

        @pl.when((kind == 0) | (kind == 5))
        def _():
            newton_wide(total)

    for place, (base, low, width) in zip((1, 3, 4, 2), MIXED):
        if place not in kinds:
            continue

        @pl.when(kind == place)
        def _():
            columns = slice(low, low + width)
            if width == D:
                total[:, columns] = newton_loop(total[:, columns], D)
            else:
                total[:, columns] = newton_loop(total[:, columns].T, D).T


def newton_kernel(local, length, *refs):
    count = 3 if local else 2
    grad, total, tiles = refs[-3:]
    outs = refs[-3 - count : -3]
    pieces, (old_ref, *rest) = refs[:2], refs[2:-3]
    kind, start = own_kind(length)
    spot = chunk_spot()

    def run():
        for index in range(CHUNKS):
            chunk = spot ^ index
            row = pl.multiple_of(lax.div(chunk, COL_CUT) * CHUNK_ROWS, CHUNK_ROWS)
            column = pl.multiple_of(lax.rem(chunk, COL_CUT) * CHUNK_COLS, CHUNK_COLS)
            rows, columns = pl.ds(row, CHUNK_ROWS), pl.ds(column, CHUNK_COLS)
            part = pieces[index // 4][index % 4]
            grad[rows, columns] = part.astype(jnp.float32)
        kinds = (0, 1, 2, 3, 4, 5)
        pl.run_scoped(
            lambda flat: load_matrix(kind, kinds, old_ref, flat, grad, total, tiles),
            pltpu.VMEM((D * FF // 128, 128), jnp.float32),
        )
        update_matrix(kind, kinds, total)
        if local:
            weights_ref, momentum_ref = rest[:2]
            grad_ref, new_momentum_ref, new_weights_ref = outs
            shard_rows(kind, kinds, start, grad, tiles, grad_ref)
            shard_rows(kind, kinds, start, total, tiles, new_weights_ref)
            new_momentum_ref[...] = momentum_decay * momentum_ref[...] + grad_ref[...]
            new_weights_ref[...] = (
                weights_ref[...] * (1.0 - matrix_rate * weight_decay)
                - matrix_rate * new_weights_ref[...]
            )
        else:
            outs[0][...] = grad[...]
            outs[1][...] = total[...]

    run()


def newton(length, pieces, old, shards):
    local = len(shards) > 0
    if local:
        outs = (jax.ShapeDtypeStruct(shards[0].shape, jnp.float32),) * 3
    else:
        outs = (jax.ShapeDtypeStruct((D, FF), jnp.float32),) * 2
    operands = (*pieces, old, *shards)

    return pl.pallas_call(
        partial(newton_kernel, local, length),
        out_shape=outs,
        in_specs=[vmem()] * len(operands),
        out_specs=(vmem(),) * len(outs),
        scratch_shapes=[
            pltpu.VMEM((D, FF), jnp.float32),
            pltpu.VMEM((D, FF), jnp.float32),
            pltpu.VMEM((5, FF, 128), jnp.float32),
        ],
        compiler_params=kernel_params,
        cost_estimate=pl.CostEstimate(
            flops=12000000000, bytes_accessed=9000000, transcendentals=0
        ),
        name="newton",
    )(*operands)


def own_rows(kind, row, shard_length, gradient, update):
    def block_case(low, width):
        def run(gradient, update):
            start = (row, low)
            size = (shard_length // width, width)
            return tuple(
                lax.dynamic_slice(whole, start, size).reshape(-1) for whole in (gradient, update)
            )

        return run

    def tall_case(gradient, update):
        start = (0, row)
        size = (D, shard_length // D)
        return tuple(
            lax.dynamic_slice(whole, start, size).T.reshape(-1) for whole in (gradient, update)
        )

    cases = [
        block_case(0, FF),
        block_case(0, D),
        block_case(FF - D, D),
        block_case(D, KV_WIDTH),
        block_case(D + KV_WIDTH, KV_WIDTH),
        tall_case,
    ]
    return lax.switch(kind, cases, gradient, update)


CORE_SWAP = [(0, 1), (1, 0), (2, 3), (3, 2)]
CHIP_SWAP = [(0, 2), (2, 0), (1, 3), (3, 1)]
SIDE_SWAP = [(0, 1), (1, 0)]
END_SWAP = [(0, 3), (3, 0), (1, 2), (2, 1)]


def plane_swap(value, bit):
    axis, swap = (("ctx", CHIP_SWAP), ("half", SIDE_SWAP), ("ctx", CORE_SWAP))[bit]
    return lax.ppermute(value, axis, swap)


def low_sum(left, right):
    return (left.astype(jnp.float32) + right.astype(jnp.float32)).astype(jnp.bfloat16)


def low_total(first, others):
    total = first.astype(jnp.float32)
    for part in others:
        total = total + part.astype(jnp.float32)
    return total.astype(jnp.bfloat16)


def plane_gather(piece, swap):
    pieces = piece[None]
    for bit in range(2):
        pieces = jnp.concatenate([pieces, swap(pieces, bit)], axis=0)
    return (pieces, swap(pieces, 2))


def depth_shift(value, shift, targets):
    pairs = [(place, (place + shift) % 4) for place in range(4)]
    return lax.ppermute(value, "quarter", [pair for pair in pairs if pair[1] in targets])


def plane_total(value):
    parts = [
        lax.ppermute(value, ("half", "ctx"), [(place, place ^ turn) for place in range(8)])
        for turn in range(1, 8)
    ]
    return value + sum(parts)


def depth_total(value):
    return value + sum(depth_shift(value, shift, range(4)) for shift in range(1, 4))


def gather_weights(low, tie):
    if lax.axis_size("rep") > 1:
        full = lax.all_gather(low, EVERY, axis=0, tiled=True).reshape(4, D * FF)
        ctx = lax.axis_index("ctx")
        spot = lax.rem(ctx, 2) * 4 + lax.axis_index("half") * 2 + ctx // 2
        chunk = jnp.arange(CHUNKS, dtype=jnp.int32) ^ spot
        order = 4 * (chunk // 2 % 2) + 2 * (chunk % 2) + chunk // 4
        mixed = full[0].reshape(CHUNKS, -1, 128)[order]
        return (mixed[:4], mixed[4:]), [
            jnp.concatenate([full[1].reshape(D, FF), full[2].reshape(D, FF)], axis=1),
            full[3].reshape(FF, D),
        ]
    first = [lax.ppermute(low, "quarter", [(0, shift)]) for shift in range(1, 4)]
    mixed = pick_first((low, *first), tie)
    others = [
        lax.ppermute(low, "quarter", [(place, (place + shift) % 4) for place in range(1, 4)])
        for shift in range(1, 4)
    ]
    rest = [
        lax.all_gather(piece, PLANE, axis=0, tiled=True)
        for piece in pick_rest((low, *others), mixed)
    ]
    return plane_gather(mixed, plane_swap), rest


def per_device(tokens, lengths, weights, momentum, norm_gains, gain_first, gain_second, cotangent):
    ctx = lax.axis_index("ctx")
    chip = ctx // 2
    reps = lax.axis_size("rep")
    shard_length = weights.shape[0]
    flat_shape = (shard_length // 128, 128)
    lengths = lengths[:, 0]
    tokens = jnp.swapaxes(tokens, 1, 2)
    cotangent = jnp.swapaxes(cotangent, 1, 2)
    gain_columns = norm_gains.T

    tokens_1 = lax.ppermute(tokens[1], "ctx", END_SWAP)
    mixed_weights, (w_gate_up, w_down) = gather_weights(
        weights.reshape(flat_shape).astype(jnp.bfloat16), tokens_1
    )
    near = chip == 0

    def slots(first, second):
        return jnp.where(near, first, second), jnp.where(near, second, first)

    x0, x1 = slots(tokens[0], tokens_1)
    begin_rows, tables = [], []
    for micro, own_lengths in enumerate(slots(lengths[0], lengths[1])):
        own_places = own_block(micro) * TOK + jnp.arange(TOK, dtype=jnp.int32)
        offsets, begins = layout(own_lengths, own_places)
        begin_rows.append(begins.reshape(1, TOK))
        tables.append(rope_tables(offsets))

    q0, q1, keyvals, w_qkv, w_out, normed = project(
        *mixed_weights, x0, x1, gain_columns, tables
    )
    queries = (q0, q1)
    far = lax.ppermute(keyvals[0], "ctx", CHIP_SWAP)
    keyvals = (
        keyvals,
        lax.ppermute(keyvals, "ctx", CORE_SWAP),
        far,
        lax.ppermute(far, "ctx", CORE_SWAP),
    )
    mixed, log_totals = [], []
    for micro in range(2):
        mixed_one, log_total = attend_forward(
            micro, lengths, queries[micro], keyvals, begin_rows[micro], norm_gains
        )
        mixed.append(mixed_one)
        log_totals.append(log_total)
    cotangent_1 = lax.ppermute(tied_cast(cotangent[1], mixed[0]), "ctx", END_SWAP)
    old = lax.all_gather(
        tied_cast(momentum.reshape(flat_shape), mixed[0]),
        ("rep", "half", "ctx"),
        axis=0,
        tiled=True,
    )
    outs = mlp(
        x0,
        x1,
        cotangent,
        cotangent_1,
        [part.reshape(D, TOK) for part in mixed],
        w_out,
        w_gate_up,
        w_down,
        norm_gains[1:2],
    )
    result, result_1, grad_state, grad_mixed_0, grad_mixed_1 = outs[:5]
    keep, send, grad_w_out, gain_two_grad = outs[5:]
    returned = lax.ppermute(result_1, "ctx", END_SWAP)

    def back_pass(micro, grad_mixed, tie):
        return attend_back(
            micro,
            lengths,
            queries[micro],
            keyvals,
            begin_rows[micro],
            mixed[micro],
            log_totals[micro],
            grad_mixed.reshape(heads_shape),
            *tables[micro],
            tie,
        )

    got = plane_swap(send, 2)
    dq0, kept0, sent0 = back_pass(0, grad_mixed_0, norm_gains)
    keep, send = late_halves(keep, got, (dq0, returned))
    got = plane_swap(send, 1)
    dq1, kept1, sent1 = back_pass(1, grad_mixed_1, keep)
    keep, send = late_halves(keep, got, (dq1, old))
    traded = lax.ppermute(tied_pair(sent0, sent1, keep), "ctx", CORE_SWAP)
    crossed = lax.ppermute(low_sum(kept1[1], traded[2]), "ctx", CHIP_SWAP)
    got = plane_swap(send, 0)
    late_keep, late_send, grad_qkv = projection_grads(
        normed,
        (dq0.reshape(D, TOK), dq1.reshape(D, TOK)),
        (kept0, kept1),
        traded,
        crossed,
        tables,
        grad_w_out,
        keep,
    )
    late_got = plane_swap(late_send, 2)
    late_keep, late_send = late_halves(late_keep, late_got, norm_gains)
    late_got = plane_swap(late_send, 1)
    early = tied_sum((keep[0], got[0]), late_keep)
    grad_inputs, grad_inputs_1, gain_one_grad = input_grads(
        grad_qkv, w_qkv, x0, x1, grad_state, gain_columns, early
    )
    late_keep, late_send = late_halves(late_keep, late_got, gain_one_grad)
    gain_grad = plane_total(
        jnp.concatenate([gain_one_grad[:, 0].reshape(1, D), gain_two_grad], axis=0)
    )
    late = low_sum(late_keep[0], plane_swap(late_send, 0)[0])
    piece, *turns = depth_turns(late, early, gain_grad)
    parts = [depth_shift(turn, shift, range(4)) for shift, turn in enumerate(turns, start=1)]
    gain_grad = depth_total(gain_grad)
    piece = tied_sum((piece, *parts), gain_grad)
    if reps > 1:
        piece = lax.psum(piece, "rep")
        gain_grad = lax.psum(gain_grad, "rep")
    pieces = plane_gather(piece, plane_swap)
    grad_inputs_1 = lax.ppermute(grad_inputs_1, "ctx", END_SWAP)

    shards = ()
    if flat_shape[0] % 8 == 0:
        shards = (weights.reshape(flat_shape), momentum.reshape(flat_shape))
    outs = newton(shard_length, pieces, old, shards)
    if len(shards) > 0:
        grad_shard, new_momentum, new_weights = [out.reshape(weights.shape) for out in outs]
    else:
        kind, start = own_kind(shard_length)
        grad_shard, update_shard = own_rows(kind, start, shard_length, *outs)
        new_momentum = momentum_decay * momentum + grad_shard
        new_weights = weights * (1.0 - matrix_rate * weight_decay) - matrix_rate * update_shard

    def placed(whole, part):
        whole = lax.dynamic_update_index_in_dim(whole, part.astype(jnp.float32), 1, 0)
        return jnp.swapaxes(whole, 1, 2)

    first_new = first_decay * gain_first + (1.0 - first_decay) * gain_grad
    second_new = second_decay * gain_second + (1.0 - second_decay) * gain_grad * gain_grad
    debiased_first_moment = first_new / (1.0 - first_decay**ADAM_STEP)
    corrected_second = second_new / (1.0 - second_decay**ADAM_STEP)
    new_gains = norm_gains * (
        1.0 - gain_rate * weight_decay
    ) - gain_rate * debiased_first_moment / (jnp.sqrt(corrected_second) + adam_epsilon)
    return (
        placed(result, returned),
        jnp.swapaxes(place_last(grad_inputs, grad_inputs_1, outs[-1]), 1, 2),
        grad_shard,
        new_momentum,
        new_weights,
        first_new,
        second_new,
        new_gains,
    )


def solution(mesh):
    devices = mesh.devices
    count = devices.size
    context = mesh.shape["ctx"]
    split = Mesh(
        devices.reshape(4, count // (8 * context), 2, context), ("quarter", "rep", "half", "ctx")
    )
    rows = P(None, EVERY, None)
    flat = P(EVERY)
    placed = (rows, P(None, ("quarter", "rep", "half"), None), flat, flat, P(), P(), P(), rows)
    return jax.shard_map(
        per_device,
        mesh=split,
        in_specs=placed,
        out_specs=(rows, rows, flat, flat, flat, P(), P(), P()),
        check_vma=False,
    )
```

```python
from functools import partial
import math

import jax
import jax.numpy as jnp
from jax import lax
from jax.experimental import pallas as pl
from jax.experimental.pallas import tpu as pltpu
from jax.sharding import Mesh, PartitionSpec as P

HEADS = 9
KV_HEADS = 3
HEAD_DIM = 64
FF = 1536
NS_STEPS = 5
ADAM_STEP = 10
D = 576
KV_WIDTH = 192
GROUPS = HEADS // KV_HEADS
TOK = 512
TILE = 256
COLS = GROUPS * TILE
ROW_CUT = 4
COL_CUT = 2
CHUNKS = ROW_CUT * COL_CUT
CHUNK_ROWS = D // ROW_CUT
CHUNK_COLS = FF // COL_CUT
PLANE = ("half", "ctx")
EVERY = ("quarter", "rep", "half", "ctx")


norm_epsilon = 1e-05
rope_base = 100000.0
masked_score = -1e30
newton_first = 3.4445
newton_second = -4.775
newton_third = 2.0315
momentum_decay = 0.95
matrix_rate = 0.2
weight_decay = 0.1
gain_rate = 0.2
first_decay = 0.9
second_decay = 0.95
adam_epsilon = 1e-08
frobenius_epsilon = 1e-07


def layout(lengths_row, places):
    finish = jnp.cumsum(lengths_row)
    firsts = finish - lengths_row
    begins = jnp.max(jnp.where(places[:, None] >= firsts[None, :], firsts[None, :], 0), axis=1)
    return (places - begins, begins)


def rope_tables(offsets):
    half_width = HEAD_DIM // 2
    inverse = jnp.exp(
        jnp.arange(half_width, dtype=jnp.float32) * (-2.0 * math.log(rope_base) / HEAD_DIM)
    )
    angles = inverse[:, None] * offsets.astype(jnp.float32)[None, :]
    return (jnp.cos(angles), jnp.sin(angles))


def dot32(left, right):
    return jnp.dot(left, right, preferred_element_type=jnp.float32)


def masked(scores, key_block, begins, places):
    keys = key_block * TILE + lax.broadcasted_iota(jnp.int32, scores.shape, 0)
    return jnp.where((keys >= begins) & (keys <= places), scores, masked_score)


def tile_row(row, tile):
    part = row[:, tile * TILE : (tile + 1) * TILE]
    return jnp.concatenate([part] * GROUPS, axis=1)


def tile_heads(ref, group, tile):
    return jnp.concatenate(
        [ref[group, head, :, tile * TILE : (tile + 1) * TILE] for head in range(GROUPS)], axis=1
    )


def positions():
    ctx = lax.axis_index("ctx")
    return (lax.axis_index("quarter"), lax.axis_index("half"), lax.div(ctx, 2), lax.rem(ctx, 2))


def chunk_spot():
    _, half, chip, core = positions()
    return core * 4 + half * 2 + chip


def first_key(lengths_ref, slot, row):
    micro = slot ^ positions()[2]
    begin = jnp.int32(0)
    first = jnp.int32(0)
    for place in range(3):
        first = first + lengths_ref[micro, place]
        begin = jnp.where(row >= first, first, begin)
    return begin


def key_loop(lengths_ref, slot, own, tile, load, process, carry):
    last = own * (TOK // TILE) + tile
    first = lax.div(first_key(lengths_ref, slot, last * TILE), TILE)
    full = lax.div(first_key(lengths_ref, slot, last * TILE + TILE - 1) + TILE - 1, TILE)
    full = jnp.minimum(full, last)
    pairs = lax.div(last - full, 2)

    def alone(block, held):
        load(0, block)
        return process(0, True, block, held)

    def couple(pair, held):
        block = full + 2 * pair
        load(1, block + 1)
        held = process(0, False, block, held)
        load(0, block + 2)
        return process(1, False, block + 1, held)

    def single(block, held):
        held = process(0, False, block, held)
        load(0, last)
        return held

    carry = lax.fori_loop(first, full, alone, carry)
    load(0, full)
    carry = lax.fori_loop(0, pairs, couple, carry)
    carry = lax.fori_loop(full + 2 * pairs, last, single, carry)
    return process(0, True, last, carry)


def key_rows(block):
    return pl.ds(pl.multiple_of(block * TILE, TILE), TILE)


def own_block(slot):
    ctx = lax.axis_index("ctx")
    return jnp.maximum(ctx, 3 - ctx) if slot else jnp.minimum(ctx, 3 - ctx)


def key_slots(own, micro, kv_ref, other_ref, far_ref, far_other_ref):
    refs = (kv_ref.at[micro], other_ref.at[micro], far_ref, far_other_ref)[: 2 + 2 * micro]
    return [(own ^ place, ref) for place, ref in enumerate(refs)]


def block_rows(block):
    return pl.ds(pl.multiple_of(block * TOK, TOK), TOK)


def forward_kernel(
    micro, lengths_ref, q_ref, kv_ref, other_ref, far_ref, far_other_ref, begin_ref, tie_ref,
    o_ref, lse_ref, k_nat, v_ext, s_ref, p_ref,
):
    own = own_block(micro)
    for block, source in key_slots(own, micro, kv_ref, other_ref, far_ref, far_other_ref):

        @pl.when(block <= own)
        def _():
            rows = block_rows(block)
            for group in range(KV_HEADS):
                low = HEAD_DIM * group
                k_nat[group, rows, :] = source[low : low + HEAD_DIM, :].T
                low = low + KV_WIDTH
                v_ext[group, :HEAD_DIM, rows] = source[low : low + HEAD_DIM, :]
                v_ext[group, HEAD_DIM:, rows] = jnp.ones((16, TOK), jnp.bfloat16)

    def one_group(group, unused):
        for tile in range(TOK // TILE):
            queries = tile_heads(q_ref, group, tile)
            begins = tile_row(begin_ref[...], tile)
            column = lax.broadcasted_iota(jnp.int32, (1, COLS), 1)
            places = own * TOK + tile * TILE + lax.rem(column, TILE)

            def load(side, block):
                s_ref[side] = dot32(k_nat[group, key_rows(block), :], queries)

            def process(side, is_masked, block, carry):
                top, total = carry
                scores_ref, probs_ref = s_ref.at[side], p_ref.at[side]
                if is_masked:
                    scores_ref[...] = masked(scores_ref[...], block, begins, places)
                highest = scores_ref[:16]
                for low in range(16, TILE, 16):
                    highest = jnp.maximum(highest, scores_ref[low : low + 16])
                new_top = jnp.maximum(top, jnp.max(highest, axis=0, keepdims=True))
                for low in range(0, TILE, 16):
                    rows = slice(low, low + 16)
                    probs_ref[rows] = jnp.exp(scores_ref[rows] - new_top).astype(jnp.bfloat16)
                total = total * jnp.exp(top - new_top) + dot32(
                    v_ext[group, :, key_rows(block)], probs_ref[...]
                )
                return (new_top, total)

            carry = (
                jnp.full((1, COLS), masked_score, jnp.float32),
                jnp.zeros((HEAD_DIM + 16, COLS), jnp.float32),
            )
            top, total = key_loop(lengths_ref, micro, own, tile, load, process, carry)
            weight = total[HEAD_DIM : HEAD_DIM + 1, :]
            mixed = (total[:HEAD_DIM, :] / weight).astype(jnp.bfloat16)
            log_total = top + jnp.log(weight)
            for head in range(GROUPS):
                o_ref[group, head, :, tile * TILE : (tile + 1) * TILE] = mixed[
                    :, head * TILE : (head + 1) * TILE
                ]
                lse_ref[group, head, :, tile * TILE : (tile + 1) * TILE] = log_total[
                    :, head * TILE : (head + 1) * TILE
                ]
        return unused

    lax.fori_loop(0, KV_HEADS, one_group, 0)


def backward_kernel(
    micro, lengths_ref, q_ref, kv_ref, other_ref, far_ref, far_other_ref, begin_ref, o_ref, lse_ref,
    do_ref, cos_ref, sin_ref, tie_ref,
    dq_ref, keep_ref, send_ref, k_nat, v_nat, k_tall, dk_ref, dv_ref, s_ref, g_ref, p_ref, ds_ref,
):
    own = own_block(micro)
    slots = key_slots(own, micro, kv_ref, other_ref, far_ref, far_other_ref)
    for block, source in slots:

        @pl.when(block <= own)
        def _():
            rows = block_rows(block)
            for group in range(KV_HEADS):
                low = HEAD_DIM * group
                k_nat[group, rows, :] = source[low : low + HEAD_DIM, :].T
                k_tall[group, :, rows] = source[low : low + HEAD_DIM, :]
                low = low + KV_WIDTH
                v_nat[group, rows, :] = source[low : low + HEAD_DIM, :].T
                dk_ref[group, rows, :] = jnp.zeros((TOK, HEAD_DIM), jnp.float32)
                dv_ref[group, rows, :] = jnp.zeros((TOK, HEAD_DIM), jnp.float32)

    def one_group(group, unused):
        for tile in range(TOK // TILE):
            queries = tile_heads(q_ref, group, tile)
            upstream = tile_heads(do_ref, group, tile)
            mixed = tile_heads(o_ref, group, tile)
            log_total = tile_heads(lse_ref, group, tile)
            delta = jnp.sum(
                upstream.astype(jnp.float32) * mixed.astype(jnp.float32), axis=0, keepdims=True
            )
            queries_nat = queries.T
            upstream_nat = upstream.T
            begins = tile_row(begin_ref[...], tile)
            column = lax.broadcasted_iota(jnp.int32, (1, COLS), 1)
            places = own * TOK + tile * TILE + lax.rem(column, TILE)

            def load(side, block):
                s_ref[side] = dot32(k_nat[group, key_rows(block), :], queries)
                g_ref[side] = dot32(v_nat[group, key_rows(block), :], upstream)

            def process(side, is_masked, block, dq):
                scores_ref, grads_ref = s_ref.at[side], g_ref.at[side]
                probs_ref, changes_ref = p_ref.at[side], ds_ref.at[side]
                if is_masked:
                    scores_ref[...] = masked(scores_ref[...], block, begins, places)
                for low in range(0, TILE, 16):
                    part = slice(low, low + 16)
                    probs = jnp.exp(scores_ref[part] - log_total)
                    probs_ref[part] = probs.astype(jnp.bfloat16)
                    changes_ref[part] = (probs * (grads_ref[part] - delta)).astype(jnp.bfloat16)
                rows = key_rows(block)
                dv_ref[group, rows, :] += dot32(probs_ref[...], upstream_nat)
                dk_ref[group, rows, :] += dot32(changes_ref[...], queries_nat)
                return dq + dot32(k_tall[group, :, rows], changes_ref[...])

            dq = jnp.zeros((HEAD_DIM, COLS), jnp.float32)
            dq = key_loop(lengths_ref, micro, own, tile, load, process, dq) * 0.125
            half_width = HEAD_DIM // 2
            cosine = tile_row(cos_ref[...], tile)
            sine = tile_row(sin_ref[...], tile)
            former, latter = dq[:half_width], dq[half_width:]
            turned = jnp.concatenate(
                [former * cosine + latter * sine, latter * cosine - former * sine], axis=0
            ).astype(jnp.bfloat16)
            for head in range(GROUPS):
                dq_ref[group, head, :, tile * TILE : (tile + 1) * TILE] = turned[
                    :, head * TILE : (head + 1) * TILE
                ]
        return unused

    lax.fori_loop(0, KV_HEADS, one_group, 0)
    for place, (block, _) in enumerate(slots):
        out_ref = (keep_ref, send_ref)[place % 2]

        @pl.when(block <= own)
        def _():
            rows = block_rows(block)
            for group in range(KV_HEADS):
                low = HEAD_DIM * group
                out_ref[place // 2, low : low + HEAD_DIM, :] = dk_ref[group, rows, :].T.astype(
                    jnp.bfloat16
                )
                low = low + KV_WIDTH
                out_ref[place // 2, low : low + HEAD_DIM, :] = dv_ref[group, rows, :].T.astype(
                    jnp.bfloat16
                )

        @pl.when(block > own)
        def _():
            out_ref[place // 2] = jnp.zeros((2 * KV_WIDTH, TOK), jnp.bfloat16)


def vmem():
    return pl.BlockSpec(memory_space=pltpu.VMEM)


def smem():
    return pl.BlockSpec(memory_space=pltpu.SMEM)


def anywhere():
    return pl.BlockSpec(memory_space=pl.ANY)


kernel_params = pltpu.CompilerParams(vmem_limit_bytes=56 * 1024 * 1024)
heads_shape = (KV_HEADS, GROUPS, HEAD_DIM, TOK)


def attend_forward(micro, lengths, queries, keyvals, begins, tie):
    return pl.pallas_call(
        partial(forward_kernel, micro),
        out_shape=(
            jax.ShapeDtypeStruct(heads_shape, jnp.bfloat16),
            jax.ShapeDtypeStruct((KV_HEADS, GROUPS, 1, TOK), jnp.float32),
        ),
        in_specs=[smem()] + [vmem()] * 6 + [anywhere()],
        out_specs=(vmem(), vmem()),
        scratch_shapes=[
            pltpu.VMEM((KV_HEADS, 4 * TOK, HEAD_DIM), jnp.bfloat16),
            pltpu.VMEM((KV_HEADS, HEAD_DIM + 16, 4 * TOK), jnp.bfloat16),
            pltpu.VMEM((2, TILE, COLS), jnp.float32),
            pltpu.VMEM((2, TILE, COLS), jnp.bfloat16),
        ],
        compiler_params=kernel_params,
        cost_estimate=pl.CostEstimate(
            flops=4 * 9 * 64 * TOK * 2048, bytes_accessed=4000000, transcendentals=9 * TOK * 2048
        ),
        name="attend_forward",
    )(lengths, queries, *keyvals, begins, tie)


def attend_back(
    micro, lengths, queries, keyvals, begins, mixed, log_total, grad_mixed, cosine, sine, tie
):
    half_shape = (1 + micro, 2 * KV_WIDTH, TOK)
    return pl.pallas_call(
        partial(backward_kernel, micro),
        out_shape=(
            jax.ShapeDtypeStruct(heads_shape, jnp.bfloat16),
            jax.ShapeDtypeStruct(half_shape, jnp.bfloat16),
            jax.ShapeDtypeStruct(half_shape, jnp.bfloat16),
        ),
        in_specs=[smem()] + [vmem()] * 11 + [anywhere()],
        out_specs=(vmem(),) * 3,
        scratch_shapes=[
            pltpu.VMEM((KV_HEADS, 4 * TOK, HEAD_DIM), jnp.bfloat16),
            pltpu.VMEM((KV_HEADS, 4 * TOK, HEAD_DIM), jnp.bfloat16),
            pltpu.VMEM((KV_HEADS, HEAD_DIM, 4 * TOK), jnp.bfloat16),
            pltpu.VMEM((KV_HEADS, 4 * TOK, HEAD_DIM), jnp.float32),
            pltpu.VMEM((KV_HEADS, 4 * TOK, HEAD_DIM), jnp.float32),
            pltpu.VMEM((2, TILE, COLS), jnp.float32),
            pltpu.VMEM((2, TILE, COLS), jnp.float32),
            pltpu.VMEM((2, TILE, COLS), jnp.bfloat16),
            pltpu.VMEM((2, TILE, COLS), jnp.bfloat16),
        ],
        compiler_params=kernel_params,
        cost_estimate=pl.CostEstimate(
            flops=10 * 9 * 64 * TOK * 2048, bytes_accessed=8000000, transcendentals=9 * TOK * 2048
        ),
        name="attend_back",
    )(lengths, queries, *keyvals, begins, mixed, log_total, grad_mixed, cosine, sine, tie)


def dot_with(left, right, left_side, right_side):
    return lax.dot_general(
        left, right, (((left_side,), (right_side,)), ((), ())), preferred_element_type=jnp.float32
    )


def norm_back(values, scaling, gain, upstream, axis):
    weighted = upstream * gain
    inner = jnp.mean(weighted * values, axis=axis, keepdims=True)
    gain_grad = jnp.sum(upstream * values * scaling, axis=1 - axis, keepdims=True)
    return (scaling * weighted - values * (scaling * scaling * scaling) * inner, gain_grad)


def norm_scaling(values, axis):
    return lax.rsqrt(jnp.mean(values * values, axis=axis, keepdims=True) + norm_epsilon)


def row_parts(held, spot, side):
    for turn in range(ROW_CUT):
        start = (turn ^ lax.div(spot, COL_CUT)) * CHUNK_ROWS
        part = held[pl.ds(pl.multiple_of(start, CHUNK_ROWS), CHUNK_ROWS), :]
        yield (turn * COL_CUT + side, part.astype(jnp.bfloat16))


def store_result(slot, result, out_ref, moved_ref):
    chip = positions()[2]

    @pl.when(chip == slot)
    def _():
        out_ref[0] = result

    @pl.when(chip != slot)
    def _():
        moved_ref[...] = result.astype(jnp.bfloat16)


def mlp_kernel(
    x_ref, x1_ref, c_ref, c1_ref, o0_ref, o1_ref, wo_ref, w_ref, wd_ref, gain_ref,
    out_ref, out1_ref, dh_ref, do0_ref, do1_ref, keep_ref, send_ref, gwo_ref, gg_ref,
    hid, dgate, dup, n2_tall, dh_low, held, gate_ref, up_ref, da_ref, c_slots,
):
    gain = gain_ref[...]
    gg_ref[...] = jnp.zeros((1, D), jnp.float32)
    block = 256
    spot = chunk_spot()
    for micro, (o_ref, do_ref) in enumerate(((o0_ref, do0_ref), (o1_ref, do1_ref))):
        rows = slice(micro * TOK, (micro + 1) * TOK)
        x_tall = (x1_ref if micro else x_ref)[...]
        c_tall_ref = c_slots.at[micro]
        chip = positions()[2]

        @pl.when(chip == micro)
        def _():
            c_tall_ref[...] = c_ref[0]

        @pl.when(chip != micro)
        def _():
            c_tall_ref[...] = c1_ref[...]

        c_tall = c_tall_ref[...]
        hidden_state = (x_tall.astype(jnp.float32) + dot_with(wo_ref[...], o_ref[...], 0, 0)).T
        scaling = norm_scaling(hidden_state, 1)
        normed = (hidden_state * scaling * gain).astype(jnp.bfloat16)
        n2_tall[:, rows] = normed.T
        back = c_tall.T
        for column in range(0, FF, block):
            columns = slice(column, column + block)
            gate_ref[...] = dot32(normed, w_ref[:, columns])
            up_ref[...] = dot32(normed, w_ref[:, FF + column : FF + column + block])
            da_ref[...] = dot_with(back, wd_ref[columns, :], 1, 1)
            for low in range(0, TOK, 32):
                part, spot_rows = slice(low, low + 32), slice(micro * TOK + low, micro * TOK + low + 32)
                gate, upward, grad_hidden = gate_ref[part], up_ref[part], da_ref[part]
                sigmoid_gate = jax.nn.sigmoid(gate)
                activated = gate * sigmoid_gate
                hid[spot_rows, columns] = (activated * upward).astype(jnp.bfloat16)
                dup[spot_rows, columns] = (grad_hidden * activated).astype(jnp.bfloat16)
                slope = sigmoid_gate * (1.0 + gate * (1.0 - sigmoid_gate))
                dgate[spot_rows, columns] = (grad_hidden * upward * slope).astype(jnp.bfloat16)
        result = (hidden_state + dot32(hid[rows, :], wd_ref[...])).T
        store_result(micro, result, out_ref, out1_ref)
        upstream = dot_with(dgate[rows, :], w_ref[:, :FF], 1, 1) + dot_with(
            dup[rows, :], w_ref[:, FF:], 1, 1
        )
        part, gain_grad = norm_back(hidden_state, scaling, gain, upstream, 1)
        gg_ref[...] += gain_grad
        grad_state = back.astype(jnp.float32) + part
        dh_low[rows, :] = grad_state.astype(jnp.bfloat16)
        grad_tall = grad_state.T
        dh_ref[micro] = grad_tall
        do_ref[...] = dot32(wo_ref[...], grad_tall.astype(jnp.bfloat16)).astype(jnp.bfloat16)
    c_parts = (c_slots.at[0], c_slots.at[1])
    for place, right in enumerate((dgate, dup, hid)):
        for side in range(COL_CUT):
            start = (side ^ lax.rem(spot, COL_CUT)) * CHUNK_COLS
            for column in range(0, CHUNK_COLS, block):
                columns = pl.ds(pl.multiple_of(start + column, block), block)
                if place < 2:
                    held[...] = dot32(n2_tall[...], right[:, columns])
                else:
                    held[...] = dot32(c_parts[0][...], right[:TOK, columns]) + dot32(
                        c_parts[1][...], right[TOK:, columns]
                    )
                for index, part in row_parts(held, spot, side):
                    out = (keep_ref, send_ref)[index // 4]
                    out[index % 4, place, :, column : column + block] = part
    gwo_ref[...] = (
        dot32(o0_ref[...], dh_low[:TOK, :]) + dot32(o1_ref[...], dh_low[TOK:, :])
    ).astype(jnp.bfloat16)


def mlp(tokens, tokens_1, cotangent, cotangent_1, mixed, w_out, w_gate_up, w_down, gain):
    rows = 2 * TOK
    low = jnp.bfloat16
    chunk_shape = (CHUNKS // 2, 3, CHUNK_ROWS, CHUNK_COLS)
    return pl.pallas_call(
        mlp_kernel,
        out_shape=(
            jax.ShapeDtypeStruct((2, D, TOK), jnp.float32),
            jax.ShapeDtypeStruct((D, TOK), low),
            jax.ShapeDtypeStruct((2, D, TOK), jnp.float32),
            jax.ShapeDtypeStruct((D, TOK), low),
            jax.ShapeDtypeStruct((D, TOK), low),
            jax.ShapeDtypeStruct(chunk_shape, low),
            jax.ShapeDtypeStruct(chunk_shape, low),
            jax.ShapeDtypeStruct((D, D), low),
            jax.ShapeDtypeStruct((1, D), jnp.float32),
        ),
        in_specs=[vmem()] * 10,
        out_specs=(vmem(),) * 9,
        scratch_shapes=[
            pltpu.VMEM((rows, FF), low),
            pltpu.VMEM((rows, FF), low),
            pltpu.VMEM((rows, FF), low),
            pltpu.VMEM((D, rows), low),
            pltpu.VMEM((rows, D), low),
            pltpu.VMEM((D, 256), jnp.float32),
            pltpu.VMEM((TOK, 256), jnp.float32),
            pltpu.VMEM((TOK, 256), jnp.float32),
            pltpu.VMEM((TOK, 256), jnp.float32),
            pltpu.VMEM((2, D, TOK), low),
        ],
        compiler_params=kernel_params,
        cost_estimate=pl.CostEstimate(
            flops=6 * rows * 3 * D * FF, bytes_accessed=25000000, transcendentals=rows * FF
        ),
        name="mlp",
    )(tokens, tokens_1, cotangent, cotangent_1, *mixed, w_out, w_gate_up, w_down, gain)


def natural_tiles(flat, base, rows, width):
    pairs, step, whole = rows // 2, width * 2 // 128, width // 128
    parts = [flat[pl.ds(base + place, pairs, stride=step), :] for place in range(step)]
    even = parts[:whole] + [parts[whole][:, :HEAD_DIM]]
    odd = jnp.concatenate([parts[whole][:, HEAD_DIM:]] + parts[whole + 1 :], axis=1)
    return even, [odd[:, low : low + 128] for low in range(0, width, 128)]


def unflatten(flat, base, rows, width, tiles):
    even, odd = natural_tiles(flat, base, rows, width)
    for place, (first, second) in enumerate(zip(even, odd)):
        breadth = first.shape[1]
        if breadth < 128:
            blank = jnp.zeros((rows // 2, 128 - breadth), jnp.float32)
            first = jnp.concatenate([first, blank], axis=1)
            second = jnp.concatenate([second, blank], axis=1)
        tiles[place, pl.ds(0, rows // 2, stride=2), :] = first
        tiles[place, pl.ds(1, rows // 2, stride=2), :] = second


def tile_widths(width):
    return [(place, low, min(128, width - low)) for place, low in enumerate(range(0, width, 128))]


MIXED = ((0, 0, D), (2592, D, KV_WIDTH), (3456, D + KV_WIDTH, KV_WIDTH), (4320, FF - D, D))


def project_kernel(
    near_ref, next_ref, x_ref, x1_ref, gain_ref, cos0_ref, sin0_ref, cos1_ref, sin1_ref,
    q0_ref, q1_ref, kv_ref, w_ref, wo_ref, n_ref, flat, tiles,
):
    spot = chunk_spot()
    length = flat.shape[0] // CHUNKS
    for index in range(CHUNKS):
        chunk = spot ^ index
        core, half, chip = lax.div(chunk, 4), lax.rem(lax.div(chunk, 2), 2), lax.rem(chunk, 2)
        start = pl.multiple_of((half * 4 + chip * 2 + core) * length, 8)
        part = (near_ref, next_ref)[index // 4][index % 4]
        flat[pl.ds(start, length), :] = part.astype(jnp.float32)
    for base, start, width in MIXED:
        unflatten(flat, base, D, width, tiles)
        for place, low, breadth in tile_widths(width):
            part = tiles[place][:D, :breadth].astype(jnp.bfloat16)
            if start < FF - D:
                w_ref[:, start + low : start + low + breadth] = part
            else:
                wo_ref[:, low : low + breadth] = part
    tall = w_ref[...].T
    half_width = HEAD_DIM // 2
    tables = ((q0_ref, cos0_ref, sin0_ref), (q1_ref, cos1_ref, sin1_ref))
    for micro, (q_ref, cos_ref, sin_ref) in enumerate(tables):
        values = (x1_ref if micro else x_ref)[...].astype(jnp.float32)
        normed = (values * norm_scaling(values, 0) * gain_ref[:, 0:1]).astype(jnp.bfloat16)
        n_ref[:, micro * TOK : (micro + 1) * TOK] = normed
        linear = dot32(tall, normed)
        cosine, sine = cos_ref[...], sin_ref[...]
        for head in range(HEADS + KV_HEADS):
            low = head * HEAD_DIM
            former = linear[low : low + half_width]
            latter = linear[low + half_width : low + HEAD_DIM]
            turned = jnp.concatenate(
                [former * cosine - latter * sine, latter * cosine + former * sine], axis=0
            ).astype(jnp.bfloat16)
            if head < HEADS:
                scaled = turned.astype(jnp.float32) * 0.125
                q_ref[head // GROUPS, head % GROUPS] = scaled.astype(jnp.bfloat16)
            else:
                low = low - D
                kv_ref[micro, low : low + HEAD_DIM, :] = turned
        kv_ref[micro, KV_WIDTH:, :] = linear[D + KV_WIDTH :].astype(jnp.bfloat16)


def project(near, following, tokens, tokens_1, gain_columns, tables):
    low = jnp.bfloat16
    return pl.pallas_call(
        project_kernel,
        out_shape=(
            jax.ShapeDtypeStruct(heads_shape, low),
            jax.ShapeDtypeStruct(heads_shape, low),
            jax.ShapeDtypeStruct((2, 2 * KV_WIDTH, TOK), low),
            jax.ShapeDtypeStruct((D, D + 2 * KV_WIDTH), low),
            jax.ShapeDtypeStruct((D, D), low),
            jax.ShapeDtypeStruct((D, 2 * TOK), low),
        ),
        in_specs=[vmem()] * 9,
        out_specs=(vmem(),) * 6,
        scratch_shapes=[
            pltpu.VMEM((D * FF // 128, 128), jnp.float32),
            pltpu.VMEM((5, D, 128), jnp.float32),
        ],
        compiler_params=kernel_params,
        cost_estimate=pl.CostEstimate(
            flops=4 * TOK * D * 960, bytes_accessed=8000000, transcendentals=0
        ),
        name="project",
    )(near, following, tokens, tokens_1, gain_columns, *tables[0], *tables[1])


def projection_kernel(
    n_ref, dq0_ref, dq1_ref, kept0_ref, kept1_ref, got_ref, far_ref,
    cos0_ref, sin0_ref, cos1_ref, sin1_ref, gwo_ref, tie_ref,
    keep_ref, send_ref, all_ref, held, cut,
):
    spot = chunk_spot()
    half_width = HEAD_DIM // 2
    parts = ((dq0_ref, kept0_ref, cos0_ref, sin0_ref), (dq1_ref, kept1_ref, cos1_ref, sin1_ref))
    for micro, (dq_ref, kept_ref, cos_ref, sin_ref) in enumerate(parts):
        columns = slice(micro * TOK, (micro + 1) * TOK)
        all_ref[:D, columns] = dq_ref[...]
        cosine, sine = cos_ref[...], sin_ref[...]
        summed = kept_ref[0].astype(jnp.float32) + got_ref[micro].astype(jnp.float32)
        if micro == 0:
            summed = summed + far_ref[...].astype(jnp.float32)
        for head in range(KV_HEADS):
            low = head * HEAD_DIM
            former = summed[low : low + half_width, :]
            latter = summed[low + half_width : low + HEAD_DIM, :]
            all_ref[D + low : D + low + half_width, columns] = (
                former * cosine + latter * sine
            ).astype(jnp.bfloat16)
            all_ref[D + low + half_width : D + low + HEAD_DIM, columns] = (
                latter * cosine - former * sine
            ).astype(jnp.bfloat16)
        all_ref[D + KV_WIDTH :, columns] = summed[KV_WIDTH:, :].astype(jnp.bfloat16)
    held[:, : D + 2 * KV_WIDTH] = dot_with(n_ref[...], all_ref[...], 1, 1)
    held[:, D + 2 * KV_WIDTH :] = gwo_ref[...].astype(jnp.float32)
    for side in range(COL_CUT):
        start = (side ^ lax.rem(spot, COL_CUT)) * CHUNK_COLS
        cut[...] = held[:, pl.ds(pl.multiple_of(start, CHUNK_COLS), CHUNK_COLS)]
        for index, part in row_parts(cut, spot, side):
            (keep_ref, send_ref)[index // 4][index % 4] = part


def projection_grads(normed, dqs, kept, got, far, tables, gwo, tie):
    rows = normed.shape[1]
    chunk_shape = (CHUNKS // 2, CHUNK_ROWS, CHUNK_COLS)
    return pl.pallas_call(
        projection_kernel,
        out_shape=(
            jax.ShapeDtypeStruct(chunk_shape, jnp.bfloat16),
            jax.ShapeDtypeStruct(chunk_shape, jnp.bfloat16),
            jax.ShapeDtypeStruct((D + 2 * KV_WIDTH, rows), jnp.bfloat16),
        ),
        in_specs=[vmem()] * 12 + [anywhere()],
        out_specs=(vmem(),) * 3,
        scratch_shapes=[
            pltpu.VMEM((D, FF), jnp.float32),
            pltpu.VMEM((D, CHUNK_COLS), jnp.float32),
        ],
        compiler_params=kernel_params,
        cost_estimate=pl.CostEstimate(
            flops=2 * rows * D * 960, bytes_accessed=8000000, transcendentals=0
        ),
        name="projection_grads",
    )(normed, *dqs, *kept, got, far, *tables[0], *tables[1], gwo, tie)


def both(left_ref, right_ref, where=...):
    total = left_ref[where].astype(jnp.float32) + right_ref[where].astype(jnp.float32)
    return total.astype(jnp.bfloat16)


def plain_call(kernel, outs, operands, ties, name):
    outs = [jax.ShapeDtypeStruct(shape, jnp.bfloat16) for shape in outs]
    ties = ties if isinstance(ties, tuple) else (ties,)
    count = len(operands)

    def run(*refs):
        kernel(*refs[: count + 1], *refs[count + len(ties) :])

    return pl.pallas_call(
        run,
        out_shape=outs,
        in_specs=[vmem()] * count + [anywhere()] * len(ties),
        out_specs=[vmem()] * len(outs),
        compiler_params=kernel_params,
        name=name,
    )(*operands, *ties)


def turns_kernel(keep_ref, got_ref, early_ref, tie_ref, *outs):
    quarter = positions()[0]
    for shift, out in enumerate(outs):
        target = lax.rem(quarter + shift, 4)

        @pl.when(target == 0)
        def _():
            out[...] = both(keep_ref, got_ref, 0)

        @pl.when(target != 0)
        def _():
            out[...] = early_ref[jnp.maximum(target - 1, 0)]


def depth_turns(keep, got, early, tie):
    return plain_call(turns_kernel, [keep.shape[1:]] * 4, (keep, got, early), tie, "depth_turns")


def sum_kernel(*refs):
    total = refs[0][...].astype(jnp.float32)
    for ref in refs[1:-2]:
        total = total + ref[...].astype(jnp.float32)
    refs[-1][...] = total.astype(jnp.bfloat16)


def tied_sum(operands, tie):
    return plain_call(sum_kernel, [operands[0].shape], operands, tie, "tied_sum")[0]


def late_kernel(keep_ref, got_ref, tie_ref, keep_out, send_out):
    size = keep_out.shape[0]
    keep_out[...] = both(keep_ref, got_ref, slice(0, size))
    send_out[...] = both(keep_ref, got_ref, slice(size, 2 * size))


def late_halves(keep, got, tie):
    shape = (keep.shape[0] // 2, *keep.shape[1:])
    return plain_call(late_kernel, [shape] * 2, (keep, got), tie, "late_halves")


def pair_kernel(first_ref, second_ref, tie_ref, out_ref):
    out_ref[:1] = first_ref[...]
    out_ref[1:] = second_ref[...]


def tied_pair(first, second, tie):
    shape = (3, *first.shape[1:])
    return plain_call(pair_kernel, [shape], (first, second), tie, "tied_pair")[0]


def pick_first_kernel(own_ref, got1_ref, got2_ref, got3_ref, tie_ref, out_ref):
    quarter = positions()[0]
    for place, ref in enumerate((own_ref, got1_ref, got2_ref, got3_ref)):

        @pl.when(quarter == place)
        def _():
            out_ref[...] = ref[...]


def pick_first(pieces, tie):
    return plain_call(pick_first_kernel, [pieces[0].shape], pieces, tie, "pick_first")[0]


def pick_rest_kernel(own_ref, got1_ref, got2_ref, got3_ref, tie_ref, gu_ref, d_ref):
    quarter = positions()[0]

    def run(flat, tiles):
        for place, out in ((1, gu_ref), (2, gu_ref), (3, d_ref)):
            for shift, ref in enumerate((own_ref, got1_ref, got2_ref, got3_ref)):

                @pl.when(lax.rem(quarter - place + 4, 4) == shift)
                def _():
                    flat[...] = ref[...].astype(jnp.float32)

            rows, width = out.shape
            if width > D:
                for tile in range(FF // 128):
                    low = (place - 1) * FF + tile * 128
                    out[:, low : low + 128] = flat[
                        pl.ds(tile, rows, stride=FF // 128), :
                    ].astype(jnp.bfloat16)
            else:
                unflatten(flat, 0, rows, width, tiles)
                for tile, low, breadth in tile_widths(width):
                    out[:, low : low + breadth] = tiles[tile][:, :breadth].astype(jnp.bfloat16)

    pl.run_scoped(
        run,
        pltpu.VMEM(own_ref.shape, jnp.float32),
        pltpu.VMEM((5, FF // CHUNKS, 128), jnp.float32),
    )


def pick_rest(pieces, tie):
    shapes = [(D // CHUNKS, 2 * FF), (FF // CHUNKS, D)]
    return plain_call(pick_rest_kernel, shapes, pieces, tie, "pick_rest")


def cast_kernel(value_ref, tie_ref, out_ref):
    out_ref[...] = value_ref[...].astype(out_ref.dtype)


def tied_cast(value, tie):
    return pl.pallas_call(
        cast_kernel,
        out_shape=jax.ShapeDtypeStruct(value.shape, jnp.bfloat16),
        in_specs=[vmem(), anywhere()],
        out_specs=vmem(),
        compiler_params=kernel_params,
        name="tied_cast",
    )(value, tie)


def inputs_kernel(
    all_ref, w_ref, x_ref, x1_ref, dh_ref, gain_ref, tie_ref, out_ref, out1_ref, gg_ref
):
    gain = gain_ref[:, 0:1]
    total = jnp.zeros((D, 1), jnp.float32)
    for micro in range(2):
        columns = slice(micro * TOK, (micro + 1) * TOK)
        upstream = dot32(w_ref[...], all_ref[:, columns])
        values = (x1_ref if micro else x_ref)[...].astype(jnp.float32)
        part, gain_grad = norm_back(values, norm_scaling(values, 0), gain, upstream, 0)
        total = total + gain_grad
        grad = dh_ref[micro] + part
        store_result(micro, grad, out_ref, out1_ref)
    gg_ref[...] = jnp.broadcast_to(total, gg_ref.shape)


def input_grads(grad_qkv, w_qkv, tokens, tokens_1, grad_state, gain_columns, tie):
    return pl.pallas_call(
        inputs_kernel,
        out_shape=(
            jax.ShapeDtypeStruct((2, D, TOK), jnp.float32),
            jax.ShapeDtypeStruct((D, TOK), jnp.bfloat16),
            jax.ShapeDtypeStruct((D, 128), jnp.float32),
        ),
        in_specs=[vmem()] * 6 + [anywhere()],
        out_specs=(vmem(),) * 3,
        compiler_params=kernel_params,
        cost_estimate=pl.CostEstimate(
            flops=4 * TOK * D * 960, bytes_accessed=8000000, transcendentals=0
        ),
        name="input_grads",
    )(grad_qkv, w_qkv, tokens, tokens_1, grad_state, gain_columns, tie)


def place_kernel(whole_ref, part_ref, tie_ref, out_ref):
    out_ref[0] = part_ref[...].astype(out_ref.dtype)


def place_last(whole, part, tie):
    return pl.pallas_call(
        place_kernel,
        out_shape=jax.ShapeDtypeStruct(whole.shape, whole.dtype),
        grid=(1,),
        in_specs=[anywhere(), pl.BlockSpec(part.shape, lambda step: (0, 0)), anywhere()],
        out_specs=pl.BlockSpec((1, *part.shape), lambda step: (1, 0, 0)),
        input_output_aliases={0: 0},
        compiler_params=kernel_params,
        name="place_last",
    )(whole, part, tie)


def newton_loop(matrix, scale):
    current = matrix / (jnp.sqrt(jnp.sum(matrix * matrix)) + frobenius_epsilon)

    def iterate(unused, held):
        low = held.astype(jnp.bfloat16)
        square = dot_with(low, low, 1, 1)
        square_low = square.astype(jnp.bfloat16)
        mixer = newton_second * square + newton_third * dot32(square_low, square_low)
        return newton_first * held + dot32(mixer.astype(jnp.bfloat16), low)

    return lax.fori_loop(0, NS_STEPS, iterate, current) * (0.2 * math.sqrt(scale))


def newton_wide(total):
    def run(low, square, square_low, mixer, step):
        height, breadth = total.shape
        block = 256

        def scale_by(factor, keep_low):
            for row in range(0, height, 16):
                part = total[row : row + 16, :] * factor
                total[row : row + 16, :] = part
                if keep_low:
                    low[row : row + 16, :] = part.astype(jnp.bfloat16)

        norm = jnp.zeros((8, breadth), jnp.float32)
        for row in range(0, height, 8):
            part = total[row : row + 8, :]
            norm = norm + part * part
        scale_by(1.0 / (jnp.sqrt(jnp.sum(norm)) + frobenius_epsilon), True)

        def iterate(unused, held):
            square[...] = dot_with(low[...], low[...], 1, 1)
            for row in range(0, height, 16):
                rows = slice(row, row + 16)
                square_low[rows, :] = square[rows, :].astype(jnp.bfloat16)
            step[:, :height] = dot32(square_low[...], square_low[...])
            for row in range(0, height, 16):
                rows = slice(row, row + 16)
                mixed = newton_second * square[rows, :] + newton_third * step[rows, :height]
                mixer[rows, :] = mixed.astype(jnp.bfloat16)
            for column in range(0, breadth, block):
                columns = slice(column, column + block)
                step[:, :block] = dot32(mixer[...], low[:, columns])
                for row in range(0, height, 32):
                    rows = slice(row, row + 32)
                    part = newton_first * total[rows, columns] + step[rows, :block]
                    total[rows, columns] = part
                    low[rows, columns] = part.astype(jnp.bfloat16)
            return held

        lax.fori_loop(0, NS_STEPS, iterate, 0)
        scale_by(0.2 * math.sqrt(breadth), False)

    height, breadth = total.shape
    pl.run_scoped(
        run,
        pltpu.VMEM((height, breadth), jnp.bfloat16),
        pltpu.VMEM((height, height), jnp.float32),
        pltpu.VMEM((height, height), jnp.bfloat16),
        pltpu.VMEM((height, height), jnp.bfloat16),
        pltpu.VMEM((height, height), jnp.float32),
    )


def flatten_rows(tiles, start, rows, width, out):
    pairs, step, whole = rows // 2, width * 2 // 128, width // 128
    spans = range(whole + 1)
    even = [tiles[place, pl.ds(start, pairs, stride=2), :] for place in spans]
    odd = [tiles[place, pl.ds(start + 1, pairs, stride=2), :] for place in spans]
    for place in range(whole):
        out[pl.ds(place, pairs, stride=step), :] = even[place]
    rest = width - whole * 128
    joined = jnp.concatenate([even[whole][:, :rest]] + odd[:whole] + [odd[whole][:, :rest]], axis=1)
    for place in range(whole, step):
        low = (place - whole) * 128
        out[pl.ds(place, pairs, stride=step), :] = joined[:, low : low + 128]


def shard_rows(kind, kinds, start, matrix, tiles, out):
    length = out.shape[0] * 128

    if 0 in kinds:

        @pl.when(kind == 0)
        def _():
            rows = length // FF
            for place in range(FF // 128):
                out[pl.ds(place, rows, stride=FF // 128), :] = matrix[
                    pl.ds(pl.multiple_of(start, 8), rows), place * 128 : (place + 1) * 128
                ]

        @pl.when(kind == 5)
        def _():
            for place, low, breadth in tile_widths(D):
                tiles[place, :, :breadth] = matrix[low : low + breadth, :].T
            flatten_rows(tiles, start, length // D, D, out)

    for place, (base, low, width) in zip((1, 3, 4, 2), MIXED):
        if place not in kinds:
            continue

        @pl.when(kind == place)
        def _():
            for tile, column, breadth in tile_widths(width):
                tiles[tile, :D, :breadth] = matrix[:, low + column : low + column + breadth]
            flatten_rows(tiles, start, length // width, width, out)


def own_kind(length):
    square, narrow = D * D, D * KV_WIDTH
    quarter = lax.axis_index("quarter")
    index = lax.axis_index("rep") * 2 + lax.axis_index("half")
    within = (index * lax.axis_size("ctx") + lax.axis_index("ctx")) * length
    kind = jnp.where(quarter == 3, 5, 0)
    start = jnp.where(quarter == 3, lax.div(within, D), lax.div(within, FF))
    edges = ((0, 1, D), (square, 3, KV_WIDTH), (square + narrow, 4, KV_WIDTH))
    for edge, place, width in (*edges, (square + 2 * narrow, 2, D)):
        inside = (quarter == 0) & (within >= edge)
        kind = jnp.where(inside, place, kind)
        start = jnp.where(inside, lax.div(within - edge, width), start)
    return (kind, start)


def load_matrix(kind, old_ref, flat, total, tiles):
    flat[...] = old_ref[...].astype(jnp.float32) * momentum_decay

    @pl.when(kind == 0)
    def _():
        for place in range(FF // 128):
            columns = slice(place * 128, (place + 1) * 128)
            total[:, columns] = flat[pl.ds(place, D, stride=FF // 128), :]

    @pl.when(kind == 5)
    def _():
        unflatten(flat, 0, FF, D, tiles)
        for place, low, breadth in tile_widths(D):
            total[low : low + breadth, :] = tiles[place].T[:breadth]

    for place, (base, low, width) in zip((1, 3, 4, 2), MIXED):

        @pl.when(kind == place)
        def _():
            unflatten(flat, base, D, width, tiles)
            for tile, column, breadth in tile_widths(width):
                total[:, low + column : low + column + breadth] = tiles[tile][:D, :breadth]


def update_matrix(kind, kinds, total):
    if 0 in kinds:

        @pl.when((kind == 0) | (kind == 5))
        def _():
            newton_wide(total)

    for place, (base, low, width) in zip((1, 3, 4, 2), MIXED):
        if place not in kinds:
            continue

        @pl.when(kind == place)
        def _():
            columns = slice(low, low + width)
            if width == D:
                total[:, columns] = newton_loop(total[:, columns], D)
            else:
                total[:, columns] = newton_loop(total[:, columns].T, D).T


def momentum_kernel(length, old_ref, tie_ref, out_ref, flat, tiles):
    kind = own_kind(length)[0]
    load_matrix(kind, old_ref, flat, out_ref, tiles)


def lay_momentum(length, old, tie):
    return pl.pallas_call(
        partial(momentum_kernel, length),
        out_shape=jax.ShapeDtypeStruct((D, FF), jnp.float32),
        in_specs=[vmem(), anywhere()],
        out_specs=vmem(),
        scratch_shapes=[
            pltpu.VMEM((D * FF // 128, 128), jnp.float32),
            pltpu.VMEM((5, FF, 128), jnp.float32),
        ],
        compiler_params=kernel_params,
        name="lay_momentum",
    )(old, tie)


def newton_kernel(local, length, *refs):
    count = 3 if local else 2
    grad, total, tiles = refs[-3:]
    outs = refs[-3 - count : -3]
    pieces, (old_ref, *rest) = refs[:2], refs[2:-3]
    kind, start = own_kind(length)
    spot = chunk_spot()

    def run():
        for index in range(CHUNKS):
            chunk = spot ^ index
            row = pl.multiple_of(lax.div(chunk, COL_CUT) * CHUNK_ROWS, CHUNK_ROWS)
            column = pl.multiple_of(lax.rem(chunk, COL_CUT) * CHUNK_COLS, CHUNK_COLS)
            rows, columns = pl.ds(row, CHUNK_ROWS), pl.ds(column, CHUNK_COLS)
            part = pieces[index // 4][index % 4]
            grad[rows, columns] = part.astype(jnp.float32)
            total[rows, columns] = old_ref[rows, columns] + part.astype(jnp.float32)
        kinds = (0, 1, 2, 3, 4, 5)
        update_matrix(kind, kinds, total)
        if local:
            weights_ref, momentum_ref = rest[:2]
            grad_ref, new_momentum_ref, new_weights_ref = outs
            shard_rows(kind, kinds, start, grad, tiles, grad_ref)
            shard_rows(kind, kinds, start, total, tiles, new_weights_ref)
            new_momentum_ref[...] = momentum_decay * momentum_ref[...] + grad_ref[...]
            new_weights_ref[...] = (
                weights_ref[...] * (1.0 - matrix_rate * weight_decay)
                - matrix_rate * new_weights_ref[...]
            )
        else:
            outs[0][...] = grad[...]
            outs[1][...] = total[...]

    run()


def newton(length, pieces, old, shards):
    local = len(shards) > 0
    if local:
        outs = (jax.ShapeDtypeStruct(shards[0].shape, jnp.float32),) * 3
    else:
        outs = (jax.ShapeDtypeStruct((D, FF), jnp.float32),) * 2
    operands = (*pieces, old, *shards)

    return pl.pallas_call(
        partial(newton_kernel, local, length),
        out_shape=outs,
        in_specs=[vmem()] * len(operands),
        out_specs=(vmem(),) * len(outs),
        scratch_shapes=[
            pltpu.VMEM((D, FF), jnp.float32),
            pltpu.VMEM((D, FF), jnp.float32),
            pltpu.VMEM((5, FF, 128), jnp.float32),
        ],
        compiler_params=kernel_params,
        cost_estimate=pl.CostEstimate(
            flops=12000000000, bytes_accessed=9000000, transcendentals=0
        ),
        name="newton",
    )(*operands)


def own_rows(kind, row, shard_length, gradient, update):
    def block_case(low, width):
        def run(gradient, update):
            start = (row, low)
            size = (shard_length // width, width)
            return tuple(
                lax.dynamic_slice(whole, start, size).reshape(-1) for whole in (gradient, update)
            )

        return run

    def tall_case(gradient, update):
        start = (0, row)
        size = (D, shard_length // D)
        return tuple(
            lax.dynamic_slice(whole, start, size).T.reshape(-1) for whole in (gradient, update)
        )

    cases = [
        block_case(0, FF),
        block_case(0, D),
        block_case(FF - D, D),
        block_case(D, KV_WIDTH),
        block_case(D + KV_WIDTH, KV_WIDTH),
        tall_case,
    ]
    return lax.switch(kind, cases, gradient, update)


CORE_SWAP = [(0, 1), (1, 0), (2, 3), (3, 2)]
CHIP_SWAP = [(0, 2), (2, 0), (1, 3), (3, 1)]
SIDE_SWAP = [(0, 1), (1, 0)]
END_SWAP = [(0, 3), (3, 0), (1, 2), (2, 1)]


def plane_swap(value, bit):
    axis, swap = (("ctx", CHIP_SWAP), ("half", SIDE_SWAP), ("ctx", CORE_SWAP))[bit]
    return lax.ppermute(value, axis, swap)


def low_sum(left, right):
    return (left.astype(jnp.float32) + right.astype(jnp.float32)).astype(jnp.bfloat16)


def low_total(first, others):
    total = first.astype(jnp.float32)
    for part in others:
        total = total + part.astype(jnp.float32)
    return total.astype(jnp.bfloat16)


def plane_gather(piece, swap):
    pieces = piece[None]
    for bit in range(2):
        pieces = jnp.concatenate([pieces, swap(pieces, bit)], axis=0)
    return (pieces, swap(pieces, 2))


def depth_shift(value, shift, targets):
    pairs = [(place, (place + shift) % 4) for place in range(4)]
    return lax.ppermute(value, "quarter", [pair for pair in pairs if pair[1] in targets])


def gather_weights(low, tie):
    if lax.axis_size("rep") > 1:
        full = lax.all_gather(low, EVERY, axis=0, tiled=True).reshape(4, D * FF)
        ctx = lax.axis_index("ctx")
        spot = lax.rem(ctx, 2) * 4 + lax.axis_index("half") * 2 + ctx // 2
        chunk = jnp.arange(CHUNKS, dtype=jnp.int32) ^ spot
        order = 4 * (chunk // 2 % 2) + 2 * (chunk % 2) + chunk // 4
        mixed = full[0].reshape(CHUNKS, -1, 128)[order]
        return (mixed[:4], mixed[4:]), [
            jnp.concatenate([full[1].reshape(D, FF), full[2].reshape(D, FF)], axis=1),
            full[3].reshape(FF, D),
        ]
    first = [lax.ppermute(low, "quarter", [(0, shift)]) for shift in range(1, 4)]
    mixed = pick_first((low, *first), tie)
    others = [
        lax.ppermute(low, "quarter", [(place, (place + shift) % 4) for place in range(1, 4)])
        for shift in range(1, 4)
    ]
    near = mixed[None]
    near = jnp.concatenate([near, plane_swap(near, 0)], axis=0)
    rest = [
        lax.all_gather(piece, PLANE, axis=0, tiled=True)
        for piece in pick_rest((low, *others), near)
    ]
    near = jnp.concatenate([near, plane_swap(near, 1)], axis=0)
    return (near, plane_swap(near, 2)), rest


def per_device(tokens, lengths, weights, momentum, norm_gains, gain_first, gain_second, cotangent):
    ctx = lax.axis_index("ctx")
    chip = ctx // 2
    reps = lax.axis_size("rep")
    shard_length = weights.shape[0]
    flat_shape = (shard_length // 128, 128)
    lengths = lengths[:, 0]
    tokens = jnp.swapaxes(tokens, 1, 2)
    cotangent = jnp.swapaxes(cotangent, 1, 2)
    gain_columns = norm_gains.T

    tokens_1 = lax.ppermute(tokens[1], "ctx", END_SWAP)
    mixed_weights, (w_gate_up, w_down) = gather_weights(
        weights.reshape(flat_shape).astype(jnp.bfloat16), tokens_1
    )
    near = chip == 0

    def slots(first, second):
        return jnp.where(near, first, second), jnp.where(near, second, first)

    x0, x1 = slots(tokens[0], tokens_1)
    begin_rows, tables = [], []
    for micro, own_lengths in enumerate(slots(lengths[0], lengths[1])):
        own_places = own_block(micro) * TOK + jnp.arange(TOK, dtype=jnp.int32)
        offsets, begins = layout(own_lengths, own_places)
        begin_rows.append(begins.reshape(1, TOK))
        tables.append(rope_tables(offsets))

    q0, q1, keyvals, w_qkv, w_out, normed = project(
        *mixed_weights, x0, x1, gain_columns, tables
    )
    queries = (q0, q1)
    far = lax.ppermute(keyvals[0], "ctx", CHIP_SWAP)
    keyvals = (
        keyvals,
        lax.ppermute(keyvals, "ctx", CORE_SWAP),
        far,
        lax.ppermute(far, "ctx", CORE_SWAP),
    )
    mixed, log_totals = [], []
    for micro in range(2):
        mixed_one, log_total = attend_forward(
            micro, lengths, queries[micro], keyvals, begin_rows[micro], norm_gains
        )
        mixed.append(mixed_one)
        log_totals.append(log_total)
    cotangent_1 = lax.ppermute(tied_cast(cotangent[1], mixed[0]), "ctx", END_SWAP)
    old = lax.all_gather(
        tied_cast(momentum.reshape(flat_shape), mixed[0]),
        ("rep", "half", "ctx"),
        axis=0,
        tiled=True,
    )
    outs = mlp(
        x0,
        x1,
        cotangent,
        cotangent_1,
        [part.reshape(D, TOK) for part in mixed],
        w_out,
        w_gate_up,
        w_down,
        norm_gains[1:2],
    )
    result, result_1, grad_state, grad_mixed_0, grad_mixed_1 = outs[:5]
    keep, send, grad_w_out, gain_two_grad = outs[5:]
    returned = lax.ppermute(result_1, "ctx", END_SWAP)

    def back_pass(micro, grad_mixed, tie):
        return attend_back(
            micro,
            lengths,
            queries[micro],
            keyvals,
            begin_rows[micro],
            mixed[micro],
            log_totals[micro],
            grad_mixed.reshape(heads_shape),
            *tables[micro],
            tie,
        )

    got = plane_swap(send, 2)
    dq0, kept0, sent0 = back_pass(0, grad_mixed_0, norm_gains)
    keep, send = late_halves(keep, got, dq0)
    got = plane_swap(send, 1)
    dq1, kept1, sent1 = back_pass(1, grad_mixed_1, keep)
    keep, send = late_halves(keep, got, (dq1, old, returned))
    traded = lax.ppermute(tied_pair(sent0, sent1, keep), "ctx", CORE_SWAP)
    crossed = lax.ppermute(low_sum(kept1[1], traded[2]), "ctx", CHIP_SWAP)
    got = plane_swap(send, 0)
    late_keep, late_send, grad_qkv = projection_grads(
        normed,
        (dq0.reshape(D, TOK), dq1.reshape(D, TOK)),
        (kept0, kept1),
        traded,
        crossed,
        tables,
        grad_w_out,
        keep,
    )
    late_got = plane_swap(late_send, 2)
    late_keep, late_send = late_halves(late_keep, late_got, norm_gains)
    late_got = plane_swap(late_send, 1)
    grad_inputs, grad_inputs_1, gain_one_grad = input_grads(
        grad_qkv, w_qkv, x0, x1, grad_state, gain_columns, late_keep
    )
    early = tied_sum((keep[0], got[0]), gain_one_grad)
    late_keep, late_send = late_halves(late_keep, late_got, early)
    gain_grad = jnp.concatenate([gain_one_grad[:, 0].reshape(1, D), gain_two_grad], axis=0)
    gain_grad = gain_grad + sum(
        lax.ppermute(gain_grad, "ctx", [(place, place ^ turn) for place in range(4)])
        for turn in range(1, 4)
    )
    piece, *turns = depth_turns(late_keep, plane_swap(late_send, 0), early, gain_grad)
    parts = [depth_shift(turn, shift, range(4)) for shift, turn in enumerate(turns, start=1)]
    gain_grad = gain_grad + sum(depth_shift(gain_grad, shift, range(4)) for shift in range(1, 4))
    old = lay_momentum(shard_length, old, piece)
    piece = tied_sum((piece, *parts), (old, gain_grad))
    if reps > 1:
        piece = lax.psum(piece, "rep")
        gain_grad = lax.psum(gain_grad, "rep")
    pieces = plane_gather(piece, plane_swap)
    gain_grad = gain_grad + plane_swap(gain_grad, 1)
    grad_inputs_1 = lax.ppermute(grad_inputs_1, "ctx", END_SWAP)

    shards = ()
    if flat_shape[0] % 8 == 0:
        shards = (weights.reshape(flat_shape), momentum.reshape(flat_shape))
    outs = newton(shard_length, pieces, old, shards)
    if len(shards) > 0:
        grad_shard, new_momentum, new_weights = [out.reshape(weights.shape) for out in outs]
    else:
        kind, start = own_kind(shard_length)
        grad_shard, update_shard = own_rows(kind, start, shard_length, *outs)
        new_momentum = momentum_decay * momentum + grad_shard
        new_weights = weights * (1.0 - matrix_rate * weight_decay) - matrix_rate * update_shard

    def placed(whole, part):
        whole = lax.dynamic_update_index_in_dim(whole, part.astype(jnp.float32), 1, 0)
        return jnp.swapaxes(whole, 1, 2)

    first_new = first_decay * gain_first + (1.0 - first_decay) * gain_grad
    second_new = second_decay * gain_second + (1.0 - second_decay) * gain_grad * gain_grad
    debiased_first_moment = first_new / (1.0 - first_decay**ADAM_STEP)
    corrected_second = second_new / (1.0 - second_decay**ADAM_STEP)
    new_gains = norm_gains * (
        1.0 - gain_rate * weight_decay
    ) - gain_rate * debiased_first_moment / (jnp.sqrt(corrected_second) + adam_epsilon)
    return (
        placed(result, returned),
        jnp.swapaxes(place_last(grad_inputs, grad_inputs_1, outs[-1]), 1, 2),
        grad_shard,
        new_momentum,
        new_weights,
        first_new,
        second_new,
        new_gains,
    )


def solution(mesh):
    devices = mesh.devices
    count = devices.size
    context = mesh.shape["ctx"]
    split = Mesh(
        devices.reshape(4, count // (8 * context), 2, context), ("quarter", "rep", "half", "ctx")
    )
    rows = P(None, EVERY, None)
    flat = P(EVERY)
    placed = (rows, P(None, ("quarter", "rep", "half"), None), flat, flat, P(), P(), P(), rows)
    return jax.shard_map(
        per_device,
        mesh=split,
        in_specs=placed,
        out_specs=(rows, rows, flat, flat, flat, P(), P(), P()),
        check_vma=False,
    )
```

```python
from functools import partial
import math

import jax
import jax.numpy as jnp
from jax import lax
from jax.experimental import pallas as pl
from jax.experimental.pallas import tpu as pltpu
from jax.sharding import Mesh, PartitionSpec as P

HEADS = 9
KV_HEADS = 3
HEAD_DIM = 64
FF = 1536
NS_STEPS = 5
ADAM_STEP = 10
D = 576
KV_WIDTH = 192
GROUPS = HEADS // KV_HEADS
TOK = 512
TILE = 256
COLS = GROUPS * TILE
ROW_CUT = 4
COL_CUT = 2
CHUNKS = ROW_CUT * COL_CUT
CHUNK_ROWS = D // ROW_CUT
CHUNK_COLS = FF // COL_CUT
PLANE = ("half", "ctx")
EVERY = ("quarter", "rep", "half", "ctx")


norm_epsilon = 1e-05
rope_base = 100000.0
masked_score = -1e30
newton_first = 3.4445
newton_second = -4.775
newton_third = 2.0315
momentum_decay = 0.95
matrix_rate = 0.2
weight_decay = 0.1
gain_rate = 0.2
first_decay = 0.9
second_decay = 0.95
adam_epsilon = 1e-08
frobenius_epsilon = 1e-07


def layout(lengths_row, places):
    finish = jnp.cumsum(lengths_row)
    firsts = finish - lengths_row
    begins = jnp.max(jnp.where(places[:, None] >= firsts[None, :], firsts[None, :], 0), axis=1)
    return (places - begins, begins)


def rope_tables(offsets):
    half_width = HEAD_DIM // 2
    inverse = jnp.exp(
        jnp.arange(half_width, dtype=jnp.float32) * (-2.0 * math.log(rope_base) / HEAD_DIM)
    )
    angles = inverse[:, None] * offsets.astype(jnp.float32)[None, :]
    return (jnp.cos(angles), jnp.sin(angles))


def dot32(left, right):
    return jnp.dot(left, right, preferred_element_type=jnp.float32)


def masked(scores, key_block, begins, places):
    keys = key_block * TILE + lax.broadcasted_iota(jnp.int32, scores.shape, 0)
    return jnp.where((keys >= begins) & (keys <= places), scores, masked_score)


def tile_row(row, tile):
    part = row[:, tile * TILE : (tile + 1) * TILE]
    return jnp.concatenate([part] * GROUPS, axis=1)


def tile_heads(ref, group, tile):
    return jnp.concatenate(
        [ref[group, head, :, tile * TILE : (tile + 1) * TILE] for head in range(GROUPS)], axis=1
    )


def positions():
    ctx = lax.axis_index("ctx")
    return (lax.axis_index("quarter"), lax.axis_index("half"), lax.div(ctx, 2), lax.rem(ctx, 2))


def chunk_spot():
    _, half, chip, core = positions()
    return core * 4 + half * 2 + chip


def first_key(lengths_ref, slot, row):
    micro = slot ^ positions()[2]
    begin = jnp.int32(0)
    first = jnp.int32(0)
    for place in range(3):
        first = first + lengths_ref[micro, place]
        begin = jnp.where(row >= first, first, begin)
    return begin


def key_loop(lengths_ref, slot, own, tile, load, process, carry):
    last = own * (TOK // TILE) + tile
    first = lax.div(first_key(lengths_ref, slot, last * TILE), TILE)
    full = lax.div(first_key(lengths_ref, slot, last * TILE + TILE - 1) + TILE - 1, TILE)
    full = jnp.minimum(full, last)
    pairs = lax.div(last - full, 2)

    def alone(block, held):
        load(0, block)
        return process(0, True, block, held)

    def couple(pair, held):
        block = full + 2 * pair
        load(1, block + 1)
        held = process(0, False, block, held)
        load(0, block + 2)
        return process(1, False, block + 1, held)

    def single(block, held):
        held = process(0, False, block, held)
        load(0, last)
        return held

    carry = lax.fori_loop(first, full, alone, carry)
    load(0, full)
    carry = lax.fori_loop(0, pairs, couple, carry)
    carry = lax.fori_loop(full + 2 * pairs, last, single, carry)
    return process(0, True, last, carry)


def plain_key_loop(lengths_ref, micro, own, tile, step, carry):
    last = own * (TOK // TILE) + tile
    first = lax.div(first_key(lengths_ref, micro, last * TILE), TILE)
    full = lax.div(first_key(lengths_ref, micro, last * TILE + TILE - 1) + TILE - 1, TILE)
    full = jnp.minimum(full, last)
    pairs = lax.div(last - full, 2)
    carry = lax.fori_loop(first, full, partial(step, True, 1), carry)
    carry = lax.fori_loop(
        0, pairs, lambda pair, held: step(False, 2, full + 2 * pair, held), carry
    )
    carry = lax.fori_loop(full + 2 * pairs, last, partial(step, False, 1), carry)
    return step(True, 1, last, carry)


def key_rows(block):
    return pl.ds(pl.multiple_of(block * TILE, TILE), TILE)


def own_block(slot):
    ctx = lax.axis_index("ctx")
    return jnp.maximum(ctx, 3 - ctx) if slot else jnp.minimum(ctx, 3 - ctx)


def key_slots(own, micro, kv_ref, other_ref, far_ref, far_other_ref):
    refs = (kv_ref.at[micro], other_ref.at[micro], far_ref, far_other_ref)[: 2 + 2 * micro]
    return [(own ^ place, ref) for place, ref in enumerate(refs)]


def block_rows(block):
    return pl.ds(pl.multiple_of(block * TOK, TOK), TOK)


def forward_kernel(
    micro, lengths_ref, q_ref, kv_ref, other_ref, far_ref, far_other_ref, begin_ref, tie_ref,
    o_ref, lse_ref, k_nat, v_ext, s_ref, p_ref,
):
    own = own_block(micro)
    for block, source in key_slots(own, micro, kv_ref, other_ref, far_ref, far_other_ref):

        @pl.when(block <= own)
        def _():
            rows = block_rows(block)
            for group in range(KV_HEADS):
                low = HEAD_DIM * group
                k_nat[group, rows, :] = source[low : low + HEAD_DIM, :].T
                low = low + KV_WIDTH
                v_ext[group, :HEAD_DIM, rows] = source[low : low + HEAD_DIM, :]
                v_ext[group, HEAD_DIM:, rows] = jnp.ones((16, TOK), jnp.bfloat16)

    def one_group(group, unused):
        for tile in range(TOK // TILE):
            queries = tile_heads(q_ref, group, tile)
            begins = tile_row(begin_ref[...], tile)
            column = lax.broadcasted_iota(jnp.int32, (1, COLS), 1)
            places = own * TOK + tile * TILE + lax.rem(column, TILE)

            def load(side, block):
                s_ref[side] = dot32(k_nat[group, key_rows(block), :], queries)

            def process(side, is_masked, block, carry):
                top, total = carry
                scores_ref, probs_ref = s_ref.at[side], p_ref.at[side]
                if is_masked:
                    scores_ref[...] = masked(scores_ref[...], block, begins, places)
                highest = scores_ref[:16]
                for low in range(16, TILE, 16):
                    highest = jnp.maximum(highest, scores_ref[low : low + 16])
                new_top = jnp.maximum(top, jnp.max(highest, axis=0, keepdims=True))
                for low in range(0, TILE, 16):
                    rows = slice(low, low + 16)
                    probs_ref[rows] = jnp.exp(scores_ref[rows] - new_top).astype(jnp.bfloat16)
                total = total * jnp.exp(top - new_top) + dot32(
                    v_ext[group, :, key_rows(block)], probs_ref[...]
                )
                return (new_top, total)

            carry = (
                jnp.full((1, COLS), masked_score, jnp.float32),
                jnp.zeros((HEAD_DIM + 16, COLS), jnp.float32),
            )
            top, total = key_loop(lengths_ref, micro, own, tile, load, process, carry)
            weight = total[HEAD_DIM : HEAD_DIM + 1, :]
            mixed = (total[:HEAD_DIM, :] / weight).astype(jnp.bfloat16)
            log_total = top + jnp.log(weight)
            for head in range(GROUPS):
                o_ref[group, head, :, tile * TILE : (tile + 1) * TILE] = mixed[
                    :, head * TILE : (head + 1) * TILE
                ]
                lse_ref[group, head, :, tile * TILE : (tile + 1) * TILE] = log_total[
                    :, head * TILE : (head + 1) * TILE
                ]
        return unused

    lax.fori_loop(0, KV_HEADS, one_group, 0)


def backward_kernel(
    micro, lengths_ref, q_ref, kv_ref, other_ref, far_ref, far_other_ref, begin_ref, o_ref, lse_ref,
    do_ref, cos_ref, sin_ref, tie_ref,
    dq_ref, keep_ref, send_ref, k_nat, v_nat, k_tall, dk_ref, dv_ref, s_ref, g_ref, p_ref, ds_ref,
):
    own = own_block(micro)
    slots = key_slots(own, micro, kv_ref, other_ref, far_ref, far_other_ref)
    for block, source in slots:

        @pl.when(block <= own)
        def _():
            rows = block_rows(block)
            for group in range(KV_HEADS):
                low = HEAD_DIM * group
                k_nat[group, rows, :] = source[low : low + HEAD_DIM, :].T
                k_tall[group, :, rows] = source[low : low + HEAD_DIM, :]
                low = low + KV_WIDTH
                v_nat[group, rows, :] = source[low : low + HEAD_DIM, :].T
                dk_ref[group, rows, :] = jnp.zeros((TOK, HEAD_DIM), jnp.float32)
                dv_ref[group, rows, :] = jnp.zeros((TOK, HEAD_DIM), jnp.float32)

    def one_group(group, unused):
        for tile in range(TOK // TILE):
            queries = tile_heads(q_ref, group, tile)
            upstream = tile_heads(do_ref, group, tile)
            mixed = tile_heads(o_ref, group, tile)
            log_total = tile_heads(lse_ref, group, tile)
            delta = jnp.sum(
                upstream.astype(jnp.float32) * mixed.astype(jnp.float32), axis=0, keepdims=True
            )
            queries_nat = queries.T
            upstream_nat = upstream.T
            begins = tile_row(begin_ref[...], tile)
            column = lax.broadcasted_iota(jnp.int32, (1, COLS), 1)
            places = own * TOK + tile * TILE + lax.rem(column, TILE)

            def step(is_masked, width, key_block, dq):
                rows = pl.ds(pl.multiple_of(key_block * TILE, TILE), width * TILE)
                count = width * TILE
                scores = dot32(k_nat[group, rows, :], queries)
                s_ref[:count] = masked(scores, key_block, begins, places) if is_masked else scores
                g_ref[:count] = dot32(v_nat[group, rows, :], upstream)
                for low in range(0, count, 16):
                    part = slice(low, low + 16)
                    probs = jnp.exp(s_ref[part] - log_total)
                    p_ref[part] = probs.astype(jnp.bfloat16)
                    ds_ref[part] = (probs * (g_ref[part] - delta)).astype(jnp.bfloat16)
                dv_ref[group, rows, :] += dot32(p_ref[:count], upstream_nat)
                dk_ref[group, rows, :] += dot32(ds_ref[:count], queries_nat)
                return dq + dot32(k_tall[group, :, rows], ds_ref[:count])

            dq = jnp.zeros((HEAD_DIM, COLS), jnp.float32)
            dq = plain_key_loop(lengths_ref, micro, own, tile, step, dq) * 0.125
            half_width = HEAD_DIM // 2
            cosine = tile_row(cos_ref[...], tile)
            sine = tile_row(sin_ref[...], tile)
            former, latter = dq[:half_width], dq[half_width:]
            turned = jnp.concatenate(
                [former * cosine + latter * sine, latter * cosine - former * sine], axis=0
            ).astype(jnp.bfloat16)
            for head in range(GROUPS):
                dq_ref[group, head, :, tile * TILE : (tile + 1) * TILE] = turned[
                    :, head * TILE : (head + 1) * TILE
                ]
        return unused

    lax.fori_loop(0, KV_HEADS, one_group, 0)
    for place, (block, _) in enumerate(slots):
        out_ref = (keep_ref, send_ref)[place % 2]

        @pl.when(block <= own)
        def _():
            rows = block_rows(block)
            for group in range(KV_HEADS):
                low = HEAD_DIM * group
                out_ref[place // 2, low : low + HEAD_DIM, :] = dk_ref[group, rows, :].T.astype(
                    jnp.bfloat16
                )
                low = low + KV_WIDTH
                out_ref[place // 2, low : low + HEAD_DIM, :] = dv_ref[group, rows, :].T.astype(
                    jnp.bfloat16
                )

        @pl.when(block > own)
        def _():
            out_ref[place // 2] = jnp.zeros((2 * KV_WIDTH, TOK), jnp.bfloat16)


def vmem():
    return pl.BlockSpec(memory_space=pltpu.VMEM)


def smem():
    return pl.BlockSpec(memory_space=pltpu.SMEM)


def anywhere():
    return pl.BlockSpec(memory_space=pl.ANY)


kernel_params = pltpu.CompilerParams(vmem_limit_bytes=56 * 1024 * 1024)
heads_shape = (KV_HEADS, GROUPS, HEAD_DIM, TOK)


def attend_forward(micro, lengths, queries, keyvals, begins, tie):
    return pl.pallas_call(
        partial(forward_kernel, micro),
        out_shape=(
            jax.ShapeDtypeStruct(heads_shape, jnp.bfloat16),
            jax.ShapeDtypeStruct((KV_HEADS, GROUPS, 1, TOK), jnp.float32),
        ),
        in_specs=[smem()] + [vmem()] * 6 + [anywhere()],
        out_specs=(vmem(), vmem()),
        scratch_shapes=[
            pltpu.VMEM((KV_HEADS, 4 * TOK, HEAD_DIM), jnp.bfloat16),
            pltpu.VMEM((KV_HEADS, HEAD_DIM + 16, 4 * TOK), jnp.bfloat16),
            pltpu.VMEM((2, TILE, COLS), jnp.float32),
            pltpu.VMEM((2, TILE, COLS), jnp.bfloat16),
        ],
        compiler_params=kernel_params,
        cost_estimate=pl.CostEstimate(
            flops=4 * 9 * 64 * TOK * 2048, bytes_accessed=4000000, transcendentals=9 * TOK * 2048
        ),
        name="attend_forward",
    )(lengths, queries, *keyvals, begins, tie)


def attend_back(
    micro, lengths, queries, keyvals, begins, mixed, log_total, grad_mixed, cosine, sine, tie
):
    half_shape = (1 + micro, 2 * KV_WIDTH, TOK)
    return pl.pallas_call(
        partial(backward_kernel, micro),
        out_shape=(
            jax.ShapeDtypeStruct(heads_shape, jnp.bfloat16),
            jax.ShapeDtypeStruct(half_shape, jnp.bfloat16),
            jax.ShapeDtypeStruct(half_shape, jnp.bfloat16),
        ),
        in_specs=[smem()] + [vmem()] * 11 + [anywhere()],
        out_specs=(vmem(),) * 3,
        scratch_shapes=[
            pltpu.VMEM((KV_HEADS, 4 * TOK, HEAD_DIM), jnp.bfloat16),
            pltpu.VMEM((KV_HEADS, 4 * TOK, HEAD_DIM), jnp.bfloat16),
            pltpu.VMEM((KV_HEADS, HEAD_DIM, 4 * TOK), jnp.bfloat16),
            pltpu.VMEM((KV_HEADS, 4 * TOK, HEAD_DIM), jnp.float32),
            pltpu.VMEM((KV_HEADS, 4 * TOK, HEAD_DIM), jnp.float32),
            pltpu.VMEM((2 * TILE, COLS), jnp.float32),
            pltpu.VMEM((2 * TILE, COLS), jnp.float32),
            pltpu.VMEM((2 * TILE, COLS), jnp.bfloat16),
            pltpu.VMEM((2 * TILE, COLS), jnp.bfloat16),
        ],
        compiler_params=kernel_params,
        cost_estimate=pl.CostEstimate(
            flops=10 * 9 * 64 * TOK * 2048, bytes_accessed=8000000, transcendentals=9 * TOK * 2048
        ),
        name="attend_back",
    )(lengths, queries, *keyvals, begins, mixed, log_total, grad_mixed, cosine, sine, tie)


def dot_with(left, right, left_side, right_side):
    return lax.dot_general(
        left, right, (((left_side,), (right_side,)), ((), ())), preferred_element_type=jnp.float32
    )


def norm_back(values, scaling, gain, upstream, axis):
    weighted = upstream * gain
    inner = jnp.mean(weighted * values, axis=axis, keepdims=True)
    gain_grad = jnp.sum(upstream * values * scaling, axis=1 - axis, keepdims=True)
    return (scaling * weighted - values * (scaling * scaling * scaling) * inner, gain_grad)


def norm_scaling(values, axis):
    return lax.rsqrt(jnp.mean(values * values, axis=axis, keepdims=True) + norm_epsilon)


def row_parts(held, spot, side):
    for turn in range(ROW_CUT):
        start = (turn ^ lax.div(spot, COL_CUT)) * CHUNK_ROWS
        part = held[pl.ds(pl.multiple_of(start, CHUNK_ROWS), CHUNK_ROWS), :]
        yield (turn * COL_CUT + side, part.astype(jnp.bfloat16))


def store_result(slot, result, out_ref, moved_ref):
    chip = positions()[2]

    @pl.when(chip == slot)
    def _():
        out_ref[0] = result

    @pl.when(chip != slot)
    def _():
        moved_ref[...] = result.astype(jnp.bfloat16)


def mlp_kernel(
    x_ref, x1_ref, c_ref, c1_ref, o0_ref, o1_ref, wo_ref, w_ref, wd_ref, gain_ref,
    out_ref, out1_ref, dh_ref, do0_ref, do1_ref, keep_ref, send_ref, gwo_ref, gg_ref,
    hid, dgate, dup, n2_tall, dh_low, held, gate_ref, up_ref, da_ref, c_slots,
):
    gain = gain_ref[...]
    gg_ref[...] = jnp.zeros((1, D), jnp.float32)
    block = 256
    spot = chunk_spot()
    for micro, (o_ref, do_ref) in enumerate(((o0_ref, do0_ref), (o1_ref, do1_ref))):
        rows = slice(micro * TOK, (micro + 1) * TOK)
        x_tall = (x1_ref if micro else x_ref)[...]
        c_tall_ref = c_slots.at[micro]
        chip = positions()[2]

        @pl.when(chip == micro)
        def _():
            c_tall_ref[...] = c_ref[0]

        @pl.when(chip != micro)
        def _():
            c_tall_ref[...] = c1_ref[...]

        c_tall = c_tall_ref[...]
        hidden_state = (x_tall.astype(jnp.float32) + dot_with(wo_ref[...], o_ref[...], 0, 0)).T
        scaling = norm_scaling(hidden_state, 1)
        normed = (hidden_state * scaling * gain).astype(jnp.bfloat16)
        n2_tall[:, rows] = normed.T
        back = c_tall.T
        for column in range(0, FF, block):
            columns = slice(column, column + block)
            gate_ref[...] = dot32(normed, w_ref[:, columns])
            up_ref[...] = dot32(normed, w_ref[:, FF + column : FF + column + block])
            da_ref[...] = dot_with(back, wd_ref[columns, :], 1, 1)
            for low in range(0, TOK, 32):
                part, spot_rows = slice(low, low + 32), slice(micro * TOK + low, micro * TOK + low + 32)
                gate, upward, grad_hidden = gate_ref[part], up_ref[part], da_ref[part]
                sigmoid_gate = jax.nn.sigmoid(gate)
                activated = gate * sigmoid_gate
                hid[spot_rows, columns] = (activated * upward).astype(jnp.bfloat16)
                dup[spot_rows, columns] = (grad_hidden * activated).astype(jnp.bfloat16)
                slope = sigmoid_gate * (1.0 + gate * (1.0 - sigmoid_gate))
                dgate[spot_rows, columns] = (grad_hidden * upward * slope).astype(jnp.bfloat16)
        result = (hidden_state + dot32(hid[rows, :], wd_ref[...])).T
        store_result(micro, result, out_ref, out1_ref)
        upstream = dot_with(dgate[rows, :], w_ref[:, :FF], 1, 1) + dot_with(
            dup[rows, :], w_ref[:, FF:], 1, 1
        )
        part, gain_grad = norm_back(hidden_state, scaling, gain, upstream, 1)
        gg_ref[...] += gain_grad
        grad_state = back.astype(jnp.float32) + part
        dh_low[rows, :] = grad_state.astype(jnp.bfloat16)
        grad_tall = grad_state.T
        dh_ref[micro] = grad_tall
        do_ref[...] = dot32(wo_ref[...], grad_tall.astype(jnp.bfloat16)).astype(jnp.bfloat16)
    c_parts = (c_slots.at[0], c_slots.at[1])
    for place, right in enumerate((dgate, dup, hid)):
        for side in range(COL_CUT):
            start = (side ^ lax.rem(spot, COL_CUT)) * CHUNK_COLS
            for column in range(0, CHUNK_COLS, block):
                columns = pl.ds(pl.multiple_of(start + column, block), block)
                if place < 2:
                    held[...] = dot32(n2_tall[...], right[:, columns])
                else:
                    held[...] = dot32(c_parts[0][...], right[:TOK, columns]) + dot32(
                        c_parts[1][...], right[TOK:, columns]
                    )
                for index, part in row_parts(held, spot, side):
                    out = (keep_ref, send_ref)[index // 4]
                    out[index % 4, place, :, column : column + block] = part
    gwo_ref[...] = (
        dot32(o0_ref[...], dh_low[:TOK, :]) + dot32(o1_ref[...], dh_low[TOK:, :])
    ).astype(jnp.bfloat16)


def mlp(tokens, tokens_1, cotangent, cotangent_1, mixed, w_out, w_gate_up, w_down, gain):
    rows = 2 * TOK
    low = jnp.bfloat16
    chunk_shape = (CHUNKS // 2, 3, CHUNK_ROWS, CHUNK_COLS)
    return pl.pallas_call(
        mlp_kernel,
        out_shape=(
            jax.ShapeDtypeStruct((2, D, TOK), jnp.float32),
            jax.ShapeDtypeStruct((D, TOK), low),
            jax.ShapeDtypeStruct((2, D, TOK), jnp.float32),
            jax.ShapeDtypeStruct((D, TOK), low),
            jax.ShapeDtypeStruct((D, TOK), low),
            jax.ShapeDtypeStruct(chunk_shape, low),
            jax.ShapeDtypeStruct(chunk_shape, low),
            jax.ShapeDtypeStruct((D, D), low),
            jax.ShapeDtypeStruct((1, D), jnp.float32),
        ),
        in_specs=[vmem()] * 10,
        out_specs=(vmem(),) * 9,
        scratch_shapes=[
            pltpu.VMEM((rows, FF), low),
            pltpu.VMEM((rows, FF), low),
            pltpu.VMEM((rows, FF), low),
            pltpu.VMEM((D, rows), low),
            pltpu.VMEM((rows, D), low),
            pltpu.VMEM((D, 256), jnp.float32),
            pltpu.VMEM((TOK, 256), jnp.float32),
            pltpu.VMEM((TOK, 256), jnp.float32),
            pltpu.VMEM((TOK, 256), jnp.float32),
            pltpu.VMEM((2, D, TOK), low),
        ],
        compiler_params=kernel_params,
        cost_estimate=pl.CostEstimate(
            flops=6 * rows * 3 * D * FF, bytes_accessed=25000000, transcendentals=rows * FF
        ),
        name="mlp",
    )(tokens, tokens_1, cotangent, cotangent_1, *mixed, w_out, w_gate_up, w_down, gain)


def natural_tiles(flat, base, rows, width):
    pairs, step, whole = rows // 2, width * 2 // 128, width // 128
    parts = [flat[pl.ds(base + place, pairs, stride=step), :] for place in range(step)]
    even = parts[:whole] + [parts[whole][:, :HEAD_DIM]]
    odd = jnp.concatenate([parts[whole][:, HEAD_DIM:]] + parts[whole + 1 :], axis=1)
    return even, [odd[:, low : low + 128] for low in range(0, width, 128)]


def unflatten(flat, base, rows, width, tiles):
    even, odd = natural_tiles(flat, base, rows, width)
    for place, (first, second) in enumerate(zip(even, odd)):
        breadth = first.shape[1]
        if breadth < 128:
            blank = jnp.zeros((rows // 2, 128 - breadth), jnp.float32)
            first = jnp.concatenate([first, blank], axis=1)
            second = jnp.concatenate([second, blank], axis=1)
        tiles[place, pl.ds(0, rows // 2, stride=2), :] = first
        tiles[place, pl.ds(1, rows // 2, stride=2), :] = second


def tile_widths(width):
    return [(place, low, min(128, width - low)) for place, low in enumerate(range(0, width, 128))]


MIXED = ((0, 0, D), (2592, D, KV_WIDTH), (3456, D + KV_WIDTH, KV_WIDTH), (4320, FF - D, D))


def project_kernel(
    near_ref, next_ref, x_ref, x1_ref, gain_ref, cos0_ref, sin0_ref, cos1_ref, sin1_ref,
    q0_ref, q1_ref, kv_ref, w_ref, wo_ref, n_ref, flat, tiles,
):
    spot = chunk_spot()
    length = flat.shape[0] // CHUNKS
    for index in range(CHUNKS):
        chunk = spot ^ index
        core, half, chip = lax.div(chunk, 4), lax.rem(lax.div(chunk, 2), 2), lax.rem(chunk, 2)
        start = pl.multiple_of((half * 4 + chip * 2 + core) * length, 8)
        part = (near_ref, next_ref)[index // 4][index % 4]
        flat[pl.ds(start, length), :] = part.astype(jnp.float32)
    for base, start, width in MIXED:
        unflatten(flat, base, D, width, tiles)
        for place, low, breadth in tile_widths(width):
            part = tiles[place][:D, :breadth].astype(jnp.bfloat16)
            if start < FF - D:
                w_ref[:, start + low : start + low + breadth] = part
            else:
                wo_ref[:, low : low + breadth] = part
    tall = w_ref[...].T
    half_width = HEAD_DIM // 2
    tables = ((q0_ref, cos0_ref, sin0_ref), (q1_ref, cos1_ref, sin1_ref))
    for micro, (q_ref, cos_ref, sin_ref) in enumerate(tables):
        values = (x1_ref if micro else x_ref)[...].astype(jnp.float32)
        normed = (values * norm_scaling(values, 0) * gain_ref[:, 0:1]).astype(jnp.bfloat16)
        n_ref[:, micro * TOK : (micro + 1) * TOK] = normed
        linear = dot32(tall, normed)
        cosine, sine = cos_ref[...], sin_ref[...]
        for head in range(HEADS + KV_HEADS):
            low = head * HEAD_DIM
            former = linear[low : low + half_width]
            latter = linear[low + half_width : low + HEAD_DIM]
            turned = jnp.concatenate(
                [former * cosine - latter * sine, latter * cosine + former * sine], axis=0
            ).astype(jnp.bfloat16)
            if head < HEADS:
                scaled = turned.astype(jnp.float32) * 0.125
                q_ref[head // GROUPS, head % GROUPS] = scaled.astype(jnp.bfloat16)
            else:
                low = low - D
                kv_ref[micro, low : low + HEAD_DIM, :] = turned
        kv_ref[micro, KV_WIDTH:, :] = linear[D + KV_WIDTH :].astype(jnp.bfloat16)


def project(near, following, tokens, tokens_1, gain_columns, tables):
    low = jnp.bfloat16
    return pl.pallas_call(
        project_kernel,
        out_shape=(
            jax.ShapeDtypeStruct(heads_shape, low),
            jax.ShapeDtypeStruct(heads_shape, low),
            jax.ShapeDtypeStruct((2, 2 * KV_WIDTH, TOK), low),
            jax.ShapeDtypeStruct((D, D + 2 * KV_WIDTH), low),
            jax.ShapeDtypeStruct((D, D), low),
            jax.ShapeDtypeStruct((D, 2 * TOK), low),
        ),
        in_specs=[vmem()] * 9,
        out_specs=(vmem(),) * 6,
        scratch_shapes=[
            pltpu.VMEM((D * FF // 128, 128), jnp.float32),
            pltpu.VMEM((5, D, 128), jnp.float32),
        ],
        compiler_params=kernel_params,
        cost_estimate=pl.CostEstimate(
            flops=4 * TOK * D * 960, bytes_accessed=8000000, transcendentals=0
        ),
        name="project",
    )(near, following, tokens, tokens_1, gain_columns, *tables[0], *tables[1])


def projection_kernel(
    n_ref, dq0_ref, dq1_ref, kept0_ref, kept1_ref, got_ref, far_ref,
    cos0_ref, sin0_ref, cos1_ref, sin1_ref, gwo_ref, tie_ref,
    keep_ref, send_ref, all_ref, held, cut,
):
    spot = chunk_spot()
    half_width = HEAD_DIM // 2
    parts = ((dq0_ref, kept0_ref, cos0_ref, sin0_ref), (dq1_ref, kept1_ref, cos1_ref, sin1_ref))
    for micro, (dq_ref, kept_ref, cos_ref, sin_ref) in enumerate(parts):
        columns = slice(micro * TOK, (micro + 1) * TOK)
        all_ref[:D, columns] = dq_ref[...]
        cosine, sine = cos_ref[...], sin_ref[...]
        summed = kept_ref[0].astype(jnp.float32) + got_ref[micro].astype(jnp.float32)
        if micro == 0:
            summed = summed + far_ref[...].astype(jnp.float32)
        for head in range(KV_HEADS):
            low = head * HEAD_DIM
            former = summed[low : low + half_width, :]
            latter = summed[low + half_width : low + HEAD_DIM, :]
            all_ref[D + low : D + low + half_width, columns] = (
                former * cosine + latter * sine
            ).astype(jnp.bfloat16)
            all_ref[D + low + half_width : D + low + HEAD_DIM, columns] = (
                latter * cosine - former * sine
            ).astype(jnp.bfloat16)
        all_ref[D + KV_WIDTH :, columns] = summed[KV_WIDTH:, :].astype(jnp.bfloat16)
    held[:, : D + 2 * KV_WIDTH] = dot_with(n_ref[...], all_ref[...], 1, 1)
    held[:, D + 2 * KV_WIDTH :] = gwo_ref[...].astype(jnp.float32)
    for side in range(COL_CUT):
        start = (side ^ lax.rem(spot, COL_CUT)) * CHUNK_COLS
        cut[...] = held[:, pl.ds(pl.multiple_of(start, CHUNK_COLS), CHUNK_COLS)]
        for index, part in row_parts(cut, spot, side):
            (keep_ref, send_ref)[index // 4][index % 4] = part


def projection_grads(normed, dqs, kept, got, far, tables, gwo, tie):
    rows = normed.shape[1]
    chunk_shape = (CHUNKS // 2, CHUNK_ROWS, CHUNK_COLS)
    return pl.pallas_call(
        projection_kernel,
        out_shape=(
            jax.ShapeDtypeStruct(chunk_shape, jnp.bfloat16),
            jax.ShapeDtypeStruct(chunk_shape, jnp.bfloat16),
            jax.ShapeDtypeStruct((D + 2 * KV_WIDTH, rows), jnp.bfloat16),
        ),
        in_specs=[vmem()] * 12 + [anywhere()],
        out_specs=(vmem(),) * 3,
        scratch_shapes=[
            pltpu.VMEM((D, FF), jnp.float32),
            pltpu.VMEM((D, CHUNK_COLS), jnp.float32),
        ],
        compiler_params=kernel_params,
        cost_estimate=pl.CostEstimate(
            flops=2 * rows * D * 960, bytes_accessed=8000000, transcendentals=0
        ),
        name="projection_grads",
    )(normed, *dqs, *kept, got, far, *tables[0], *tables[1], gwo, tie)


def both(left_ref, right_ref, where=...):
    total = left_ref[where].astype(jnp.float32) + right_ref[where].astype(jnp.float32)
    return total.astype(jnp.bfloat16)


def plain_call(kernel, outs, operands, ties, name):
    outs = [jax.ShapeDtypeStruct(shape, jnp.bfloat16) for shape in outs]
    ties = ties if isinstance(ties, tuple) else (ties,)
    count = len(operands)

    def run(*refs):
        kernel(*refs[: count + 1], *refs[count + len(ties) :])

    return pl.pallas_call(
        run,
        out_shape=outs,
        in_specs=[vmem()] * count + [anywhere()] * len(ties),
        out_specs=[vmem()] * len(outs),
        compiler_params=kernel_params,
        name=name,
    )(*operands, *ties)


def turns_kernel(keep_ref, got_ref, early_ref, tie_ref, *outs):
    quarter = positions()[0]
    for shift, out in enumerate(outs):
        target = lax.rem(quarter + shift, 4)

        @pl.when(target == 0)
        def _():
            out[...] = both(keep_ref, got_ref, 0)

        @pl.when(target != 0)
        def _():
            out[...] = early_ref[jnp.maximum(target - 1, 0)]


def depth_turns(keep, got, early, tie):
    return plain_call(turns_kernel, [keep.shape[1:]] * 4, (keep, got, early), tie, "depth_turns")


def sum_kernel(*refs):
    total = refs[0][...].astype(jnp.float32)
    for ref in refs[1:-2]:
        total = total + ref[...].astype(jnp.float32)
    refs[-1][...] = total.astype(jnp.bfloat16)


def tied_sum(operands, tie):
    return plain_call(sum_kernel, [operands[0].shape], operands, tie, "tied_sum")[0]


def late_kernel(keep_ref, got_ref, tie_ref, keep_out, send_out):
    size = keep_out.shape[0]
    keep_out[...] = both(keep_ref, got_ref, slice(0, size))
    send_out[...] = both(keep_ref, got_ref, slice(size, 2 * size))


def late_halves(keep, got, tie):
    shape = (keep.shape[0] // 2, *keep.shape[1:])
    return plain_call(late_kernel, [shape] * 2, (keep, got), tie, "late_halves")


def pair_kernel(first_ref, second_ref, tie_ref, out_ref):
    out_ref[:1] = first_ref[...]
    out_ref[1:] = second_ref[...]


def tied_pair(first, second, tie):
    shape = (3, *first.shape[1:])
    return plain_call(pair_kernel, [shape], (first, second), tie, "tied_pair")[0]


def pick_first_kernel(own_ref, got1_ref, got2_ref, got3_ref, tie_ref, out_ref):
    quarter = positions()[0]
    for place, ref in enumerate((own_ref, got1_ref, got2_ref, got3_ref)):

        @pl.when(quarter == place)
        def _():
            out_ref[...] = ref[...]


def pick_first(pieces, tie):
    return plain_call(pick_first_kernel, [pieces[0].shape], pieces, tie, "pick_first")[0]


def pick_rest_kernel(own_ref, got1_ref, got2_ref, got3_ref, tie_ref, gu_ref, d_ref):
    quarter = positions()[0]

    def run(flat, tiles):
        for place, out in ((1, gu_ref), (2, gu_ref), (3, d_ref)):
            for shift, ref in enumerate((own_ref, got1_ref, got2_ref, got3_ref)):

                @pl.when(lax.rem(quarter - place + 4, 4) == shift)
                def _():
                    flat[...] = ref[...].astype(jnp.float32)

            rows, width = out.shape
            if width > D:
                for tile in range(FF // 128):
                    low = (place - 1) * FF + tile * 128
                    out[:, low : low + 128] = flat[
                        pl.ds(tile, rows, stride=FF // 128), :
                    ].astype(jnp.bfloat16)
            else:
                unflatten(flat, 0, rows, width, tiles)
                for tile, low, breadth in tile_widths(width):
                    out[:, low : low + breadth] = tiles[tile][:, :breadth].astype(jnp.bfloat16)

    pl.run_scoped(
        run,
        pltpu.VMEM(own_ref.shape, jnp.float32),
        pltpu.VMEM((5, FF // CHUNKS, 128), jnp.float32),
    )


def pick_rest(pieces, tie):
    shapes = [(D // CHUNKS, 2 * FF), (FF // CHUNKS, D)]
    return plain_call(pick_rest_kernel, shapes, pieces, tie, "pick_rest")


def cast_kernel(value_ref, tie_ref, out_ref):
    out_ref[...] = value_ref[...].astype(out_ref.dtype)


def tied_cast(value, tie):
    return pl.pallas_call(
        cast_kernel,
        out_shape=jax.ShapeDtypeStruct(value.shape, jnp.bfloat16),
        in_specs=[vmem(), anywhere()],
        out_specs=vmem(),
        compiler_params=kernel_params,
        name="tied_cast",
    )(value, tie)


def inputs_kernel(
    all_ref, w_ref, x_ref, x1_ref, dh_ref, gain_ref, tie_ref, out_ref, out1_ref, gg_ref
):
    gain = gain_ref[:, 0:1]
    total = jnp.zeros((D, 1), jnp.float32)
    for micro in range(2):
        columns = slice(micro * TOK, (micro + 1) * TOK)
        upstream = dot32(w_ref[...], all_ref[:, columns])
        values = (x1_ref if micro else x_ref)[...].astype(jnp.float32)
        part, gain_grad = norm_back(values, norm_scaling(values, 0), gain, upstream, 0)
        total = total + gain_grad
        grad = dh_ref[micro] + part
        store_result(micro, grad, out_ref, out1_ref)
    gg_ref[...] = jnp.broadcast_to(total, gg_ref.shape)


def input_grads(grad_qkv, w_qkv, tokens, tokens_1, grad_state, gain_columns, tie):
    return pl.pallas_call(
        inputs_kernel,
        out_shape=(
            jax.ShapeDtypeStruct((2, D, TOK), jnp.float32),
            jax.ShapeDtypeStruct((D, TOK), jnp.bfloat16),
            jax.ShapeDtypeStruct((D, 128), jnp.float32),
        ),
        in_specs=[vmem()] * 6 + [anywhere()],
        out_specs=(vmem(),) * 3,
        compiler_params=kernel_params,
        cost_estimate=pl.CostEstimate(
            flops=4 * TOK * D * 960, bytes_accessed=8000000, transcendentals=0
        ),
        name="input_grads",
    )(grad_qkv, w_qkv, tokens, tokens_1, grad_state, gain_columns, tie)


def place_kernel(whole_ref, part_ref, tie_ref, out_ref):
    out_ref[0] = part_ref[...].astype(out_ref.dtype)


def place_last(whole, part, tie):
    return pl.pallas_call(
        place_kernel,
        out_shape=jax.ShapeDtypeStruct(whole.shape, whole.dtype),
        grid=(1,),
        in_specs=[anywhere(), pl.BlockSpec(part.shape, lambda step: (0, 0)), anywhere()],
        out_specs=pl.BlockSpec((1, *part.shape), lambda step: (1, 0, 0)),
        input_output_aliases={0: 0},
        compiler_params=kernel_params,
        name="place_last",
    )(whole, part, tie)


def newton_loop(matrix, scale):
    current = matrix / (jnp.sqrt(jnp.sum(matrix * matrix)) + frobenius_epsilon)

    def iterate(unused, held):
        low = held.astype(jnp.bfloat16)
        square = dot_with(low, low, 1, 1)
        square_low = square.astype(jnp.bfloat16)
        mixer = newton_second * square + newton_third * dot32(square_low, square_low)
        return newton_first * held + dot32(mixer.astype(jnp.bfloat16), low)

    return lax.fori_loop(0, NS_STEPS, iterate, current) * (0.2 * math.sqrt(scale))


def newton_wide(total):
    def run(low, square, square_low, mixer, step):
        height, breadth = total.shape
        block = 256

        def scale_by(factor, keep_low):
            for row in range(0, height, 16):
                part = total[row : row + 16, :] * factor
                total[row : row + 16, :] = part
                if keep_low:
                    low[row : row + 16, :] = part.astype(jnp.bfloat16)

        norm = jnp.zeros((8, breadth), jnp.float32)
        for row in range(0, height, 8):
            part = total[row : row + 8, :]
            norm = norm + part * part
        scale_by(1.0 / (jnp.sqrt(jnp.sum(norm)) + frobenius_epsilon), True)

        def iterate(unused, held):
            square[...] = dot_with(low[...], low[...], 1, 1)
            for row in range(0, height, 16):
                rows = slice(row, row + 16)
                square_low[rows, :] = square[rows, :].astype(jnp.bfloat16)
            step[:, :height] = dot32(square_low[...], square_low[...])
            for row in range(0, height, 16):
                rows = slice(row, row + 16)
                mixed = newton_second * square[rows, :] + newton_third * step[rows, :height]
                mixer[rows, :] = mixed.astype(jnp.bfloat16)
            for column in range(0, breadth, block):
                columns = slice(column, column + block)
                step[:, :block] = dot32(mixer[...], low[:, columns])
                for row in range(0, height, 32):
                    rows = slice(row, row + 32)
                    part = newton_first * total[rows, columns] + step[rows, :block]
                    total[rows, columns] = part
                    low[rows, columns] = part.astype(jnp.bfloat16)
            return held

        lax.fori_loop(0, NS_STEPS, iterate, 0)
        scale_by(0.2 * math.sqrt(breadth), False)

    height, breadth = total.shape
    pl.run_scoped(
        run,
        pltpu.VMEM((height, breadth), jnp.bfloat16),
        pltpu.VMEM((height, height), jnp.float32),
        pltpu.VMEM((height, height), jnp.bfloat16),
        pltpu.VMEM((height, height), jnp.bfloat16),
        pltpu.VMEM((height, height), jnp.float32),
    )


def flatten_rows(tiles, start, rows, width, out):
    pairs, step, whole = rows // 2, width * 2 // 128, width // 128
    spans = range(whole + 1)
    even = [tiles[place, pl.ds(start, pairs, stride=2), :] for place in spans]
    odd = [tiles[place, pl.ds(start + 1, pairs, stride=2), :] for place in spans]
    for place in range(whole):
        out[pl.ds(place, pairs, stride=step), :] = even[place]
    rest = width - whole * 128
    joined = jnp.concatenate([even[whole][:, :rest]] + odd[:whole] + [odd[whole][:, :rest]], axis=1)
    for place in range(whole, step):
        low = (place - whole) * 128
        out[pl.ds(place, pairs, stride=step), :] = joined[:, low : low + 128]


def shard_rows(kind, kinds, start, matrix, tiles, out):
    length = out.shape[0] * 128

    if 0 in kinds:

        @pl.when(kind == 0)
        def _():
            rows = length // FF
            for place in range(FF // 128):
                out[pl.ds(place, rows, stride=FF // 128), :] = matrix[
                    pl.ds(pl.multiple_of(start, 8), rows), place * 128 : (place + 1) * 128
                ]

        @pl.when(kind == 5)
        def _():
            window = pl.multiple_of(lax.div(start, 128) * 128, 128)
            for place, low, breadth in tile_widths(D):
                part = matrix[low : low + breadth, pl.ds(window, 256)]
                tiles[place, :256, :breadth] = part.T
            flatten_rows(tiles, start - window, length // D, D, out)

    for place, (base, low, width) in zip((1, 3, 4, 2), MIXED):
        if place not in kinds:
            continue

        @pl.when(kind == place)
        def _():
            for tile, column, breadth in tile_widths(width):
                tiles[tile, :D, :breadth] = matrix[:, low + column : low + column + breadth]
            flatten_rows(tiles, start, length // width, width, out)


def own_kind(length):
    square, narrow = D * D, D * KV_WIDTH
    quarter = lax.axis_index("quarter")
    index = lax.axis_index("rep") * 2 + lax.axis_index("half")
    within = (index * lax.axis_size("ctx") + lax.axis_index("ctx")) * length
    kind = jnp.where(quarter == 3, 5, 0)
    start = jnp.where(quarter == 3, lax.div(within, D), lax.div(within, FF))
    edges = ((0, 1, D), (square, 3, KV_WIDTH), (square + narrow, 4, KV_WIDTH))
    for edge, place, width in (*edges, (square + 2 * narrow, 2, D)):
        inside = (quarter == 0) & (within >= edge)
        kind = jnp.where(inside, place, kind)
        start = jnp.where(inside, lax.div(within - edge, width), start)
    return (kind, start)


def load_matrix(kind, old_ref, flat, total, tiles):
    flat[...] = old_ref[...].astype(jnp.float32) * momentum_decay

    @pl.when(kind == 0)
    def _():
        for place in range(FF // 128):
            columns = slice(place * 128, (place + 1) * 128)
            total[:, columns] = flat[pl.ds(place, D, stride=FF // 128), :]

    @pl.when(kind == 5)
    def _():
        unflatten(flat, 0, FF, D, tiles)
        for place, low, breadth in tile_widths(D):
            total[low : low + breadth, :] = tiles[place].T[:breadth]

    for place, (base, low, width) in zip((1, 3, 4, 2), MIXED):

        @pl.when(kind == place)
        def _():
            unflatten(flat, base, D, width, tiles)
            for tile, column, breadth in tile_widths(width):
                total[:, low + column : low + column + breadth] = tiles[tile][:D, :breadth]


def update_matrix(kind, kinds, total):
    if 0 in kinds:

        @pl.when((kind == 0) | (kind == 5))
        def _():
            newton_wide(total)

    for place, (base, low, width) in zip((1, 3, 4, 2), MIXED):
        if place not in kinds:
            continue

        @pl.when(kind == place)
        def _():
            columns = slice(low, low + width)
            if width == D:
                total[:, columns] = newton_loop(total[:, columns], D)
            else:
                total[:, columns] = newton_loop(total[:, columns].T, D).T


def momentum_kernel(length, old_ref, tie_ref, out_ref, flat, tiles):
    kind = own_kind(length)[0]
    load_matrix(kind, old_ref, flat, out_ref, tiles)


def lay_momentum(length, old, tie):
    return pl.pallas_call(
        partial(momentum_kernel, length),
        out_shape=jax.ShapeDtypeStruct((D, FF), jnp.float32),
        in_specs=[vmem(), anywhere()],
        out_specs=vmem(),
        scratch_shapes=[
            pltpu.VMEM((D * FF // 128, 128), jnp.float32),
            pltpu.VMEM((5, FF, 128), jnp.float32),
        ],
        compiler_params=kernel_params,
        name="lay_momentum",
    )(old, tie)


def newton_kernel(local, length, *refs):
    count = 3 if local else 2
    grad, total, tiles = refs[-3:]
    outs = refs[-3 - count : -3]
    pieces, (old_ref, *rest) = refs[:2], refs[2:-3]
    kind, start = own_kind(length)
    spot = chunk_spot()

    def run():
        for index in range(CHUNKS):
            chunk = spot ^ index
            row = pl.multiple_of(lax.div(chunk, COL_CUT) * CHUNK_ROWS, CHUNK_ROWS)
            column = pl.multiple_of(lax.rem(chunk, COL_CUT) * CHUNK_COLS, CHUNK_COLS)
            rows, columns = pl.ds(row, CHUNK_ROWS), pl.ds(column, CHUNK_COLS)
            part = pieces[index // 4][index % 4]
            grad[rows, columns] = part.astype(jnp.float32)
            total[rows, columns] = old_ref[rows, columns] + part.astype(jnp.float32)
        kinds = (0, 1, 2, 3, 4, 5)
        update_matrix(kind, kinds, total)
        if local:
            weights_ref, momentum_ref = rest[:2]
            grad_ref, new_momentum_ref, new_weights_ref = outs
            shard_rows(kind, kinds, start, grad, tiles, grad_ref)
            shard_rows(kind, kinds, start, total, tiles, new_weights_ref)
            new_momentum_ref[...] = momentum_decay * momentum_ref[...] + grad_ref[...]
            new_weights_ref[...] = (
                weights_ref[...] * (1.0 - matrix_rate * weight_decay)
                - matrix_rate * new_weights_ref[...]
            )
        else:
            outs[0][...] = grad[...]
            outs[1][...] = total[...]

    run()


def newton(length, pieces, old, shards):
    local = len(shards) > 0
    if local:
        outs = (jax.ShapeDtypeStruct(shards[0].shape, jnp.float32),) * 3
    else:
        outs = (jax.ShapeDtypeStruct((D, FF), jnp.float32),) * 2
    operands = (*pieces, old, *shards)

    return pl.pallas_call(
        partial(newton_kernel, local, length),
        out_shape=outs,
        in_specs=[vmem()] * len(operands),
        out_specs=(vmem(),) * len(outs),
        scratch_shapes=[
            pltpu.VMEM((D, FF), jnp.float32),
            pltpu.VMEM((D, FF), jnp.float32),
            pltpu.VMEM((5, FF, 128), jnp.float32),
        ],
        compiler_params=kernel_params,
        cost_estimate=pl.CostEstimate(
            flops=12000000000, bytes_accessed=9000000, transcendentals=0
        ),
        name="newton",
    )(*operands)


def own_rows(kind, row, shard_length, gradient, update):
    def block_case(low, width):
        def run(gradient, update):
            start = (row, low)
            size = (shard_length // width, width)
            return tuple(
                lax.dynamic_slice(whole, start, size).reshape(-1) for whole in (gradient, update)
            )

        return run

    def tall_case(gradient, update):
        start = (0, row)
        size = (D, shard_length // D)
        return tuple(
            lax.dynamic_slice(whole, start, size).T.reshape(-1) for whole in (gradient, update)
        )

    cases = [
        block_case(0, FF),
        block_case(0, D),
        block_case(FF - D, D),
        block_case(D, KV_WIDTH),
        block_case(D + KV_WIDTH, KV_WIDTH),
        tall_case,
    ]
    return lax.switch(kind, cases, gradient, update)


CORE_SWAP = [(0, 1), (1, 0), (2, 3), (3, 2)]
CHIP_SWAP = [(0, 2), (2, 0), (1, 3), (3, 1)]
SIDE_SWAP = [(0, 1), (1, 0)]
END_SWAP = [(0, 3), (3, 0), (1, 2), (2, 1)]


def plane_swap(value, bit):
    axis, swap = (("ctx", CHIP_SWAP), ("half", SIDE_SWAP), ("ctx", CORE_SWAP))[bit]
    return lax.ppermute(value, axis, swap)


def low_sum(left, right):
    return (left.astype(jnp.float32) + right.astype(jnp.float32)).astype(jnp.bfloat16)


def low_total(first, others):
    total = first.astype(jnp.float32)
    for part in others:
        total = total + part.astype(jnp.float32)
    return total.astype(jnp.bfloat16)


def plane_gather(piece, swap):
    pieces = piece[None]
    for bit in range(2):
        pieces = jnp.concatenate([pieces, swap(pieces, bit)], axis=0)
    return (pieces, swap(pieces, 2))


def depth_shift(value, shift, targets):
    pairs = [(place, (place + shift) % 4) for place in range(4)]
    return lax.ppermute(value, "quarter", [pair for pair in pairs if pair[1] in targets])


def gather_weights(low, tie):
    if lax.axis_size("rep") > 1:
        full = lax.all_gather(low, EVERY, axis=0, tiled=True).reshape(4, D * FF)
        ctx = lax.axis_index("ctx")
        spot = lax.rem(ctx, 2) * 4 + lax.axis_index("half") * 2 + ctx // 2
        chunk = jnp.arange(CHUNKS, dtype=jnp.int32) ^ spot
        order = 4 * (chunk // 2 % 2) + 2 * (chunk % 2) + chunk // 4
        mixed = full[0].reshape(CHUNKS, -1, 128)[order]
        return (mixed[:4], mixed[4:]), [
            jnp.concatenate([full[1].reshape(D, FF), full[2].reshape(D, FF)], axis=1),
            full[3].reshape(FF, D),
        ]
    first = [lax.ppermute(low, "quarter", [(0, shift)]) for shift in range(1, 4)]
    mixed = pick_first((low, *first), tie)
    others = [
        lax.ppermute(low, "quarter", [(place, (place + shift) % 4) for place in range(1, 4)])
        for shift in range(1, 4)
    ]
    rest = [
        lax.all_gather(piece, PLANE, axis=0, tiled=True)
        for piece in pick_rest((low, *others), mixed)
    ]
    return plane_gather(mixed, plane_swap), rest


def per_device(tokens, lengths, weights, momentum, norm_gains, gain_first, gain_second, cotangent):
    ctx = lax.axis_index("ctx")
    chip = ctx // 2
    reps = lax.axis_size("rep")
    shard_length = weights.shape[0]
    flat_shape = (shard_length // 128, 128)
    lengths = lengths[:, 0]
    tokens = jnp.swapaxes(tokens, 1, 2)
    cotangent = jnp.swapaxes(cotangent, 1, 2)
    gain_columns = norm_gains.T

    tokens_1 = lax.ppermute(tokens[1], "ctx", END_SWAP)
    mixed_weights, (w_gate_up, w_down) = gather_weights(
        weights.reshape(flat_shape).astype(jnp.bfloat16), tokens_1
    )
    near = chip == 0

    def slots(first, second):
        return jnp.where(near, first, second), jnp.where(near, second, first)

    x0, x1 = slots(tokens[0], tokens_1)
    begin_rows, tables = [], []
    for micro, own_lengths in enumerate(slots(lengths[0], lengths[1])):
        own_places = own_block(micro) * TOK + jnp.arange(TOK, dtype=jnp.int32)
        offsets, begins = layout(own_lengths, own_places)
        begin_rows.append(begins.reshape(1, TOK))
        tables.append(rope_tables(offsets))

    q0, q1, keyvals, w_qkv, w_out, normed = project(
        *mixed_weights, x0, x1, gain_columns, tables
    )
    queries = (q0, q1)
    far = lax.ppermute(keyvals[0], "ctx", CHIP_SWAP)
    keyvals = (
        keyvals,
        lax.ppermute(keyvals, "ctx", CORE_SWAP),
        far,
        lax.ppermute(far, "ctx", CORE_SWAP),
    )
    mixed, log_totals = [], []
    for micro in range(2):
        mixed_one, log_total = attend_forward(
            micro, lengths, queries[micro], keyvals, begin_rows[micro], norm_gains
        )
        mixed.append(mixed_one)
        log_totals.append(log_total)
    cotangent_1 = lax.ppermute(tied_cast(cotangent[1], mixed[0]), "ctx", END_SWAP)
    old = lax.all_gather(
        tied_cast(momentum.reshape(flat_shape), mixed[0]),
        ("rep", "half", "ctx"),
        axis=0,
        tiled=True,
    )
    outs = mlp(
        x0,
        x1,
        cotangent,
        cotangent_1,
        [part.reshape(D, TOK) for part in mixed],
        w_out,
        w_gate_up,
        w_down,
        norm_gains[1:2],
    )
    result, result_1, grad_state, grad_mixed_0, grad_mixed_1 = outs[:5]
    keep, send, grad_w_out, gain_two_grad = outs[5:]
    returned = lax.ppermute(result_1, "ctx", END_SWAP)

    def back_pass(micro, grad_mixed, tie):
        return attend_back(
            micro,
            lengths,
            queries[micro],
            keyvals,
            begin_rows[micro],
            mixed[micro],
            log_totals[micro],
            grad_mixed.reshape(heads_shape),
            *tables[micro],
            tie,
        )

    got = plane_swap(send, 2)
    dq0, kept0, sent0 = back_pass(0, grad_mixed_0, norm_gains)
    keep, send = late_halves(keep, got, dq0)
    got = plane_swap(send, 1)
    dq1, kept1, sent1 = back_pass(1, grad_mixed_1, keep)
    keep, send = late_halves(keep, got, (dq1, old, returned))
    traded = lax.ppermute(tied_pair(sent0, sent1, keep), "ctx", CORE_SWAP)
    crossed = lax.ppermute(low_sum(kept1[1], traded[2]), "ctx", CHIP_SWAP)
    got = plane_swap(send, 0)
    late_keep, late_send, grad_qkv = projection_grads(
        normed,
        (dq0.reshape(D, TOK), dq1.reshape(D, TOK)),
        (kept0, kept1),
        traded,
        crossed,
        tables,
        grad_w_out,
        keep,
    )
    late_got = plane_swap(late_send, 2)
    late_keep, late_send = late_halves(late_keep, late_got, norm_gains)
    late_got = plane_swap(late_send, 1)
    grad_inputs, grad_inputs_1, gain_one_grad = input_grads(
        grad_qkv, w_qkv, x0, x1, grad_state, gain_columns, late_keep
    )
    early = tied_sum((keep[0], got[0]), gain_one_grad)
    late_keep, late_send = late_halves(late_keep, late_got, early)
    gain_grad = jnp.concatenate([gain_one_grad[:, 0].reshape(1, D), gain_two_grad], axis=0)
    gain_grad = gain_grad + sum(
        lax.ppermute(gain_grad, "ctx", [(place, place ^ turn) for place in range(4)])
        for turn in range(1, 4)
    )
    piece, *turns = depth_turns(late_keep, plane_swap(late_send, 0), early, gain_grad)
    parts = [depth_shift(turn, shift, range(4)) for shift, turn in enumerate(turns, start=1)]
    gain_grad = gain_grad + sum(depth_shift(gain_grad, shift, range(4)) for shift in range(1, 4))
    old = lay_momentum(shard_length, old, piece)
    piece = tied_sum((piece, *parts), (old, gain_grad))
    if reps > 1:
        piece = lax.psum(piece, "rep")
        gain_grad = lax.psum(gain_grad, "rep")
    pieces = plane_gather(piece, plane_swap)
    gain_grad = gain_grad + plane_swap(gain_grad, 1)
    grad_inputs_1 = lax.ppermute(grad_inputs_1, "ctx", END_SWAP)

    shards = ()
    if flat_shape[0] % 8 == 0:
        shards = (weights.reshape(flat_shape), momentum.reshape(flat_shape))
    outs = newton(shard_length, pieces, old, shards)
    if len(shards) > 0:
        grad_shard, new_momentum, new_weights = [out.reshape(weights.shape) for out in outs]
    else:
        kind, start = own_kind(shard_length)
        grad_shard, update_shard = own_rows(kind, start, shard_length, *outs)
        new_momentum = momentum_decay * momentum + grad_shard
        new_weights = weights * (1.0 - matrix_rate * weight_decay) - matrix_rate * update_shard

    def placed(whole, part):
        whole = lax.dynamic_update_index_in_dim(whole, part.astype(jnp.float32), 1, 0)
        return jnp.swapaxes(whole, 1, 2)

    first_new = first_decay * gain_first + (1.0 - first_decay) * gain_grad
    second_new = second_decay * gain_second + (1.0 - second_decay) * gain_grad * gain_grad
    debiased_first_moment = first_new / (1.0 - first_decay**ADAM_STEP)
    corrected_second = second_new / (1.0 - second_decay**ADAM_STEP)
    new_gains = norm_gains * (
        1.0 - gain_rate * weight_decay
    ) - gain_rate * debiased_first_moment / (jnp.sqrt(corrected_second) + adam_epsilon)
    return (
        placed(result, returned),
        jnp.swapaxes(place_last(grad_inputs, grad_inputs_1, outs[-1]), 1, 2),
        grad_shard,
        new_momentum,
        new_weights,
        first_new,
        second_new,
        new_gains,
    )


def solution(mesh):
    devices = mesh.devices
    count = devices.size
    context = mesh.shape["ctx"]
    split = Mesh(
        devices.reshape(4, count // (8 * context), 2, context), ("quarter", "rep", "half", "ctx")
    )
    rows = P(None, EVERY, None)
    flat = P(EVERY)
    placed = (rows, P(None, ("quarter", "rep", "half"), None), flat, flat, P(), P(), P(), rows)
    return jax.shard_map(
        per_device,
        mesh=split,
        in_specs=placed,
        out_specs=(rows, rows, flat, flat, flat, P(), P(), P()),
        check_vma=False,
    )
```

```python
from functools import partial
import math

import jax
import jax.numpy as jnp
from jax import lax
from jax.experimental import pallas as pl
from jax.experimental.pallas import tpu as pltpu
from jax.sharding import Mesh, PartitionSpec as P

HEADS = 9
KV_HEADS = 3
HEAD_DIM = 64
FF = 1536
NS_STEPS = 5
ADAM_STEP = 10
D = 576
KV_WIDTH = 192
GROUPS = HEADS // KV_HEADS
TOK = 512
TILE = 256
COLS = GROUPS * TILE
ROW_CUT = 4
COL_CUT = 2
CHUNKS = ROW_CUT * COL_CUT
CHUNK_ROWS = D // ROW_CUT
CHUNK_COLS = FF // COL_CUT
PLANE = ("half", "ctx")
EVERY = ("quarter", "rep", "half", "ctx")


norm_epsilon = 1e-05
rope_base = 100000.0
masked_score = -1e30
newton_first = 3.4445
newton_second = -4.775
newton_third = 2.0315
momentum_decay = 0.95
matrix_rate = 0.2
weight_decay = 0.1
gain_rate = 0.2
first_decay = 0.9
second_decay = 0.95
adam_epsilon = 1e-08
frobenius_epsilon = 1e-07


def layout(lengths_row, places):
    finish = jnp.cumsum(lengths_row)
    firsts = finish - lengths_row
    begins = jnp.max(jnp.where(places[:, None] >= firsts[None, :], firsts[None, :], 0), axis=1)
    return (places - begins, begins)


def rope_tables(offsets):
    half_width = HEAD_DIM // 2
    inverse = jnp.exp(
        jnp.arange(half_width, dtype=jnp.float32) * (-2.0 * math.log(rope_base) / HEAD_DIM)
    )
    angles = inverse[:, None] * offsets.astype(jnp.float32)[None, :]
    return (jnp.cos(angles), jnp.sin(angles))


def dot32(left, right):
    return jnp.dot(left, right, preferred_element_type=jnp.float32)


def masked(scores, key_block, begins, places):
    keys = key_block * TILE + lax.broadcasted_iota(jnp.int32, scores.shape, 0)
    return jnp.where((keys >= begins) & (keys <= places), scores, masked_score)


def tile_row(row, tile):
    part = row[:, tile * TILE : (tile + 1) * TILE]
    return jnp.concatenate([part] * GROUPS, axis=1)


def tile_heads(ref, group, tile):
    return jnp.concatenate(
        [ref[group, head, :, tile * TILE : (tile + 1) * TILE] for head in range(GROUPS)], axis=1
    )


def positions():
    ctx = lax.axis_index("ctx")
    return (lax.axis_index("quarter"), lax.axis_index("half"), lax.div(ctx, 2), lax.rem(ctx, 2))


def chunk_spot():
    _, half, chip, core = positions()
    return core * 4 + half * 2 + chip


def first_key(lengths_ref, slot, row):
    micro = slot ^ positions()[2]
    begin = jnp.int32(0)
    first = jnp.int32(0)
    for place in range(3):
        first = first + lengths_ref[micro, place]
        begin = jnp.where(row >= first, first, begin)
    return begin


def key_loop(lengths_ref, slot, own, tile, load, process, carry):
    last = own * (TOK // TILE) + tile
    first = lax.div(first_key(lengths_ref, slot, last * TILE), TILE)
    full = lax.div(first_key(lengths_ref, slot, last * TILE + TILE - 1) + TILE - 1, TILE)
    full = jnp.minimum(full, last)
    pairs = lax.div(last - full, 2)

    def alone(block, held):
        load(0, block)
        return process(0, True, block, held)

    def couple(pair, held):
        block = full + 2 * pair
        load(1, block + 1)
        held = process(0, False, block, held)
        load(0, block + 2)
        return process(1, False, block + 1, held)

    def single(block, held):
        held = process(0, False, block, held)
        load(0, last)
        return held

    carry = lax.fori_loop(first, full, alone, carry)
    load(0, full)
    carry = lax.fori_loop(0, pairs, couple, carry)
    carry = lax.fori_loop(full + 2 * pairs, last, single, carry)
    return process(0, True, last, carry)


def plain_key_loop(lengths_ref, micro, own, tile, step, carry):
    last = own * (TOK // TILE) + tile
    first = lax.div(first_key(lengths_ref, micro, last * TILE), TILE)
    full = lax.div(first_key(lengths_ref, micro, last * TILE + TILE - 1) + TILE - 1, TILE)
    full = jnp.minimum(full, last)
    pairs = lax.div(last - full, 2)
    carry = lax.fori_loop(first, full, partial(step, True, 1), carry)
    carry = lax.fori_loop(
        0, pairs, lambda pair, held: step(False, 2, full + 2 * pair, held), carry
    )
    carry = lax.fori_loop(full + 2 * pairs, last, partial(step, False, 1), carry)
    return step(True, 1, last, carry)


def key_rows(block):
    return pl.ds(pl.multiple_of(block * TILE, TILE), TILE)


def own_block(slot):
    ctx = lax.axis_index("ctx")
    return jnp.maximum(ctx, 3 - ctx) if slot else jnp.minimum(ctx, 3 - ctx)


def key_slots(own, micro, kv_ref, other_ref, far_ref, far_other_ref):
    refs = (kv_ref.at[micro], other_ref.at[micro], far_ref, far_other_ref)[: 2 + 2 * micro]
    return [(own ^ place, ref) for place, ref in enumerate(refs)]


def block_rows(block):
    return pl.ds(pl.multiple_of(block * TOK, TOK), TOK)


def forward_kernel(
    micro, lengths_ref, q_ref, kv_ref, other_ref, far_ref, far_other_ref, begin_ref, tie_ref,
    o_ref, lse_ref, k_nat, v_ext, s_ref, p_ref,
):
    own = own_block(micro)
    for block, source in key_slots(own, micro, kv_ref, other_ref, far_ref, far_other_ref):

        @pl.when(block <= own)
        def _():
            rows = block_rows(block)
            for group in range(KV_HEADS):
                low = HEAD_DIM * group
                k_nat[group, rows, :] = source[low : low + HEAD_DIM, :].T
                low = low + KV_WIDTH
                v_ext[group, :HEAD_DIM, rows] = source[low : low + HEAD_DIM, :]
                v_ext[group, HEAD_DIM:, rows] = jnp.ones((16, TOK), jnp.bfloat16)

    def one_group(group, unused):
        for tile in range(TOK // TILE):
            queries = tile_heads(q_ref, group, tile)
            begins = tile_row(begin_ref[...], tile)
            column = lax.broadcasted_iota(jnp.int32, (1, COLS), 1)
            places = own * TOK + tile * TILE + lax.rem(column, TILE)

            def load(side, block):
                s_ref[side] = dot32(k_nat[group, key_rows(block), :], queries)

            def process(side, is_masked, block, carry):
                top, total = carry
                scores_ref, probs_ref = s_ref.at[side], p_ref.at[side]
                if is_masked:
                    scores_ref[...] = masked(scores_ref[...], block, begins, places)
                highest = scores_ref[:16]
                for low in range(16, TILE, 16):
                    highest = jnp.maximum(highest, scores_ref[low : low + 16])
                new_top = jnp.maximum(top, jnp.max(highest, axis=0, keepdims=True))
                for low in range(0, TILE, 16):
                    rows = slice(low, low + 16)
                    probs_ref[rows] = jnp.exp(scores_ref[rows] - new_top).astype(jnp.bfloat16)
                total = total * jnp.exp(top - new_top) + dot32(
                    v_ext[group, :, key_rows(block)], probs_ref[...]
                )
                return (new_top, total)

            carry = (
                jnp.full((1, COLS), masked_score, jnp.float32),
                jnp.zeros((HEAD_DIM + 16, COLS), jnp.float32),
            )
            top, total = key_loop(lengths_ref, micro, own, tile, load, process, carry)
            weight = total[HEAD_DIM : HEAD_DIM + 1, :]
            mixed = (total[:HEAD_DIM, :] / weight).astype(jnp.bfloat16)
            log_total = top + jnp.log(weight)
            for head in range(GROUPS):
                o_ref[group, head, :, tile * TILE : (tile + 1) * TILE] = mixed[
                    :, head * TILE : (head + 1) * TILE
                ]
                lse_ref[group, head, :, tile * TILE : (tile + 1) * TILE] = log_total[
                    :, head * TILE : (head + 1) * TILE
                ]
        return unused

    lax.fori_loop(0, KV_HEADS, one_group, 0)


def backward_kernel(
    micro, lengths_ref, q_ref, kv_ref, other_ref, far_ref, far_other_ref, begin_ref, o_ref, lse_ref,
    do_ref, cos_ref, sin_ref, *refs,
):
    if micro:
        first_ref, *refs = refs
    tie_ref, dq_ref, keep_ref, send_ref, k_nat, v_nat, k_tall, dk_ref, dv_ref, *refs = refs
    s_ref, g_ref, p_ref, ds_ref = refs
    if micro:
        send_ref[:1] = first_ref[...]
    own = own_block(micro)
    slots = key_slots(own, micro, kv_ref, other_ref, far_ref, far_other_ref)
    for block, source in slots:

        @pl.when(block <= own)
        def _():
            rows = block_rows(block)
            for group in range(KV_HEADS):
                low = HEAD_DIM * group
                k_nat[group, rows, :] = source[low : low + HEAD_DIM, :].T
                k_tall[group, :, rows] = source[low : low + HEAD_DIM, :]
                low = low + KV_WIDTH
                v_nat[group, rows, :] = source[low : low + HEAD_DIM, :].T
                dk_ref[group, rows, :] = jnp.zeros((TOK, HEAD_DIM), jnp.float32)
                dv_ref[group, rows, :] = jnp.zeros((TOK, HEAD_DIM), jnp.float32)

    def one_group(group, unused):
        for tile in range(TOK // TILE):
            queries = tile_heads(q_ref, group, tile)
            upstream = tile_heads(do_ref, group, tile)
            mixed = tile_heads(o_ref, group, tile)
            log_total = tile_heads(lse_ref, group, tile)
            delta = jnp.sum(
                upstream.astype(jnp.float32) * mixed.astype(jnp.float32), axis=0, keepdims=True
            )
            queries_nat = queries.T
            upstream_nat = upstream.T
            begins = tile_row(begin_ref[...], tile)
            column = lax.broadcasted_iota(jnp.int32, (1, COLS), 1)
            places = own * TOK + tile * TILE + lax.rem(column, TILE)

            def step(is_masked, width, key_block, dq):
                rows = pl.ds(pl.multiple_of(key_block * TILE, TILE), width * TILE)
                count = width * TILE
                scores = dot32(k_nat[group, rows, :], queries)
                s_ref[:count] = masked(scores, key_block, begins, places) if is_masked else scores
                g_ref[:count] = dot32(v_nat[group, rows, :], upstream)
                for low in range(0, count, 16):
                    part = slice(low, low + 16)
                    probs = jnp.exp(s_ref[part] - log_total)
                    p_ref[part] = probs.astype(jnp.bfloat16)
                    ds_ref[part] = (probs * (g_ref[part] - delta)).astype(jnp.bfloat16)
                dv_ref[group, rows, :] += dot32(p_ref[:count], upstream_nat)
                dk_ref[group, rows, :] += dot32(ds_ref[:count], queries_nat)
                return dq + dot32(k_tall[group, :, rows], ds_ref[:count])

            dq = jnp.zeros((HEAD_DIM, COLS), jnp.float32)
            dq = plain_key_loop(lengths_ref, micro, own, tile, step, dq) * 0.125
            half_width = HEAD_DIM // 2
            cosine = tile_row(cos_ref[...], tile)
            sine = tile_row(sin_ref[...], tile)
            former, latter = dq[:half_width], dq[half_width:]
            turned = jnp.concatenate(
                [former * cosine + latter * sine, latter * cosine - former * sine], axis=0
            ).astype(jnp.bfloat16)
            for head in range(GROUPS):
                dq_ref[group, head, :, tile * TILE : (tile + 1) * TILE] = turned[
                    :, head * TILE : (head + 1) * TILE
                ]
        return unused

    lax.fori_loop(0, KV_HEADS, one_group, 0)
    for place, (block, _) in enumerate(slots):
        out_ref = (keep_ref, send_ref)[place % 2]
        index = place // 2 + micro * (place % 2)

        @pl.when(block <= own)
        def _():
            rows = block_rows(block)
            for group in range(KV_HEADS):
                low = HEAD_DIM * group
                out_ref[index, low : low + HEAD_DIM, :] = dk_ref[group, rows, :].T.astype(
                    jnp.bfloat16
                )
                low = low + KV_WIDTH
                out_ref[index, low : low + HEAD_DIM, :] = dv_ref[group, rows, :].T.astype(
                    jnp.bfloat16
                )

        @pl.when(block > own)
        def _():
            out_ref[index] = jnp.zeros((2 * KV_WIDTH, TOK), jnp.bfloat16)


def vmem():
    return pl.BlockSpec(memory_space=pltpu.VMEM)


def smem():
    return pl.BlockSpec(memory_space=pltpu.SMEM)


def anywhere():
    return pl.BlockSpec(memory_space=pl.ANY)


kernel_params = pltpu.CompilerParams(vmem_limit_bytes=56 * 1024 * 1024)
heads_shape = (KV_HEADS, GROUPS, HEAD_DIM, TOK)


def attend_forward(micro, lengths, queries, keyvals, begins, tie):
    return pl.pallas_call(
        partial(forward_kernel, micro),
        out_shape=(
            jax.ShapeDtypeStruct(heads_shape, jnp.bfloat16),
            jax.ShapeDtypeStruct((KV_HEADS, GROUPS, 1, TOK), jnp.float32),
        ),
        in_specs=[smem()] + [vmem()] * 6 + [anywhere()],
        out_specs=(vmem(), vmem()),
        scratch_shapes=[
            pltpu.VMEM((KV_HEADS, 4 * TOK, HEAD_DIM), jnp.bfloat16),
            pltpu.VMEM((KV_HEADS, HEAD_DIM + 16, 4 * TOK), jnp.bfloat16),
            pltpu.VMEM((2, TILE, COLS), jnp.float32),
            pltpu.VMEM((2, TILE, COLS), jnp.bfloat16),
        ],
        compiler_params=kernel_params,
        cost_estimate=pl.CostEstimate(
            flops=4 * 9 * 64 * TOK * 2048, bytes_accessed=4000000, transcendentals=9 * TOK * 2048
        ),
        name="attend_forward",
    )(lengths, queries, *keyvals, begins, tie)


def attend_back(
    micro, lengths, queries, keyvals, begins, mixed, log_total, grad_mixed, cosine, sine, before, tie
):
    half_shape = (1 + micro, 2 * KV_WIDTH, TOK)
    send_shape = (1 + 2 * micro, 2 * KV_WIDTH, TOK)
    return pl.pallas_call(
        partial(backward_kernel, micro),
        out_shape=(
            jax.ShapeDtypeStruct(heads_shape, jnp.bfloat16),
            jax.ShapeDtypeStruct(half_shape, jnp.bfloat16),
            jax.ShapeDtypeStruct(send_shape, jnp.bfloat16),
        ),
        in_specs=[smem()] + [vmem()] * (11 + len(before)) + [anywhere()],
        out_specs=(vmem(),) * 3,
        scratch_shapes=[
            pltpu.VMEM((KV_HEADS, 4 * TOK, HEAD_DIM), jnp.bfloat16),
            pltpu.VMEM((KV_HEADS, 4 * TOK, HEAD_DIM), jnp.bfloat16),
            pltpu.VMEM((KV_HEADS, HEAD_DIM, 4 * TOK), jnp.bfloat16),
            pltpu.VMEM((KV_HEADS, 4 * TOK, HEAD_DIM), jnp.float32),
            pltpu.VMEM((KV_HEADS, 4 * TOK, HEAD_DIM), jnp.float32),
            pltpu.VMEM((2 * TILE, COLS), jnp.float32),
            pltpu.VMEM((2 * TILE, COLS), jnp.float32),
            pltpu.VMEM((2 * TILE, COLS), jnp.bfloat16),
            pltpu.VMEM((2 * TILE, COLS), jnp.bfloat16),
        ],
        compiler_params=kernel_params,
        cost_estimate=pl.CostEstimate(
            flops=10 * 9 * 64 * TOK * 2048, bytes_accessed=8000000, transcendentals=9 * TOK * 2048
        ),
        name="attend_back",
    )(lengths, queries, *keyvals, begins, mixed, log_total, grad_mixed, cosine, sine, *before, tie)


def dot_with(left, right, left_side, right_side):
    return lax.dot_general(
        left, right, (((left_side,), (right_side,)), ((), ())), preferred_element_type=jnp.float32
    )


def norm_back(values, scaling, gain, upstream, axis):
    weighted = upstream * gain
    inner = jnp.mean(weighted * values, axis=axis, keepdims=True)
    gain_grad = jnp.sum(upstream * values * scaling, axis=1 - axis, keepdims=True)
    return (scaling * weighted - values * (scaling * scaling * scaling) * inner, gain_grad)


def norm_scaling(values, axis):
    return lax.rsqrt(jnp.mean(values * values, axis=axis, keepdims=True) + norm_epsilon)


def row_parts(held, spot, side):
    for turn in range(ROW_CUT):
        start = (turn ^ lax.div(spot, COL_CUT)) * CHUNK_ROWS
        part = held[pl.ds(pl.multiple_of(start, CHUNK_ROWS), CHUNK_ROWS), :]
        yield (turn * COL_CUT + side, part.astype(jnp.bfloat16))


def store_result(slot, result, out_ref, moved_ref):
    chip = positions()[2]

    @pl.when(chip == slot)
    def _():
        out_ref[0] = result

    @pl.when(chip != slot)
    def _():
        moved_ref[...] = result.astype(jnp.bfloat16)


def mlp_kernel(
    x_ref, x1_ref, c_ref, c1_ref, o0_ref, o1_ref, wo_ref, w_ref, wd_ref, gain_ref,
    out_ref, out1_ref, dh_ref, do0_ref, do1_ref, keep_ref, send_ref, gwo_ref, gg_ref,
    hid, dgate, dup, n2_tall, dh_low, held, gate_ref, up_ref, da_ref, c_slots,
):
    gain = gain_ref[...]
    gg_ref[...] = jnp.zeros((1, D), jnp.float32)
    block = 256
    spot = chunk_spot()
    for micro, (o_ref, do_ref) in enumerate(((o0_ref, do0_ref), (o1_ref, do1_ref))):
        rows = slice(micro * TOK, (micro + 1) * TOK)
        x_tall = (x1_ref if micro else x_ref)[...]
        c_tall_ref = c_slots.at[micro]
        chip = positions()[2]

        @pl.when(chip == micro)
        def _():
            c_tall_ref[...] = c_ref[0]

        @pl.when(chip != micro)
        def _():
            c_tall_ref[...] = c1_ref[...]

        c_tall = c_tall_ref[...]
        hidden_state = (x_tall.astype(jnp.float32) + dot_with(wo_ref[...], o_ref[...], 0, 0)).T
        scaling = norm_scaling(hidden_state, 1)
        normed = (hidden_state * scaling * gain).astype(jnp.bfloat16)
        n2_tall[:, rows] = normed.T
        back = c_tall.T
        for column in range(0, FF, block):
            columns = slice(column, column + block)
            gate_ref[...] = dot32(normed, w_ref[:, columns])
            up_ref[...] = dot32(normed, w_ref[:, FF + column : FF + column + block])
            da_ref[...] = dot_with(back, wd_ref[columns, :], 1, 1)
            for low in range(0, TOK, 32):
                part, spot_rows = slice(low, low + 32), slice(micro * TOK + low, micro * TOK + low + 32)
                gate, upward, grad_hidden = gate_ref[part], up_ref[part], da_ref[part]
                sigmoid_gate = jax.nn.sigmoid(gate)
                activated = gate * sigmoid_gate
                hid[spot_rows, columns] = (activated * upward).astype(jnp.bfloat16)
                dup[spot_rows, columns] = (grad_hidden * activated).astype(jnp.bfloat16)
                slope = sigmoid_gate * (1.0 + gate * (1.0 - sigmoid_gate))
                dgate[spot_rows, columns] = (grad_hidden * upward * slope).astype(jnp.bfloat16)
        result = (hidden_state + dot32(hid[rows, :], wd_ref[...])).T
        store_result(micro, result, out_ref, out1_ref)
        upstream = dot_with(dgate[rows, :], w_ref[:, :FF], 1, 1) + dot_with(
            dup[rows, :], w_ref[:, FF:], 1, 1
        )
        part, gain_grad = norm_back(hidden_state, scaling, gain, upstream, 1)
        gg_ref[...] += gain_grad
        grad_state = back.astype(jnp.float32) + part
        dh_low[rows, :] = grad_state.astype(jnp.bfloat16)
        grad_tall = grad_state.T
        dh_ref[micro] = grad_tall
        do_ref[...] = dot32(wo_ref[...], grad_tall.astype(jnp.bfloat16)).astype(jnp.bfloat16)
    c_parts = (c_slots.at[0], c_slots.at[1])
    for place, right in enumerate((dgate, dup, hid)):
        for side in range(COL_CUT):
            start = (side ^ lax.rem(spot, COL_CUT)) * CHUNK_COLS
            for column in range(0, CHUNK_COLS, block):
                columns = pl.ds(pl.multiple_of(start + column, block), block)
                if place < 2:
                    held[...] = dot32(n2_tall[...], right[:, columns])
                else:
                    held[...] = dot32(c_parts[0][...], right[:TOK, columns]) + dot32(
                        c_parts[1][...], right[TOK:, columns]
                    )
                for index, part in row_parts(held, spot, side):
                    out = (keep_ref, send_ref)[index // 4]
                    out[index % 4, place, :, column : column + block] = part
    gwo_ref[...] = (
        dot32(o0_ref[...], dh_low[:TOK, :]) + dot32(o1_ref[...], dh_low[TOK:, :])
    ).astype(jnp.bfloat16)


def mlp(tokens, tokens_1, cotangent, cotangent_1, mixed, w_out, w_gate_up, w_down, gain):
    rows = 2 * TOK
    low = jnp.bfloat16
    chunk_shape = (CHUNKS // 2, 3, CHUNK_ROWS, CHUNK_COLS)
    return pl.pallas_call(
        mlp_kernel,
        out_shape=(
            jax.ShapeDtypeStruct((2, D, TOK), jnp.float32),
            jax.ShapeDtypeStruct((D, TOK), low),
            jax.ShapeDtypeStruct((2, D, TOK), jnp.float32),
            jax.ShapeDtypeStruct((D, TOK), low),
            jax.ShapeDtypeStruct((D, TOK), low),
            jax.ShapeDtypeStruct(chunk_shape, low),
            jax.ShapeDtypeStruct(chunk_shape, low),
            jax.ShapeDtypeStruct((D, D), low),
            jax.ShapeDtypeStruct((1, D), jnp.float32),
        ),
        in_specs=[vmem()] * 10,
        out_specs=(vmem(),) * 9,
        scratch_shapes=[
            pltpu.VMEM((rows, FF), low),
            pltpu.VMEM((rows, FF), low),
            pltpu.VMEM((rows, FF), low),
            pltpu.VMEM((D, rows), low),
            pltpu.VMEM((rows, D), low),
            pltpu.VMEM((D, 256), jnp.float32),
            pltpu.VMEM((TOK, 256), jnp.float32),
            pltpu.VMEM((TOK, 256), jnp.float32),
            pltpu.VMEM((TOK, 256), jnp.float32),
            pltpu.VMEM((2, D, TOK), low),
        ],
        compiler_params=kernel_params,
        cost_estimate=pl.CostEstimate(
            flops=6 * rows * 3 * D * FF, bytes_accessed=25000000, transcendentals=rows * FF
        ),
        name="mlp",
    )(tokens, tokens_1, cotangent, cotangent_1, *mixed, w_out, w_gate_up, w_down, gain)


def natural_tiles(flat, base, rows, width):
    pairs, step, whole = rows // 2, width * 2 // 128, width // 128
    parts = [flat[pl.ds(base + place, pairs, stride=step), :] for place in range(step)]
    even = parts[:whole] + [parts[whole][:, :HEAD_DIM]]
    odd = jnp.concatenate([parts[whole][:, HEAD_DIM:]] + parts[whole + 1 :], axis=1)
    return even, [odd[:, low : low + 128] for low in range(0, width, 128)]


def unflatten(flat, base, rows, width, tiles):
    even, odd = natural_tiles(flat, base, rows, width)
    for place, (first, second) in enumerate(zip(even, odd)):
        breadth = first.shape[1]
        if breadth < 128:
            blank = jnp.zeros((rows // 2, 128 - breadth), jnp.float32)
            first = jnp.concatenate([first, blank], axis=1)
            second = jnp.concatenate([second, blank], axis=1)
        tiles[place, pl.ds(0, rows // 2, stride=2), :] = first
        tiles[place, pl.ds(1, rows // 2, stride=2), :] = second


def tile_widths(width):
    return [(place, low, min(128, width - low)) for place, low in enumerate(range(0, width, 128))]


MIXED = ((0, 0, D), (2592, D, KV_WIDTH), (3456, D + KV_WIDTH, KV_WIDTH), (4320, FF - D, D))


def project_kernel(
    near_ref, next_ref, x_ref, x1_ref, gain_ref, cos0_ref, sin0_ref, cos1_ref, sin1_ref,
    q0_ref, q1_ref, kv_ref, w_ref, wo_ref, n_ref, flat, tiles,
):
    spot = chunk_spot()
    length = flat.shape[0] // CHUNKS
    for index in range(CHUNKS):
        chunk = spot ^ index
        core, half, chip = lax.div(chunk, 4), lax.rem(lax.div(chunk, 2), 2), lax.rem(chunk, 2)
        start = pl.multiple_of((half * 4 + chip * 2 + core) * length, 8)
        part = (near_ref, next_ref)[index // 4][index % 4]
        flat[pl.ds(start, length), :] = part.astype(jnp.float32)
    for base, start, width in MIXED:
        unflatten(flat, base, D, width, tiles)
        for place, low, breadth in tile_widths(width):
            part = tiles[place][:D, :breadth].astype(jnp.bfloat16)
            if start < FF - D:
                w_ref[:, start + low : start + low + breadth] = part
            else:
                wo_ref[:, low : low + breadth] = part
    tall = w_ref[...].T
    half_width = HEAD_DIM // 2
    tables = ((q0_ref, cos0_ref, sin0_ref), (q1_ref, cos1_ref, sin1_ref))
    for micro, (q_ref, cos_ref, sin_ref) in enumerate(tables):
        values = (x1_ref if micro else x_ref)[...].astype(jnp.float32)
        normed = (values * norm_scaling(values, 0) * gain_ref[:, 0:1]).astype(jnp.bfloat16)
        n_ref[:, micro * TOK : (micro + 1) * TOK] = normed
        linear = dot32(tall, normed)
        cosine, sine = cos_ref[...], sin_ref[...]
        for head in range(HEADS + KV_HEADS):
            low = head * HEAD_DIM
            former = linear[low : low + half_width]
            latter = linear[low + half_width : low + HEAD_DIM]
            turned = jnp.concatenate(
                [former * cosine - latter * sine, latter * cosine + former * sine], axis=0
            ).astype(jnp.bfloat16)
            if head < HEADS:
                scaled = turned.astype(jnp.float32) * 0.125
                q_ref[head // GROUPS, head % GROUPS] = scaled.astype(jnp.bfloat16)
            else:
                low = low - D
                kv_ref[micro, low : low + HEAD_DIM, :] = turned
        kv_ref[micro, KV_WIDTH:, :] = linear[D + KV_WIDTH :].astype(jnp.bfloat16)


def project(near, following, tokens, tokens_1, gain_columns, tables):
    low = jnp.bfloat16
    return pl.pallas_call(
        project_kernel,
        out_shape=(
            jax.ShapeDtypeStruct(heads_shape, low),
            jax.ShapeDtypeStruct(heads_shape, low),
            jax.ShapeDtypeStruct((2, 2 * KV_WIDTH, TOK), low),
            jax.ShapeDtypeStruct((D, D + 2 * KV_WIDTH), low),
            jax.ShapeDtypeStruct((D, D), low),
            jax.ShapeDtypeStruct((D, 2 * TOK), low),
        ),
        in_specs=[vmem()] * 9,
        out_specs=(vmem(),) * 6,
        scratch_shapes=[
            pltpu.VMEM((D * FF // 128, 128), jnp.float32),
            pltpu.VMEM((5, D, 128), jnp.float32),
        ],
        compiler_params=kernel_params,
        cost_estimate=pl.CostEstimate(
            flops=4 * TOK * D * 960, bytes_accessed=8000000, transcendentals=0
        ),
        name="project",
    )(near, following, tokens, tokens_1, gain_columns, *tables[0], *tables[1])


def projection_kernel(
    n_ref, dq0_ref, dq1_ref, kept0_ref, kept1_ref, got_ref, far_ref,
    cos0_ref, sin0_ref, cos1_ref, sin1_ref, gwo_ref, tie_ref,
    keep_ref, send_ref, all_ref, held, cut,
):
    spot = chunk_spot()
    half_width = HEAD_DIM // 2
    parts = ((dq0_ref, kept0_ref, cos0_ref, sin0_ref), (dq1_ref, kept1_ref, cos1_ref, sin1_ref))
    for micro, (dq_ref, kept_ref, cos_ref, sin_ref) in enumerate(parts):
        columns = slice(micro * TOK, (micro + 1) * TOK)
        all_ref[:D, columns] = dq_ref[...]
        cosine, sine = cos_ref[...], sin_ref[...]
        summed = kept_ref[0].astype(jnp.float32) + got_ref[micro].astype(jnp.float32)
        if micro == 0:
            summed = summed + far_ref[...].astype(jnp.float32)
        for head in range(KV_HEADS):
            low = head * HEAD_DIM
            former = summed[low : low + half_width, :]
            latter = summed[low + half_width : low + HEAD_DIM, :]
            all_ref[D + low : D + low + half_width, columns] = (
                former * cosine + latter * sine
            ).astype(jnp.bfloat16)
            all_ref[D + low + half_width : D + low + HEAD_DIM, columns] = (
                latter * cosine - former * sine
            ).astype(jnp.bfloat16)
        all_ref[D + KV_WIDTH :, columns] = summed[KV_WIDTH:, :].astype(jnp.bfloat16)
    held[:, : D + 2 * KV_WIDTH] = dot_with(n_ref[...], all_ref[...], 1, 1)
    held[:, D + 2 * KV_WIDTH :] = gwo_ref[...].astype(jnp.float32)
    for side in range(COL_CUT):
        start = (side ^ lax.rem(spot, COL_CUT)) * CHUNK_COLS
        cut[...] = held[:, pl.ds(pl.multiple_of(start, CHUNK_COLS), CHUNK_COLS)]
        for index, part in row_parts(cut, spot, side):
            (keep_ref, send_ref)[index // 4][index % 4] = part


def projection_grads(normed, dqs, kept, got, far, tables, gwo, tie):
    rows = normed.shape[1]
    chunk_shape = (CHUNKS // 2, CHUNK_ROWS, CHUNK_COLS)
    return pl.pallas_call(
        projection_kernel,
        out_shape=(
            jax.ShapeDtypeStruct(chunk_shape, jnp.bfloat16),
            jax.ShapeDtypeStruct(chunk_shape, jnp.bfloat16),
            jax.ShapeDtypeStruct((D + 2 * KV_WIDTH, rows), jnp.bfloat16),
        ),
        in_specs=[vmem()] * 12 + [anywhere()],
        out_specs=(vmem(),) * 3,
        scratch_shapes=[
            pltpu.VMEM((D, FF), jnp.float32),
            pltpu.VMEM((D, CHUNK_COLS), jnp.float32),
        ],
        compiler_params=kernel_params,
        cost_estimate=pl.CostEstimate(
            flops=2 * rows * D * 960, bytes_accessed=8000000, transcendentals=0
        ),
        name="projection_grads",
    )(normed, *dqs, *kept, got, far, *tables[0], *tables[1], gwo, tie)


def both(left_ref, right_ref, where=...):
    total = left_ref[where].astype(jnp.float32) + right_ref[where].astype(jnp.float32)
    return total.astype(jnp.bfloat16)


def plain_call(kernel, outs, operands, ties, name):
    outs = [jax.ShapeDtypeStruct(shape, jnp.bfloat16) for shape in outs]
    ties = ties if isinstance(ties, tuple) else (ties,)
    count = len(operands)

    def run(*refs):
        kernel(*refs[: count + 1], *refs[count + len(ties) :])

    return pl.pallas_call(
        run,
        out_shape=outs,
        in_specs=[vmem()] * count + [anywhere()] * len(ties),
        out_specs=[vmem()] * len(outs),
        compiler_params=kernel_params,
        name=name,
    )(*operands, *ties)


def turns_kernel(keep_ref, got_ref, early_ref, tie_ref, *outs):
    quarter = positions()[0]
    for shift, out in enumerate(outs):
        target = lax.rem(quarter + shift, 4)

        @pl.when(target == 0)
        def _():
            out[...] = both(keep_ref, got_ref, 0)

        @pl.when(target != 0)
        def _():
            out[...] = early_ref[jnp.maximum(target - 1, 0)]


def depth_turns(keep, got, early, tie):
    return plain_call(turns_kernel, [keep.shape[1:]] * 4, (keep, got, early), tie, "depth_turns")


def sum_kernel(*refs):
    total = refs[0][...].astype(jnp.float32)
    for ref in refs[1:-2]:
        total = total + ref[...].astype(jnp.float32)
    refs[-1][...] = total.astype(jnp.bfloat16)


def tied_sum(operands, tie):
    return plain_call(sum_kernel, [operands[0].shape], operands, tie, "tied_sum")[0]


def late_kernel(keep_ref, got_ref, tie_ref, keep_out, send_out):
    size = keep_out.shape[0]
    keep_out[...] = both(keep_ref, got_ref, slice(0, size))
    send_out[...] = both(keep_ref, got_ref, slice(size, 2 * size))


def late_halves(keep, got, tie):
    shape = (keep.shape[0] // 2, *keep.shape[1:])
    return plain_call(late_kernel, [shape] * 2, (keep, got), tie, "late_halves")


def early_halves(keep, got, ties, passed=None):
    count, quarters, rows, columns = keep.shape
    held = () if passed is None else (passed,)

    def block(size):
        return pl.BlockSpec((size, 1, rows, columns), lambda place: (0, place, 0, 0))

    def kernel(keep_ref, got_ref, *refs):
        keep_out, send_out = refs[len(held) + len(ties) :][:2]
        late_kernel(keep_ref, got_ref, None, keep_out, send_out)

    half = jax.ShapeDtypeStruct((count // 2, quarters, rows, columns), jnp.bfloat16)
    return pl.pallas_call(
        kernel,
        out_shape=[half, half] + [jax.ShapeDtypeStruct(one.shape, one.dtype) for one in held],
        grid=(quarters,),
        in_specs=[block(count)] * 2 + [anywhere()] * (len(held) + len(ties)),
        out_specs=[block(count // 2)] * 2 + [anywhere()] * len(held),
        input_output_aliases={2: 2} if held else {},
        compiler_params=kernel_params,
        name="early_halves",
    )(keep, got, *held, *ties)


def finish_kernel(keep_ref, got_ref, late_ref, late_got_ref, tie_ref, early_out, keep_out, send_out):
    early_out[...] = both(keep_ref, got_ref, 0)
    late_kernel(late_ref, late_got_ref, None, keep_out, send_out)


def finish_early(keep, got, late_keep, late_got, tie):
    half = (late_keep.shape[0] // 2, *late_keep.shape[1:])
    operands = (keep, got, late_keep, late_got)
    return plain_call(finish_kernel, [keep.shape[1:], half, half], operands, tie, "finish_early")


def pick_first_kernel(own_ref, got1_ref, got2_ref, got3_ref, tie_ref, out_ref):
    quarter = positions()[0]
    for place, ref in enumerate((own_ref, got1_ref, got2_ref, got3_ref)):

        @pl.when(quarter == place)
        def _():
            out_ref[...] = ref[...]


def pick_first(pieces, tie):
    return plain_call(pick_first_kernel, [pieces[0].shape], pieces, tie, "pick_first")[0]


def pick_rest_kernel(own_ref, got1_ref, got2_ref, got3_ref, tie_ref, gu_ref, d_ref):
    quarter = positions()[0]

    def run(flat, tiles):
        for place, out in ((1, gu_ref), (2, gu_ref), (3, d_ref)):
            for shift, ref in enumerate((own_ref, got1_ref, got2_ref, got3_ref)):

                @pl.when(lax.rem(quarter - place + 4, 4) == shift)
                def _():
                    flat[...] = ref[...].astype(jnp.float32)

            rows, width = out.shape
            if width > D:
                for tile in range(FF // 128):
                    low = (place - 1) * FF + tile * 128
                    out[:, low : low + 128] = flat[
                        pl.ds(tile, rows, stride=FF // 128), :
                    ].astype(jnp.bfloat16)
            else:
                unflatten(flat, 0, rows, width, tiles)
                for tile, low, breadth in tile_widths(width):
                    out[:, low : low + breadth] = tiles[tile][:, :breadth].astype(jnp.bfloat16)

    pl.run_scoped(
        run,
        pltpu.VMEM(own_ref.shape, jnp.float32),
        pltpu.VMEM((5, FF // CHUNKS, 128), jnp.float32),
    )


def pick_rest(pieces, tie):
    shapes = [(D // CHUNKS, 2 * FF), (FF // CHUNKS, D)]
    return plain_call(pick_rest_kernel, shapes, pieces, tie, "pick_rest")


def copies_kernel(first_ref, second_ref, tie_ref, first_out, second_out):
    first_out[...] = first_ref[...].astype(jnp.bfloat16)
    second_out[...] = second_ref[...]


def low_copies(first, second, tie):
    shapes = [first.shape, second.shape]
    return plain_call(copies_kernel, shapes, (first, second), tie, "low_copies")


def inputs_kernel(
    all_ref, w_ref, x_ref, x1_ref, dh_ref, gain_ref, tie_ref, out_ref, out1_ref, gg_ref
):
    gain = gain_ref[:, 0:1]
    total = jnp.zeros((D, 1), jnp.float32)
    for micro in range(2):
        columns = slice(micro * TOK, (micro + 1) * TOK)
        upstream = dot32(w_ref[...], all_ref[:, columns])
        values = (x1_ref if micro else x_ref)[...].astype(jnp.float32)
        part, gain_grad = norm_back(values, norm_scaling(values, 0), gain, upstream, 0)
        total = total + gain_grad
        grad = dh_ref[micro] + part
        store_result(micro, grad, out_ref, out1_ref)
    gg_ref[...] = jnp.broadcast_to(total, gg_ref.shape)


def input_grads(grad_qkv, w_qkv, tokens, tokens_1, grad_state, gain_columns, tie):
    return pl.pallas_call(
        inputs_kernel,
        out_shape=(
            jax.ShapeDtypeStruct((2, D, TOK), jnp.float32),
            jax.ShapeDtypeStruct((D, TOK), jnp.bfloat16),
            jax.ShapeDtypeStruct((D, 128), jnp.float32),
        ),
        in_specs=[vmem()] * 6 + [anywhere()],
        out_specs=(vmem(),) * 3,
        compiler_params=kernel_params,
        cost_estimate=pl.CostEstimate(
            flops=4 * TOK * D * 960, bytes_accessed=8000000, transcendentals=0
        ),
        name="input_grads",
    )(grad_qkv, w_qkv, tokens, tokens_1, grad_state, gain_columns, tie)


def place_kernel(whole_ref, part_ref, tie_ref, out_ref):
    out_ref[0] = part_ref[...].astype(out_ref.dtype)


def place_last(whole, part, tie):
    return pl.pallas_call(
        place_kernel,
        out_shape=jax.ShapeDtypeStruct(whole.shape, whole.dtype),
        grid=(1,),
        in_specs=[anywhere(), pl.BlockSpec(part.shape, lambda step: (0, 0)), anywhere()],
        out_specs=pl.BlockSpec((1, *part.shape), lambda step: (1, 0, 0)),
        input_output_aliases={0: 0},
        compiler_params=kernel_params,
        name="place_last",
    )(whole, part, tie)


def newton_loop(matrix, scale):
    current = matrix / (jnp.sqrt(jnp.sum(matrix * matrix)) + frobenius_epsilon)

    def iterate(unused, held):
        low = held.astype(jnp.bfloat16)
        square = dot_with(low, low, 1, 1)
        square_low = square.astype(jnp.bfloat16)
        mixer = newton_second * square + newton_third * dot32(square_low, square_low)
        return newton_first * held + dot32(mixer.astype(jnp.bfloat16), low)

    return lax.fori_loop(0, NS_STEPS, iterate, current) * (0.2 * math.sqrt(scale))


def newton_wide(total):
    def run(low, square, square_low, mixer, step):
        height, breadth = total.shape
        block = 256

        def scale_by(factor, keep_low):
            for row in range(0, height, 16):
                part = total[row : row + 16, :] * factor
                total[row : row + 16, :] = part
                if keep_low:
                    low[row : row + 16, :] = part.astype(jnp.bfloat16)

        norm = jnp.zeros((8, breadth), jnp.float32)
        for row in range(0, height, 8):
            part = total[row : row + 8, :]
            norm = norm + part * part
        scale_by(1.0 / (jnp.sqrt(jnp.sum(norm)) + frobenius_epsilon), True)

        def iterate(unused, held):
            square[...] = dot_with(low[...], low[...], 1, 1)
            for row in range(0, height, 16):
                rows = slice(row, row + 16)
                square_low[rows, :] = square[rows, :].astype(jnp.bfloat16)
            step[:, :height] = dot32(square_low[...], square_low[...])
            for row in range(0, height, 16):
                rows = slice(row, row + 16)
                mixed = newton_second * square[rows, :] + newton_third * step[rows, :height]
                mixer[rows, :] = mixed.astype(jnp.bfloat16)
            for column in range(0, breadth, block):
                columns = slice(column, column + block)
                step[:, :block] = dot32(mixer[...], low[:, columns])
                for row in range(0, height, 32):
                    rows = slice(row, row + 32)
                    part = newton_first * total[rows, columns] + step[rows, :block]
                    total[rows, columns] = part
                    low[rows, columns] = part.astype(jnp.bfloat16)
            return held

        lax.fori_loop(0, NS_STEPS, iterate, 0)
        scale_by(0.2 * math.sqrt(breadth), False)

    height, breadth = total.shape
    pl.run_scoped(
        run,
        pltpu.VMEM((height, breadth), jnp.bfloat16),
        pltpu.VMEM((height, height), jnp.float32),
        pltpu.VMEM((height, height), jnp.bfloat16),
        pltpu.VMEM((height, height), jnp.bfloat16),
        pltpu.VMEM((height, height), jnp.float32),
    )


def flatten_rows(tiles, start, rows, width, out):
    pairs, step, whole = rows // 2, width * 2 // 128, width // 128
    spans = range(whole + 1)
    even = [tiles[place, pl.ds(start, pairs, stride=2), :] for place in spans]
    odd = [tiles[place, pl.ds(start + 1, pairs, stride=2), :] for place in spans]
    for place in range(whole):
        out[pl.ds(place, pairs, stride=step), :] = even[place]
    rest = width - whole * 128
    joined = jnp.concatenate([even[whole][:, :rest]] + odd[:whole] + [odd[whole][:, :rest]], axis=1)
    for place in range(whole, step):
        low = (place - whole) * 128
        out[pl.ds(place, pairs, stride=step), :] = joined[:, low : low + 128]


def shard_rows(kind, kinds, start, matrix, tiles, out):
    length = out.shape[0] * 128

    if 0 in kinds:

        @pl.when(kind == 0)
        def _():
            rows = length // FF
            for place in range(FF // 128):
                out[pl.ds(place, rows, stride=FF // 128), :] = matrix[
                    pl.ds(pl.multiple_of(start, 8), rows), place * 128 : (place + 1) * 128
                ]

        @pl.when(kind == 5)
        def _():
            window = pl.multiple_of(lax.div(start, 128) * 128, 128)
            for place, low, breadth in tile_widths(D):
                part = matrix[low : low + breadth, pl.ds(window, 256)]
                tiles[place, :256, :breadth] = part.T
            flatten_rows(tiles, start - window, length // D, D, out)

    for place, (base, low, width) in zip((1, 3, 4, 2), MIXED):
        if place not in kinds:
            continue

        @pl.when(kind == place)
        def _():
            for tile, column, breadth in tile_widths(width):
                tiles[tile, :D, :breadth] = matrix[:, low + column : low + column + breadth]
            flatten_rows(tiles, start, length // width, width, out)


def own_kind(length):
    square, narrow = D * D, D * KV_WIDTH
    quarter = lax.axis_index("quarter")
    index = lax.axis_index("rep") * 2 + lax.axis_index("half")
    within = (index * lax.axis_size("ctx") + lax.axis_index("ctx")) * length
    kind = jnp.where(quarter == 3, 5, 0)
    start = jnp.where(quarter == 3, lax.div(within, D), lax.div(within, FF))
    edges = ((0, 1, D), (square, 3, KV_WIDTH), (square + narrow, 4, KV_WIDTH))
    for edge, place, width in (*edges, (square + 2 * narrow, 2, D)):
        inside = (quarter == 0) & (within >= edge)
        kind = jnp.where(inside, place, kind)
        start = jnp.where(inside, lax.div(within - edge, width), start)
    return (kind, start)


def load_matrix(kind, old_ref, flat, total, tiles):
    flat[...] = old_ref[...].astype(jnp.float32) * momentum_decay

    @pl.when(kind == 0)
    def _():
        for place in range(FF // 128):
            columns = slice(place * 128, (place + 1) * 128)
            total[:, columns] = flat[pl.ds(place, D, stride=FF // 128), :]

    @pl.when(kind == 5)
    def _():
        unflatten(flat, 0, FF, D, tiles)
        for place, low, breadth in tile_widths(D):
            total[low : low + breadth, :] = tiles[place].T[:breadth]

    for place, (base, low, width) in zip((1, 3, 4, 2), MIXED):

        @pl.when(kind == place)
        def _():
            unflatten(flat, base, D, width, tiles)
            for tile, column, breadth in tile_widths(width):
                total[:, low + column : low + column + breadth] = tiles[tile][:D, :breadth]


def update_matrix(kind, kinds, total):
    if 0 in kinds:

        @pl.when((kind == 0) | (kind == 5))
        def _():
            newton_wide(total)

    for place, (base, low, width) in zip((1, 3, 4, 2), MIXED):
        if place not in kinds:
            continue

        @pl.when(kind == place)
        def _():
            columns = slice(low, low + width)
            if width == D:
                total[:, columns] = newton_loop(total[:, columns], D)
            else:
                total[:, columns] = newton_loop(total[:, columns].T, D).T


def momentum_kernel(length, old_ref, tie_ref, out_ref, flat, tiles):
    kind = own_kind(length)[0]
    load_matrix(kind, old_ref, flat, out_ref, tiles)


def lay_momentum(length, old, tie):
    return pl.pallas_call(
        partial(momentum_kernel, length),
        out_shape=jax.ShapeDtypeStruct((D, FF), jnp.float32),
        in_specs=[vmem(), anywhere()],
        out_specs=vmem(),
        scratch_shapes=[
            pltpu.VMEM((D * FF // 128, 128), jnp.float32),
            pltpu.VMEM((5, FF, 128), jnp.float32),
        ],
        compiler_params=kernel_params,
        name="lay_momentum",
    )(old, tie)


def newton_kernel(local, length, *refs):
    count = 3 if local else 2
    grad, total, tiles = refs[-3:]
    outs = refs[-3 - count : -3]
    pieces, (old_ref, *rest) = refs[:2], refs[2:-3]
    kind, start = own_kind(length)
    spot = chunk_spot()

    def run():
        for index in range(CHUNKS):
            chunk = spot ^ index
            row = pl.multiple_of(lax.div(chunk, COL_CUT) * CHUNK_ROWS, CHUNK_ROWS)
            column = pl.multiple_of(lax.rem(chunk, COL_CUT) * CHUNK_COLS, CHUNK_COLS)
            rows, columns = pl.ds(row, CHUNK_ROWS), pl.ds(column, CHUNK_COLS)
            part = pieces[index // 4][index % 4]
            grad[rows, columns] = part.astype(jnp.float32)
            total[rows, columns] = old_ref[rows, columns] + part.astype(jnp.float32)
        kinds = (0, 1, 2, 3, 4, 5)
        update_matrix(kind, kinds, total)
        if local:
            weights_ref, momentum_ref = rest[:2]
            grad_ref, new_momentum_ref, new_weights_ref = outs
            shard_rows(kind, kinds, start, grad, tiles, grad_ref)
            shard_rows(kind, kinds, start, total, tiles, new_weights_ref)
            new_momentum_ref[...] = momentum_decay * momentum_ref[...] + grad_ref[...]
            new_weights_ref[...] = (
                weights_ref[...] * (1.0 - matrix_rate * weight_decay)
                - matrix_rate * new_weights_ref[...]
            )
        else:
            outs[0][...] = grad[...]
            outs[1][...] = total[...]

    run()


def newton(length, pieces, old, shards):
    local = len(shards) > 0
    if local:
        outs = (jax.ShapeDtypeStruct(shards[0].shape, jnp.float32),) * 3
    else:
        outs = (jax.ShapeDtypeStruct((D, FF), jnp.float32),) * 2
    operands = (*pieces, old, *shards)

    return pl.pallas_call(
        partial(newton_kernel, local, length),
        out_shape=outs,
        in_specs=[vmem()] * len(operands),
        out_specs=(vmem(),) * len(outs),
        scratch_shapes=[
            pltpu.VMEM((D, FF), jnp.float32),
            pltpu.VMEM((D, FF), jnp.float32),
            pltpu.VMEM((5, FF, 128), jnp.float32),
        ],
        compiler_params=kernel_params,
        cost_estimate=pl.CostEstimate(
            flops=12000000000, bytes_accessed=9000000, transcendentals=0
        ),
        name="newton",
    )(*operands)


def own_rows(kind, row, shard_length, gradient, update):
    def block_case(low, width):
        def run(gradient, update):
            start = (row, low)
            size = (shard_length // width, width)
            return tuple(
                lax.dynamic_slice(whole, start, size).reshape(-1) for whole in (gradient, update)
            )

        return run

    def tall_case(gradient, update):
        start = (0, row)
        size = (D, shard_length // D)
        return tuple(
            lax.dynamic_slice(whole, start, size).T.reshape(-1) for whole in (gradient, update)
        )

    cases = [
        block_case(0, FF),
        block_case(0, D),
        block_case(FF - D, D),
        block_case(D, KV_WIDTH),
        block_case(D + KV_WIDTH, KV_WIDTH),
        tall_case,
    ]
    return lax.switch(kind, cases, gradient, update)


CORE_SWAP = [(0, 1), (1, 0), (2, 3), (3, 2)]
CHIP_SWAP = [(0, 2), (2, 0), (1, 3), (3, 1)]
SIDE_SWAP = [(0, 1), (1, 0)]
END_SWAP = [(0, 3), (3, 0), (1, 2), (2, 1)]


def plane_swap(value, bit):
    axis, swap = (("ctx", CHIP_SWAP), ("half", SIDE_SWAP), ("ctx", CORE_SWAP))[bit]
    return lax.ppermute(value, axis, swap)


def low_sum(left, right):
    return (left.astype(jnp.float32) + right.astype(jnp.float32)).astype(jnp.bfloat16)


def low_total(first, others):
    total = first.astype(jnp.float32)
    for part in others:
        total = total + part.astype(jnp.float32)
    return total.astype(jnp.bfloat16)


def plane_gather(piece, swap):
    pieces = piece[None]
    for bit in range(2):
        pieces = jnp.concatenate([pieces, swap(pieces, bit)], axis=0)
    return (pieces, swap(pieces, 2))


def depth_shift(value, shift, targets):
    pairs = [(place, (place + shift) % 4) for place in range(4)]
    return lax.ppermute(value, "quarter", [pair for pair in pairs if pair[1] in targets])


def gather_weights(low, tie):
    if lax.axis_size("rep") > 1:
        full = lax.all_gather(low, EVERY, axis=0, tiled=True).reshape(4, D * FF)
        ctx = lax.axis_index("ctx")
        spot = lax.rem(ctx, 2) * 4 + lax.axis_index("half") * 2 + ctx // 2
        chunk = jnp.arange(CHUNKS, dtype=jnp.int32) ^ spot
        order = 4 * (chunk // 2 % 2) + 2 * (chunk % 2) + chunk // 4
        mixed = full[0].reshape(CHUNKS, -1, 128)[order]
        return (mixed[:4], mixed[4:]), [
            jnp.concatenate([full[1].reshape(D, FF), full[2].reshape(D, FF)], axis=1),
            full[3].reshape(FF, D),
        ]
    first = [lax.ppermute(low, "quarter", [(0, shift)]) for shift in range(1, 4)]
    mixed = pick_first((low, *first), tie)
    others = [
        lax.ppermute(low, "quarter", [(place, (place + shift) % 4) for place in range(1, 4)])
        for shift in range(1, 4)
    ]
    rest = [
        lax.all_gather(piece, PLANE, axis=0, tiled=True)
        for piece in pick_rest((low, *others), mixed)
    ]
    return plane_gather(mixed, plane_swap), rest


def per_device(tokens, lengths, weights, momentum, norm_gains, gain_first, gain_second, cotangent):
    ctx = lax.axis_index("ctx")
    chip = ctx // 2
    reps = lax.axis_size("rep")
    shard_length = weights.shape[0]
    flat_shape = (shard_length // 128, 128)
    lengths = lengths[:, 0]
    tokens = jnp.swapaxes(tokens, 1, 2)
    cotangent = jnp.swapaxes(cotangent, 1, 2)
    gain_columns = norm_gains.T

    tokens_1 = lax.ppermute(tokens[1], "ctx", END_SWAP)
    mixed_weights, (w_gate_up, w_down) = gather_weights(
        weights.reshape(flat_shape).astype(jnp.bfloat16), tokens_1
    )
    near = chip == 0

    def slots(first, second):
        return jnp.where(near, first, second), jnp.where(near, second, first)

    x0, x1 = slots(tokens[0], tokens_1)
    begin_rows, tables = [], []
    for micro, own_lengths in enumerate(slots(lengths[0], lengths[1])):
        own_places = own_block(micro) * TOK + jnp.arange(TOK, dtype=jnp.int32)
        offsets, begins = layout(own_lengths, own_places)
        begin_rows.append(begins.reshape(1, TOK))
        tables.append(rope_tables(offsets))

    q0, q1, keyvals, w_qkv, w_out, normed = project(
        *mixed_weights, x0, x1, gain_columns, tables
    )
    queries = (q0, q1)
    far = lax.ppermute(keyvals[0], "ctx", CHIP_SWAP)
    keyvals = (
        keyvals,
        lax.ppermute(keyvals, "ctx", CORE_SWAP),
        far,
        lax.ppermute(far, "ctx", CORE_SWAP),
    )
    low_momentum, moving = low_copies(momentum.reshape(flat_shape), cotangent[1], q1)
    mixed, log_totals = [], []
    for micro in range(2):
        mixed_one, log_total = attend_forward(
            micro, lengths, queries[micro], keyvals, begin_rows[micro], (low_momentum, norm_gains)[micro]
        )
        mixed.append(mixed_one)
        log_totals.append(log_total)
    cotangent_1 = lax.ppermute(moving, "ctx", END_SWAP)
    old = lax.all_gather(
        low_momentum,
        ("rep", "half", "ctx"),
        axis=0,
        tiled=True,
    )
    outs = mlp(
        x0,
        x1,
        cotangent,
        cotangent_1,
        [part.reshape(D, TOK) for part in mixed],
        w_out,
        w_gate_up,
        w_down,
        norm_gains[1:2],
    )
    result, result_1, grad_state, grad_mixed_0, grad_mixed_1 = outs[:5]
    keep, send, grad_w_out, gain_two_grad = outs[5:]
    returned = lax.ppermute(result_1, "ctx", END_SWAP)

    def back_pass(micro, grad_mixed, before, tie):
        return attend_back(
            micro,
            lengths,
            queries[micro],
            keyvals,
            begin_rows[micro],
            mixed[micro],
            log_totals[micro],
            grad_mixed.reshape(heads_shape),
            *tables[micro],
            before,
            tie,
        )

    got = plane_swap(send, 2)
    dq0, kept0, sent0 = back_pass(0, grad_mixed_0, (), norm_gains)
    keep, send = early_halves(keep, got, (dq0,))
    got = plane_swap(send, 1)
    dq1, kept1, sent = back_pass(1, grad_mixed_1, (sent0,), keep)
    keep, send, sent = early_halves(keep, got, (old, returned), sent)
    traded = lax.ppermute(sent, "ctx", CORE_SWAP)
    crossed = lax.ppermute(low_sum(kept1[1], traded[2]), "ctx", CHIP_SWAP)
    got = plane_swap(send, 0)
    late_keep, late_send, grad_qkv = projection_grads(
        normed,
        (dq0.reshape(D, TOK), dq1.reshape(D, TOK)),
        (kept0, kept1),
        traded,
        crossed,
        tables,
        grad_w_out,
        keep,
    )
    late_got = plane_swap(late_send, 2)
    late_keep, late_send = late_halves(late_keep, late_got, norm_gains)
    late_got = plane_swap(late_send, 1)
    grad_inputs, grad_inputs_1, gain_one_grad = input_grads(
        grad_qkv, w_qkv, x0, x1, grad_state, gain_columns, late_keep
    )
    early, late_keep, late_send = finish_early(keep, got, late_keep, late_got, gain_one_grad)
    gain_grad = jnp.concatenate([gain_one_grad[:, 0].reshape(1, D), gain_two_grad], axis=0)
    gain_grad = gain_grad + sum(
        lax.ppermute(gain_grad, "ctx", [(place, place ^ turn) for place in range(4)])
        for turn in range(1, 4)
    )
    piece, *turns = depth_turns(late_keep, plane_swap(late_send, 0), early, gain_grad)
    parts = [depth_shift(turn, shift, range(4)) for shift, turn in enumerate(turns, start=1)]
    gain_grad = gain_grad + sum(depth_shift(gain_grad, shift, range(4)) for shift in range(1, 4))
    old = lay_momentum(shard_length, old, piece)
    piece = tied_sum((piece, *parts), (old, gain_grad))
    if reps > 1:
        piece = lax.psum(piece, "rep")
        gain_grad = lax.psum(gain_grad, "rep")
    pieces = plane_gather(piece, plane_swap)
    gain_grad = gain_grad + plane_swap(gain_grad, 1)
    grad_inputs_1 = lax.ppermute(grad_inputs_1, "ctx", END_SWAP)

    shards = ()
    if flat_shape[0] % 8 == 0:
        shards = (weights.reshape(flat_shape), momentum.reshape(flat_shape))
    outs = newton(shard_length, pieces, old, shards)
    if len(shards) > 0:
        grad_shard, new_momentum, new_weights = [out.reshape(weights.shape) for out in outs]
    else:
        kind, start = own_kind(shard_length)
        grad_shard, update_shard = own_rows(kind, start, shard_length, *outs)
        new_momentum = momentum_decay * momentum + grad_shard
        new_weights = weights * (1.0 - matrix_rate * weight_decay) - matrix_rate * update_shard

    def placed(whole, part):
        whole = lax.dynamic_update_index_in_dim(whole, part.astype(jnp.float32), 1, 0)
        return jnp.swapaxes(whole, 1, 2)

    first_new = first_decay * gain_first + (1.0 - first_decay) * gain_grad
    second_new = second_decay * gain_second + (1.0 - second_decay) * gain_grad * gain_grad
    debiased_first_moment = first_new / (1.0 - first_decay**ADAM_STEP)
    corrected_second = second_new / (1.0 - second_decay**ADAM_STEP)
    new_gains = norm_gains * (
        1.0 - gain_rate * weight_decay
    ) - gain_rate * debiased_first_moment / (jnp.sqrt(corrected_second) + adam_epsilon)
    return (
        placed(result, returned),
        jnp.swapaxes(place_last(grad_inputs, grad_inputs_1, outs[-1]), 1, 2),
        grad_shard,
        new_momentum,
        new_weights,
        first_new,
        second_new,
        new_gains,
    )


def solution(mesh):
    devices = mesh.devices
    count = devices.size
    context = mesh.shape["ctx"]
    split = Mesh(
        devices.reshape(4, count // (8 * context), 2, context), ("quarter", "rep", "half", "ctx")
    )
    rows = P(None, EVERY, None)
    flat = P(EVERY)
    placed = (rows, P(None, ("quarter", "rep", "half"), None), flat, flat, P(), P(), P(), rows)
    return jax.shard_map(
        per_device,
        mesh=split,
        in_specs=placed,
        out_specs=(rows, rows, flat, flat, flat, P(), P(), P()),
        check_vma=False,
    )
```
